32 devices in a mesh: ctx: 32 (over z, y, x, core).
Axes of the slice: x: 2, y: 2, z: 4, core: 2. Of those that a mesh axis runs over, the one named last changes fastest.
Arguments:
- hidden_in: bfloat16 [16384, 768], P('ctx'), may hold values from -12 to 12
- block_pairs: int32 [32], replicated, may hold values from 0 to 15, as said below
- ln1_gain: bfloat16 [768], P('ctx'), may hold values from 0.5 to 1.5
- ln1_bias: bfloat16 [768], P('ctx'), may hold values from -1.25 to 1.25
- qkv_weight: bfloat16 [768, 2304], P('ctx'), may hold values from -0.21875 to 0.21875
- query_bias: bfloat16 [768], P('ctx'), may hold values from -1.25 to 1.25
- value_bias: bfloat16 [768], P('ctx'), may hold values from -1.25 to 1.25
- out_weight: bfloat16 [768, 768], P('ctx'), may hold values from -2.5 to 2.5
- out_bias: bfloat16 [768], P('ctx'), may hold values from -1.25 to 1.25
- ln2_gain: bfloat16 [768], P('ctx'), may hold values from 0.5 to 1.5
- ln2_bias: bfloat16 [768], P('ctx'), may hold values from -1.25 to 1.25
- fc_weight: bfloat16 [768, 3072], P('ctx'), may hold values from -0.21875 to 0.21875
- fc_bias: bfloat16 [3072], P('ctx'), may hold values from -1.25 to 1.25
- proj_weight: bfloat16 [3072, 768], P('ctx'), may hold values from -0.109375 to 0.109375
- proj_bias: bfloat16 [768], P('ctx'), may hold values from -1.25 to 1.25
- out_grad: bfloat16 [16384, 768], P('ctx'), may hold values from -12 to 12
Outputs:
- layer_out: bfloat16 [16384, 768], P('ctx')
- grad_hidden: bfloat16 [16384, 768], P('ctx')
- grad_ln1_gain: float32 [768], P('ctx')
- grad_ln1_bias: float32 [768], P('ctx')
- grad_qkv_weight: float32 [768, 2304], P('ctx')
- grad_query_bias: float32 [768], P('ctx')
- grad_value_bias: float32 [768], P('ctx')
- grad_out_weight: float32 [768, 768], P('ctx')
- grad_out_bias: float32 [768], P('ctx')
- grad_ln2_gain: float32 [768], P('ctx')
- grad_ln2_bias: float32 [768], P('ctx')
- grad_fc_weight: float32 [768, 3072], P('ctx')
- grad_fc_bias: float32 [3072], P('ctx')
- grad_proj_weight: float32 [3072, 768], P('ctx')
- grad_proj_bias: float32 [768], P('ctx')
The draws below stay inside these ranges and needn't reach their ends.
Inputs may be any that keep to these rules, and one draw needn't show every extreme that they name: `block_pairs`: entries 2 i and 2 i + 1 are equal, and each number of 0 to 15 appears exactly twice.
All inputs are finite; a program needn't handle non-finite values.
Results may differ from the reference program's by a relative error of at most 0.02.
Values may be sent and summed in bfloat16 or wider, within the bound.
A program may use at most 768 MiB of HBM per device.

```python
import math
import jax
import jax.numpy as jnp
from jax import lax

D = 768
HEADS = 12
HEAD_DIM = 64
FF = 3072
SEQS = 4
UNIT = 128
PAIRS = 16
SEQLEN = 4096
TOKENS = 16384
N_CTX = 32


def draw_block_pairs(key, part):
    order = jax.random.permutation(jax.random.fold_in(key, 7), PAIRS)
    return jnp.repeat(order.astype(jnp.int32), 2)


def with_spikes(array, rng, source, target, shards_of, factor):
    def block_of(axis_at):
        return (jnp.arange(array.shape[axis_at]) // (array.shape[axis_at] // shards_of)).reshape((-1,) + (1,) * (array.ndim - 1 - axis_at))

    first = jax.random.permutation(rng, shards_of)[block_of(target)]
    other_side = (block_of(target) + shards_of // 2) % shards_of
    return jnp.where((block_of(source) == first) | (block_of(source) == other_side), factor * array, array)


def level_of(stream_key, extent, cuts, smallest, largest):
    def one(position, shards_of):
        draws = jax.random.uniform(jax.random.fold_in(jax.random.fold_in(stream_key, 6), position), (shards_of,), jnp.float32, smallest / len(cuts), largest / len(cuts))
        return jnp.repeat(jnp.exp(draws), extent[position] // shards_of).reshape((-1,) + (1,) * (len(extent) - position - 1))

    factor_of = one(*cuts[0])
    for cut in cuts[1:]:
        factor_of = factor_of * one(*cut)
    return factor_of


def noise(stream_key, extent, scale, bound, cuts=(), held_as=jnp.bfloat16):
    array = scale * jax.random.normal(stream_key, extent, jnp.float32)
    if cuts:
        array = array * level_of(stream_key, extent, cuts, -0.22, 0.18)
    return jnp.clip(array, -bound, bound).astype(held_as)


def noise_with(key, dims, deviation, most, split, heavy, dtype=jnp.bfloat16):
    values = deviation * jax.random.normal(key, dims, jnp.float32)
    if split:
        values = values * level_of(key, dims, split, -0.22, 0.18)
    return jnp.clip(with_spikes(values, jax.random.fold_in(key, 3), *heavy), -most, most).astype(dtype)


def setup_inputs(seed: int = 0) -> dict:
    key_of = jax.random.split(jax.random.key(seed), 17)
    hidden_in = noise_with(key_of[0], (TOKENS, D), 1.0, 12.0, ((0, 32),), (0, 1, 32, 2.75))
    block_pairs = draw_block_pairs(jax.random.fold_in(key_of[16], 71), 0)
    ln1_gain = jnp.clip(1.0 + 0.1 * jax.random.normal(key_of[2], (D,), jnp.float32), 0.5, 1.5).astype(jnp.bfloat16)
    ln1_bias = noise(key_of[3], (D,), 0.2, 1.25, ((0, 32),))
    qkv_weight = noise(key_of[4], (D, 3 * D), D ** -0.5, 0.21875, ((0, 32),))
    query_bias = noise(key_of[5], (D,), 0.2, 1.25, ((0, 32),))
    value_bias = noise(key_of[6], (D,), 0.2, 1.25, ((0, 32),))
    out_weight = noise(key_of[7], (D, D), (max(2, D * 32 // (UNIT * N_CTX))) ** -0.5, 2.5, ((0, 32),))
    out_bias = noise(key_of[8], (D,), 0.2, 1.25, ((0, 32),))
    ln2_gain = jnp.clip(1.0 + 0.1 * jax.random.normal(key_of[9], (D,), jnp.float32), 0.5, 1.5).astype(jnp.bfloat16)
    ln2_bias = noise(key_of[10], (D,), 0.2, 1.25, ((0, 32),))
    fc_weight = noise(key_of[11], (D, FF), D ** -0.5, 0.21875, ((0, 32),))
    fc_bias = noise(key_of[12], (FF,), 0.2, 1.25, ((0, 32),))
    proj_weight = noise(key_of[13], (FF, D), FF ** -0.5, 0.109375, ((0, 32),))
    proj_bias = noise(key_of[14], (D,), 0.2, 1.25, ((0, 32),))
    out_grad = noise_with(key_of[15], (TOKENS, D), 1.0, 12.0, ((0, 32),), (0, 1, 32, 2.75))
    return dict(hidden_in=hidden_in, block_pairs=block_pairs, ln1_gain=ln1_gain, ln1_bias=ln1_bias, qkv_weight=qkv_weight, query_bias=query_bias, value_bias=value_bias, out_weight=out_weight, out_bias=out_bias, ln2_gain=ln2_gain, ln2_bias=ln2_bias, fc_weight=fc_weight, fc_bias=fc_bias, proj_weight=proj_weight, proj_bias=proj_bias, out_grad=out_grad)


@jax.custom_vjp
def low(v):
    return lax.optimization_barrier(v.astype(jnp.bfloat16)).astype(jnp.float32)

@jax.custom_vjp
def low_back(v):
    return v

def low_keep(v):
    return (low(v), None)

def low_pass(kept, grad):
    return (grad,)

def back_keep(v):
    return (v, None)

def back_low(kept, grad):
    return (low(grad),)
low.defvjp(low_keep, low_pass)
low_back.defvjp(back_keep, back_low)

def layer_norm(values, gain, bias):
    center = values - lax.optimization_barrier(jnp.mean(values, axis=-1, keepdims=True))
    spread_sq = lax.optimization_barrier(jnp.mean(center * center, axis=-1, keepdims=True))
    return center * lax.rsqrt(spread_sq + 1e-05) * gain + bias

def matmul_high(left, right):
    return jnp.dot(left, right, precision=lax.Precision.HIGHEST, preferred_element_type=jnp.float32)

def reference(hidden_in, block_pairs, ln1_gain, ln1_bias, qkv_weight, query_bias, value_bias, out_weight, out_bias, ln2_gain, ln2_bias, fc_weight, fc_bias, proj_weight, proj_bias, out_grad):
    device_blocks = block_pairs.astype(jnp.int32)
    sequence_rows = []
    for seq_index in range(SEQS):
        if seq_index % 2 == 0:
            one_seq = device_blocks
        else:
            one_seq = PAIRS - 1 - device_blocks
        sequence_rows.append(jnp.repeat(one_seq, UNIT))
    seq_blocks = jnp.stack(sequence_rows).astype(jnp.int32)
    query_rows = min(512, SEQLEN)
    score_scale = 1.0 / math.sqrt(HEAD_DIM)

    def regroup(tensor):
        shaped = tensor.reshape(N_CTX, SEQS, UNIT, HEADS, HEAD_DIM).transpose(1, 0, 2, 3, 4)
        return shaped.reshape(SEQS, SEQLEN, HEADS, HEAD_DIM)

    def ungroup(tensor):
        return tensor.reshape(SEQS, N_CTX, UNIT, D).transpose(1, 0, 2, 3).reshape(TOKENS, D)

    def attend_one(packed):
        queries, keys, values, blocks = packed

        def block_rows(inner):
            query_block, block_ids = inner
            scores = jnp.einsum('qhe,khe->hqk', query_block, keys, precision=lax.Precision.HIGHEST) * score_scale
            scores = low_back(scores)
            visible = blocks[None, :] <= block_ids[:, None]
            scores = jnp.where(visible[None], scores, -1e+30)
            probs = low(jax.nn.softmax(scores, axis=-1))
            return jnp.einsum('hqk,khe->qhe', probs, values, precision=lax.Precision.HIGHEST)
        outcome = lax.map(jax.checkpoint(block_rows), (queries.reshape(SEQLEN // query_rows, query_rows, HEADS, HEAD_DIM), blocks.reshape(SEQLEN // query_rows, query_rows)))
        return outcome.reshape(SEQLEN, HEADS, HEAD_DIM)

    def forward(inputs, gain_one, bias_one, w_qkv, b_query, b_value, w_out, b_out, gain_two, bias_two, w_fc, b_fc, w_proj, b_proj):
        normed = low(layer_norm(inputs, gain_one, bias_one))
        mixed_proj = matmul_high(normed, w_qkv)
        queries = low_back(low(mixed_proj[:, :D] + b_query))
        keys = low_back(low(mixed_proj[:, D:2 * D]))
        values = low_back(low(mixed_proj[:, 2 * D:] + b_value))
        attended = lax.map(attend_one, (regroup(queries), regroup(keys), regroup(values), seq_blocks))
        attended = low_back(low(ungroup(attended.reshape(SEQS, SEQLEN, D))))
        branch = low_back(matmul_high(attended, w_out) + b_out)
        middle = inputs + branch
        normed_two = low(layer_norm(middle, gain_two, bias_two))
        pre_act = low_back(matmul_high(normed_two, w_fc) + b_fc)
        activation = low(jax.nn.gelu(pre_act, approximate=True))
        branch_two = low_back(matmul_high(activation, w_proj) + b_proj)
        return middle + branch_two
    primals = (hidden_in.astype(jnp.float32), ln1_gain.astype(jnp.float32), ln1_bias.astype(jnp.float32), qkv_weight.astype(jnp.float32), query_bias.astype(jnp.float32), value_bias.astype(jnp.float32), out_weight.astype(jnp.float32), out_bias.astype(jnp.float32), ln2_gain.astype(jnp.float32), ln2_bias.astype(jnp.float32), fc_weight.astype(jnp.float32), fc_bias.astype(jnp.float32), proj_weight.astype(jnp.float32), proj_bias.astype(jnp.float32))
    layer_out, pullback = jax.vjp(forward, primals[0], primals[1], primals[2], primals[3], primals[4], primals[5], primals[6], primals[7], primals[8], primals[9], primals[10], primals[11], primals[12], primals[13])
    grads = pullback(out_grad.astype(jnp.float32))
    return (layer_out.astype(jnp.bfloat16), grads[0].astype(jnp.bfloat16), grads[1], grads[2], grads[3], grads[4], grads[5], grads[6], grads[7], grads[8], grads[9], grads[10], grads[11], grads[12], grads[13])
```

```python
from functools import partial
import math

import jax
import jax.numpy as jnp
from jax import lax
from jax.sharding import PartitionSpec as P
from jax.experimental import pallas as pl
from jax.experimental.pallas import tpu as pltpu
from jax.sharding import Mesh

HEADS = 12
SEQS = 4


NEG = -1e30


def from_partner(value, axis, bit):
    return lax.ppermute(value, axis, [(i, i ^ 1 << bit) for i in range(lax.axis_size(axis))])


def layer_norm(values, gain, bias):
    center = values - jnp.mean(values, axis=-1, keepdims=True)
    spread_sq = jnp.mean(center * center, axis=-1, keepdims=True)
    return center * lax.rsqrt(spread_sq + 1e-05) * gain + bias


def gelu_tanh(values):
    return jax.nn.gelu(values, approximate=True)


def heads_of(tensor, head_count):
    return tensor.reshape(tensor.shape[:-1] + (head_count, tensor.shape[-1] // head_count))


def pick_own(owned, chosen):
    selector = chosen.reshape((1, -1) + (1,) * (owned.ndim - 2))
    return jnp.where(selector, owned[:, 0:1], owned[:, 1:2])


def pick_piece(piece, chosen):
    selector = chosen.reshape((1, -1) + (1,) * (piece.ndim - 3))
    return jnp.where(selector, piece[:, 0], piece[:, 1])


def parity_masks(chosen, usable):
    return jnp.stack([chosen & usable, jnp.logical_not(chosen) & usable])


def spread(values, parity):
    shaped = parity.reshape((1,) + parity.shape + (1,) * (values.ndim - 2))
    return jnp.sum(jnp.where(shaped, values[:, None], 0.0), axis=2)


def group_loop(pieces, unit_rows, table, stepper, carried):
    piece_rows = pieces[0].shape[2]
    group_size = min(unit_rows, piece_rows)
    group_count = piece_rows // group_size
    batch_groups = math.gcd(group_count, max(1, 1024 // group_size))
    turn_count = group_count // batch_groups
    shaped = tuple(
        (
            item.reshape(item.shape[:2] + (group_count, group_size) + item.shape[3:])
            for item in pieces
        )
    )
    device_ids = jnp.arange(group_count, dtype=jnp.int32) * group_size // unit_rows
    table_size = table.shape[0]
    blocks = jnp.sum(
        jnp.where(
            device_ids[:, None] == jnp.arange(table_size, dtype=jnp.int32)[None, :],
            table[None, :],
            0,
        ),
        axis=1,
    )

    def one_turn(position, current):
        pieces_now = tuple(
            (
                lax.dynamic_slice_in_dim(item, position * batch_groups, batch_groups, 2)
                for item in shaped
            )
        )
        chosen = lax.dynamic_slice_in_dim(blocks, position * batch_groups, batch_groups, 0)
        return stepper(current, pieces_now, chosen)

    return lax.fori_loop(0, turn_count, one_turn, carried)


def attend_step(q_heads, my_block, score_scale, head_count, carried, pieces_now, chosen):
    key_piece = heads_of(pieces_now[0], head_count)
    value_piece = heads_of(pieces_now[1], head_count)
    earlier = chosen < my_block
    usable = chosen != my_block
    parity = parity_masks(earlier, usable)
    query_sel = pick_own(q_heads, earlier)
    key_sel = pick_piece(key_piece, earlier)
    value_sel = pick_piece(value_piece, earlier)
    scores = (
        jnp.einsum("jgqhe,jgkhe->jghqk", query_sel, key_sel, preferred_element_type=jnp.float32)
        * score_scale
    )
    usable_mask = usable.reshape(1, -1, 1, 1, 1)
    scores = jnp.where(usable_mask, scores, NEG)
    old_max, old_total, old_sum = carried
    group_max = jnp.max(scores, axis=-1)
    candidate = jnp.max(jnp.where(parity.reshape(1, 2, -1, 1, 1), group_max[:, None], NEG), axis=2)
    new_max = jnp.maximum(old_max, candidate)
    max_sel = pick_own(new_max, earlier)
    weights_exp = jnp.where(usable_mask, jnp.exp(scores - max_sel[..., None]), 0.0)
    moved = jnp.einsum(
        "jghqk,jgkhe->jgqhe",
        weights_exp.astype(jnp.bfloat16),
        value_sel,
        preferred_element_type=jnp.float32,
    )
    factor = jnp.exp(old_max - new_max)
    new_total = old_total * factor + spread(jnp.sum(weights_exp, axis=-1), parity)
    new_sum = old_sum * jnp.swapaxes(factor, 2, 3)[..., None] + spread(moved, parity)
    return (new_max, new_total, new_sum)


def query_grad_step(
    q_heads,
    grad_heads,
    lse_heads,
    delta_heads,
    my_block,
    score_scale,
    head_count,
    carried,
    pieces_now,
    chosen,
):
    key_piece = heads_of(pieces_now[0], head_count)
    value_piece = heads_of(pieces_now[1], head_count)
    earlier = chosen < my_block
    usable = chosen != my_block
    parity = parity_masks(earlier, usable)
    query_sel = pick_own(q_heads, earlier)
    grad_sel = pick_own(grad_heads, earlier)
    lse_sel = pick_own(lse_heads, earlier)
    delta_sel = pick_own(delta_heads, earlier)
    key_sel = pick_piece(key_piece, earlier)
    value_sel = pick_piece(value_piece, earlier)
    scores = (
        jnp.einsum("jgqhe,jgkhe->jghqk", query_sel, key_sel, preferred_element_type=jnp.float32)
        * score_scale
    )
    usable_mask = usable.reshape(1, -1, 1, 1, 1)
    probabilities = jnp.where(usable_mask, jnp.exp(scores - lse_sel[..., None]), 0.0)
    grad_probs = jnp.einsum(
        "jgqhe,jgkhe->jghqk", grad_sel, value_sel, preferred_element_type=jnp.float32
    )
    grad_scores = (probabilities * (grad_probs - delta_sel[..., None])).astype(jnp.bfloat16)
    term = (
        jnp.einsum("jghqk,jgkhe->jgqhe", grad_scores, key_sel, preferred_element_type=jnp.float32)
        * score_scale
    )
    return carried + spread(term, parity)


def key_grad_step(k_heads, v_heads, my_block, score_scale, head_count, carried, pieces_now, chosen):
    query_piece = heads_of(pieces_now[0], head_count)
    grad_piece = heads_of(pieces_now[1], head_count)
    later = my_block < chosen
    usable = chosen != my_block
    parity = parity_masks(later, usable)
    query_sel = pick_piece(query_piece, later)
    grad_sel = pick_piece(grad_piece, later)
    lse_sel = jnp.swapaxes(pick_piece(pieces_now[2], later), 2, 3)
    delta_sel = jnp.swapaxes(pick_piece(pieces_now[3], later), 2, 3)
    key_sel = pick_own(k_heads, later)
    value_sel = pick_own(v_heads, later)
    scores = (
        jnp.einsum("jgqhe,jgkhe->jghqk", query_sel, key_sel, preferred_element_type=jnp.float32)
        * score_scale
    )
    usable_mask = usable.reshape(1, -1, 1, 1, 1)
    probabilities = jnp.where(usable_mask, jnp.exp(scores - lse_sel[..., None]), 0.0)
    grad_probs = jnp.einsum(
        "jgqhe,jgkhe->jghqk", grad_sel, value_sel, preferred_element_type=jnp.float32
    )
    grad_scores = (probabilities * (grad_probs - delta_sel[..., None])).astype(jnp.bfloat16)
    key_term = (
        jnp.einsum("jghqk,jgqhe->jgkhe", grad_scores, query_sel, preferred_element_type=jnp.float32)
        * score_scale
    )
    value_term = jnp.einsum(
        "jghqk,jgqhe->jgkhe",
        probabilities.astype(jnp.bfloat16),
        grad_sel,
        preferred_element_type=jnp.float32,
    )
    return (carried[0] + spread(key_term, parity), carried[1] + spread(value_term, parity))


def shards(
    hidden_in,
    block_pairs,
    ln1_gain,
    ln1_bias,
    qkv_weight,
    query_bias,
    value_bias,
    out_weight,
    out_bias,
    ln2_gain,
    ln2_bias,
    fc_weight,
    fc_bias,
    proj_weight,
    proj_bias,
    out_grad,
):
    params = (
        ln1_gain,
        ln1_bias,
        qkv_weight,
        query_bias,
        value_bias,
        out_weight,
        out_bias,
        ln2_gain,
        ln2_bias,
        fc_weight,
        fc_bias,
        proj_weight,
        proj_bias,
    )
    gathered = (
        lax.all_gather(params[0], "ctx", axis=0, tiled=True),
        lax.all_gather(params[1], "ctx", axis=0, tiled=True),
        lax.all_gather(params[2], "ctx", axis=0, tiled=True),
        lax.all_gather(params[3], "ctx", axis=0, tiled=True),
        lax.all_gather(params[4], "ctx", axis=0, tiled=True),
        lax.all_gather(params[5], "ctx", axis=0, tiled=True),
        lax.all_gather(params[6], "ctx", axis=0, tiled=True),
        lax.all_gather(params[7], "ctx", axis=0, tiled=True),
        lax.all_gather(params[8], "ctx", axis=0, tiled=True),
        lax.all_gather(params[9], "ctx", axis=0, tiled=True),
        lax.all_gather(params[10], "ctx", axis=0, tiled=True),
        lax.all_gather(params[11], "ctx", axis=0, tiled=True),
        lax.all_gather(params[12], "ctx", axis=0, tiled=True),
    )
    (
        gain_one,
        bias_one,
        w_qkv,
        b_query,
        b_value,
        w_out,
        b_out,
        gain_two,
        bias_two,
        w_fc,
        b_fc,
        w_proj,
        b_proj,
    ) = gathered
    device = lax.axis_index("ctx")
    partner = device + 1 - 2 * (device % 2)
    row_count = hidden_in.shape[0]
    model_width = hidden_in.shape[1]
    unit_rows = row_count // SEQS
    halves = SEQS // 2
    head_count = HEADS
    head_size = model_width // head_count
    score_scale = 1.0 / math.sqrt(head_size)
    my_block = block_pairs[device]
    seq_shape = (halves, 2, unit_rows, model_width)
    head_shape = (halves, 2, unit_rows, head_count, head_size)
    inputs = hidden_in.astype(jnp.float32)
    normed = layer_norm(inputs, gain_one.astype(jnp.float32), bias_one.astype(jnp.float32)).astype(
        jnp.bfloat16
    )
    mixed_proj = jnp.dot(normed, w_qkv, preferred_element_type=jnp.float32)
    queries = (mixed_proj[:, :model_width] + b_query.astype(jnp.float32)).astype(jnp.bfloat16)
    key_rows = mixed_proj[:, model_width : 2 * model_width].astype(jnp.bfloat16)
    value_rows = (mixed_proj[:, 2 * model_width :] + b_value.astype(jnp.float32)).astype(
        jnp.bfloat16
    )
    q_seq = queries.reshape(seq_shape)
    k_seq = key_rows.reshape(seq_shape)
    v_seq = value_rows.reshape(seq_shape)
    q_heads = queries.reshape(head_shape)
    k_heads = key_rows.reshape(head_shape)
    v_heads = value_rows.reshape(head_shape)
    far_keys, far_values = from_partner((k_seq, v_seq), "ctx", 0)
    near_keys = jnp.concatenate([k_heads, heads_of(far_keys, head_count)], axis=2)
    near_values = jnp.concatenate([v_heads, heads_of(far_values, head_count)], axis=2)
    scores = (
        jnp.einsum("jpqhe,jpkhe->jphqk", q_heads, near_keys, preferred_element_type=jnp.float32)
        * score_scale
    )
    row_max = jnp.max(scores, axis=-1)
    weights_exp = jnp.exp(scores - row_max[..., None])
    row_total = jnp.sum(weights_exp, axis=-1)
    summed = jnp.einsum(
        "jphqk,jpkhe->jpqhe",
        weights_exp.astype(jnp.bfloat16),
        near_values,
        preferred_element_type=jnp.float32,
    )
    forward_stepper = partial(attend_step, q_heads, my_block, score_scale, head_count)
    row_max, row_total, summed = group_loop(
        (
            lax.all_gather(k_seq, "ctx", axis=2, tiled=True),
            lax.all_gather(v_seq, "ctx", axis=2, tiled=True),
        ),
        unit_rows,
        block_pairs,
        forward_stepper,
        (row_max, row_total, summed),
    )
    attended = summed / jnp.swapaxes(row_total, 2, 3)[..., None]
    log_total = row_max + jnp.log(row_total)
    att_low = attended.reshape(row_count, model_width).astype(jnp.bfloat16)
    branch = jnp.dot(att_low, w_out, preferred_element_type=jnp.float32) + b_out.astype(jnp.float32)
    middle = inputs + branch
    normed_two = layer_norm(
        middle, gain_two.astype(jnp.float32), bias_two.astype(jnp.float32)
    ).astype(jnp.bfloat16)
    pre_act = jnp.dot(normed_two, w_fc, preferred_element_type=jnp.float32) + b_fc.astype(
        jnp.float32
    )
    activation = gelu_tanh(pre_act).astype(jnp.bfloat16)
    result = (
        middle
        + jnp.dot(activation, w_proj, preferred_element_type=jnp.float32)
        + b_proj.astype(jnp.float32)
    )
    layer_out = result.astype(jnp.bfloat16)
    grad_out = out_grad.astype(jnp.float32)
    grad_proj = jnp.dot(activation.T, out_grad, preferred_element_type=jnp.float32)
    grad_bproj = jnp.sum(grad_out, axis=0)
    grad_activ = jnp.dot(out_grad, w_proj.T, preferred_element_type=jnp.float32)
    _, gelu_back = jax.vjp(gelu_tanh, pre_act)
    grad_pre = gelu_back(grad_activ)[0].astype(jnp.bfloat16)
    grad_fc = jnp.dot(normed_two.T, grad_pre, preferred_element_type=jnp.float32)
    grad_bfc = jnp.sum(grad_pre.astype(jnp.float32), axis=0)
    grad_normed_two = jnp.dot(grad_pre, w_fc.T, preferred_element_type=jnp.float32)
    _, norm_back_two = jax.vjp(
        layer_norm, middle, gain_two.astype(jnp.float32), bias_two.astype(jnp.float32)
    )
    grad_middle, grad_gain_two, grad_bias_two = norm_back_two(grad_normed_two)
    grad_middle = grad_middle + grad_out
    grad_branch = grad_middle.astype(jnp.bfloat16)
    grad_wout = jnp.dot(att_low.T, grad_branch, preferred_element_type=jnp.float32)
    grad_bout = jnp.sum(grad_branch.astype(jnp.float32), axis=0)
    grad_att = jnp.dot(grad_branch, w_out.T, preferred_element_type=jnp.float32).astype(
        jnp.bfloat16
    )
    grad_seq = grad_att.reshape(seq_shape)
    grad_heads = grad_att.reshape(head_shape)
    row_delta = jnp.sum(grad_heads.astype(jnp.float32) * attended, axis=-1)
    delta_heads = jnp.swapaxes(row_delta, 2, 3)
    all_lse, all_delta = (
        lax.all_gather(jnp.swapaxes(log_total, 2, 3), "ctx", axis=2, tiled=True),
        lax.all_gather(row_delta, "ctx", axis=2, tiled=True),
    )
    partner_lse = jnp.swapaxes(
        lax.dynamic_slice_in_dim(all_lse, partner * unit_rows, unit_rows, 2), 2, 3
    )
    partner_delta = jnp.swapaxes(
        lax.dynamic_slice_in_dim(all_delta, partner * unit_rows, unit_rows, 2), 2, 3
    )
    far_queries, far_grads = from_partner((q_seq, grad_seq), "ctx", 0)
    near_queries = jnp.concatenate([q_heads, heads_of(far_queries, head_count)], axis=2)
    near_grads = jnp.concatenate([grad_heads, heads_of(far_grads, head_count)], axis=2)
    near_lse = jnp.concatenate([log_total, partner_lse], axis=3)
    near_delta = jnp.concatenate([delta_heads, partner_delta], axis=3)
    local_scores = (
        jnp.einsum(
            "jpqhe,jpkhe->jphqk", near_queries, near_keys, preferred_element_type=jnp.float32
        )
        * score_scale
    )
    probabilities = jnp.exp(local_scores - near_lse[..., None])
    grad_probs = jnp.einsum(
        "jpqhe,jpkhe->jphqk", near_grads, near_values, preferred_element_type=jnp.float32
    )
    grad_scores = (probabilities * (grad_probs - near_delta[..., None])).astype(jnp.bfloat16)
    grad_q_local = (
        jnp.einsum(
            "jphqk,jpkhe->jpqhe",
            grad_scores[:, :, :, :unit_rows, :],
            near_keys,
            preferred_element_type=jnp.float32,
        )
        * score_scale
    )
    grad_k_local = (
        jnp.einsum(
            "jphqk,jpqhe->jpkhe",
            grad_scores[..., :unit_rows],
            near_queries,
            preferred_element_type=jnp.float32,
        )
        * score_scale
    )
    grad_v_local = jnp.einsum(
        "jphqk,jpqhe->jpkhe",
        probabilities.astype(jnp.bfloat16)[..., :unit_rows],
        near_grads,
        preferred_element_type=jnp.float32,
    )
    query_stepper = partial(
        query_grad_step,
        q_heads,
        grad_heads,
        log_total,
        delta_heads,
        my_block,
        score_scale,
        head_count,
    )
    key_stepper = partial(key_grad_step, k_heads, v_heads, my_block, score_scale, head_count)

    def query_piece(carried, pieces, offset):
        return group_loop(pieces, unit_rows, block_pairs, query_stepper, carried)

    def key_piece(carried, pieces, offset):
        return group_loop(
            (pieces[0], pieces[1], all_lse, all_delta), unit_rows, block_pairs, key_stepper, carried
        )

    grad_q_all = query_piece(
        grad_q_local,
        (
            lax.all_gather(k_seq, "ctx", axis=2, tiled=True),
            lax.all_gather(v_seq, "ctx", axis=2, tiled=True),
        ),
        jnp.int32(0),
    )
    grad_k_all, grad_v_all = key_piece(
        (grad_k_local, grad_v_local),
        (
            lax.all_gather(q_seq, "ctx", axis=2, tiled=True),
            lax.all_gather(grad_seq, "ctx", axis=2, tiled=True),
        ),
        jnp.int32(0),
    )
    grad_queries = grad_q_all.reshape(row_count, model_width).astype(jnp.bfloat16)
    grad_keys = grad_k_all.reshape(row_count, model_width).astype(jnp.bfloat16)
    grad_values = grad_v_all.reshape(row_count, model_width).astype(jnp.bfloat16)
    grad_mixed = jnp.concatenate([grad_queries, grad_keys, grad_values], axis=1)
    grad_qkv = jnp.dot(normed.T, grad_mixed, preferred_element_type=jnp.float32)
    grad_bquery = jnp.sum(grad_queries.astype(jnp.float32), axis=0)
    grad_bvalue = jnp.sum(grad_values.astype(jnp.float32), axis=0)
    grad_normed = jnp.dot(grad_mixed, w_qkv.T, preferred_element_type=jnp.float32)
    _, norm_back_one = jax.vjp(
        layer_norm, inputs, gain_one.astype(jnp.float32), bias_one.astype(jnp.float32)
    )
    grad_inputs, grad_gain_one, grad_bias_one = norm_back_one(grad_normed)
    grad_hidden = (grad_inputs + grad_middle).astype(jnp.bfloat16)
    totals = (
        lax.psum_scatter(grad_gain_one, "ctx", scatter_dimension=0, tiled=True),
        lax.psum_scatter(grad_bias_one, "ctx", scatter_dimension=0, tiled=True),
        lax.psum_scatter(grad_qkv, "ctx", scatter_dimension=0, tiled=True),
        lax.psum_scatter(grad_bquery, "ctx", scatter_dimension=0, tiled=True),
        lax.psum_scatter(grad_bvalue, "ctx", scatter_dimension=0, tiled=True),
        lax.psum_scatter(grad_wout, "ctx", scatter_dimension=0, tiled=True),
        lax.psum_scatter(grad_bout, "ctx", scatter_dimension=0, tiled=True),
        lax.psum_scatter(grad_gain_two, "ctx", scatter_dimension=0, tiled=True),
        lax.psum_scatter(grad_bias_two, "ctx", scatter_dimension=0, tiled=True),
        lax.psum_scatter(grad_fc, "ctx", scatter_dimension=0, tiled=True),
        lax.psum_scatter(grad_bfc, "ctx", scatter_dimension=0, tiled=True),
        lax.psum_scatter(grad_proj, "ctx", scatter_dimension=0, tiled=True),
        lax.psum_scatter(grad_bproj, "ctx", scatter_dimension=0, tiled=True),
    )
    return (
        layer_out,
        grad_hidden,
        totals[0],
        totals[1],
        totals[2],
        totals[3],
        totals[4],
        totals[5],
        totals[6],
        totals[7],
        totals[8],
        totals[9],
        totals[10],
        totals[11],
        totals[12],
    )


HD = 64


def attend_kernel(inv, q_ref, k_ref, v_ref, o_ref, lse_ref, qt, ks, vt):
    W = q_ref.shape[1]
    nh = W // HD
    npair = inv.shape[0]
    U = q_ref.shape[0] // npair
    B = k_ref.shape[0] // npair
    TQ, TK = 2 * U, 2 * B

    @pl.loop(0, npair)
    def _(i):
        p = inv[i]
        qc = q_ref[pl.ds(p * U, U), :]
        qt[:, pl.ds(pl.multiple_of(i * U, U), U)] = qc.T
        kc = k_ref[pl.ds(p * B, B), :]
        for h in range(nh):
            ks[h, pl.ds(i * B, B), :] = kc[:, h * HD:(h + 1) * HD]
        vc = v_ref[pl.ds(p * B, B), :]
        vct = vc.T
        for h in range(nh):
            vt[h, 0:HD, pl.ds(pl.multiple_of(i * B, B), B)] = vct[h * HD:(h + 1) * HD]
            vt[h, HD:, pl.ds(pl.multiple_of(i * B, B), B)] = jnp.ones((vt.shape[1] - HD, B), vt.dtype)

    def tile(m, c, carry, masked):
        out = []
        for h in range(nh):
            mx, acc = carry[h]
            qh = qt[h * HD:(h + 1) * HD, pl.ds(pl.multiple_of(m * TQ, TQ), TQ)]
            kh = ks[h, pl.ds(pl.multiple_of(c * TK, TK), TK), :]
            s = jnp.dot(kh, qh, preferred_element_type=jnp.float32)
            if masked:
                row = lax.broadcasted_iota(jnp.int32, s.shape, 0)
                col = lax.broadcasted_iota(jnp.int32, s.shape, 1)
                s = jnp.where((row >= B) & (col < U), NEG, s)
            new = jnp.maximum(mx, jnp.max(s, axis=0, keepdims=True))
            p = jnp.exp(s - new).astype(jnp.bfloat16)
            vh = vt[h, :, pl.ds(pl.multiple_of(c * TK, TK), TK)]
            acc = acc * jnp.exp(mx - new) + jnp.dot(vh, p, preferred_element_type=jnp.float32)
            out.append((new, acc))
        return tuple(out)

    @pl.loop(0, npair // 2)
    def _(m):
        init = tuple((jnp.full((1, TQ), NEG, jnp.float32), jnp.zeros((vt.shape[1], TQ), jnp.float32)) for _ in range(nh))
        carry = lax.fori_loop(0, m, lambda c, x: tile(m, c, x, False), init)
        carry = tile(m, m, carry, True)
        outs = []
        for h in range(nh):
            mx, acc = carry[h]
            tot = acc[HD:HD + 1]
            outs.append(acc[:HD] / tot)
            lse_ref[h:h + 1, pl.ds(pl.multiple_of(m * TQ, TQ), TQ)] = mx + jnp.log(tot)
        o = jnp.concatenate(outs, axis=0).T
        for half in range(2):
            o_ref[pl.ds(inv[2 * m + half] * U, U), :] = o[half * U:(half + 1) * U]


def attend(inv, q, k, v):
    R, W = q.shape
    K = k.shape[0]
    nh = W // HD
    return pl.pallas_call(
        attend_kernel,
        grid_spec=pltpu.PrefetchScalarGridSpec(
            num_scalar_prefetch=1, grid=(),
            in_specs=[pl.BlockSpec(memory_space=pltpu.VMEM)] * 3,
            out_specs=[pl.BlockSpec(memory_space=pltpu.VMEM)] * 2,
            scratch_shapes=[
                pltpu.VMEM((W, R), jnp.bfloat16),
                pltpu.VMEM((nh, K, HD), jnp.bfloat16),
                pltpu.VMEM((nh, HD + 16, K), jnp.bfloat16),
            ]),
        out_shape=[jax.ShapeDtypeStruct((R, W), jnp.float32), jax.ShapeDtypeStruct((8, R), jnp.float32)],
        compiler_params=pltpu.CompilerParams(vmem_limit_bytes=56 << 20),
        name="attend",
    )(inv, q, k, v)


def attend_back_kernel(inv, q_ref, k_ref, v_ref, g_ref, o_ref, lse_ref, dq_ref, dk_ref, dv_ref,
                       qt, gt, qx, gx, ks, vs, kt, delta, dkv):
    W = q_ref.shape[1]
    nh = W // HD
    npair = inv.shape[0]
    U = q_ref.shape[0] // npair
    B = k_ref.shape[0] // npair
    TQ, TK = 2 * U, 2 * B

    @pl.loop(0, npair)
    def _(i):
        p = inv[i]
        qc = q_ref[pl.ds(p * U, U), :]
        gc = g_ref[pl.ds(p * U, U), :]
        oc = o_ref[pl.ds(p * U, U), :]
        cols = pl.ds(pl.multiple_of(i * U, U), U)
        qt[:, cols] = qc.T
        gt[:, cols] = gc.T
        prod = (oc * gc.astype(jnp.float32)).T
        zero = jnp.zeros((U, HD), jnp.bfloat16)
        for h in range(nh):
            delta[h:h + 1, cols] = jnp.sum(prod[h * HD:(h + 1) * HD], axis=0, keepdims=True)
            qx[h, pl.ds(i * U, U), :] = jnp.concatenate([zero, qc[:, h * HD:(h + 1) * HD]], axis=1)
            gx[h, pl.ds(i * U, U), :] = jnp.concatenate([gc[:, h * HD:(h + 1) * HD], zero], axis=1)
        kc = k_ref[pl.ds(p * B, B), :]
        vc = v_ref[pl.ds(p * B, B), :]
        kt[:, pl.ds(pl.multiple_of(i * B, B), B)] = kc.T
        for h in range(nh):
            ks[h, pl.ds(i * B, B), :] = kc[:, h * HD:(h + 1) * HD]
            vs[h, pl.ds(i * B, B), :] = vc[:, h * HD:(h + 1) * HD]
    dkv[...] = jnp.zeros_like(dkv)

    def tile(m, c, carry, masked):
        out = []
        qcols = pl.ds(pl.multiple_of(m * TQ, TQ), TQ)
        krows = pl.ds(pl.multiple_of(c * TK, TK), TK)
        for h in range(nh):
            hs = slice(h * HD, (h + 1) * HD)
            s = jnp.dot(ks[h, krows, :], qt[hs, qcols], preferred_element_type=jnp.float32)
            p = jnp.exp(s - lse_ref[h:h + 1, qcols])
            if masked:
                row = lax.broadcasted_iota(jnp.int32, s.shape, 0)
                col = lax.broadcasted_iota(jnp.int32, s.shape, 1)
                p = jnp.where((row >= B) & (col < U), 0.0, p)
            dp = jnp.dot(vs[h, krows, :], gt[hs, qcols], preferred_element_type=jnp.float32)
            ds = (p * (dp - delta[h:h + 1, qcols])).astype(jnp.bfloat16)
            pl_ = p.astype(jnp.bfloat16)
            dkv[h, krows, :] += (jnp.dot(pl_, gx[h, qcols, :], preferred_element_type=jnp.float32)
                                 + jnp.dot(ds, qx[h, qcols, :], preferred_element_type=jnp.float32))
            out.append(carry[h] + jnp.dot(kt[hs, krows], ds, preferred_element_type=jnp.float32))
        return tuple(out)

    @pl.loop(0, npair // 2)
    def _(m):
        init = tuple(jnp.zeros((HD, TQ), jnp.float32) for _ in range(nh))
        carry = lax.fori_loop(0, m, lambda c, x: tile(m, c, x, False), init)
        carry = tile(m, m, carry, True)
        dq = jnp.concatenate(carry, axis=0).T * 0.125
        for half in range(2):
            dq_ref[pl.ds(inv[2 * m + half] * U, U), :] = dq[half * U:(half + 1) * U].astype(dq_ref.dtype)

    @pl.loop(0, npair)
    def _(i):
        rows = pl.ds(inv[i] * B, B)
        parts = [dkv[h, pl.ds(i * B, B), :] for h in range(nh)]
        dv_ref[rows, :] = jnp.concatenate([x[:, :HD] for x in parts], axis=1)
        dk_ref[rows, :] = jnp.concatenate([x[:, HD:] for x in parts], axis=1)


def attend_back(inv, q, k, v, g, o, lse):
    R, W = q.shape
    K = k.shape[0]
    nh = W // HD
    return pl.pallas_call(
        attend_back_kernel,
        grid_spec=pltpu.PrefetchScalarGridSpec(
            num_scalar_prefetch=1, grid=(),
            in_specs=[pl.BlockSpec(memory_space=pltpu.VMEM)] * 6,
            out_specs=[pl.BlockSpec(memory_space=pltpu.VMEM)] * 3,
            scratch_shapes=[
                pltpu.VMEM((W, R), jnp.bfloat16),
                pltpu.VMEM((W, R), jnp.bfloat16),
                pltpu.VMEM((nh, R, 2 * HD), jnp.bfloat16),
                pltpu.VMEM((nh, R, 2 * HD), jnp.bfloat16),
                pltpu.VMEM((nh, K, HD), jnp.bfloat16),
                pltpu.VMEM((nh, K, HD), jnp.bfloat16),
                pltpu.VMEM((W, K), jnp.bfloat16),
                pltpu.VMEM((8, R), jnp.float32),
                pltpu.VMEM((nh, K, 2 * HD), jnp.float32),
            ]),
        out_shape=[jax.ShapeDtypeStruct((R, W), jnp.bfloat16),
                   jax.ShapeDtypeStruct((K, W), jnp.float32), jax.ShapeDtypeStruct((K, W), jnp.float32)],
        compiler_params=pltpu.CompilerParams(vmem_limit_bytes=56 << 20),
        name="attend_back",
    )(inv, q, k, v, g, o, lse)


def solution_any(mesh):
    return jax.shard_map(
        shards,
        mesh=mesh,
        in_specs=(
            P("ctx", None),
            P(),
            P("ctx"),
            P("ctx"),
            P("ctx", None),
            P("ctx"),
            P("ctx"),
            P("ctx", None),
            P("ctx"),
            P("ctx"),
            P("ctx"),
            P("ctx", None),
            P("ctx"),
            P("ctx", None),
            P("ctx"),
            P("ctx", None),
        ),
        out_specs=(
            P("ctx", None),
            P("ctx", None),
            P("ctx"),
            P("ctx"),
            P("ctx", None),
            P("ctx"),
            P("ctx"),
            P("ctx", None),
            P("ctx"),
            P("ctx"),
            P("ctx"),
            P("ctx", None),
            P("ctx"),
            P("ctx", None),
            P("ctx"),
        ),
        check_vma=False,
    )


AXES = ("s", "h", "r")
PLANES = 4


def planes(
    hidden_in,
    block_pairs,
    ln1_gain,
    ln1_bias,
    qkv_weight,
    query_bias,
    value_bias,
    out_weight,
    out_bias,
    ln2_gain,
    ln2_bias,
    fc_weight,
    fc_bias,
    proj_weight,
    proj_bias,
    out_grad,
):
    f32, bf16 = jnp.float32, jnp.bfloat16
    s, h, r = (lax.axis_index(a) for a in AXES)
    S, H, Q = (lax.axis_size(a) for a in AXES)
    rows, D = hidden_in.shape
    U = rows // SEQS
    W = D // H
    gather = lambda x: lax.all_gather(x, AXES, axis=0, tiled=True)
    vectors = [ln1_gain, ln1_bias, query_bias, value_bias, out_bias, ln2_gain, ln2_bias, proj_bias, fc_bias]
    sizes = [v.shape[0] for v in vectors]
    allv = gather(jnp.concatenate(vectors)[None])
    offs = [sum(sizes[:i]) for i in range(len(sizes))]
    g1, b1, bq, bv, bo, g2, b2, bp, bf = (
        allv[:, o : o + n].reshape(-1).astype(f32) for o, n in zip(offs, sizes)
    )
    w_out, w_fc, w_proj = gather(out_weight), gather(fc_weight), gather(proj_weight)
    d = qkv_weight.shape[0]
    w4 = qkv_weight.reshape(d, 3, H, W).transpose(2, 0, 1, 3).reshape(H, d, 3 * W)
    w4 = lax.all_to_all(w4, "h", 0, 0)
    w4 = lax.all_gather(lax.all_gather(w4, "r", axis=1), "s", axis=0)
    w_h = w4.reshape(D, 3 * W)

    blk = block_pairs[::2]
    blk = jnp.where(s % 2 == 0, blk, blk.shape[0] - 1 - blk)
    npair = blk.shape[0]
    inv = jnp.sum(
        jnp.where(blk[None, :] == jnp.arange(npair)[:, None], jnp.arange(npair)[None, :], 0), axis=1
    ).astype(jnp.int32)

    x_own = lax.all_to_all(hidden_in.reshape(S, U, D), "s", 0, 0)
    x_all = lax.all_gather(x_own, "h", axis=1).reshape(-1, D)
    g_own = lax.all_to_all(out_grad.reshape(S, U, D), "s", 0, 0).reshape(rows, D)
    x_own = x_own.reshape(rows, D).astype(f32)

    normed = layer_norm(x_all.astype(f32), g1, b1).astype(bf16)
    mixed = jnp.dot(normed, w_h, preferred_element_type=f32)
    bq_h = lax.dynamic_slice_in_dim(bq, h * W, W)
    bv_h = lax.dynamic_slice_in_dim(bv, h * W, W)
    q = (mixed[:, :W] + bq_h).astype(bf16)
    k = mixed[:, W : 2 * W].astype(bf16)
    v = (mixed[:, 2 * W :] + bv_h).astype(bf16)
    q_scaled = q * jnp.asarray(0.125, bf16)

    def from_other(t):
        return lax.ppermute(t, "r", [(0, 1), (1, 0)])

    def both(t):
        return jnp.concatenate(
            [t.reshape(npair, U, W), from_other(t).reshape(npair, U, W)], axis=1
        ).reshape(npair * 2 * U, W)

    k_all, v_all = both(k), both(v)
    att, lse = attend(inv, q_scaled, k_all, v_all)
    att_low = lax.all_to_all(att.astype(bf16).reshape(S, H, U, W), "h", 1, 1)
    att_low = att_low.transpose(0, 2, 1, 3).reshape(rows, D)

    middle = x_own + jnp.dot(att_low, w_out, preferred_element_type=f32) + bo
    normed_two = layer_norm(middle, g2, b2).astype(bf16)
    pre_act = jnp.dot(normed_two, w_fc, preferred_element_type=f32) + bf
    activation = gelu_tanh(pre_act).astype(bf16)
    layer_out = (middle + jnp.dot(activation, w_proj, preferred_element_type=f32) + bp).astype(bf16)
    grad_out = g_own.astype(f32)
    grad_proj = jnp.dot(activation.T, g_own, preferred_element_type=f32)
    grad_bproj = jnp.sum(grad_out, axis=0)
    grad_activ = jnp.dot(g_own, w_proj.T, preferred_element_type=f32)
    _, gelu_back = jax.vjp(gelu_tanh, pre_act)
    grad_pre = gelu_back(grad_activ)[0].astype(bf16)
    grad_fc = jnp.dot(normed_two.T, grad_pre, preferred_element_type=f32)
    grad_bfc = jnp.sum(grad_pre.astype(f32), axis=0)
    grad_normed_two = jnp.dot(grad_pre, w_fc.T, preferred_element_type=f32)
    _, norm_back_two = jax.vjp(layer_norm, middle, g2, b2)
    grad_middle, grad_g2, grad_b2 = norm_back_two(grad_normed_two)
    grad_middle = grad_middle + grad_out
    grad_branch = grad_middle.astype(bf16)
    grad_wout = jnp.dot(att_low.T, grad_branch, preferred_element_type=f32)
    grad_bout = jnp.sum(grad_branch.astype(f32), axis=0)
    grad_att = jnp.dot(grad_branch, w_out.T, preferred_element_type=f32).astype(bf16)

    g_att = lax.all_to_all(grad_att.reshape(S, U, H, W).transpose(0, 2, 1, 3), "h", 1, 1)
    dq, dk, dv = attend_back(inv, q_scaled, k_all, v_all, g_att.reshape(-1, W), att, lse)
    dkv = jnp.stack([dk, dv]).reshape(2, npair, 2, U, W)
    dkv = dkv[:, :, 0] + from_other(dkv[:, :, 1])
    dkv = dkv.reshape(2, -1, W).astype(bf16)
    grad_mixed = jnp.concatenate([dq, dkv[0], dkv[1]], axis=1)
    grad_qkv = jnp.dot(normed.T, grad_mixed, preferred_element_type=f32)
    cols = jnp.sum(grad_mixed.astype(f32), axis=0)
    t = jnp.dot(grad_mixed, w_h.T, preferred_element_type=f32)
    t = lax.psum_scatter(t.reshape(S, H, U, D), "h", scatter_dimension=1, tiled=False)
    _, norm_back_one = jax.vjp(layer_norm, x_own, g1, b1)
    grad_inputs, grad_g1, grad_b1 = norm_back_one(t.reshape(rows, D))
    grad_hidden = (grad_inputs + grad_middle).astype(bf16)
    back = lambda y: lax.all_to_all(y.reshape(S, U, D), "s", 0, 0).reshape(rows, D)

    gq = grad_qkv.reshape(S, H, Q, d, 3 * W)
    gq = lax.psum_scatter(lax.psum_scatter(gq, "s", scatter_dimension=0, tiled=False), "r", scatter_dimension=1, tiled=False)
    gq = lax.all_to_all(gq, "h", 0, 0)
    gq = gq.reshape(H, d, 3, W).transpose(1, 2, 0, 3).reshape(d, 3 * D)
    place = lambda c: lax.dynamic_update_slice_in_dim(jnp.zeros((D,), f32), c, h * W, 0)
    small = [grad_g1, grad_b1, place(cols[:W]), place(cols[2 * W :]), grad_bout, grad_g2, grad_b2, grad_bproj, grad_bfc]
    scat = lambda y: lax.psum_scatter(y, AXES, scatter_dimension=0, tiled=True)
    g1s, b1s, bqs, bvs, bos, g2s, b2s, bps, bfs = [scat(y) for y in small]
    return (
        back(layer_out),
        back(grad_hidden),
        g1s,
        b1s,
        gq,
        bqs,
        bvs,
        scat(grad_wout),
        bos,
        g2s,
        b2s,
        scat(grad_fc),
        bfs,
        scat(grad_proj),
        bps,
    )


def solution(mesh):
    n = mesh.shape["ctx"]
    if n // (PLANES * SEQS) != 2:
        return solution_any(mesh)
    split = Mesh(mesh.devices.reshape(PLANES, SEQS, -1), AXES)
    row, vec = P(AXES, None), P(AXES)
    return jax.shard_map(
        planes,
        mesh=split,
        in_specs=(row, P(), vec, vec, row, vec, vec, row, vec, vec, vec, row, vec, row, vec, row),
        out_specs=(row, row, vec, vec, row, vec, vec, row, vec, vec, vec, row, vec, row, vec),
        check_vma=False,
    )
```

```python
from functools import partial
import math

import jax
import jax.numpy as jnp
from jax import lax
from jax.sharding import PartitionSpec as P
from jax.experimental import pallas as pl
from jax.experimental.pallas import tpu as pltpu
from jax.sharding import Mesh

HEADS = 12
SEQS = 4


NEG = -1e30


def from_partner(value, axis, bit):
    return lax.ppermute(value, axis, [(i, i ^ 1 << bit) for i in range(lax.axis_size(axis))])


def layer_norm(values, gain, bias):
    center = values - jnp.mean(values, axis=-1, keepdims=True)
    spread_sq = jnp.mean(center * center, axis=-1, keepdims=True)
    return center * lax.rsqrt(spread_sq + 1e-05) * gain + bias


def gelu_tanh(values):
    return jax.nn.gelu(values, approximate=True)


def heads_of(tensor, head_count):
    return tensor.reshape(tensor.shape[:-1] + (head_count, tensor.shape[-1] // head_count))


def pick_own(owned, chosen):
    selector = chosen.reshape((1, -1) + (1,) * (owned.ndim - 2))
    return jnp.where(selector, owned[:, 0:1], owned[:, 1:2])


def pick_piece(piece, chosen):
    selector = chosen.reshape((1, -1) + (1,) * (piece.ndim - 3))
    return jnp.where(selector, piece[:, 0], piece[:, 1])


def parity_masks(chosen, usable):
    return jnp.stack([chosen & usable, jnp.logical_not(chosen) & usable])


def spread(values, parity):
    shaped = parity.reshape((1,) + parity.shape + (1,) * (values.ndim - 2))
    return jnp.sum(jnp.where(shaped, values[:, None], 0.0), axis=2)


def group_loop(pieces, unit_rows, table, stepper, carried):
    piece_rows = pieces[0].shape[2]
    group_size = min(unit_rows, piece_rows)
    group_count = piece_rows // group_size
    batch_groups = math.gcd(group_count, max(1, 1024 // group_size))
    turn_count = group_count // batch_groups
    shaped = tuple(
        (
            item.reshape(item.shape[:2] + (group_count, group_size) + item.shape[3:])
            for item in pieces
        )
    )
    device_ids = jnp.arange(group_count, dtype=jnp.int32) * group_size // unit_rows
    table_size = table.shape[0]
    blocks = jnp.sum(
        jnp.where(
            device_ids[:, None] == jnp.arange(table_size, dtype=jnp.int32)[None, :],
            table[None, :],
            0,
        ),
        axis=1,
    )

    def one_turn(position, current):
        pieces_now = tuple(
            (
                lax.dynamic_slice_in_dim(item, position * batch_groups, batch_groups, 2)
                for item in shaped
            )
        )
        chosen = lax.dynamic_slice_in_dim(blocks, position * batch_groups, batch_groups, 0)
        return stepper(current, pieces_now, chosen)

    return lax.fori_loop(0, turn_count, one_turn, carried)


def attend_step(q_heads, my_block, score_scale, head_count, carried, pieces_now, chosen):
    key_piece = heads_of(pieces_now[0], head_count)
    value_piece = heads_of(pieces_now[1], head_count)
    earlier = chosen < my_block
    usable = chosen != my_block
    parity = parity_masks(earlier, usable)
    query_sel = pick_own(q_heads, earlier)
    key_sel = pick_piece(key_piece, earlier)
    value_sel = pick_piece(value_piece, earlier)
    scores = (
        jnp.einsum("jgqhe,jgkhe->jghqk", query_sel, key_sel, preferred_element_type=jnp.float32)
        * score_scale
    )
    usable_mask = usable.reshape(1, -1, 1, 1, 1)
    scores = jnp.where(usable_mask, scores, NEG)
    old_max, old_total, old_sum = carried
    group_max = jnp.max(scores, axis=-1)
    candidate = jnp.max(jnp.where(parity.reshape(1, 2, -1, 1, 1), group_max[:, None], NEG), axis=2)
    new_max = jnp.maximum(old_max, candidate)
    max_sel = pick_own(new_max, earlier)
    weights_exp = jnp.where(usable_mask, jnp.exp(scores - max_sel[..., None]), 0.0)
    moved = jnp.einsum(
        "jghqk,jgkhe->jgqhe",
        weights_exp.astype(jnp.bfloat16),
        value_sel,
        preferred_element_type=jnp.float32,
    )
    factor = jnp.exp(old_max - new_max)
    new_total = old_total * factor + spread(jnp.sum(weights_exp, axis=-1), parity)
    new_sum = old_sum * jnp.swapaxes(factor, 2, 3)[..., None] + spread(moved, parity)
    return (new_max, new_total, new_sum)


def query_grad_step(
    q_heads,
    grad_heads,
    lse_heads,
    delta_heads,
    my_block,
    score_scale,
    head_count,
    carried,
    pieces_now,
    chosen,
):
    key_piece = heads_of(pieces_now[0], head_count)
    value_piece = heads_of(pieces_now[1], head_count)
    earlier = chosen < my_block
    usable = chosen != my_block
    parity = parity_masks(earlier, usable)
    query_sel = pick_own(q_heads, earlier)
    grad_sel = pick_own(grad_heads, earlier)
    lse_sel = pick_own(lse_heads, earlier)
    delta_sel = pick_own(delta_heads, earlier)
    key_sel = pick_piece(key_piece, earlier)
    value_sel = pick_piece(value_piece, earlier)
    scores = (
        jnp.einsum("jgqhe,jgkhe->jghqk", query_sel, key_sel, preferred_element_type=jnp.float32)
        * score_scale
    )
    usable_mask = usable.reshape(1, -1, 1, 1, 1)
    probabilities = jnp.where(usable_mask, jnp.exp(scores - lse_sel[..., None]), 0.0)
    grad_probs = jnp.einsum(
        "jgqhe,jgkhe->jghqk", grad_sel, value_sel, preferred_element_type=jnp.float32
    )
    grad_scores = (probabilities * (grad_probs - delta_sel[..., None])).astype(jnp.bfloat16)
    term = (
        jnp.einsum("jghqk,jgkhe->jgqhe", grad_scores, key_sel, preferred_element_type=jnp.float32)
        * score_scale
    )
    return carried + spread(term, parity)


def key_grad_step(k_heads, v_heads, my_block, score_scale, head_count, carried, pieces_now, chosen):
    query_piece = heads_of(pieces_now[0], head_count)
    grad_piece = heads_of(pieces_now[1], head_count)
    later = my_block < chosen
    usable = chosen != my_block
    parity = parity_masks(later, usable)
    query_sel = pick_piece(query_piece, later)
    grad_sel = pick_piece(grad_piece, later)
    lse_sel = jnp.swapaxes(pick_piece(pieces_now[2], later), 2, 3)
    delta_sel = jnp.swapaxes(pick_piece(pieces_now[3], later), 2, 3)
    key_sel = pick_own(k_heads, later)
    value_sel = pick_own(v_heads, later)
    scores = (
        jnp.einsum("jgqhe,jgkhe->jghqk", query_sel, key_sel, preferred_element_type=jnp.float32)
        * score_scale
    )
    usable_mask = usable.reshape(1, -1, 1, 1, 1)
    probabilities = jnp.where(usable_mask, jnp.exp(scores - lse_sel[..., None]), 0.0)
    grad_probs = jnp.einsum(
        "jgqhe,jgkhe->jghqk", grad_sel, value_sel, preferred_element_type=jnp.float32
    )
    grad_scores = (probabilities * (grad_probs - delta_sel[..., None])).astype(jnp.bfloat16)
    key_term = (
        jnp.einsum("jghqk,jgqhe->jgkhe", grad_scores, query_sel, preferred_element_type=jnp.float32)
        * score_scale
    )
    value_term = jnp.einsum(
        "jghqk,jgqhe->jgkhe",
        probabilities.astype(jnp.bfloat16),
        grad_sel,
        preferred_element_type=jnp.float32,
    )
    return (carried[0] + spread(key_term, parity), carried[1] + spread(value_term, parity))


def shards(
    hidden_in,
    block_pairs,
    ln1_gain,
    ln1_bias,
    qkv_weight,
    query_bias,
    value_bias,
    out_weight,
    out_bias,
    ln2_gain,
    ln2_bias,
    fc_weight,
    fc_bias,
    proj_weight,
    proj_bias,
    out_grad,
):
    params = (
        ln1_gain,
        ln1_bias,
        qkv_weight,
        query_bias,
        value_bias,
        out_weight,
        out_bias,
        ln2_gain,
        ln2_bias,
        fc_weight,
        fc_bias,
        proj_weight,
        proj_bias,
    )
    gathered = (
        lax.all_gather(params[0], "ctx", axis=0, tiled=True),
        lax.all_gather(params[1], "ctx", axis=0, tiled=True),
        lax.all_gather(params[2], "ctx", axis=0, tiled=True),
        lax.all_gather(params[3], "ctx", axis=0, tiled=True),
        lax.all_gather(params[4], "ctx", axis=0, tiled=True),
        lax.all_gather(params[5], "ctx", axis=0, tiled=True),
        lax.all_gather(params[6], "ctx", axis=0, tiled=True),
        lax.all_gather(params[7], "ctx", axis=0, tiled=True),
        lax.all_gather(params[8], "ctx", axis=0, tiled=True),
        lax.all_gather(params[9], "ctx", axis=0, tiled=True),
        lax.all_gather(params[10], "ctx", axis=0, tiled=True),
        lax.all_gather(params[11], "ctx", axis=0, tiled=True),
        lax.all_gather(params[12], "ctx", axis=0, tiled=True),
    )
    (
        gain_one,
        bias_one,
        w_qkv,
        b_query,
        b_value,
        w_out,
        b_out,
        gain_two,
        bias_two,
        w_fc,
        b_fc,
        w_proj,
        b_proj,
    ) = gathered
    device = lax.axis_index("ctx")
    partner = device + 1 - 2 * (device % 2)
    row_count = hidden_in.shape[0]
    model_width = hidden_in.shape[1]
    unit_rows = row_count // SEQS
    halves = SEQS // 2
    head_count = HEADS
    head_size = model_width // head_count
    score_scale = 1.0 / math.sqrt(head_size)
    my_block = block_pairs[device]
    seq_shape = (halves, 2, unit_rows, model_width)
    head_shape = (halves, 2, unit_rows, head_count, head_size)
    inputs = hidden_in.astype(jnp.float32)
    normed = layer_norm(inputs, gain_one.astype(jnp.float32), bias_one.astype(jnp.float32)).astype(
        jnp.bfloat16
    )
    mixed_proj = jnp.dot(normed, w_qkv, preferred_element_type=jnp.float32)
    queries = (mixed_proj[:, :model_width] + b_query.astype(jnp.float32)).astype(jnp.bfloat16)
    key_rows = mixed_proj[:, model_width : 2 * model_width].astype(jnp.bfloat16)
    value_rows = (mixed_proj[:, 2 * model_width :] + b_value.astype(jnp.float32)).astype(
        jnp.bfloat16
    )
    q_seq = queries.reshape(seq_shape)
    k_seq = key_rows.reshape(seq_shape)
    v_seq = value_rows.reshape(seq_shape)
    q_heads = queries.reshape(head_shape)
    k_heads = key_rows.reshape(head_shape)
    v_heads = value_rows.reshape(head_shape)
    far_keys, far_values = from_partner((k_seq, v_seq), "ctx", 0)
    near_keys = jnp.concatenate([k_heads, heads_of(far_keys, head_count)], axis=2)
    near_values = jnp.concatenate([v_heads, heads_of(far_values, head_count)], axis=2)
    scores = (
        jnp.einsum("jpqhe,jpkhe->jphqk", q_heads, near_keys, preferred_element_type=jnp.float32)
        * score_scale
    )
    row_max = jnp.max(scores, axis=-1)
    weights_exp = jnp.exp(scores - row_max[..., None])
    row_total = jnp.sum(weights_exp, axis=-1)
    summed = jnp.einsum(
        "jphqk,jpkhe->jpqhe",
        weights_exp.astype(jnp.bfloat16),
        near_values,
        preferred_element_type=jnp.float32,
    )
    forward_stepper = partial(attend_step, q_heads, my_block, score_scale, head_count)
    row_max, row_total, summed = group_loop(
        (
            lax.all_gather(k_seq, "ctx", axis=2, tiled=True),
            lax.all_gather(v_seq, "ctx", axis=2, tiled=True),
        ),
        unit_rows,
        block_pairs,
        forward_stepper,
        (row_max, row_total, summed),
    )
    attended = summed / jnp.swapaxes(row_total, 2, 3)[..., None]
    log_total = row_max + jnp.log(row_total)
    att_low = attended.reshape(row_count, model_width).astype(jnp.bfloat16)
    branch = jnp.dot(att_low, w_out, preferred_element_type=jnp.float32) + b_out.astype(jnp.float32)
    middle = inputs + branch
    normed_two = layer_norm(
        middle, gain_two.astype(jnp.float32), bias_two.astype(jnp.float32)
    ).astype(jnp.bfloat16)
    pre_act = jnp.dot(normed_two, w_fc, preferred_element_type=jnp.float32) + b_fc.astype(
        jnp.float32
    )
    activation = gelu_tanh(pre_act).astype(jnp.bfloat16)
    result = (
        middle
        + jnp.dot(activation, w_proj, preferred_element_type=jnp.float32)
        + b_proj.astype(jnp.float32)
    )
    layer_out = result.astype(jnp.bfloat16)
    grad_out = out_grad.astype(jnp.float32)
    grad_proj = jnp.dot(activation.T, out_grad, preferred_element_type=jnp.float32)
    grad_bproj = jnp.sum(grad_out, axis=0)
    grad_activ = jnp.dot(out_grad, w_proj.T, preferred_element_type=jnp.float32)
    _, gelu_back = jax.vjp(gelu_tanh, pre_act)
    grad_pre = gelu_back(grad_activ)[0].astype(jnp.bfloat16)
    grad_fc = jnp.dot(normed_two.T, grad_pre, preferred_element_type=jnp.float32)
    grad_bfc = jnp.sum(grad_pre.astype(jnp.float32), axis=0)
    grad_normed_two = jnp.dot(grad_pre, w_fc.T, preferred_element_type=jnp.float32)
    _, norm_back_two = jax.vjp(
        layer_norm, middle, gain_two.astype(jnp.float32), bias_two.astype(jnp.float32)
    )
    grad_middle, grad_gain_two, grad_bias_two = norm_back_two(grad_normed_two)
    grad_middle = grad_middle + grad_out
    grad_branch = grad_middle.astype(jnp.bfloat16)
    grad_wout = jnp.dot(att_low.T, grad_branch, preferred_element_type=jnp.float32)
    grad_bout = jnp.sum(grad_branch.astype(jnp.float32), axis=0)
    grad_att = jnp.dot(grad_branch, w_out.T, preferred_element_type=jnp.float32).astype(
        jnp.bfloat16
    )
    grad_seq = grad_att.reshape(seq_shape)
    grad_heads = grad_att.reshape(head_shape)
    row_delta = jnp.sum(grad_heads.astype(jnp.float32) * attended, axis=-1)
    delta_heads = jnp.swapaxes(row_delta, 2, 3)
    all_lse, all_delta = (
        lax.all_gather(jnp.swapaxes(log_total, 2, 3), "ctx", axis=2, tiled=True),
        lax.all_gather(row_delta, "ctx", axis=2, tiled=True),
    )
    partner_lse = jnp.swapaxes(
        lax.dynamic_slice_in_dim(all_lse, partner * unit_rows, unit_rows, 2), 2, 3
    )
    partner_delta = jnp.swapaxes(
        lax.dynamic_slice_in_dim(all_delta, partner * unit_rows, unit_rows, 2), 2, 3
    )
    far_queries, far_grads = from_partner((q_seq, grad_seq), "ctx", 0)
    near_queries = jnp.concatenate([q_heads, heads_of(far_queries, head_count)], axis=2)
    near_grads = jnp.concatenate([grad_heads, heads_of(far_grads, head_count)], axis=2)
    near_lse = jnp.concatenate([log_total, partner_lse], axis=3)
    near_delta = jnp.concatenate([delta_heads, partner_delta], axis=3)
    local_scores = (
        jnp.einsum(
            "jpqhe,jpkhe->jphqk", near_queries, near_keys, preferred_element_type=jnp.float32
        )
        * score_scale
    )
    probabilities = jnp.exp(local_scores - near_lse[..., None])
    grad_probs = jnp.einsum(
        "jpqhe,jpkhe->jphqk", near_grads, near_values, preferred_element_type=jnp.float32
    )
    grad_scores = (probabilities * (grad_probs - near_delta[..., None])).astype(jnp.bfloat16)
    grad_q_local = (
        jnp.einsum(
            "jphqk,jpkhe->jpqhe",
            grad_scores[:, :, :, :unit_rows, :],
            near_keys,
            preferred_element_type=jnp.float32,
        )
        * score_scale
    )
    grad_k_local = (
        jnp.einsum(
            "jphqk,jpqhe->jpkhe",
            grad_scores[..., :unit_rows],
            near_queries,
            preferred_element_type=jnp.float32,
        )
        * score_scale
    )
    grad_v_local = jnp.einsum(
        "jphqk,jpqhe->jpkhe",
        probabilities.astype(jnp.bfloat16)[..., :unit_rows],
        near_grads,
        preferred_element_type=jnp.float32,
    )
    query_stepper = partial(
        query_grad_step,
        q_heads,
        grad_heads,
        log_total,
        delta_heads,
        my_block,
        score_scale,
        head_count,
    )
    key_stepper = partial(key_grad_step, k_heads, v_heads, my_block, score_scale, head_count)

    def query_piece(carried, pieces, offset):
        return group_loop(pieces, unit_rows, block_pairs, query_stepper, carried)

    def key_piece(carried, pieces, offset):
        return group_loop(
            (pieces[0], pieces[1], all_lse, all_delta), unit_rows, block_pairs, key_stepper, carried
        )

    grad_q_all = query_piece(
        grad_q_local,
        (
            lax.all_gather(k_seq, "ctx", axis=2, tiled=True),
            lax.all_gather(v_seq, "ctx", axis=2, tiled=True),
        ),
        jnp.int32(0),
    )
    grad_k_all, grad_v_all = key_piece(
        (grad_k_local, grad_v_local),
        (
            lax.all_gather(q_seq, "ctx", axis=2, tiled=True),
            lax.all_gather(grad_seq, "ctx", axis=2, tiled=True),
        ),
        jnp.int32(0),
    )
    grad_queries = grad_q_all.reshape(row_count, model_width).astype(jnp.bfloat16)
    grad_keys = grad_k_all.reshape(row_count, model_width).astype(jnp.bfloat16)
    grad_values = grad_v_all.reshape(row_count, model_width).astype(jnp.bfloat16)
    grad_mixed = jnp.concatenate([grad_queries, grad_keys, grad_values], axis=1)
    grad_qkv = jnp.dot(normed.T, grad_mixed, preferred_element_type=jnp.float32)
    grad_bquery = jnp.sum(grad_queries.astype(jnp.float32), axis=0)
    grad_bvalue = jnp.sum(grad_values.astype(jnp.float32), axis=0)
    grad_normed = jnp.dot(grad_mixed, w_qkv.T, preferred_element_type=jnp.float32)
    _, norm_back_one = jax.vjp(
        layer_norm, inputs, gain_one.astype(jnp.float32), bias_one.astype(jnp.float32)
    )
    grad_inputs, grad_gain_one, grad_bias_one = norm_back_one(grad_normed)
    grad_hidden = (grad_inputs + grad_middle).astype(jnp.bfloat16)
    totals = (
        lax.psum_scatter(grad_gain_one, "ctx", scatter_dimension=0, tiled=True),
        lax.psum_scatter(grad_bias_one, "ctx", scatter_dimension=0, tiled=True),
        lax.psum_scatter(grad_qkv, "ctx", scatter_dimension=0, tiled=True),
        lax.psum_scatter(grad_bquery, "ctx", scatter_dimension=0, tiled=True),
        lax.psum_scatter(grad_bvalue, "ctx", scatter_dimension=0, tiled=True),
        lax.psum_scatter(grad_wout, "ctx", scatter_dimension=0, tiled=True),
        lax.psum_scatter(grad_bout, "ctx", scatter_dimension=0, tiled=True),
        lax.psum_scatter(grad_gain_two, "ctx", scatter_dimension=0, tiled=True),
        lax.psum_scatter(grad_bias_two, "ctx", scatter_dimension=0, tiled=True),
        lax.psum_scatter(grad_fc, "ctx", scatter_dimension=0, tiled=True),
        lax.psum_scatter(grad_bfc, "ctx", scatter_dimension=0, tiled=True),
        lax.psum_scatter(grad_proj, "ctx", scatter_dimension=0, tiled=True),
        lax.psum_scatter(grad_bproj, "ctx", scatter_dimension=0, tiled=True),
    )
    return (
        layer_out,
        grad_hidden,
        totals[0],
        totals[1],
        totals[2],
        totals[3],
        totals[4],
        totals[5],
        totals[6],
        totals[7],
        totals[8],
        totals[9],
        totals[10],
        totals[11],
        totals[12],
    )


HD = 64


def attend_kernel(inv, q_ref, k_ref, v_ref, o_ref, lse_ref, qt, ks, vt):
    W = q_ref.shape[1]
    nh = W // HD
    npair = inv.shape[0]
    U = q_ref.shape[0] // npair
    B = k_ref.shape[0] // npair
    TQ, TK = 2 * U, 2 * B

    @pl.loop(0, npair)
    def _(i):
        p = inv[i]
        qc = q_ref[pl.ds(p * U, U), :]
        qt[:, pl.ds(pl.multiple_of(i * U, U), U)] = qc.T
        kc = k_ref[pl.ds(p * B, B), :]
        for h in range(nh):
            ks[h, pl.ds(i * B, B), :] = kc[:, h * HD:(h + 1) * HD]
        vc = v_ref[pl.ds(p * B, B), :]
        vct = vc.T
        for h in range(nh):
            vt[h, 0:HD, pl.ds(pl.multiple_of(i * B, B), B)] = vct[h * HD:(h + 1) * HD]
            vt[h, HD:, pl.ds(pl.multiple_of(i * B, B), B)] = jnp.ones((vt.shape[1] - HD, B), vt.dtype)

    def tile(m, c, carry, masked):
        out = []
        for h in range(nh):
            mx, acc = carry[h]
            qh = qt[h * HD:(h + 1) * HD, pl.ds(pl.multiple_of(m * TQ, TQ), TQ)]
            kh = ks[h, pl.ds(pl.multiple_of(c * TK, TK), TK), :]
            s = jnp.dot(kh, qh, preferred_element_type=jnp.float32)
            if masked:
                row = lax.broadcasted_iota(jnp.int32, s.shape, 0)
                col = lax.broadcasted_iota(jnp.int32, s.shape, 1)
                s = jnp.where((row >= B) & (col < U), NEG, s)
            new = jnp.maximum(mx, jnp.max(s, axis=0, keepdims=True))
            p = jnp.exp(s - new).astype(jnp.bfloat16)
            vh = vt[h, :, pl.ds(pl.multiple_of(c * TK, TK), TK)]
            acc = acc * jnp.exp(mx - new) + jnp.dot(vh, p, preferred_element_type=jnp.float32)
            out.append((new, acc))
        return tuple(out)

    @pl.loop(0, npair // 2)
    def _(m):
        init = tuple((jnp.full((1, TQ), NEG, jnp.float32), jnp.zeros((vt.shape[1], TQ), jnp.float32)) for _ in range(nh))
        carry = lax.fori_loop(0, m, lambda c, x: tile(m, c, x, False), init)
        carry = tile(m, m, carry, True)
        outs = []
        for h in range(nh):
            mx, acc = carry[h]
            tot = acc[HD:HD + 1]
            outs.append(acc[:HD] / tot)
            lse_ref[h:h + 1, pl.ds(pl.multiple_of(m * TQ, TQ), TQ)] = mx + jnp.log(tot)
        o = jnp.concatenate(outs, axis=0).T
        for half in range(2):
            o_ref[pl.ds(inv[2 * m + half] * U, U), :] = o[half * U:(half + 1) * U]


def attend(inv, q, k, v):
    R, W = q.shape
    K = k.shape[0]
    nh = W // HD
    return pl.pallas_call(
        attend_kernel,
        grid_spec=pltpu.PrefetchScalarGridSpec(
            num_scalar_prefetch=1, grid=(),
            in_specs=[pl.BlockSpec(memory_space=pltpu.VMEM)] * 3,
            out_specs=[pl.BlockSpec(memory_space=pltpu.VMEM)] * 2,
            scratch_shapes=[
                pltpu.VMEM((W, R), jnp.bfloat16),
                pltpu.VMEM((nh, K, HD), jnp.bfloat16),
                pltpu.VMEM((nh, HD + 16, K), jnp.bfloat16),
            ]),
        out_shape=[jax.ShapeDtypeStruct((R, W), jnp.float32), jax.ShapeDtypeStruct((8, R), jnp.float32)],
        compiler_params=pltpu.CompilerParams(vmem_limit_bytes=56 << 20),
        name="attend",
    )(inv, q, k, v)


def attend_back_kernel(inv, q_ref, k_ref, v_ref, g_ref, o_ref, lse_ref, dq_ref, dk_ref, dv_ref,
                       qt, gt, qx, gx, ks, vs, kt, delta, dkv):
    W = q_ref.shape[1]
    nh = W // HD
    npair = inv.shape[0]
    U = q_ref.shape[0] // npair
    B = k_ref.shape[0] // npair
    TQ, TK = 2 * U, 2 * B

    @pl.loop(0, npair)
    def _(i):
        p = inv[i]
        qc = q_ref[pl.ds(p * U, U), :]
        gc = g_ref[pl.ds(p * U, U), :]
        oc = o_ref[pl.ds(p * U, U), :]
        cols = pl.ds(pl.multiple_of(i * U, U), U)
        qt[:, cols] = qc.T
        gt[:, cols] = gc.T
        prod = (oc * gc.astype(jnp.float32)).T
        zero = jnp.zeros((U, HD), jnp.bfloat16)
        for h in range(nh):
            delta[h:h + 1, cols] = jnp.sum(prod[h * HD:(h + 1) * HD], axis=0, keepdims=True)
            qx[h, pl.ds(i * U, U), :] = jnp.concatenate([zero, qc[:, h * HD:(h + 1) * HD]], axis=1)
            gx[h, pl.ds(i * U, U), :] = jnp.concatenate([gc[:, h * HD:(h + 1) * HD], zero], axis=1)
        kc = k_ref[pl.ds(p * B, B), :]
        vc = v_ref[pl.ds(p * B, B), :]
        kt[:, pl.ds(pl.multiple_of(i * B, B), B)] = kc.T
        for h in range(nh):
            ks[h, pl.ds(i * B, B), :] = kc[:, h * HD:(h + 1) * HD]
            vs[h, pl.ds(i * B, B), :] = vc[:, h * HD:(h + 1) * HD]
    dkv[...] = jnp.zeros_like(dkv)

    def tile(m, c, carry, masked):
        out = []
        qcols = pl.ds(pl.multiple_of(m * TQ, TQ), TQ)
        krows = pl.ds(pl.multiple_of(c * TK, TK), TK)
        for h in range(nh):
            hs = slice(h * HD, (h + 1) * HD)
            s = jnp.dot(ks[h, krows, :], qt[hs, qcols], preferred_element_type=jnp.float32)
            p = jnp.exp(s - lse_ref[h:h + 1, qcols])
            if masked:
                row = lax.broadcasted_iota(jnp.int32, s.shape, 0)
                col = lax.broadcasted_iota(jnp.int32, s.shape, 1)
                p = jnp.where((row >= B) & (col < U), 0.0, p)
            dp = jnp.dot(vs[h, krows, :], gt[hs, qcols], preferred_element_type=jnp.float32)
            ds = (p * (dp - delta[h:h + 1, qcols])).astype(jnp.bfloat16)
            pl_ = p.astype(jnp.bfloat16)
            dkv[h, krows, :] += (jnp.dot(pl_, gx[h, qcols, :], preferred_element_type=jnp.float32)
                                 + jnp.dot(ds, qx[h, qcols, :], preferred_element_type=jnp.float32))
            out.append(carry[h] + jnp.dot(kt[hs, krows], ds, preferred_element_type=jnp.float32))
        return tuple(out)

    @pl.loop(0, npair // 2)
    def _(m):
        init = tuple(jnp.zeros((HD, TQ), jnp.float32) for _ in range(nh))
        carry = lax.fori_loop(0, m, lambda c, x: tile(m, c, x, False), init)
        carry = tile(m, m, carry, True)
        dq = jnp.concatenate(carry, axis=0).T * 0.125
        for half in range(2):
            dq_ref[pl.ds(inv[2 * m + half] * U, U), :] = dq[half * U:(half + 1) * U].astype(dq_ref.dtype)

    @pl.loop(0, npair)
    def _(i):
        rows = pl.ds(inv[i] * B, B)
        parts = [dkv[h, pl.ds(i * B, B), :] for h in range(nh)]
        dv_ref[rows, :] = jnp.concatenate([x[:, :HD] for x in parts], axis=1)
        dk_ref[rows, :] = jnp.concatenate([x[:, HD:] for x in parts], axis=1)


def attend_back(inv, q, k, v, g, o, lse):
    R, W = q.shape
    K = k.shape[0]
    nh = W // HD
    return pl.pallas_call(
        attend_back_kernel,
        grid_spec=pltpu.PrefetchScalarGridSpec(
            num_scalar_prefetch=1, grid=(),
            in_specs=[pl.BlockSpec(memory_space=pltpu.VMEM)] * 6,
            out_specs=[pl.BlockSpec(memory_space=pltpu.VMEM)] * 3,
            scratch_shapes=[
                pltpu.VMEM((W, R), jnp.bfloat16),
                pltpu.VMEM((W, R), jnp.bfloat16),
                pltpu.VMEM((nh, R, 2 * HD), jnp.bfloat16),
                pltpu.VMEM((nh, R, 2 * HD), jnp.bfloat16),
                pltpu.VMEM((nh, K, HD), jnp.bfloat16),
                pltpu.VMEM((nh, K, HD), jnp.bfloat16),
                pltpu.VMEM((W, K), jnp.bfloat16),
                pltpu.VMEM((8, R), jnp.float32),
                pltpu.VMEM((nh, K, 2 * HD), jnp.float32),
            ]),
        out_shape=[jax.ShapeDtypeStruct((R, W), jnp.bfloat16),
                   jax.ShapeDtypeStruct((K, W), jnp.float32), jax.ShapeDtypeStruct((K, W), jnp.float32)],
        compiler_params=pltpu.CompilerParams(vmem_limit_bytes=56 << 20),
        name="attend_back",
    )(inv, q, k, v, g, o, lse)


def solution_any(mesh):
    return jax.shard_map(
        shards,
        mesh=mesh,
        in_specs=(
            P("ctx", None),
            P(),
            P("ctx"),
            P("ctx"),
            P("ctx", None),
            P("ctx"),
            P("ctx"),
            P("ctx", None),
            P("ctx"),
            P("ctx"),
            P("ctx"),
            P("ctx", None),
            P("ctx"),
            P("ctx", None),
            P("ctx"),
            P("ctx", None),
        ),
        out_specs=(
            P("ctx", None),
            P("ctx", None),
            P("ctx"),
            P("ctx"),
            P("ctx", None),
            P("ctx"),
            P("ctx"),
            P("ctx", None),
            P("ctx"),
            P("ctx"),
            P("ctx"),
            P("ctx", None),
            P("ctx"),
            P("ctx", None),
            P("ctx"),
        ),
        check_vma=False,
    )


AXES = ("s", "h", "r")
PLANES = 4


MESH_IDS = pl.DeviceIdType.MESH


class Exchange:
    def __init__(self, send, recv):
        self.send, self.recv, self.used, self.open = send, recv, 0, []
        self.s, self.h, self.r = (lax.axis_index(a) for a in AXES)
        self.planes = lax.axis_size("s")
        self.xn = self.h + 1 - 2 * lax.rem(self.h, 2)
        self.yn = lax.rem(self.h + 2, 4)
        self.dn = lax.rem(self.xn + 2, 4)
        self.z = lambda j: lax.rem(self.s + j, self.planes)
        self.X, self.Y, self.D = ({"h": i} for i in (self.xn, self.yn, self.dn))
        self.C = {"r": 1 - self.r}
        self.Z = [None] + [{"s": self.z(j)} for j in range(1, self.planes)]

    def greet(self, peers):
        barrier = pltpu.get_barrier_semaphore()
        for peer in peers:
            pl.semaphore_signal(barrier, inc=1, device_id=peer, device_id_type=MESH_IDS)
        pl.semaphore_wait(barrier, len(peers))

    def slots(self, count):
        self.used += count
        return range(self.used - count, self.used)

    def copy(self, i, src, dst, peer):
        return pltpu.make_async_remote_copy(
            src_ref=src,
            dst_ref=dst,
            send_sem=self.send.at[i],
            recv_sem=self.recv.at[i],
            device_id=peer,
            device_id_type=MESH_IDS,
        )

    def put(self, i, src, dst, peer):
        moved = self.copy(i, src, dst, peer)
        moved.start()
        self.open.append(moved)

    def got(self, i, dst):
        self.copy(i, dst, dst, self.X).wait_recv()

    def close(self):
        for moved in self.open:
            moved.wait_send()


def spread_kernel(x_ref, g_ref, w_ref, xa_ref, ga_ref, wa_ref, send, recv, local):
    ex = Exchange(send, recv)
    s, h, r, n = ex.s, ex.h, ex.r, ex.planes
    own = [
        pltpu.make_async_copy(x_ref.at[s], xa_ref.at[s, h], local.at[0]),
        pltpu.make_async_copy(w_ref.at[h], wa_ref.at[s, h, r], local.at[1]),
        pltpu.make_async_copy(g_ref.at[s], ga_ref.at[s], local.at[2]),
    ]
    for c in own:
        c.start()
    ex.greet([ex.X, ex.Y, ex.D, ex.C] + ex.Z[1:])
    iz, iw, ig = ex.slots(n), ex.slots(4), ex.slots(n)
    ix, iy, ir = ex.slots(n), ex.slots(n), ex.slots(n)
    iwz, iwc = ex.slots(n), ex.slots(n)
    for j in range(1, n):
        ex.put(iz[j], x_ref.at[ex.z(j)], xa_ref.at[s, h], ex.Z[j])
    for k, (peer, to) in enumerate(((ex.X, ex.xn), (ex.Y, ex.yn), (ex.D, ex.dn))):
        ex.put(iw[k], w_ref.at[to], wa_ref.at[s, h, r], peer)
    own[0].wait()

    def forward(j):
        t = ex.z(j)
        ex.put(ix[j], xa_ref.at[t, h], xa_ref.at[t, h], ex.X)
        ex.put(iy[j], xa_ref.at[t, h], xa_ref.at[t, h], ex.Y)

    def relay(j):
        t = ex.z(j)
        if j < n // 2:
            ex.got(ix[j], xa_ref.at[t, ex.xn])
            ex.put(ir[j], xa_ref.at[t, ex.xn], xa_ref.at[t, ex.xn], ex.Y)
        else:
            ex.got(iy[j], xa_ref.at[t, ex.yn])
            ex.put(ir[j], xa_ref.at[t, ex.yn], xa_ref.at[t, ex.yn], ex.X)

    forward(0)
    own[1].wait()
    for k, frm in enumerate((ex.xn, ex.yn, ex.dn)):
        ex.got(iw[k], wa_ref.at[s, frm, r])
    for j in range(1, n):
        ex.put(iwz[j], wa_ref.at[s, :, r], wa_ref.at[s, :, r], ex.Z[j])
    ex.put(iwc[0], wa_ref.at[s, :, r], wa_ref.at[s, :, r], ex.C)
    for j in (1, 3, 2):
        ex.got(iz[n - j], xa_ref.at[ex.z(j), h])
        forward(j)
    for j in range(1, n):
        ex.put(ig[j], g_ref.at[ex.z(j)], ga_ref.at[s], ex.Z[j])
    relay(0)
    for j in range(1, n):
        t = ex.z(j)
        ex.got(iwz[n - j], wa_ref.at[t, :, r])
        ex.put(iwc[j], wa_ref.at[t, :, r], wa_ref.at[t, :, r], ex.C)
    for j in (1, 3, 2):
        relay(j)
    for j in range(n):
        t = ex.z(j)
        if j < n // 2:
            ex.got(iy[j], xa_ref.at[t, ex.yn])
        else:
            ex.got(ix[j], xa_ref.at[t, ex.xn])
        ex.got(ir[j], xa_ref.at[t, ex.dn])
    for j in range(1, n):
        ex.got(ig[n - j], ga_ref.at[ex.z(j)])
    for j in range(n):
        ex.got(iwc[j], wa_ref.at[ex.z(j), :, 1 - r])
    own[2].wait()
    ex.close()


def remote_call(kernel, cid, out_shape, in_specs, out_specs, scratch, sems, name, vmem=56 << 20):
    return pl.pallas_call(
        kernel,
        out_shape=out_shape,
        in_specs=in_specs,
        out_specs=out_specs,
        scratch_shapes=scratch
        + [pltpu.SemaphoreType.DMA((sems,)), pltpu.SemaphoreType.DMA((sems,)), pltpu.SemaphoreType.DMA((8,))],
        compiler_params=pltpu.CompilerParams(
            collective_id=cid, has_side_effects=True, vmem_limit_bytes=vmem
        ),
        name=name,
    )


ANY = pl.BlockSpec(memory_space=pl.ANY)
VMEM = pl.BlockSpec(memory_space=pltpu.VMEM)


def spread_rows(x, g, w):
    S, U, D = x.shape
    H, d, N = w.shape
    Q = lax.axis_size("r")
    bf16 = jnp.bfloat16
    return remote_call(
        spread_kernel,
        0,
        [
            jax.ShapeDtypeStruct((S, H, U, D), bf16),
            jax.ShapeDtypeStruct((S, U, D), bf16),
            jax.ShapeDtypeStruct((S, H, Q, d, N), bf16),
        ],
        [ANY] * 3,
        [ANY] * 3,
        [],
        8 * S + 4,
        "spread",
    )(x, g, w)


def gather_kernel(count, *refs):
    ins, outs, (send, recv, local) = refs[:count], refs[count : 2 * count], refs[2 * count :]
    ex = Exchange(send, recv)
    s, h, r, n = ex.s, ex.h, ex.r, ex.planes
    own = [pltpu.make_async_copy(a, o.at[s, h, r], local.at[i]) for i, (a, o) in enumerate(zip(ins, outs))]
    for c in own:
        c.start()
    ex.greet([ex.X, ex.Y, ex.C] + ex.Z[1:])
    iz, ix, iy, ir, ic = ([ex.slots(n) for _ in outs] for _ in range(5))
    for j in range(1, n):
        for k, (a, o) in enumerate(zip(ins, outs)):
            ex.put(iz[k][j], a, o.at[s, h, r], ex.Z[j])
    for c in own:
        c.wait()

    def forward(j):
        t = ex.z(j)
        for k, o in enumerate(outs):
            if j:
                ex.got(iz[k][n - j], o.at[t, h, r])
            ex.put(ix[k][j], o.at[t, h, r], o.at[t, h, r], ex.X)
            ex.put(iy[k][j], o.at[t, h, r], o.at[t, h, r], ex.Y)

    def relay(j):
        t = ex.z(j)
        for k, o in enumerate(outs):
            if j < n // 2:
                ex.got(ix[k][j], o.at[t, ex.xn, r])
                ex.put(ir[k][j], o.at[t, ex.xn, r], o.at[t, ex.xn, r], ex.Y)
            else:
                ex.got(iy[k][j], o.at[t, ex.yn, r])
                ex.put(ir[k][j], o.at[t, ex.yn, r], o.at[t, ex.yn, r], ex.X)

    def across(j):
        t = ex.z(j)
        for k, o in enumerate(outs):
            if j < n // 2:
                ex.got(iy[k][j], o.at[t, ex.yn, r])
            else:
                ex.got(ix[k][j], o.at[t, ex.xn, r])
            ex.got(ir[k][j], o.at[t, ex.dn, r])
            ex.put(ic[k][j], o.at[t, :, r], o.at[t, :, r], ex.C)

    order = (0, 1, 3, 2)
    forward(0)
    for a, b in zip(order, order[1:]):
        forward(b)
        relay(a)
    relay(order[-1])
    for j in order:
        across(j)
    for j in order:
        for k, o in enumerate(outs):
            ex.got(ic[k][j], o.at[ex.z(j), :, 1 - r])
    ex.close()


def gather_all(*arrays):
    S, H, Q = (lax.axis_size(a) for a in AXES)
    n = len(arrays)
    return remote_call(
        partial(gather_kernel, n),
        1,
        [jax.ShapeDtypeStruct((S, H, Q) + a.shape, a.dtype) for a in arrays],
        [ANY] * n,
        [ANY] * n,
        [],
        5 * S * n,
        "gather_all",
    )(*arrays)


def by_tile(shape, step):
    height, width = shape
    if height % 16:

        @pl.loop(0, width // 768)
        def _(i):
            step(slice(None), pl.ds(pl.multiple_of(i * 768, 768), 768))
    else:

        @pl.loop(0, height // 32)
        def _(i):
            step(pl.ds(pl.multiple_of(i * 32, 32), 32), slice(None))


def reduce_kernel(count, *refs):
    ins, outs, rest = refs[:count], refs[count : 2 * count], refs[2 * count :]
    mine, from_c, one, two, from_z = (rest[i * count : (i + 1) * count] for i in range(5))
    send, recv, local = rest[5 * count :]
    ex = Exchange(send, recv)
    s, h, r, n = ex.s, ex.h, ex.r, ex.planes
    own = [
        pltpu.make_async_copy(a.at[:, :, r], m, local.at[k]) for k, (a, m) in enumerate(zip(ins, mine))
    ]
    for c in own:
        c.start()
    ex.greet([ex.X, ex.Y, ex.C] + ex.Z[1:])
    ic, i1, i2, iz = ([ex.slots(n) for _ in ins] for _ in range(4))
    i1b = [ex.slots(n) for _ in ins]
    order = (0, n // 2, 1, n // 2 + 1)
    for t in order:
        for k, a in enumerate(ins):
            ex.put(ic[k][t], a.at[t, :, 1 - r], from_c[k].at[t], ex.C)
    for c in own:
        c.wait()

    def add(to, part):
        def step(rows, cols):
            to[rows, cols] = (to[rows, cols].astype(jnp.float32) + part[rows, cols].astype(jnp.float32)).astype(to.dtype)

        by_tile(to.shape, step)

    def first(t):
        peer, near, other = (ex.X, ex.xn, ex.yn) if t < n // 2 else (ex.Y, ex.yn, ex.xn)
        for k, m in enumerate(mine):
            ex.got(ic[k][t], from_c[k].at[t])
            for i, to in ((i1, near), (i1b, ex.dn)):
                add(m.at[t, to], from_c[k].at[t, to])
                ex.put(i[k][t], m.at[t, to], one[k].at[t, 0 if i is i1 else 1], peer)
            for to in (h, other):
                add(m.at[t, to], from_c[k].at[t, to])

    def second(t):
        peer, other = (ex.Y, ex.yn) if t < n // 2 else (ex.X, ex.xn)
        for k, m in enumerate(mine):
            ex.got(i1b[k][t], one[k].at[t, 1])
            add(m.at[t, other], one[k].at[t, 1])
            ex.put(i2[k][t], m.at[t, other], two[k].at[t], peer)
            ex.got(i1[k][t], one[k].at[t, 0])
            add(m.at[t, h], one[k].at[t, 0])

    def third(t):
        for k, m in enumerate(mine):
            ex.got(i2[k][t], two[k].at[t])
            add(m.at[t, h], two[k].at[t])

    def far(j):
        t = ex.z(j)
        for k, m in enumerate(mine):
            ex.put(iz[k][j], m.at[t, h], from_z[k].at[j], ex.Z[j])

    for a, b in zip((None,) + order, order + (None,)):
        if b is not None:
            first(b)
        if a is not None:
            second(a)
    for t in order:
        third(t)
    for j in range(1, n):
        far(j)
    for k, (m, o) in enumerate(zip(mine, outs)):
        for j in range(1, n):
            ex.got(iz[k][j], from_z[k].at[j])

        def step(rows, cols):
            total = m[s, h, rows, cols].astype(jnp.float32)
            for j in range(1, n):
                total += from_z[k][j, rows, cols].astype(jnp.float32)
            o[rows, cols] = total

        by_tile(o.shape, step)

    ex.close()


def reduce_all(*arrays):
    S, H, Q = (lax.axis_size(a) for a in AXES)
    n = len(arrays)
    tails = [a.shape[3:] for a in arrays]
    buffers = [
        [pltpu.VMEM(lead + t, jnp.bfloat16) for t in tails] for lead in ((S, H), (S, H), (S, 2), (S,), (S,))
    ]
    return remote_call(
        partial(reduce_kernel, n),
        2,
        [jax.ShapeDtypeStruct(t, jnp.float32) for t in tails],
        [ANY] * n,
        [VMEM] * n,
        sum(buffers, []),
        5 * S * n,
        "reduce_all",
    )(*arrays)


def planes(
    hidden_in,
    block_pairs,
    ln1_gain,
    ln1_bias,
    qkv_weight,
    query_bias,
    value_bias,
    out_weight,
    out_bias,
    ln2_gain,
    ln2_bias,
    fc_weight,
    fc_bias,
    proj_weight,
    proj_bias,
    out_grad,
):
    f32, bf16 = jnp.float32, jnp.bfloat16
    s, h, r = (lax.axis_index(a) for a in AXES)
    S, H, Q = (lax.axis_size(a) for a in AXES)
    rows, D = hidden_in.shape
    U = rows // SEQS
    W = D // H
    bfn = fc_bias.shape[0]
    d = qkv_weight.shape[0]
    vectors = [ln1_gain, ln1_bias, query_bias, value_bias, out_bias, ln2_gain, ln2_bias, proj_bias, fc_bias]
    sizes = [v.shape[0] for v in vectors]
    offs = [sum(sizes[:i]) for i in range(len(sizes))]
    line = jnp.concatenate(vectors)
    w4 = qkv_weight.reshape(d, 3, H, W).transpose(2, 0, 1, 3).reshape(H, d, 3 * W)
    line = jnp.zeros((8, 3 * W), bf16).at[0, : line.shape[0]].set(line)
    w4 = jnp.concatenate([w4, jnp.broadcast_to(line[None], (H,) + line.shape)], axis=1)
    x_all, g_own, w_all = spread_rows(hidden_in.reshape(S, U, D), out_grad.reshape(S, U, D), w4)
    w_all = w_all.reshape(-1, d + 8, 3 * W)
    w_h = w_all[:, :d].reshape(D, 3 * W)
    allv = w_all[:, d, : sum(sizes)]
    g1, b1, bq, bv, bo, g2, b2, bp, bf = (
        allv[:, o : o + n].reshape(-1).astype(f32) for o, n in zip(offs, sizes)
    )
    pad8 = lambda y: jnp.concatenate([y, jnp.zeros((8, y.shape[1]), y.dtype)])
    w_fc, w_proj, w_out = gather_all(fc_weight, proj_weight, pad8(out_weight))
    w_fc, w_proj = w_fc.reshape(D, -1), w_proj.reshape(-1, D)
    w_out = w_out.reshape(-1, d + 8, D)[:, :d].reshape(D, D)

    blk = block_pairs[::2]
    blk = jnp.where(s % 2 == 0, blk, blk.shape[0] - 1 - blk)
    npair = blk.shape[0]
    inv = jnp.sum(
        jnp.where(blk[None, :] == jnp.arange(npair)[:, None], jnp.arange(npair)[None, :], 0), axis=1
    ).astype(jnp.int32)

    x_own = lax.dynamic_index_in_dim(x_all, h, 1, keepdims=False).reshape(rows, D).astype(f32)
    x_all = x_all.reshape(-1, D)
    g_own = g_own.reshape(rows, D)

    normed = layer_norm(x_all.astype(f32), g1, b1).astype(bf16)
    mixed = jnp.dot(normed, w_h, preferred_element_type=f32)
    bq_h = lax.dynamic_slice_in_dim(bq, h * W, W)
    bv_h = lax.dynamic_slice_in_dim(bv, h * W, W)
    q = (mixed[:, :W] + bq_h).astype(bf16)
    k = mixed[:, W : 2 * W].astype(bf16)
    v = (mixed[:, 2 * W :] + bv_h).astype(bf16)
    q_scaled = q * jnp.asarray(0.125, bf16)

    def from_other(t):
        return lax.ppermute(t, "r", [(0, 1), (1, 0)])

    def both(t):
        return jnp.concatenate(
            [t.reshape(npair, U, W), from_other(t).reshape(npair, U, W)], axis=1
        ).reshape(npair * 2 * U, W)

    k_all, v_all = both(k), both(v)
    att, lse = attend(inv, q_scaled, k_all, v_all)
    att_low = lax.all_to_all(att.astype(bf16).reshape(S, H, U, W), "h", 1, 1)
    att_low = att_low.transpose(0, 2, 1, 3).reshape(rows, D)

    middle = x_own + jnp.dot(att_low, w_out, preferred_element_type=f32) + bo
    normed_two = layer_norm(middle, g2, b2).astype(bf16)
    pre_act = jnp.dot(normed_two, w_fc, preferred_element_type=f32) + bf
    activation = gelu_tanh(pre_act).astype(bf16)
    layer_out = (middle + jnp.dot(activation, w_proj, preferred_element_type=f32) + bp).astype(bf16)
    grad_out = g_own.astype(f32)
    grad_proj = jnp.dot(activation.T, g_own, preferred_element_type=f32)
    grad_bproj = jnp.sum(grad_out, axis=0)
    grad_activ = jnp.dot(g_own, w_proj.T, preferred_element_type=f32)
    _, gelu_back = jax.vjp(gelu_tanh, pre_act)
    grad_pre = gelu_back(grad_activ)[0].astype(bf16)
    grad_fc = jnp.dot(normed_two.T, grad_pre, preferred_element_type=f32)
    grad_bfc = jnp.sum(grad_pre.astype(f32), axis=0)
    grad_normed_two = jnp.dot(grad_pre, w_fc.T, preferred_element_type=f32)
    _, norm_back_two = jax.vjp(layer_norm, middle, g2, b2)
    grad_middle, grad_g2, grad_b2 = norm_back_two(grad_normed_two)
    grad_middle = grad_middle + grad_out
    grad_branch = grad_middle.astype(bf16)
    grad_wout = jnp.dot(att_low.T, grad_branch, preferred_element_type=f32)
    grad_bout = jnp.sum(grad_branch.astype(f32), axis=0)
    grad_att = jnp.dot(grad_branch, w_out.T, preferred_element_type=f32).astype(bf16)

    g_att = lax.all_to_all(grad_att.reshape(S, U, H, W).transpose(0, 2, 1, 3), "h", 1, 1)
    dq, dk, dv = attend_back(inv, q_scaled, k_all, v_all, g_att.reshape(-1, W), att, lse)
    dkv = jnp.stack([dk, dv]).reshape(2, npair, 2, U, W)
    dkv = dkv[:, :, 0] + from_other(dkv[:, :, 1])
    dkv = dkv.reshape(2, -1, W).astype(bf16)
    grad_mixed = jnp.concatenate([dq, dkv[0], dkv[1]], axis=1)
    grad_qkv = jnp.dot(normed.T, grad_mixed, preferred_element_type=f32)
    cols = jnp.sum(grad_mixed.astype(f32), axis=0)
    t = jnp.dot(grad_mixed, w_h.T, preferred_element_type=f32)
    t = lax.psum_scatter(t.reshape(S, H, U, D), "h", scatter_dimension=1, tiled=False)
    _, norm_back_one = jax.vjp(layer_norm, x_own, g1, b1)
    grad_inputs, grad_g1, grad_b1 = norm_back_one(t.reshape(rows, D))
    grad_hidden = (grad_inputs + grad_middle).astype(bf16)
    back = lambda y: lax.all_to_all(y.reshape(S, U, D), "s", 0, 0).reshape(rows, D)

    gq = grad_qkv.reshape(S, H, Q, d, 3 * W)
    gq = lax.psum_scatter(lax.psum_scatter(gq, "s", scatter_dimension=0, tiled=False), "r", scatter_dimension=1, tiled=False)
    gq = lax.all_to_all(gq, "h", 0, 0)
    gq = gq.reshape(H, d, 3, W).transpose(1, 2, 0, 3).reshape(d, 3 * D)
    place = lambda c: lax.dynamic_update_slice_in_dim(jnp.zeros((D,), f32), c, h * W, 0)
    scat = lambda y: lax.psum_scatter(y, AXES, scatter_dimension=0, tiled=True)
    early = [grad_bout, grad_g2, grad_b2, grad_bproj]
    line = jnp.concatenate([y.reshape(-1, d) for y in early] + [grad_bfc.reshape(-1, bfn)], axis=1)
    line = jnp.concatenate([line, jnp.zeros((line.shape[0], D - line.shape[1]), f32)], axis=1)
    slab = jnp.concatenate(
        [grad_wout.reshape(-1, d, D), line[:, None], jnp.zeros((line.shape[0], 7, D), f32)], axis=1
    )
    shard = lambda y: y.astype(bf16).reshape((S, H, Q) + y.shape[1:])
    gfc, gproj, gslab = reduce_all(
        shard(grad_fc.reshape(S * H * Q, d, -1)), shard(grad_proj.reshape(S * H * Q, -1, D)), shard(slab)
    )
    g1s, b1s, bqs, bvs = [scat(y) for y in (grad_g1, grad_b1, place(cols[:W]), place(cols[2 * W :]))]
    row = gslab[d]
    return (
        back(layer_out),
        back(grad_hidden),
        g1s,
        b1s,
        gq,
        bqs,
        bvs,
        gslab[:d],
        row[:d],
        row[d : 2 * d],
        row[2 * d : 3 * d],
        gfc,
        row[4 * d : 4 * d + bfn],
        gproj,
        row[3 * d : 4 * d],
    )


def solution(mesh):
    n = mesh.shape["ctx"]
    if n // (PLANES * SEQS) != 2:
        return solution_any(mesh)
    split = Mesh(mesh.devices.reshape(PLANES, SEQS, -1), AXES)
    row, vec = P(AXES, None), P(AXES)
    return jax.shard_map(
        planes,
        mesh=split,
        in_specs=(row, P(), vec, vec, row, vec, vec, row, vec, vec, vec, row, vec, row, vec, row),
        out_specs=(row, row, vec, vec, row, vec, vec, row, vec, vec, vec, row, vec, row, vec),
        check_vma=False,
    )
```

```python
from functools import partial
import math

import jax
import jax.numpy as jnp
from jax import lax
from jax.sharding import PartitionSpec as P
from jax.experimental import pallas as pl
from jax.experimental.pallas import tpu as pltpu
from jax.sharding import Mesh

HEADS = 12
SEQS = 4


NEG = -1e30


def from_partner(value, axis, bit):
    return lax.ppermute(value, axis, [(i, i ^ 1 << bit) for i in range(lax.axis_size(axis))])


def layer_norm(values, gain, bias):
    center = values - jnp.mean(values, axis=-1, keepdims=True)
    spread_sq = jnp.mean(center * center, axis=-1, keepdims=True)
    return center * lax.rsqrt(spread_sq + 1e-05) * gain + bias


def gelu_tanh(values):
    return jax.nn.gelu(values, approximate=True)


def heads_of(tensor, head_count):
    return tensor.reshape(tensor.shape[:-1] + (head_count, tensor.shape[-1] // head_count))


def pick_own(owned, chosen):
    selector = chosen.reshape((1, -1) + (1,) * (owned.ndim - 2))
    return jnp.where(selector, owned[:, 0:1], owned[:, 1:2])


def pick_piece(piece, chosen):
    selector = chosen.reshape((1, -1) + (1,) * (piece.ndim - 3))
    return jnp.where(selector, piece[:, 0], piece[:, 1])


def parity_masks(chosen, usable):
    return jnp.stack([chosen & usable, jnp.logical_not(chosen) & usable])


def spread(values, parity):
    shaped = parity.reshape((1,) + parity.shape + (1,) * (values.ndim - 2))
    return jnp.sum(jnp.where(shaped, values[:, None], 0.0), axis=2)


def group_loop(pieces, unit_rows, table, stepper, carried):
    piece_rows = pieces[0].shape[2]
    group_size = min(unit_rows, piece_rows)
    group_count = piece_rows // group_size
    batch_groups = math.gcd(group_count, max(1, 1024 // group_size))
    turn_count = group_count // batch_groups
    shaped = tuple(
        (
            item.reshape(item.shape[:2] + (group_count, group_size) + item.shape[3:])
            for item in pieces
        )
    )
    device_ids = jnp.arange(group_count, dtype=jnp.int32) * group_size // unit_rows
    table_size = table.shape[0]
    blocks = jnp.sum(
        jnp.where(
            device_ids[:, None] == jnp.arange(table_size, dtype=jnp.int32)[None, :],
            table[None, :],
            0,
        ),
        axis=1,
    )

    def one_turn(position, current):
        pieces_now = tuple(
            (
                lax.dynamic_slice_in_dim(item, position * batch_groups, batch_groups, 2)
                for item in shaped
            )
        )
        chosen = lax.dynamic_slice_in_dim(blocks, position * batch_groups, batch_groups, 0)
        return stepper(current, pieces_now, chosen)

    return lax.fori_loop(0, turn_count, one_turn, carried)


def attend_step(q_heads, my_block, score_scale, head_count, carried, pieces_now, chosen):
    key_piece = heads_of(pieces_now[0], head_count)
    value_piece = heads_of(pieces_now[1], head_count)
    earlier = chosen < my_block
    usable = chosen != my_block
    parity = parity_masks(earlier, usable)
    query_sel = pick_own(q_heads, earlier)
    key_sel = pick_piece(key_piece, earlier)
    value_sel = pick_piece(value_piece, earlier)
    scores = (
        jnp.einsum("jgqhe,jgkhe->jghqk", query_sel, key_sel, preferred_element_type=jnp.float32)
        * score_scale
    )
    usable_mask = usable.reshape(1, -1, 1, 1, 1)
    scores = jnp.where(usable_mask, scores, NEG)
    old_max, old_total, old_sum = carried
    group_max = jnp.max(scores, axis=-1)
    candidate = jnp.max(jnp.where(parity.reshape(1, 2, -1, 1, 1), group_max[:, None], NEG), axis=2)
    new_max = jnp.maximum(old_max, candidate)
    max_sel = pick_own(new_max, earlier)
    weights_exp = jnp.where(usable_mask, jnp.exp(scores - max_sel[..., None]), 0.0)
    moved = jnp.einsum(
        "jghqk,jgkhe->jgqhe",
        weights_exp.astype(jnp.bfloat16),
        value_sel,
        preferred_element_type=jnp.float32,
    )
    factor = jnp.exp(old_max - new_max)
    new_total = old_total * factor + spread(jnp.sum(weights_exp, axis=-1), parity)
    new_sum = old_sum * jnp.swapaxes(factor, 2, 3)[..., None] + spread(moved, parity)
    return (new_max, new_total, new_sum)


def query_grad_step(
    q_heads,
    grad_heads,
    lse_heads,
    delta_heads,
    my_block,
    score_scale,
    head_count,
    carried,
    pieces_now,
    chosen,
):
    key_piece = heads_of(pieces_now[0], head_count)
    value_piece = heads_of(pieces_now[1], head_count)
    earlier = chosen < my_block
    usable = chosen != my_block
    parity = parity_masks(earlier, usable)
    query_sel = pick_own(q_heads, earlier)
    grad_sel = pick_own(grad_heads, earlier)
    lse_sel = pick_own(lse_heads, earlier)
    delta_sel = pick_own(delta_heads, earlier)
    key_sel = pick_piece(key_piece, earlier)
    value_sel = pick_piece(value_piece, earlier)
    scores = (
        jnp.einsum("jgqhe,jgkhe->jghqk", query_sel, key_sel, preferred_element_type=jnp.float32)
        * score_scale
    )
    usable_mask = usable.reshape(1, -1, 1, 1, 1)
    probabilities = jnp.where(usable_mask, jnp.exp(scores - lse_sel[..., None]), 0.0)
    grad_probs = jnp.einsum(
        "jgqhe,jgkhe->jghqk", grad_sel, value_sel, preferred_element_type=jnp.float32
    )
    grad_scores = (probabilities * (grad_probs - delta_sel[..., None])).astype(jnp.bfloat16)
    term = (
        jnp.einsum("jghqk,jgkhe->jgqhe", grad_scores, key_sel, preferred_element_type=jnp.float32)
        * score_scale
    )
    return carried + spread(term, parity)


def key_grad_step(k_heads, v_heads, my_block, score_scale, head_count, carried, pieces_now, chosen):
    query_piece = heads_of(pieces_now[0], head_count)
    grad_piece = heads_of(pieces_now[1], head_count)
    later = my_block < chosen
    usable = chosen != my_block
    parity = parity_masks(later, usable)
    query_sel = pick_piece(query_piece, later)
    grad_sel = pick_piece(grad_piece, later)
    lse_sel = jnp.swapaxes(pick_piece(pieces_now[2], later), 2, 3)
    delta_sel = jnp.swapaxes(pick_piece(pieces_now[3], later), 2, 3)
    key_sel = pick_own(k_heads, later)
    value_sel = pick_own(v_heads, later)
    scores = (
        jnp.einsum("jgqhe,jgkhe->jghqk", query_sel, key_sel, preferred_element_type=jnp.float32)
        * score_scale
    )
    usable_mask = usable.reshape(1, -1, 1, 1, 1)
    probabilities = jnp.where(usable_mask, jnp.exp(scores - lse_sel[..., None]), 0.0)
    grad_probs = jnp.einsum(
        "jgqhe,jgkhe->jghqk", grad_sel, value_sel, preferred_element_type=jnp.float32
    )
    grad_scores = (probabilities * (grad_probs - delta_sel[..., None])).astype(jnp.bfloat16)
    key_term = (
        jnp.einsum("jghqk,jgqhe->jgkhe", grad_scores, query_sel, preferred_element_type=jnp.float32)
        * score_scale
    )
    value_term = jnp.einsum(
        "jghqk,jgqhe->jgkhe",
        probabilities.astype(jnp.bfloat16),
        grad_sel,
        preferred_element_type=jnp.float32,
    )
    return (carried[0] + spread(key_term, parity), carried[1] + spread(value_term, parity))


def shards(
    hidden_in,
    block_pairs,
    ln1_gain,
    ln1_bias,
    qkv_weight,
    query_bias,
    value_bias,
    out_weight,
    out_bias,
    ln2_gain,
    ln2_bias,
    fc_weight,
    fc_bias,
    proj_weight,
    proj_bias,
    out_grad,
):
    params = (
        ln1_gain,
        ln1_bias,
        qkv_weight,
        query_bias,
        value_bias,
        out_weight,
        out_bias,
        ln2_gain,
        ln2_bias,
        fc_weight,
        fc_bias,
        proj_weight,
        proj_bias,
    )
    gathered = (
        lax.all_gather(params[0], "ctx", axis=0, tiled=True),
        lax.all_gather(params[1], "ctx", axis=0, tiled=True),
        lax.all_gather(params[2], "ctx", axis=0, tiled=True),
        lax.all_gather(params[3], "ctx", axis=0, tiled=True),
        lax.all_gather(params[4], "ctx", axis=0, tiled=True),
        lax.all_gather(params[5], "ctx", axis=0, tiled=True),
        lax.all_gather(params[6], "ctx", axis=0, tiled=True),
        lax.all_gather(params[7], "ctx", axis=0, tiled=True),
        lax.all_gather(params[8], "ctx", axis=0, tiled=True),
        lax.all_gather(params[9], "ctx", axis=0, tiled=True),
        lax.all_gather(params[10], "ctx", axis=0, tiled=True),
        lax.all_gather(params[11], "ctx", axis=0, tiled=True),
        lax.all_gather(params[12], "ctx", axis=0, tiled=True),
    )
    (
        gain_one,
        bias_one,
        w_qkv,
        b_query,
        b_value,
        w_out,
        b_out,
        gain_two,
        bias_two,
        w_fc,
        b_fc,
        w_proj,
        b_proj,
    ) = gathered
    device = lax.axis_index("ctx")
    partner = device + 1 - 2 * (device % 2)
    row_count = hidden_in.shape[0]
    model_width = hidden_in.shape[1]
    unit_rows = row_count // SEQS
    halves = SEQS // 2
    head_count = HEADS
    head_size = model_width // head_count
    score_scale = 1.0 / math.sqrt(head_size)
    my_block = block_pairs[device]
    seq_shape = (halves, 2, unit_rows, model_width)
    head_shape = (halves, 2, unit_rows, head_count, head_size)
    inputs = hidden_in.astype(jnp.float32)
    normed = layer_norm(inputs, gain_one.astype(jnp.float32), bias_one.astype(jnp.float32)).astype(
        jnp.bfloat16
    )
    mixed_proj = jnp.dot(normed, w_qkv, preferred_element_type=jnp.float32)
    queries = (mixed_proj[:, :model_width] + b_query.astype(jnp.float32)).astype(jnp.bfloat16)
    key_rows = mixed_proj[:, model_width : 2 * model_width].astype(jnp.bfloat16)
    value_rows = (mixed_proj[:, 2 * model_width :] + b_value.astype(jnp.float32)).astype(
        jnp.bfloat16
    )
    q_seq = queries.reshape(seq_shape)
    k_seq = key_rows.reshape(seq_shape)
    v_seq = value_rows.reshape(seq_shape)
    q_heads = queries.reshape(head_shape)
    k_heads = key_rows.reshape(head_shape)
    v_heads = value_rows.reshape(head_shape)
    far_keys, far_values = from_partner((k_seq, v_seq), "ctx", 0)
    near_keys = jnp.concatenate([k_heads, heads_of(far_keys, head_count)], axis=2)
    near_values = jnp.concatenate([v_heads, heads_of(far_values, head_count)], axis=2)
    scores = (
        jnp.einsum("jpqhe,jpkhe->jphqk", q_heads, near_keys, preferred_element_type=jnp.float32)
        * score_scale
    )
    row_max = jnp.max(scores, axis=-1)
    weights_exp = jnp.exp(scores - row_max[..., None])
    row_total = jnp.sum(weights_exp, axis=-1)
    summed = jnp.einsum(
        "jphqk,jpkhe->jpqhe",
        weights_exp.astype(jnp.bfloat16),
        near_values,
        preferred_element_type=jnp.float32,
    )
    forward_stepper = partial(attend_step, q_heads, my_block, score_scale, head_count)
    row_max, row_total, summed = group_loop(
        (
            lax.all_gather(k_seq, "ctx", axis=2, tiled=True),
            lax.all_gather(v_seq, "ctx", axis=2, tiled=True),
        ),
        unit_rows,
        block_pairs,
        forward_stepper,
        (row_max, row_total, summed),
    )
    attended = summed / jnp.swapaxes(row_total, 2, 3)[..., None]
    log_total = row_max + jnp.log(row_total)
    att_low = attended.reshape(row_count, model_width).astype(jnp.bfloat16)
    branch = jnp.dot(att_low, w_out, preferred_element_type=jnp.float32) + b_out.astype(jnp.float32)
    middle = inputs + branch
    normed_two = layer_norm(
        middle, gain_two.astype(jnp.float32), bias_two.astype(jnp.float32)
    ).astype(jnp.bfloat16)
    pre_act = jnp.dot(normed_two, w_fc, preferred_element_type=jnp.float32) + b_fc.astype(
        jnp.float32
    )
    activation = gelu_tanh(pre_act).astype(jnp.bfloat16)
    result = (
        middle
        + jnp.dot(activation, w_proj, preferred_element_type=jnp.float32)
        + b_proj.astype(jnp.float32)
    )
    layer_out = result.astype(jnp.bfloat16)
    grad_out = out_grad.astype(jnp.float32)
    grad_proj = jnp.dot(activation.T, out_grad, preferred_element_type=jnp.float32)
    grad_bproj = jnp.sum(grad_out, axis=0)
    grad_activ = jnp.dot(out_grad, w_proj.T, preferred_element_type=jnp.float32)
    _, gelu_back = jax.vjp(gelu_tanh, pre_act)
    grad_pre = gelu_back(grad_activ)[0].astype(jnp.bfloat16)
    grad_fc = jnp.dot(normed_two.T, grad_pre, preferred_element_type=jnp.float32)
    grad_bfc = jnp.sum(grad_pre.astype(jnp.float32), axis=0)
    grad_normed_two = jnp.dot(grad_pre, w_fc.T, preferred_element_type=jnp.float32)
    _, norm_back_two = jax.vjp(
        layer_norm, middle, gain_two.astype(jnp.float32), bias_two.astype(jnp.float32)
    )
    grad_middle, grad_gain_two, grad_bias_two = norm_back_two(grad_normed_two)
    grad_middle = grad_middle + grad_out
    grad_branch = grad_middle.astype(jnp.bfloat16)
    grad_wout = jnp.dot(att_low.T, grad_branch, preferred_element_type=jnp.float32)
    grad_bout = jnp.sum(grad_branch.astype(jnp.float32), axis=0)
    grad_att = jnp.dot(grad_branch, w_out.T, preferred_element_type=jnp.float32).astype(
        jnp.bfloat16
    )
    grad_seq = grad_att.reshape(seq_shape)
    grad_heads = grad_att.reshape(head_shape)
    row_delta = jnp.sum(grad_heads.astype(jnp.float32) * attended, axis=-1)
    delta_heads = jnp.swapaxes(row_delta, 2, 3)
    all_lse, all_delta = (
        lax.all_gather(jnp.swapaxes(log_total, 2, 3), "ctx", axis=2, tiled=True),
        lax.all_gather(row_delta, "ctx", axis=2, tiled=True),
    )
    partner_lse = jnp.swapaxes(
        lax.dynamic_slice_in_dim(all_lse, partner * unit_rows, unit_rows, 2), 2, 3
    )
    partner_delta = jnp.swapaxes(
        lax.dynamic_slice_in_dim(all_delta, partner * unit_rows, unit_rows, 2), 2, 3
    )
    far_queries, far_grads = from_partner((q_seq, grad_seq), "ctx", 0)
    near_queries = jnp.concatenate([q_heads, heads_of(far_queries, head_count)], axis=2)
    near_grads = jnp.concatenate([grad_heads, heads_of(far_grads, head_count)], axis=2)
    near_lse = jnp.concatenate([log_total, partner_lse], axis=3)
    near_delta = jnp.concatenate([delta_heads, partner_delta], axis=3)
    local_scores = (
        jnp.einsum(
            "jpqhe,jpkhe->jphqk", near_queries, near_keys, preferred_element_type=jnp.float32
        )
        * score_scale
    )
    probabilities = jnp.exp(local_scores - near_lse[..., None])
    grad_probs = jnp.einsum(
        "jpqhe,jpkhe->jphqk", near_grads, near_values, preferred_element_type=jnp.float32
    )
    grad_scores = (probabilities * (grad_probs - near_delta[..., None])).astype(jnp.bfloat16)
    grad_q_local = (
        jnp.einsum(
            "jphqk,jpkhe->jpqhe",
            grad_scores[:, :, :, :unit_rows, :],
            near_keys,
            preferred_element_type=jnp.float32,
        )
        * score_scale
    )
    grad_k_local = (
        jnp.einsum(
            "jphqk,jpqhe->jpkhe",
            grad_scores[..., :unit_rows],
            near_queries,
            preferred_element_type=jnp.float32,
        )
        * score_scale
    )
    grad_v_local = jnp.einsum(
        "jphqk,jpqhe->jpkhe",
        probabilities.astype(jnp.bfloat16)[..., :unit_rows],
        near_grads,
        preferred_element_type=jnp.float32,
    )
    query_stepper = partial(
        query_grad_step,
        q_heads,
        grad_heads,
        log_total,
        delta_heads,
        my_block,
        score_scale,
        head_count,
    )
    key_stepper = partial(key_grad_step, k_heads, v_heads, my_block, score_scale, head_count)

    def query_piece(carried, pieces, offset):
        return group_loop(pieces, unit_rows, block_pairs, query_stepper, carried)

    def key_piece(carried, pieces, offset):
        return group_loop(
            (pieces[0], pieces[1], all_lse, all_delta), unit_rows, block_pairs, key_stepper, carried
        )

    grad_q_all = query_piece(
        grad_q_local,
        (
            lax.all_gather(k_seq, "ctx", axis=2, tiled=True),
            lax.all_gather(v_seq, "ctx", axis=2, tiled=True),
        ),
        jnp.int32(0),
    )
    grad_k_all, grad_v_all = key_piece(
        (grad_k_local, grad_v_local),
        (
            lax.all_gather(q_seq, "ctx", axis=2, tiled=True),
            lax.all_gather(grad_seq, "ctx", axis=2, tiled=True),
        ),
        jnp.int32(0),
    )
    grad_queries = grad_q_all.reshape(row_count, model_width).astype(jnp.bfloat16)
    grad_keys = grad_k_all.reshape(row_count, model_width).astype(jnp.bfloat16)
    grad_values = grad_v_all.reshape(row_count, model_width).astype(jnp.bfloat16)
    grad_mixed = jnp.concatenate([grad_queries, grad_keys, grad_values], axis=1)
    grad_qkv = jnp.dot(normed.T, grad_mixed, preferred_element_type=jnp.float32)
    grad_bquery = jnp.sum(grad_queries.astype(jnp.float32), axis=0)
    grad_bvalue = jnp.sum(grad_values.astype(jnp.float32), axis=0)
    grad_normed = jnp.dot(grad_mixed, w_qkv.T, preferred_element_type=jnp.float32)
    _, norm_back_one = jax.vjp(
        layer_norm, inputs, gain_one.astype(jnp.float32), bias_one.astype(jnp.float32)
    )
    grad_inputs, grad_gain_one, grad_bias_one = norm_back_one(grad_normed)
    grad_hidden = (grad_inputs + grad_middle).astype(jnp.bfloat16)
    totals = (
        lax.psum_scatter(grad_gain_one, "ctx", scatter_dimension=0, tiled=True),
        lax.psum_scatter(grad_bias_one, "ctx", scatter_dimension=0, tiled=True),
        lax.psum_scatter(grad_qkv, "ctx", scatter_dimension=0, tiled=True),
        lax.psum_scatter(grad_bquery, "ctx", scatter_dimension=0, tiled=True),
        lax.psum_scatter(grad_bvalue, "ctx", scatter_dimension=0, tiled=True),
        lax.psum_scatter(grad_wout, "ctx", scatter_dimension=0, tiled=True),
        lax.psum_scatter(grad_bout, "ctx", scatter_dimension=0, tiled=True),
        lax.psum_scatter(grad_gain_two, "ctx", scatter_dimension=0, tiled=True),
        lax.psum_scatter(grad_bias_two, "ctx", scatter_dimension=0, tiled=True),
        lax.psum_scatter(grad_fc, "ctx", scatter_dimension=0, tiled=True),
        lax.psum_scatter(grad_bfc, "ctx", scatter_dimension=0, tiled=True),
        lax.psum_scatter(grad_proj, "ctx", scatter_dimension=0, tiled=True),
        lax.psum_scatter(grad_bproj, "ctx", scatter_dimension=0, tiled=True),
    )
    return (
        layer_out,
        grad_hidden,
        totals[0],
        totals[1],
        totals[2],
        totals[3],
        totals[4],
        totals[5],
        totals[6],
        totals[7],
        totals[8],
        totals[9],
        totals[10],
        totals[11],
        totals[12],
    )


def solution_any(mesh):
    return jax.shard_map(
        shards,
        mesh=mesh,
        in_specs=(
            P("ctx", None),
            P(),
            P("ctx"),
            P("ctx"),
            P("ctx", None),
            P("ctx"),
            P("ctx"),
            P("ctx", None),
            P("ctx"),
            P("ctx"),
            P("ctx"),
            P("ctx", None),
            P("ctx"),
            P("ctx", None),
            P("ctx"),
            P("ctx", None),
        ),
        out_specs=(
            P("ctx", None),
            P("ctx", None),
            P("ctx"),
            P("ctx"),
            P("ctx", None),
            P("ctx"),
            P("ctx"),
            P("ctx", None),
            P("ctx"),
            P("ctx"),
            P("ctx"),
            P("ctx", None),
            P("ctx"),
            P("ctx", None),
            P("ctx"),
        ),
        check_vma=False,
    )


AXES = ("s", "h", "r")
PLANES = 4


MESH_IDS = pl.DeviceIdType.MESH


class At:
    def __init__(self, ref, *index):
        self.ref, self.index = ref, index

    def now(self):
        return self.ref.at[self.index]

    def still(self):
        return self.ref.at[tuple(i if isinstance(i, slice) else 0 for i in self.index)]


ALL = slice(None)


class Exchange:
    def __init__(self, send, recv):
        self.send, self.recv, self.used, self.open = send, recv, 0, []
        self.s, self.h, self.r = (lax.axis_index(a) for a in AXES)
        self.planes = lax.axis_size("s")
        self.xn = self.h + 1 - 2 * lax.rem(self.h, 2)
        self.yn = lax.rem(self.h + 2, 4)
        self.dn = lax.rem(self.xn + 2, 4)
        self.z = lambda j: lax.rem(self.s + j, self.planes)
        self.X, self.Y, self.D = ({"h": i} for i in (self.xn, self.yn, self.dn))
        self.C = {"r": 1 - self.r}
        self.Z = [None] + [{"s": self.z(j)} for j in range(1, self.planes)]

    def greet(self, peers):
        barrier = pltpu.get_barrier_semaphore()
        for peer in peers:
            pl.semaphore_signal(barrier, inc=1, device_id=peer, device_id_type=MESH_IDS)
        pl.semaphore_wait(barrier, len(peers))

    def slots(self, count):
        self.used += count
        return range(self.used - count, self.used)

    def copy(self, i, src, dst, peer):
        return pltpu.make_async_remote_copy(
            src_ref=src,
            dst_ref=dst,
            send_sem=self.send.at[i],
            recv_sem=self.recv.at[i],
            device_id=peer,
            device_id_type=MESH_IDS,
        )

    def put(self, i, src, dst, peer):
        self.copy(i, src.now() if isinstance(src, At) else src, dst, peer).start()
        self.open.append((i, src))

    def got(self, i, dst):
        self.copy(i, dst, dst, self.X).wait_recv()

    def close(self):
        for i, src in self.open:
            src = src.still() if isinstance(src, At) else src
            self.copy(i, src, src, self.X).wait_send()


def remote_call(kernel, cid, out_shape, in_specs, out_specs, scratch, sems, name, vmem=56 << 20):
    return pl.pallas_call(
        kernel,
        out_shape=out_shape,
        in_specs=in_specs,
        out_specs=out_specs,
        scratch_shapes=scratch
        + [pltpu.SemaphoreType.DMA((sems,)), pltpu.SemaphoreType.DMA((sems,)), pltpu.SemaphoreType.DMA((8,))],
        compiler_params=pltpu.CompilerParams(
            collective_id=cid, has_side_effects=True, vmem_limit_bytes=vmem
        ),
        name=name,
    )


ANY = pl.BlockSpec(memory_space=pl.ANY)
VMEM = pl.BlockSpec(memory_space=pltpu.VMEM)


GATHER_ORDER = (2, 0, 1)


def by_x(k, j):
    return (k + j) % 2 == 0


def act(plan, steps, m, c, last_tile):
    for (em, ec), todo in plan.items():
        if (em == ec) == last_tile:

            @pl.when(m == em if last_tile else (m == em) & (c == ec))
            def _():
                for step, k, *js in todo:
                    for j in js:
                        steps[step](k, j)


def gather_steps(ins, outs, g_ref, ga_ref, send, recv, local):
    ex = Exchange(send, recv)
    s, h, r, n = ex.s, ex.h, ex.r, ex.planes
    own = [pltpu.make_async_copy(a, o.at[s, h, r], local.at[i]) for i, (a, o) in enumerate(zip(ins, outs))]
    own.append(pltpu.make_async_copy(g_ref.at[s], ga_ref.at[s], local.at[len(ins)]))
    for c in own:
        c.start()
    ex.greet([ex.X, ex.Y, ex.C] + ex.Z[1:])
    iz, ix, iy, ir, ic = ([ex.slots(n) for _ in outs] for _ in range(5))
    ig = ex.slots(n)
    for k in GATHER_ORDER:
        for j in range(1, n):
            ex.put(iz[k][j], ins[k], outs[k].at[s, h, r], ex.Z[j])
    for j in range(1, n):
        ex.put(ig[j], g_ref.at[ex.z(j)], ga_ref.at[s], ex.Z[j])
    for c in own:
        c.wait()

    def forward(k, j):
        t, o = ex.z(j), outs[k]
        if j:
            ex.got(iz[k][n - j], o.at[t, h, r])
        ex.put(ix[k][j], At(o, t, h, r), o.at[t, h, r], ex.X)
        ex.put(iy[k][j], At(o, t, h, r), o.at[t, h, r], ex.Y)

    def relay(k, j):
        t, o = ex.z(j), outs[k]
        slots, frm, peer = (ix, ex.xn, ex.Y) if by_x(k, j) else (iy, ex.yn, ex.X)
        ex.got(slots[k][j], o.at[t, frm, r])
        ex.put(ir[k][j], At(o, t, frm, r), o.at[t, frm, r], peer)

    def across(k, j):
        t, o = ex.z(j), outs[k]
        slots, frm = (iy, ex.yn) if by_x(k, j) else (ix, ex.xn)
        ex.got(slots[k][j], o.at[t, frm, r])
        ex.got(ir[k][j], o.at[t, ex.dn, r])
        ex.put(ic[k][j], At(o, t, ALL, r), o.at[t, :, r], ex.C)

    def last():
        for j in range(n):
            for k, o in enumerate(outs):
                ex.got(ic[k][j], o.at[ex.z(j), :, 1 - r])
        for j in range(1, n):
            ex.got(ig[n - j], ga_ref.at[ex.z(j)])
        ex.close()

    for k in GATHER_ORDER:
        forward(k, 0)
    return dict(forward=forward, relay=relay, across=across), last


def by_tile(shape, step):
    height, width = shape
    if height % 16:

        @pl.loop(0, width // 768)
        def _(i):
            step(slice(None), pl.ds(pl.multiple_of(i * 768, 768), 768))
    else:

        @pl.loop(0, height // 32)
        def _(i):
            step(pl.ds(pl.multiple_of(i * 32, 32), 32), slice(None))


def reduce_steps(ins, outs, bufs, send, recv, local):
    count = len(ins)
    mine, from_c, one, two, from_z = (bufs[i * count : (i + 1) * count] for i in range(5))
    ex = Exchange(send, recv)
    s, h, r, n = ex.s, ex.h, ex.r, ex.planes
    own = [
        pltpu.make_async_copy(a.at[:, :, r], m, local.at[k]) for k, (a, m) in enumerate(zip(ins, mine))
    ]
    for c in own:
        c.start()
    ex.greet([ex.X, ex.Y, ex.C] + ex.Z[1:])
    ic, i1, i2, iz = ([ex.slots(n) for _ in ins] for _ in range(4))
    i1b = [ex.slots(n) for _ in ins]
    for k in (1, 0, 2):
        for j in range(n):
            ex.put(ic[k][j], At(ins[k], ex.z(j), ALL, 1 - r), from_c[k].at[ex.z(j)], ex.C)
    for c in own:
        c.wait()

    def add(to, part):
        def step(rows, cols):
            to[rows, cols] = (to[rows, cols].astype(jnp.float32) + part[rows, cols].astype(jnp.float32)).astype(to.dtype)

        by_tile(to.shape, step)

    def first(k, j):
        t, m = ex.z(j), mine[k]
        peer, near, other = (ex.X, ex.xn, ex.yn) if by_x(k, j) else (ex.Y, ex.yn, ex.xn)
        ex.got(ic[k][j], from_c[k].at[t])
        for slots, at, to in ((i1b, 1, ex.dn), (i1, 0, near)):
            add(m.at[t, to], from_c[k].at[t, to])
            ex.put(slots[k][j], At(m, t, to), one[k].at[j, at], peer)
        for to in (h, other):
            add(m.at[t, to], from_c[k].at[t, to])

    def second(k, j):
        t, m = ex.z(j), mine[k]
        peer, other = (ex.Y, ex.yn) if by_x(k, j) else (ex.X, ex.xn)
        ex.got(i1b[k][j], one[k].at[j, 1])
        add(m.at[t, other], one[k].at[j, 1])
        ex.put(i2[k][j], At(m, t, other), two[k].at[j], peer)
        ex.got(i1[k][j], one[k].at[j, 0])
        add(m.at[t, h], one[k].at[j, 0])

    def third(k, j):
        t, m = ex.z(j), mine[k]
        ex.got(i2[k][j], two[k].at[j])
        add(m.at[t, h], two[k].at[j])
        if j:
            ex.put(iz[k][j], At(m, t, h), from_z[k].at[j], ex.Z[j])

    def last():
        for k, (m, o) in enumerate(zip(mine, outs)):
            for j in range(1, n):
                ex.got(iz[k][j], from_z[k].at[j])

            def step(rows, cols):
                total = m[s, h, rows, cols].astype(jnp.float32)
                for j in range(1, n):
                    total += from_z[k][j, rows, cols].astype(jnp.float32)
                o[rows, cols] = total

            by_tile(o.shape, step)

        ex.close()

    return ex, dict(first=first, second=second, third=third), last


HD = 64


GATHER_PLAN = {
    (2, 0): [("forward", 2, 1, 3, 2)],
    (3, 0): [("relay", 0, 0), ("relay", 1, 0), ("relay", 2, 0)],
    (4, 0): [("relay", 2, 1, 3, 2)],
    (4, 3): [("forward", 0, 1, 3, 2)],
    (5, 1): [("relay", 0, 1, 3)],
    (6, 0): [("forward", 1, 1, 3, 2), ("relay", 0, 2)],
    (6, 3): [("across", 2, 0, 1, 3, 2), ("across", 0, 0, 1, 3)],
    (7, 0): [("relay", 1, 1, 3, 2)],
    (7, 3): [("across", 0, 2), ("across", 1, 0)],
    (7, 7): [("across", 1, 1, 3, 2)],
}


def attend_kernel(count, inv, blk, q_ref, kv_ref, g_ref, *refs):
    ins, outs = refs[:count], refs[count + 4 : 2 * count + 4]
    o_ref, low_ref, lse_ref, ga_ref = refs[count : count + 4]
    qt, ks, vt, os, send, recv, local = refs[2 * count + 4 :]
    npair, U, W = q_ref.shape
    nh = W // HD
    B = kv_ref.shape[1]
    TQ, TK = 2 * U, 2 * B
    steps, last = gather_steps(ins, outs, g_ref, ga_ref, send, recv, local)

    @pl.loop(0, npair)
    def _(i):
        p = inv[i]
        qt[:, pl.ds(pl.multiple_of(i * U, U), U)] = q_ref[p].T
        kv = kv_ref[p]
        for h in range(nh):
            ks[h, pl.ds(i * B, B), :] = kv[:, h * HD : (h + 1) * HD]
        vct = kv[:, W:].T
        for h in range(nh):
            vt[h, 0:HD, pl.ds(pl.multiple_of(i * B, B), B)] = vct[h * HD : (h + 1) * HD]
            vt[h, HD:, pl.ds(pl.multiple_of(i * B, B), B)] = jnp.ones((vt.shape[1] - HD, B), vt.dtype)

    def tile(m, c, carry, masked):
        out = []
        for h in range(nh):
            mx, acc = carry[h]
            qh = qt[h * HD : (h + 1) * HD, pl.ds(pl.multiple_of(m * TQ, TQ), TQ)]
            kh = ks[h, pl.ds(pl.multiple_of(c * TK, TK), TK), :]
            s = jnp.dot(kh, qh, preferred_element_type=jnp.float32)
            if masked:
                row = lax.broadcasted_iota(jnp.int32, s.shape, 0)
                col = lax.broadcasted_iota(jnp.int32, s.shape, 1)
                s = jnp.where((row >= B) & (col < U), NEG, s)
            new = jnp.maximum(mx, jnp.max(s, axis=0, keepdims=True))
            p = jnp.exp(s - new).astype(jnp.bfloat16)
            vh = vt[h, :, pl.ds(pl.multiple_of(c * TK, TK), TK)]
            acc = acc * jnp.exp(mx - new) + jnp.dot(vh, p, preferred_element_type=jnp.float32)
            out.append((new, acc))
        return tuple(out)

    @pl.loop(0, npair // 2)
    def _(m):
        init = tuple(
            (jnp.full((1, TQ), NEG, jnp.float32), jnp.zeros((vt.shape[1], TQ), jnp.float32)) for _ in range(nh)
        )

        def step(c, x):
            x = tile(m, c, x, False)
            act(GATHER_PLAN, steps, m, c, False)
            return x

        carry = lax.fori_loop(0, m, step, init)
        carry = tile(m, m, carry, True)
        rows = []
        for h in range(nh):
            mx, acc = carry[h]
            tot = acc[HD : HD + 1]
            rows.append(acc[:HD] / tot)
            lse_ref[h : h + 1, pl.ds(pl.multiple_of(m * TQ, TQ), TQ)] = mx + jnp.log(tot)
        os[pl.ds(pl.multiple_of(m * TQ, TQ), TQ), :] = jnp.concatenate(rows, axis=0).T
        act(GATHER_PLAN, steps, m, m, True)

    @pl.loop(0, npair)
    def _(p):
        o = os[pl.ds(blk[p] * U, U), :]
        o_ref[pl.ds(pl.multiple_of(p * U, U), U), :] = o
        low_ref[pl.ds(pl.multiple_of(p * U, U), U), :] = o.astype(jnp.bfloat16)

    last()


SMEM = pl.BlockSpec(memory_space=pltpu.SMEM)


def attend(inv, blk, q, kv, g, *weights):
    npair, U, W = q.shape
    R, K = npair * U, npair * kv.shape[1]
    nh = W // HD
    S, H, Q = (lax.axis_size(a) for a in AXES)
    n = len(weights)
    f32, bf16 = jnp.float32, jnp.bfloat16
    return remote_call(
        partial(attend_kernel, n),
        1,
        [
            jax.ShapeDtypeStruct((R, W), f32),
            jax.ShapeDtypeStruct((R, W), bf16),
            jax.ShapeDtypeStruct((8, R), f32),
            jax.ShapeDtypeStruct(g.shape, bf16),
        ]
        + [jax.ShapeDtypeStruct((S, H, Q) + a.shape, a.dtype) for a in weights],
        [SMEM] * 2 + [VMEM] * 2 + [ANY] * (n + 1),
        [VMEM] * 3 + [ANY] * (n + 1),
        [
            pltpu.VMEM((W, R), bf16),
            pltpu.VMEM((nh, K, HD), bf16),
            pltpu.VMEM((nh, HD + 16, K), bf16),
            pltpu.VMEM((R, W), f32),
        ],
        5 * S * n + S,
        "attend",
    )(inv, blk, q, kv, g, *weights)


REDUCE_PLAN = {
    (7, 2): [("first", 1, 1, 2, 3, 0)],
    (7, 6): [("first", 0, 1, 2, 3, 0)],
    (6, 3): [("second", 1, 1, 2, 3, 0)],
    (6, 4): [("first", 2, 1, 2, 3, 0)],
    (5, 3): [("third", 1, 1, 2, 3, 0)],
    (4, 2): [("second", 0, 1, 2, 3, 0)],
    (4, 3): [("second", 2, 1, 2, 3, 0)],
    (3, 1): [("third", 0, 1, 2, 3, 0)],
    (3, 2): [("third", 2, 1, 2, 3, 0)],
}


def attend_back_kernel(count, inv, blk, q_ref, kv_ref, g_ref, o_ref, lse_ref, *refs):
    ins, gm_ref, outs = refs[:count], refs[count], refs[count + 1 : 2 * count + 1]
    bufs = refs[2 * count + 1 : 7 * count + 1]
    qt, gt, qx, gx, ks, vs, kt, delta, dkv, dqs, over, back, send, recv, local = refs[7 * count + 1 :]
    npair, U, W = q_ref.shape
    nh = W // HD
    B = kv_ref.shape[1]
    TQ, TK = 2 * U, 2 * B
    f32, bf16 = jnp.float32, jnp.bfloat16
    ex, steps, last = reduce_steps(ins, outs, bufs, send, recv, local)
    swap = ex.slots(npair // 2)

    @pl.loop(0, npair)
    def _(i):
        p = inv[i]
        qc = q_ref[p]
        gc = g_ref[p]
        oc = o_ref[pl.ds(p * U, U), :]
        cols = pl.ds(pl.multiple_of(i * U, U), U)
        qt[:, cols] = qc.T
        gt[:, cols] = gc.T
        prod = (oc * gc.astype(f32)).T
        zero = jnp.zeros((U, HD), bf16)
        for h in range(nh):
            delta[h : h + 1, cols] = jnp.sum(prod[h * HD : (h + 1) * HD], axis=0, keepdims=True)
            qx[h, pl.ds(i * U, U), :] = jnp.concatenate([zero, qc[:, h * HD : (h + 1) * HD]], axis=1)
            gx[h, pl.ds(i * U, U), :] = jnp.concatenate([gc[:, h * HD : (h + 1) * HD], zero], axis=1)
        kv = kv_ref[p]
        kc, vc = kv[:, :W], kv[:, W:]
        kt[:, pl.ds(pl.multiple_of(i * B, B), B)] = kc.T
        for h in range(nh):
            ks[h, pl.ds(i * B, B), :] = kc[:, h * HD : (h + 1) * HD]
            vs[h, pl.ds(i * B, B), :] = vc[:, h * HD : (h + 1) * HD]

    dkv[...] = jnp.zeros_like(dkv)

    def tile(m, c, carry, masked):
        out = []
        qcols = pl.ds(pl.multiple_of(m * TQ, TQ), TQ)
        krows = pl.ds(pl.multiple_of(c * TK, TK), TK)
        for h in range(nh):
            hs = slice(h * HD, (h + 1) * HD)
            s = jnp.dot(ks[h, krows, :], qt[hs, qcols], preferred_element_type=f32)
            p = jnp.exp(s - lse_ref[h : h + 1, qcols])
            if masked:
                row = lax.broadcasted_iota(jnp.int32, s.shape, 0)
                col = lax.broadcasted_iota(jnp.int32, s.shape, 1)
                p = jnp.where((row >= B) & (col < U), 0.0, p)
            dp = jnp.dot(vs[h, krows, :], gt[hs, qcols], preferred_element_type=f32)
            ds = (p * (dp - delta[h : h + 1, qcols])).astype(bf16)
            dkv[h, krows, :] += jnp.dot(
                p.astype(bf16), gx[h, qcols, :], preferred_element_type=f32
            ) + jnp.dot(ds, qx[h, qcols, :], preferred_element_type=f32)
            out.append(carry[h] + jnp.dot(kt[hs, krows], ds, preferred_element_type=f32))
        return tuple(out)

    def halves(b, half):
        rows = pl.ds(pl.multiple_of(b * B + half * U, U), U)
        parts = [dkv[h, rows, :] for h in range(nh)]
        return jnp.concatenate([x[:, HD:] for x in parts] + [x[:, :HD] for x in parts], axis=1)

    @pl.loop(0, npair // 2)
    def _(turn):
        m = npair // 2 - 1 - turn
        init = tuple(jnp.zeros((HD, TQ), f32) for _ in range(nh))

        def step(c, x):
            x = tile(m, c, x, False)
            act(REDUCE_PLAN, steps, m, c, False)
            return x

        carry = lax.fori_loop(0, m, step, init)
        carry = tile(m, m, carry, True)
        dqs[pl.ds(pl.multiple_of(m * TQ, TQ), TQ), :] = (jnp.concatenate(carry, axis=0).T * 0.125).astype(bf16)
        for k in range(2):
            over[2 * m + k] = halves(2 * m + k, 1).astype(bf16)
        ex.copy(swap[0] + m, over.at[pl.ds(2 * m, 2)], back.at[pl.ds(2 * m, 2)], ex.C).start()
        act(REDUCE_PLAN, steps, m, m, True)

    @pl.loop(0, npair // 2)
    def _(m):
        moved = ex.copy(swap[0] + m, over.at[pl.ds(2 * m, 2)], back.at[pl.ds(2 * m, 2)], ex.C)
        moved.wait_recv()
        moved.wait_send()

    @pl.loop(0, npair)
    def _(p):
        b = blk[p]
        rows = pl.ds(b * B, U)
        parts = [dkv[h, rows, :] for h in range(nh)]
        own = jnp.concatenate([x[:, HD:] for x in parts] + [x[:, :HD] for x in parts], axis=1)
        own = (own + back[b].astype(f32)).astype(bf16)
        gm_ref[p] = jnp.concatenate([dqs[pl.ds(b * U, U), :], own], axis=1)

    last()


def attend_back(inv, blk, q, kv, g, o, lse, *grads):
    npair, U, W = q.shape
    R, K = npair * U, npair * kv.shape[1]
    nh = W // HD
    S, H, Q = (lax.axis_size(a) for a in AXES)
    n = len(grads)
    f32, bf16 = jnp.float32, jnp.bfloat16
    tails = [a.shape[3:] for a in grads]
    buffers = [[pltpu.VMEM(lead + t, bf16) for t in tails] for lead in ((S, H), (S, H), (S, 2), (S,), (S,))]
    return remote_call(
        partial(attend_back_kernel, n),
        2,
        [jax.ShapeDtypeStruct((npair, R // npair, 3 * W), bf16)] + [jax.ShapeDtypeStruct(t, f32) for t in tails],
        [SMEM] * 2 + [VMEM] * 5 + [ANY] * n,
        [VMEM] * (n + 1),
        sum(buffers, [])
        + [
            pltpu.VMEM((W, R), bf16),
            pltpu.VMEM((W, R), bf16),
            pltpu.VMEM((nh, R, 2 * HD), bf16),
            pltpu.VMEM((nh, R, 2 * HD), bf16),
            pltpu.VMEM((nh, K, HD), bf16),
            pltpu.VMEM((nh, K, HD), bf16),
            pltpu.VMEM((W, K), bf16),
            pltpu.VMEM((8, R), f32),
            pltpu.VMEM((nh, K, 2 * HD), f32),
            pltpu.VMEM((R, W), bf16),
            pltpu.VMEM((npair, R // npair, 2 * W), bf16),
            pltpu.VMEM((npair, R // npair, 2 * W), bf16),
        ],
        5 * S * n + npair // 2,
        "attend_back",
        60 << 20,
    )(inv, blk, q, kv, g, o, lse, *grads)


def front_kernel(
    x_ref, w_ref, v_ref, norm_ref, q_ref, kv_ref, wt_ref, vec_ref, xo_ref,
    xa, ws, wa, wf, kv_far, send, recv, local,
):
    f32, bf16 = jnp.float32, jnp.bfloat16
    ex = Exchange(send, recv)
    s, h, r, n = ex.s, ex.h, ex.r, ex.planes
    H, U, D = xa.shape[1:]
    d, N = w_ref.shape
    W = N // 3 // H
    own = pltpu.make_async_copy(x_ref.at[s], xa.at[s, h], local.at[0])
    own.start()
    for k in range(H):
        ws[k] = jnp.concatenate(
            [w_ref[:, c * D + k * W : c * D + (k + 1) * W] for c in range(3)] + [v_ref[...]], axis=1
        )
    ex.greet([ex.X, ex.Y, ex.D, ex.C] + ex.Z[1:])
    iw, ix, iy, ir, iz, iwz, iwc, ik = (ex.slots(n) for _ in range(8))
    for j in range(1, n):
        ex.put(iz[j], x_ref.at[ex.z(j)], xa.at[s, h], ex.Z[j])
    for k, (peer, to) in enumerate(((ex.X, ex.xn), (ex.Y, ex.yn), (ex.D, ex.dn))):
        ex.put(iw[k], ws.at[to], wa.at[s, h, r], peer)
    wa[s, h, r] = ws[h]
    own.wait()

    def forward(j):
        t = ex.z(j)
        if j:
            ex.got(iz[n - j], xa.at[t, h])
        ex.put(ix[j], xa.at[t, h], xa.at[t, h], ex.X)
        ex.put(iy[j], xa.at[t, h], xa.at[t, h], ex.Y)

    def relay(j):
        t = ex.z(j)
        slots, frm, peer = (ix, ex.xn, ex.Y) if by_x(0, j) else (iy, ex.yn, ex.X)
        ex.got(slots[j], xa.at[t, frm])
        ex.put(ir[j], xa.at[t, frm], xa.at[t, frm], peer)

    def weights(j):
        if j:
            ex.got(iwz[n - j], wa.at[ex.z(j), :, r])
        ex.put(iwc[j], wa.at[ex.z(j), :, r], wa.at[ex.z(j), :, r], ex.C)

    forward(0)
    for k, frm in enumerate((ex.xn, ex.yn, ex.dn)):
        ex.got(iw[k], wa.at[s, frm, r])
    for j in range(1, n):
        ex.put(iwz[j], wa.at[s, :, r], wa.at[s, :, r], ex.Z[j])
    weights(0)
    relay(0)
    for a, b in ((1, None), (3, 1), (2, 3)):
        forward(a)
        if b is not None:
            relay(b)
    for j in (1, 3, 2):
        weights(j)
    for j in range(n):
        ex.got(iwc[j], wa.at[ex.z(j), :, 1 - r])
    rows = H * 2 * d
    for t in range(n):
        block = wa[t].astype(f32).reshape(rows, N // H + 128)
        wf[t * rows : (t + 1) * rows] = block
    wt_ref[...] = wf[:, : N // H].T.astype(bf16)
    vec_ref[...] = wf[:, N // H :].T[:16]
    w = wf[:, : N // H].astype(bf16)
    gain, bias = vec_ref[0:1], vec_ref[1:2]

    def mine(row):
        picked = jnp.zeros((1, W), f32)
        for k in range(H):
            picked = jnp.where(h == k, vec_ref[row : row + 1, k * W : (k + 1) * W], picked)
        return picked

    bq, bv = mine(2), mine(3)

    def batch(j):
        t = ex.z(j)
        slots, frm = (iy, ex.yn) if by_x(0, j) else (ix, ex.xn)
        ex.got(slots[j], xa.at[t, frm])
        ex.got(ir[j], xa.at[t, ex.dn])
        x = xa[t].reshape(H * U, D).astype(f32)
        normed = layer_norm(x, gain, bias).astype(bf16)
        norm_ref[t] = normed.reshape(H, U, D)
        mixed = jnp.dot(normed, w, preferred_element_type=f32)
        q = (mixed[:, :W] + bq).astype(bf16) * jnp.asarray(0.125, bf16)
        q_ref[t] = q.reshape(H, U, W)
        kv = jnp.concatenate([mixed[:, W : 2 * W], mixed[:, 2 * W :] + bv], axis=1).astype(bf16)
        kv_ref[t, :, 0] = kv.reshape(H, U, 2 * W)
        ex.put(ik[j], kv_ref.at[t, :, 0], kv_far.at[t], ex.C)

    batch(0)
    relay(2)
    batch(1)
    batch(3)
    batch(2)
    out = pltpu.make_async_copy(xa.at[:, h], xo_ref, local.at[1])
    out.start()
    for j in (0, 1, 3, 2):
        t = ex.z(j)
        ex.got(ik[j], kv_far.at[t])
        kv_ref[t, :, 1] = kv_far[t]
    out.wait()
    ex.close()


def front(x, w, v):
    S, U, D = x.shape
    d, N = w.shape
    H, Q = (lax.axis_size(a) for a in AXES[1:])
    W = N // 3 // H
    f32, bf16 = jnp.float32, jnp.bfloat16
    return remote_call(
        front_kernel,
        0,
        [
            jax.ShapeDtypeStruct((S, H, U, D), bf16),
            jax.ShapeDtypeStruct((S, H, U, W), bf16),
            jax.ShapeDtypeStruct((S, H, Q, U, 2 * W), bf16),
            jax.ShapeDtypeStruct((N // H, D), bf16),
            jax.ShapeDtypeStruct((16, D), f32),
            jax.ShapeDtypeStruct((S, U, D), bf16),
        ],
        [ANY, VMEM, VMEM],
        [VMEM] * 6,
        [
            pltpu.VMEM((S, H, U, D), bf16),
            pltpu.VMEM((H, d, N // H + 128), bf16),
            pltpu.VMEM((S, H, Q, d, N // H + 128), bf16),
            pltpu.VMEM((D, N // H + 128), f32),
            pltpu.VMEM((S, H, U, 2 * W), bf16),
        ],
        8 * S,
        "front",
    )(x, w, v)


def norm_back(x, t, gain, grad):
    mean = jnp.mean(x, axis=-1, keepdims=True)
    center = x - mean
    rstd = lax.rsqrt(jnp.mean(center * center, axis=-1, keepdims=True) + 1e-05)
    z = center * rstd
    e = t * gain
    inner = e - jnp.mean(e, axis=-1, keepdims=True) - z * jnp.mean(e * z, axis=-1, keepdims=True)
    return grad + rstd * inner


def finish_kernel(
    gm_ref, wt_ref, norm_ref, x_ref, gmid_ref, gain_ref, small_ref, out_ref,
    gh_ref, lo_ref, gq_ref, vec_ref,
    t_ref, one, two, hid, gw, gw_c, gw_z, gw_sum, vec, send, recv, local,
):
    f32, bf16 = jnp.float32, jnp.bfloat16
    ex = Exchange(send, recv)
    s, h, r, n = ex.s, ex.h, ex.r, ex.planes
    half = n // 2
    H, N = gm_ref.shape[1], gm_ref.shape[3]
    U, D = t_ref.shape[2], t_ref.shape[3]
    W = N // 3
    d = gw.shape[3]
    keep = pltpu.make_async_copy(out_ref.at[s], lo_ref.at[s], local.at[0])
    keep.start()
    ex.greet([ex.X, ex.Y, ex.D, ex.C] + ex.Z[1:])
    i1, i1b, i2, ih, il, ic, iz, iq = (ex.slots(n) for _ in range(8))
    iv = ex.slots(3 + n)
    acc = [jnp.zeros((1, D), f32), jnp.zeros((1, D), f32)]

    def product(j0, to):
        planes = [ex.z(j) for j in range(j0, j0 + half)]
        g = jnp.concatenate([gm_ref[t, to] for t in planes], axis=0)
        prod = jnp.dot(g, wt_ref[...], preferred_element_type=f32)
        for k, t in enumerate(planes):
            part = prod[k * U : (k + 1) * U]
            t_ref[t, to] = part.astype(bf16)
            acc[0] += jnp.sum(part * norm_ref[t, to].astype(f32), axis=0, keepdims=True)
            acc[1] += jnp.sum(part, axis=0, keepdims=True)

    ways = ((0, ex.X, ex.xn, ex.yn), (half, ex.Y, ex.yn, ex.xn))
    for j0, peer, near, other in ways:
        product(j0, ex.dn)
        for j in range(j0, j0 + half):
            ex.put(i1b[j], t_ref.at[ex.z(j), ex.dn], one.at[j, 1], peer)
    for j0, peer, near, other in ways:
        product(j0, near)
        for j in range(j0, j0 + half):
            ex.put(i1[j], t_ref.at[ex.z(j), near], one.at[j, 0], peer)
    for j in range(1, n):
        ex.put(il[j], out_ref.at[ex.z(j)], lo_ref.at[s], ex.Z[j])
    for j0, peer, near, other in ways:
        product(j0, other)
        product(j0, h)

    g_all = gm_ref[...].reshape(n * H * U, N)
    cols = jnp.sum(g_all.astype(f32), axis=0, keepdims=True)
    lane = lax.broadcasted_iota(jnp.int32, (1, D), 1) // W

    def placed(c):
        return jnp.where(lane == h, jnp.concatenate([c] * H, axis=1), 0.0)

    vec[0, 0:1] = acc[0]
    vec[0, 1:2] = acc[1]
    vec[0, 2:3] = placed(cols[:, :W])
    vec[0, 3:4] = placed(cols[:, 2 * W :])
    vec[0, 4:8] = jnp.zeros((4, D), f32)
    vec[0, 8:] = small_ref[...]
    ex.put(iv[0], vec.at[0], vec.at[1], ex.C)

    def qkv_rows(t0):
        width = H * 2 * d
        nt = norm_ref[:, :, :, t0 * width : (t0 + half) * width].reshape(n * H * U, half * width)
        part = lax.dot_general(nt, g_all, (((0,), (0,)), ((), ())), preferred_element_type=f32)
        gw[t0 : t0 + half] = part.reshape(half, H, 2, d, N).astype(bf16)
        for t in range(t0, t0 + half):
            ex.put(ic[t], gw.at[t, :, 1 - r], gw_c.at[t], ex.C)

    def relay(j):
        t = ex.z(j)
        peer, other = (ex.Y, ex.yn) if j < half else (ex.X, ex.xn)
        ex.got(i1b[j], one.at[j, 1])
        t_ref[t, other] = (t_ref[t, other].astype(f32) + one[j, 1].astype(f32)).astype(bf16)
        ex.put(i2[j], t_ref.at[t, other], two.at[j], peer)

    def done(j):
        t = ex.z(j)
        ex.got(i1[j], one.at[j, 0])
        ex.got(i2[j], two.at[j])
        total = t_ref[t, h].astype(f32) + one[j, 0].astype(f32) + two[j].astype(f32)
        hid[t] = norm_back(x_ref[t].astype(f32), total, gain_ref[0:1], gmid_ref[t]).astype(bf16)
        if j:
            ex.put(ih[j], hid.at[t], gh_ref.at[s], ex.Z[j])

    def to_plane(j):
        t = ex.z(j)
        if j:
            ex.put(iz[j], gw_c.at[t], gw_z.at[s], ex.Z[j])

    qkv_rows(0)
    relay(0)
    relay(half)
    ex.got(iv[0], vec.at[1])
    vec[2] = vec[0] + vec[1]
    ex.put(iv[1], vec.at[2], vec.at[3], ex.X)
    qkv_rows(half)
    relay(1)
    relay(half + 1)
    for t in range(n):
        ex.got(ic[t], gw_c.at[t])
        gw_c[t] = (gw_c[t].astype(f32) + gw[t, :, r].astype(f32)).astype(bf16)
    for j in range(1, n):
        ex.put(iz[j], gw_c.at[ex.z(j)], gw_z.at[s], ex.Z[j])
    ex.got(iv[1], vec.at[3])
    vec[4] = vec[2] + vec[3]
    ex.put(iv[2], vec.at[4], vec.at[5], ex.Y)
    done(1)
    done(half + 1)
    ex.got(iv[2], vec.at[5])
    vec[6] = vec[4] + vec[5]
    for j in range(1, n):
        ex.put(iv[2 + j], vec.at[6], vec.at[6 + j], ex.Z[j])
    done(half)
    done(0)
    own = pltpu.make_async_copy(hid.at[s], gh_ref.at[s], local.at[1])
    own.start()
    total = gw_c[s].astype(f32)
    for j in range(1, n):
        ex.got(iz[n - j], gw_z.at[ex.z(j)])
        total += gw_z[ex.z(j)].astype(f32)
    gw_sum[...] = total
    for k, (peer, to) in enumerate(((ex.X, ex.xn), (ex.Y, ex.yn), (ex.D, ex.dn))):
        ex.put(iq[k], gw_sum.at[to], gq_ref.at[h], peer)
    mine = pltpu.make_async_copy(gw_sum.at[h], gq_ref.at[h], local.at[2])
    mine.start()
    for j in range(1, n):
        ex.got(iv[2 + j], vec.at[6 + j])
    vec_ref[...] = vec[6] + vec[7] + vec[8] + vec[9]
    for k, frm in enumerate((ex.xn, ex.yn, ex.dn)):
        ex.got(iq[k], gq_ref.at[frm])
    for j in range(1, n):
        ex.got(il[n - j], lo_ref.at[ex.z(j)])
        ex.got(ih[n - j], gh_ref.at[ex.z(j)])
    for c in (keep, own, mine):
        c.wait()
    ex.close()


def finish(gm, wt, norm, x, gmid, gain, small, out):
    S, H, U, N = gm.shape
    D = wt.shape[1]
    Q = lax.axis_size("r")
    d = D // (S * H * Q)
    f32, bf16 = jnp.float32, jnp.bfloat16
    return remote_call(
        finish_kernel,
        3,
        [
            jax.ShapeDtypeStruct((S, U, D), bf16),
            jax.ShapeDtypeStruct((S, U, D), bf16),
            jax.ShapeDtypeStruct((H, d, N), f32),
            jax.ShapeDtypeStruct((16, D), f32),
        ],
        [VMEM] * 7 + [ANY],
        [ANY, ANY, ANY, VMEM],
        [
            pltpu.VMEM((S, H, U, D), bf16),
            pltpu.VMEM((S, 2, U, D), bf16),
            pltpu.VMEM((S, U, D), bf16),
            pltpu.VMEM((S, U, D), bf16),
            pltpu.VMEM((S, H, Q, d, N), bf16),
            pltpu.VMEM((S, H, d, N), bf16),
            pltpu.VMEM((S, H, d, N), bf16),
            pltpu.VMEM((H, d, N), f32),
            pltpu.VMEM((10, 16, D), f32),
        ],
        9 * S + 3,
        "finish",
    )(gm, wt, norm, x, gmid, gain, small, out)


def planes(
    hidden_in,
    block_pairs,
    ln1_gain,
    ln1_bias,
    qkv_weight,
    query_bias,
    value_bias,
    out_weight,
    out_bias,
    ln2_gain,
    ln2_bias,
    fc_weight,
    fc_bias,
    proj_weight,
    proj_bias,
    out_grad,
):
    f32, bf16 = jnp.float32, jnp.bfloat16
    s, h, r = (lax.axis_index(a) for a in AXES)
    S, H, Q = (lax.axis_size(a) for a in AXES)
    rows, D = hidden_in.shape
    U = rows // SEQS
    W = D // H
    bfn = fc_bias.shape[0]
    d = qkv_weight.shape[0]
    lines = [ln1_gain, ln1_bias, query_bias, value_bias, out_bias, ln2_gain, ln2_bias, proj_bias]
    lines = jnp.concatenate([jnp.stack(lines), fc_bias.reshape(-1, d)]).T
    lines = jnp.pad(lines, ((0, 0), (0, 128 - lines.shape[1])))
    normed, q_all, kv_all, w_t, vecs, x_own = front(hidden_in.reshape(S, U, D), qkv_weight, lines)
    g1, b1, _, _, bo, g2, b2, bp = (vecs[i] for i in range(8))
    bf = vecs[8 : 8 + bfn // d].reshape(-1, S * H * Q, d).swapaxes(0, 1).reshape(-1)
    pad8 = lambda y: jnp.concatenate([y, jnp.zeros((8, y.shape[1]), y.dtype)])

    blk = block_pairs[::2]
    blk = jnp.where(s % 2 == 0, blk, blk.shape[0] - 1 - blk)
    blk = blk.astype(jnp.int32)
    npair = blk.shape[0]
    inv = jnp.sum(
        jnp.where(blk[None, :] == jnp.arange(npair)[:, None], jnp.arange(npair)[None, :], 0), axis=1
    ).astype(jnp.int32)

    x_own = x_own.reshape(rows, D).astype(f32)
    q_all = q_all.reshape(npair, U, W)
    kv_all = kv_all.reshape(npair, 2 * U, 2 * W)
    att, att_low, lse, g_own, w_fc, w_proj, w_out = attend(
        inv, blk, q_all, kv_all, out_grad.reshape(S, U, D), fc_weight, proj_weight, pad8(out_weight)
    )
    g_own = g_own.reshape(rows, D)
    w_fc, w_proj = w_fc.reshape(D, -1), w_proj.reshape(-1, D)
    w_out = w_out.reshape(-1, d + 8, D)[:, :d].reshape(D, D)
    att_low = lax.all_to_all(att_low.reshape(S, H, U, W), "h", 1, 1)
    att_low = att_low.transpose(0, 2, 1, 3).reshape(rows, D)

    middle = x_own + jnp.dot(att_low, w_out, preferred_element_type=f32) + bo
    normed_two = layer_norm(middle, g2, b2).astype(bf16)
    pre_act = jnp.dot(normed_two, w_fc, preferred_element_type=f32) + bf
    activation = gelu_tanh(pre_act).astype(bf16)
    layer_out = (middle + jnp.dot(activation, w_proj, preferred_element_type=f32) + bp).astype(bf16)
    grad_out = g_own.astype(f32)
    grad_proj = jnp.dot(activation.T, g_own, preferred_element_type=f32)
    grad_bproj = jnp.sum(grad_out, axis=0)
    grad_activ = jnp.dot(g_own, w_proj.T, preferred_element_type=f32)
    _, gelu_back = jax.vjp(gelu_tanh, pre_act)
    grad_pre = gelu_back(grad_activ)[0].astype(bf16)
    grad_fc = jnp.dot(normed_two.T, grad_pre, preferred_element_type=f32)
    grad_bfc = jnp.sum(grad_pre.astype(f32), axis=0)
    grad_normed_two = jnp.dot(grad_pre, w_fc.T, preferred_element_type=f32)
    _, norm_back_two = jax.vjp(layer_norm, middle, g2, b2)
    grad_middle, grad_g2, grad_b2 = norm_back_two(grad_normed_two)
    grad_middle = grad_middle + grad_out
    grad_branch = grad_middle.astype(bf16)
    grad_wout = jnp.dot(att_low.T, grad_branch, preferred_element_type=f32)
    grad_bout = jnp.sum(grad_branch.astype(f32), axis=0)
    grad_att = jnp.dot(grad_branch, w_out.T, preferred_element_type=f32).astype(bf16)

    g_att = lax.all_to_all(grad_att.reshape(S, U, H, W).transpose(0, 2, 1, 3), "h", 1, 1)
    shard = lambda y: y.astype(bf16).reshape((S, H, Q) + y.shape[1:])
    grad_mixed, gfc, gproj, gout = attend_back(
        inv,
        blk,
        q_all,
        kv_all,
        g_att.reshape(npair, U, W),
        att,
        lse,
        shard(grad_fc.reshape(S * H * Q, d, -1)),
        shard(grad_proj.reshape(S * H * Q, -1, D)),
        shard(jnp.pad(grad_wout.reshape(-1, d, D), ((0, 0), (0, 8), (0, 0)))),
    )
    fc_rows = [grad_bfc.reshape(-1, D)]
    small = jnp.concatenate([y[None] for y in (grad_bout, grad_g2, grad_b2, grad_bproj)] + fc_rows)
    grad_hidden, layer_out, gq, vec = finish(
        grad_mixed.reshape(S, H, U, 3 * W),
        w_t,
        normed,
        x_own.reshape(S, U, D).astype(bf16),
        grad_middle.reshape(S, U, D),
        jnp.broadcast_to(g1[None], (8, D)),
        small,
        layer_out.reshape(S, U, D),
    )
    gq = gq.reshape(H, d, 3, W).transpose(1, 2, 0, 3).reshape(d, 3 * D)
    index = (s * H + h) * Q + r
    pick = lambda v: lax.dynamic_slice_in_dim(v, index * d, d)
    return (
        layer_out.reshape(rows, D),
        grad_hidden.reshape(rows, D),
        pick((vec[0] - b1 * vec[1]) / g1),
        pick(vec[1]),
        gq,
        pick(vec[2]),
        pick(vec[3]),
        gout[:d],
        pick(vec[8]),
        pick(vec[9]),
        pick(vec[10]),
        gfc,
        lax.dynamic_slice_in_dim(vec[12:].reshape(-1), index * bfn, bfn),
        gproj,
        pick(vec[11]),
    )


def solution(mesh):
    n = mesh.shape["ctx"]
    if n // (PLANES * SEQS) != 2:
        return solution_any(mesh)
    split = Mesh(mesh.devices.reshape(PLANES, SEQS, -1), AXES)
    row, vec = P(AXES, None), P(AXES)
    return jax.shard_map(
        planes,
        mesh=split,
        in_specs=(row, P(), vec, vec, row, vec, vec, row, vec, vec, vec, row, vec, row, vec, row),
        out_specs=(row, row, vec, vec, row, vec, vec, row, vec, vec, vec, row, vec, row, vec),
        check_vma=False,
    )
```

```python
from functools import partial
import math

import jax
import jax.numpy as jnp
from jax import lax
from jax.sharding import PartitionSpec as P
from jax.experimental import pallas as pl
from jax.experimental.pallas import tpu as pltpu
from jax.sharding import Mesh

HEADS = 12
SEQS = 4


NEG = -1e30


def from_partner(value, axis, bit):
    return lax.ppermute(value, axis, [(i, i ^ 1 << bit) for i in range(lax.axis_size(axis))])


def layer_norm(values, gain, bias):
    center = values - jnp.mean(values, axis=-1, keepdims=True)
    spread_sq = jnp.mean(center * center, axis=-1, keepdims=True)
    return center * lax.rsqrt(spread_sq + 1e-05) * gain + bias


def gelu_tanh(values):
    return jax.nn.gelu(values, approximate=True)


def heads_of(tensor, head_count):
    return tensor.reshape(tensor.shape[:-1] + (head_count, tensor.shape[-1] // head_count))


def pick_own(owned, chosen):
    selector = chosen.reshape((1, -1) + (1,) * (owned.ndim - 2))
    return jnp.where(selector, owned[:, 0:1], owned[:, 1:2])


def pick_piece(piece, chosen):
    selector = chosen.reshape((1, -1) + (1,) * (piece.ndim - 3))
    return jnp.where(selector, piece[:, 0], piece[:, 1])


def parity_masks(chosen, usable):
    return jnp.stack([chosen & usable, jnp.logical_not(chosen) & usable])


def spread(values, parity):
    shaped = parity.reshape((1,) + parity.shape + (1,) * (values.ndim - 2))
    return jnp.sum(jnp.where(shaped, values[:, None], 0.0), axis=2)


def group_loop(pieces, unit_rows, table, stepper, carried):
    piece_rows = pieces[0].shape[2]
    group_size = min(unit_rows, piece_rows)
    group_count = piece_rows // group_size
    batch_groups = math.gcd(group_count, max(1, 1024 // group_size))
    turn_count = group_count // batch_groups
    shaped = tuple(
        (
            item.reshape(item.shape[:2] + (group_count, group_size) + item.shape[3:])
            for item in pieces
        )
    )
    device_ids = jnp.arange(group_count, dtype=jnp.int32) * group_size // unit_rows
    table_size = table.shape[0]
    blocks = jnp.sum(
        jnp.where(
            device_ids[:, None] == jnp.arange(table_size, dtype=jnp.int32)[None, :],
            table[None, :],
            0,
        ),
        axis=1,
    )

    def one_turn(position, current):
        pieces_now = tuple(
            (
                lax.dynamic_slice_in_dim(item, position * batch_groups, batch_groups, 2)
                for item in shaped
            )
        )
        chosen = lax.dynamic_slice_in_dim(blocks, position * batch_groups, batch_groups, 0)
        return stepper(current, pieces_now, chosen)

    return lax.fori_loop(0, turn_count, one_turn, carried)


def attend_step(q_heads, my_block, score_scale, head_count, carried, pieces_now, chosen):
    key_piece = heads_of(pieces_now[0], head_count)
    value_piece = heads_of(pieces_now[1], head_count)
    earlier = chosen < my_block
    usable = chosen != my_block
    parity = parity_masks(earlier, usable)
    query_sel = pick_own(q_heads, earlier)
    key_sel = pick_piece(key_piece, earlier)
    value_sel = pick_piece(value_piece, earlier)
    scores = (
        jnp.einsum("jgqhe,jgkhe->jghqk", query_sel, key_sel, preferred_element_type=jnp.float32)
        * score_scale
    )
    usable_mask = usable.reshape(1, -1, 1, 1, 1)
    scores = jnp.where(usable_mask, scores, NEG)
    old_max, old_total, old_sum = carried
    group_max = jnp.max(scores, axis=-1)
    candidate = jnp.max(jnp.where(parity.reshape(1, 2, -1, 1, 1), group_max[:, None], NEG), axis=2)
    new_max = jnp.maximum(old_max, candidate)
    max_sel = pick_own(new_max, earlier)
    weights_exp = jnp.where(usable_mask, jnp.exp(scores - max_sel[..., None]), 0.0)
    moved = jnp.einsum(
        "jghqk,jgkhe->jgqhe",
        weights_exp.astype(jnp.bfloat16),
        value_sel,
        preferred_element_type=jnp.float32,
    )
    factor = jnp.exp(old_max - new_max)
    new_total = old_total * factor + spread(jnp.sum(weights_exp, axis=-1), parity)
    new_sum = old_sum * jnp.swapaxes(factor, 2, 3)[..., None] + spread(moved, parity)
    return (new_max, new_total, new_sum)


def query_grad_step(
    q_heads,
    grad_heads,
    lse_heads,
    delta_heads,
    my_block,
    score_scale,
    head_count,
    carried,
    pieces_now,
    chosen,
):
    key_piece = heads_of(pieces_now[0], head_count)
    value_piece = heads_of(pieces_now[1], head_count)
    earlier = chosen < my_block
    usable = chosen != my_block
    parity = parity_masks(earlier, usable)
    query_sel = pick_own(q_heads, earlier)
    grad_sel = pick_own(grad_heads, earlier)
    lse_sel = pick_own(lse_heads, earlier)
    delta_sel = pick_own(delta_heads, earlier)
    key_sel = pick_piece(key_piece, earlier)
    value_sel = pick_piece(value_piece, earlier)
    scores = (
        jnp.einsum("jgqhe,jgkhe->jghqk", query_sel, key_sel, preferred_element_type=jnp.float32)
        * score_scale
    )
    usable_mask = usable.reshape(1, -1, 1, 1, 1)
    probabilities = jnp.where(usable_mask, jnp.exp(scores - lse_sel[..., None]), 0.0)
    grad_probs = jnp.einsum(
        "jgqhe,jgkhe->jghqk", grad_sel, value_sel, preferred_element_type=jnp.float32
    )
    grad_scores = (probabilities * (grad_probs - delta_sel[..., None])).astype(jnp.bfloat16)
    term = (
        jnp.einsum("jghqk,jgkhe->jgqhe", grad_scores, key_sel, preferred_element_type=jnp.float32)
        * score_scale
    )
    return carried + spread(term, parity)


def key_grad_step(k_heads, v_heads, my_block, score_scale, head_count, carried, pieces_now, chosen):
    query_piece = heads_of(pieces_now[0], head_count)
    grad_piece = heads_of(pieces_now[1], head_count)
    later = my_block < chosen
    usable = chosen != my_block
    parity = parity_masks(later, usable)
    query_sel = pick_piece(query_piece, later)
    grad_sel = pick_piece(grad_piece, later)
    lse_sel = jnp.swapaxes(pick_piece(pieces_now[2], later), 2, 3)
    delta_sel = jnp.swapaxes(pick_piece(pieces_now[3], later), 2, 3)
    key_sel = pick_own(k_heads, later)
    value_sel = pick_own(v_heads, later)
    scores = (
        jnp.einsum("jgqhe,jgkhe->jghqk", query_sel, key_sel, preferred_element_type=jnp.float32)
        * score_scale
    )
    usable_mask = usable.reshape(1, -1, 1, 1, 1)
    probabilities = jnp.where(usable_mask, jnp.exp(scores - lse_sel[..., None]), 0.0)
    grad_probs = jnp.einsum(
        "jgqhe,jgkhe->jghqk", grad_sel, value_sel, preferred_element_type=jnp.float32
    )
    grad_scores = (probabilities * (grad_probs - delta_sel[..., None])).astype(jnp.bfloat16)
    key_term = (
        jnp.einsum("jghqk,jgqhe->jgkhe", grad_scores, query_sel, preferred_element_type=jnp.float32)
        * score_scale
    )
    value_term = jnp.einsum(
        "jghqk,jgqhe->jgkhe",
        probabilities.astype(jnp.bfloat16),
        grad_sel,
        preferred_element_type=jnp.float32,
    )
    return (carried[0] + spread(key_term, parity), carried[1] + spread(value_term, parity))


def shards(
    hidden_in,
    block_pairs,
    ln1_gain,
    ln1_bias,
    qkv_weight,
    query_bias,
    value_bias,
    out_weight,
    out_bias,
    ln2_gain,
    ln2_bias,
    fc_weight,
    fc_bias,
    proj_weight,
    proj_bias,
    out_grad,
):
    params = (
        ln1_gain,
        ln1_bias,
        qkv_weight,
        query_bias,
        value_bias,
        out_weight,
        out_bias,
        ln2_gain,
        ln2_bias,
        fc_weight,
        fc_bias,
        proj_weight,
        proj_bias,
    )
    gathered = (
        lax.all_gather(params[0], "ctx", axis=0, tiled=True),
        lax.all_gather(params[1], "ctx", axis=0, tiled=True),
        lax.all_gather(params[2], "ctx", axis=0, tiled=True),
        lax.all_gather(params[3], "ctx", axis=0, tiled=True),
        lax.all_gather(params[4], "ctx", axis=0, tiled=True),
        lax.all_gather(params[5], "ctx", axis=0, tiled=True),
        lax.all_gather(params[6], "ctx", axis=0, tiled=True),
        lax.all_gather(params[7], "ctx", axis=0, tiled=True),
        lax.all_gather(params[8], "ctx", axis=0, tiled=True),
        lax.all_gather(params[9], "ctx", axis=0, tiled=True),
        lax.all_gather(params[10], "ctx", axis=0, tiled=True),
        lax.all_gather(params[11], "ctx", axis=0, tiled=True),
        lax.all_gather(params[12], "ctx", axis=0, tiled=True),
    )
    (
        gain_one,
        bias_one,
        w_qkv,
        b_query,
        b_value,
        w_out,
        b_out,
        gain_two,
        bias_two,
        w_fc,
        b_fc,
        w_proj,
        b_proj,
    ) = gathered
    device = lax.axis_index("ctx")
    partner = device + 1 - 2 * (device % 2)
    row_count = hidden_in.shape[0]
    model_width = hidden_in.shape[1]
    unit_rows = row_count // SEQS
    halves = SEQS // 2
    head_count = HEADS
    head_size = model_width // head_count
    score_scale = 1.0 / math.sqrt(head_size)
    my_block = block_pairs[device]
    seq_shape = (halves, 2, unit_rows, model_width)
    head_shape = (halves, 2, unit_rows, head_count, head_size)
    inputs = hidden_in.astype(jnp.float32)
    normed = layer_norm(inputs, gain_one.astype(jnp.float32), bias_one.astype(jnp.float32)).astype(
        jnp.bfloat16
    )
    mixed_proj = jnp.dot(normed, w_qkv, preferred_element_type=jnp.float32)
    queries = (mixed_proj[:, :model_width] + b_query.astype(jnp.float32)).astype(jnp.bfloat16)
    key_rows = mixed_proj[:, model_width : 2 * model_width].astype(jnp.bfloat16)
    value_rows = (mixed_proj[:, 2 * model_width :] + b_value.astype(jnp.float32)).astype(
        jnp.bfloat16
    )
    q_seq = queries.reshape(seq_shape)
    k_seq = key_rows.reshape(seq_shape)
    v_seq = value_rows.reshape(seq_shape)
    q_heads = queries.reshape(head_shape)
    k_heads = key_rows.reshape(head_shape)
    v_heads = value_rows.reshape(head_shape)
    far_keys, far_values = from_partner((k_seq, v_seq), "ctx", 0)
    near_keys = jnp.concatenate([k_heads, heads_of(far_keys, head_count)], axis=2)
    near_values = jnp.concatenate([v_heads, heads_of(far_values, head_count)], axis=2)
    scores = (
        jnp.einsum("jpqhe,jpkhe->jphqk", q_heads, near_keys, preferred_element_type=jnp.float32)
        * score_scale
    )
    row_max = jnp.max(scores, axis=-1)
    weights_exp = jnp.exp(scores - row_max[..., None])
    row_total = jnp.sum(weights_exp, axis=-1)
    summed = jnp.einsum(
        "jphqk,jpkhe->jpqhe",
        weights_exp.astype(jnp.bfloat16),
        near_values,
        preferred_element_type=jnp.float32,
    )
    forward_stepper = partial(attend_step, q_heads, my_block, score_scale, head_count)
    row_max, row_total, summed = group_loop(
        (
            lax.all_gather(k_seq, "ctx", axis=2, tiled=True),
            lax.all_gather(v_seq, "ctx", axis=2, tiled=True),
        ),
        unit_rows,
        block_pairs,
        forward_stepper,
        (row_max, row_total, summed),
    )
    attended = summed / jnp.swapaxes(row_total, 2, 3)[..., None]
    log_total = row_max + jnp.log(row_total)
    att_low = attended.reshape(row_count, model_width).astype(jnp.bfloat16)
    branch = jnp.dot(att_low, w_out, preferred_element_type=jnp.float32) + b_out.astype(jnp.float32)
    middle = inputs + branch
    normed_two = layer_norm(
        middle, gain_two.astype(jnp.float32), bias_two.astype(jnp.float32)
    ).astype(jnp.bfloat16)
    pre_act = jnp.dot(normed_two, w_fc, preferred_element_type=jnp.float32) + b_fc.astype(
        jnp.float32
    )
    activation = gelu_tanh(pre_act).astype(jnp.bfloat16)
    result = (
        middle
        + jnp.dot(activation, w_proj, preferred_element_type=jnp.float32)
        + b_proj.astype(jnp.float32)
    )
    layer_out = result.astype(jnp.bfloat16)
    grad_out = out_grad.astype(jnp.float32)
    grad_proj = jnp.dot(activation.T, out_grad, preferred_element_type=jnp.float32)
    grad_bproj = jnp.sum(grad_out, axis=0)
    grad_activ = jnp.dot(out_grad, w_proj.T, preferred_element_type=jnp.float32)
    _, gelu_back = jax.vjp(gelu_tanh, pre_act)
    grad_pre = gelu_back(grad_activ)[0].astype(jnp.bfloat16)
    grad_fc = jnp.dot(normed_two.T, grad_pre, preferred_element_type=jnp.float32)
    grad_bfc = jnp.sum(grad_pre.astype(jnp.float32), axis=0)
    grad_normed_two = jnp.dot(grad_pre, w_fc.T, preferred_element_type=jnp.float32)
    _, norm_back_two = jax.vjp(
        layer_norm, middle, gain_two.astype(jnp.float32), bias_two.astype(jnp.float32)
    )
    grad_middle, grad_gain_two, grad_bias_two = norm_back_two(grad_normed_two)
    grad_middle = grad_middle + grad_out
    grad_branch = grad_middle.astype(jnp.bfloat16)
    grad_wout = jnp.dot(att_low.T, grad_branch, preferred_element_type=jnp.float32)
    grad_bout = jnp.sum(grad_branch.astype(jnp.float32), axis=0)
    grad_att = jnp.dot(grad_branch, w_out.T, preferred_element_type=jnp.float32).astype(
        jnp.bfloat16
    )
    grad_seq = grad_att.reshape(seq_shape)
    grad_heads = grad_att.reshape(head_shape)
    row_delta = jnp.sum(grad_heads.astype(jnp.float32) * attended, axis=-1)
    delta_heads = jnp.swapaxes(row_delta, 2, 3)
    all_lse, all_delta = (
        lax.all_gather(jnp.swapaxes(log_total, 2, 3), "ctx", axis=2, tiled=True),
        lax.all_gather(row_delta, "ctx", axis=2, tiled=True),
    )
    partner_lse = jnp.swapaxes(
        lax.dynamic_slice_in_dim(all_lse, partner * unit_rows, unit_rows, 2), 2, 3
    )
    partner_delta = jnp.swapaxes(
        lax.dynamic_slice_in_dim(all_delta, partner * unit_rows, unit_rows, 2), 2, 3
    )
    far_queries, far_grads = from_partner((q_seq, grad_seq), "ctx", 0)
    near_queries = jnp.concatenate([q_heads, heads_of(far_queries, head_count)], axis=2)
    near_grads = jnp.concatenate([grad_heads, heads_of(far_grads, head_count)], axis=2)
    near_lse = jnp.concatenate([log_total, partner_lse], axis=3)
    near_delta = jnp.concatenate([delta_heads, partner_delta], axis=3)
    local_scores = (
        jnp.einsum(
            "jpqhe,jpkhe->jphqk", near_queries, near_keys, preferred_element_type=jnp.float32
        )
        * score_scale
    )
    probabilities = jnp.exp(local_scores - near_lse[..., None])
    grad_probs = jnp.einsum(
        "jpqhe,jpkhe->jphqk", near_grads, near_values, preferred_element_type=jnp.float32
    )
    grad_scores = (probabilities * (grad_probs - near_delta[..., None])).astype(jnp.bfloat16)
    grad_q_local = (
        jnp.einsum(
            "jphqk,jpkhe->jpqhe",
            grad_scores[:, :, :, :unit_rows, :],
            near_keys,
            preferred_element_type=jnp.float32,
        )
        * score_scale
    )
    grad_k_local = (
        jnp.einsum(
            "jphqk,jpqhe->jpkhe",
            grad_scores[..., :unit_rows],
            near_queries,
            preferred_element_type=jnp.float32,
        )
        * score_scale
    )
    grad_v_local = jnp.einsum(
        "jphqk,jpqhe->jpkhe",
        probabilities.astype(jnp.bfloat16)[..., :unit_rows],
        near_grads,
        preferred_element_type=jnp.float32,
    )
    query_stepper = partial(
        query_grad_step,
        q_heads,
        grad_heads,
        log_total,
        delta_heads,
        my_block,
        score_scale,
        head_count,
    )
    key_stepper = partial(key_grad_step, k_heads, v_heads, my_block, score_scale, head_count)

    def query_piece(carried, pieces, offset):
        return group_loop(pieces, unit_rows, block_pairs, query_stepper, carried)

    def key_piece(carried, pieces, offset):
        return group_loop(
            (pieces[0], pieces[1], all_lse, all_delta), unit_rows, block_pairs, key_stepper, carried
        )

    grad_q_all = query_piece(
        grad_q_local,
        (
            lax.all_gather(k_seq, "ctx", axis=2, tiled=True),
            lax.all_gather(v_seq, "ctx", axis=2, tiled=True),
        ),
        jnp.int32(0),
    )
    grad_k_all, grad_v_all = key_piece(
        (grad_k_local, grad_v_local),
        (
            lax.all_gather(q_seq, "ctx", axis=2, tiled=True),
            lax.all_gather(grad_seq, "ctx", axis=2, tiled=True),
        ),
        jnp.int32(0),
    )
    grad_queries = grad_q_all.reshape(row_count, model_width).astype(jnp.bfloat16)
    grad_keys = grad_k_all.reshape(row_count, model_width).astype(jnp.bfloat16)
    grad_values = grad_v_all.reshape(row_count, model_width).astype(jnp.bfloat16)
    grad_mixed = jnp.concatenate([grad_queries, grad_keys, grad_values], axis=1)
    grad_qkv = jnp.dot(normed.T, grad_mixed, preferred_element_type=jnp.float32)
    grad_bquery = jnp.sum(grad_queries.astype(jnp.float32), axis=0)
    grad_bvalue = jnp.sum(grad_values.astype(jnp.float32), axis=0)
    grad_normed = jnp.dot(grad_mixed, w_qkv.T, preferred_element_type=jnp.float32)
    _, norm_back_one = jax.vjp(
        layer_norm, inputs, gain_one.astype(jnp.float32), bias_one.astype(jnp.float32)
    )
    grad_inputs, grad_gain_one, grad_bias_one = norm_back_one(grad_normed)
    grad_hidden = (grad_inputs + grad_middle).astype(jnp.bfloat16)
    totals = (
        lax.psum_scatter(grad_gain_one, "ctx", scatter_dimension=0, tiled=True),
        lax.psum_scatter(grad_bias_one, "ctx", scatter_dimension=0, tiled=True),
        lax.psum_scatter(grad_qkv, "ctx", scatter_dimension=0, tiled=True),
        lax.psum_scatter(grad_bquery, "ctx", scatter_dimension=0, tiled=True),
        lax.psum_scatter(grad_bvalue, "ctx", scatter_dimension=0, tiled=True),
        lax.psum_scatter(grad_wout, "ctx", scatter_dimension=0, tiled=True),
        lax.psum_scatter(grad_bout, "ctx", scatter_dimension=0, tiled=True),
        lax.psum_scatter(grad_gain_two, "ctx", scatter_dimension=0, tiled=True),
        lax.psum_scatter(grad_bias_two, "ctx", scatter_dimension=0, tiled=True),
        lax.psum_scatter(grad_fc, "ctx", scatter_dimension=0, tiled=True),
        lax.psum_scatter(grad_bfc, "ctx", scatter_dimension=0, tiled=True),
        lax.psum_scatter(grad_proj, "ctx", scatter_dimension=0, tiled=True),
        lax.psum_scatter(grad_bproj, "ctx", scatter_dimension=0, tiled=True),
    )
    return (
        layer_out,
        grad_hidden,
        totals[0],
        totals[1],
        totals[2],
        totals[3],
        totals[4],
        totals[5],
        totals[6],
        totals[7],
        totals[8],
        totals[9],
        totals[10],
        totals[11],
        totals[12],
    )


def solution_any(mesh):
    return jax.shard_map(
        shards,
        mesh=mesh,
        in_specs=(
            P("ctx", None),
            P(),
            P("ctx"),
            P("ctx"),
            P("ctx", None),
            P("ctx"),
            P("ctx"),
            P("ctx", None),
            P("ctx"),
            P("ctx"),
            P("ctx"),
            P("ctx", None),
            P("ctx"),
            P("ctx", None),
            P("ctx"),
            P("ctx", None),
        ),
        out_specs=(
            P("ctx", None),
            P("ctx", None),
            P("ctx"),
            P("ctx"),
            P("ctx", None),
            P("ctx"),
            P("ctx"),
            P("ctx", None),
            P("ctx"),
            P("ctx"),
            P("ctx"),
            P("ctx", None),
            P("ctx"),
            P("ctx", None),
            P("ctx"),
        ),
        check_vma=False,
    )


AXES = ("s", "h", "r")
PLANES = 4


MESH_IDS = pl.DeviceIdType.MESH


class At:
    def __init__(self, ref, *index):
        self.ref, self.index = ref, index

    def now(self):
        return self.ref.at[self.index]

    def still(self):
        return self.ref.at[tuple(i if isinstance(i, slice) else 0 for i in self.index)]


ALL = slice(None)


class Exchange:
    def __init__(self, send, recv):
        self.send, self.recv, self.used, self.open = send, recv, 0, []
        self.s, self.h, self.r = (lax.axis_index(a) for a in AXES)
        self.planes = lax.axis_size("s")
        self.xn = self.h + 1 - 2 * lax.rem(self.h, 2)
        self.yn = lax.rem(self.h + 2, 4)
        self.dn = lax.rem(self.xn + 2, 4)
        self.z = lambda j: lax.rem(self.s + j, self.planes)
        self.X, self.Y, self.D = ({"h": i} for i in (self.xn, self.yn, self.dn))
        self.C = {"r": 1 - self.r}
        self.Z = [None] + [{"s": self.z(j)} for j in range(1, self.planes)]

    def greet(self, peers):
        barrier = pltpu.get_barrier_semaphore()
        for peer in peers:
            pl.semaphore_signal(barrier, inc=1, device_id=peer, device_id_type=MESH_IDS)
        pl.semaphore_wait(barrier, len(peers))

    def slots(self, count):
        self.used += count
        return range(self.used - count, self.used)

    def copy(self, i, src, dst, peer):
        return pltpu.make_async_remote_copy(
            src_ref=src,
            dst_ref=dst,
            send_sem=self.send.at[i],
            recv_sem=self.recv.at[i],
            device_id=peer,
            device_id_type=MESH_IDS,
        )

    def put(self, i, src, dst, peer):
        self.copy(i, src.now() if isinstance(src, At) else src, dst, peer).start()
        self.open.append((i, src))

    def got(self, i, dst):
        self.copy(i, dst, dst, self.X).wait_recv()

    def close(self):
        for i, src in self.open:
            src = src.still() if isinstance(src, At) else src
            self.copy(i, src, src, self.X).wait_send()


def remote_call(kernel, cid, out_shape, in_specs, out_specs, scratch, sems, name, vmem=56 << 20):
    return pl.pallas_call(
        kernel,
        out_shape=out_shape,
        in_specs=in_specs,
        out_specs=out_specs,
        scratch_shapes=scratch
        + [pltpu.SemaphoreType.DMA((sems,)), pltpu.SemaphoreType.DMA((sems,)), pltpu.SemaphoreType.DMA((8,))],
        compiler_params=pltpu.CompilerParams(
            collective_id=cid, has_side_effects=True, vmem_limit_bytes=vmem
        ),
        name=name,
    )


ANY = pl.BlockSpec(memory_space=pl.ANY)
VMEM = pl.BlockSpec(memory_space=pltpu.VMEM)


GATHER_ORDER = (1, 0, 2)


def by_x(k, j):
    return (k + j) % 2 == 0


def act(plan, steps, m, c, last_tile):
    for (em, ec), todo in plan.items():
        if (em == ec) == last_tile:

            @pl.when(m == em if last_tile else (m == em) & (c == ec))
            def _():
                for step, k, *js in todo:
                    steps[step](k, js)


def gather_steps(ins, outs, send, recv, local):
    ex = Exchange(send, recv)
    s, h, r, n = ex.s, ex.h, ex.r, ex.planes
    part = len(ins) - 1
    place = lambda k, t, c: (t, c) if k == part else (t, c, r)
    slab = lambda k, t, c: outs[k].at[place(k, t, c)]
    own = [pltpu.make_async_copy(ins[k], slab(k, s, h), local.at[k]) for k in range(part + 1)]
    for c in own:
        c.start()
    ex.greet([ex.X, ex.Y, ex.C] + ex.Z[1:])
    iz, ix, iy, ir, ic = ([ex.slots(n) for _ in outs] for _ in range(5))
    for k in GATHER_ORDER:
        for j in range(1, n):
            ex.put(iz[k][j], ins[k], slab(k, s, h), ex.Z[j])

    def forward(k, j):
        t = ex.z(j)
        if j:
            ex.got(iz[k][n - j], slab(k, t, h))
        src = At(outs[k], *place(k, t, h)) if j else ins[k]
        ex.put(ix[k][j], src, slab(k, t, h), ex.X)
        ex.put(iy[k][j], src, slab(k, t, h), ex.Y)

    def relay(k, j):
        t = ex.z(j)
        slots, frm, peer = (ix, ex.xn, ex.Y) if by_x(k, j) else (iy, ex.yn, ex.X)
        ex.got(slots[k][j], slab(k, t, frm))
        ex.put(ir[k][j], At(outs[k], *place(k, t, frm)), slab(k, t, frm), peer)

    def across(k, j):
        t = ex.z(j)
        slots, frm = (iy, ex.yn) if by_x(k, j) else (ix, ex.xn)
        ex.got(slots[k][j], slab(k, t, frm))
        ex.got(ir[k][j], slab(k, t, ex.dn))
        if not j:
            own[k].wait()
        ex.put(ic[k][j], At(outs[k], t, ALL, r), outs[k].at[t, :, r], ex.C)

    def last():
        for j in range(n):
            for k in range(part):
                ex.got(ic[k][j], outs[k].at[ex.z(j), :, 1 - r])
            ex.got(ix[part][j], slab(part, ex.z(j), ex.xn))
            ex.got(iy[part][j], slab(part, ex.z(j), ex.yn))
        own[part].wait()
        ex.close()

    for k in GATHER_ORDER:
        forward(k, 0)
    each = lambda step: lambda k, js: [step(k, j) for j in js]
    return dict(forward=each(forward), relay=each(relay), across=each(across)), last


def by_tile(shape, step):
    height, width = shape
    if height % 16:

        @pl.loop(0, width // 768)
        def _(i):
            step(slice(None), pl.ds(pl.multiple_of(i * 768, 768), 768))
    else:

        @pl.loop(0, height // 32)
        def _(i):
            step(pl.ds(pl.multiple_of(i * 32, 32), 32), slice(None))


def reduce_steps(ins, outs, bufs, send, recv, local):
    count = len(ins)
    mine, from_c, one, two, from_z = (bufs[i * count : (i + 1) * count] for i in range(5))
    ex = Exchange(send, recv)
    s, h, r, n = ex.s, ex.h, ex.r, ex.planes
    own = [
        pltpu.make_async_copy(a.at[:, :, r], m, local.at[k]) for k, (a, m) in enumerate(zip(ins, mine))
    ]
    for c in own:
        c.start()
    ex.greet([ex.X, ex.Y, ex.C] + ex.Z[1:])
    ic, i1, i2, iz = ([ex.slots(n) for _ in ins] for _ in range(4))
    i1b = [ex.slots(n) for _ in ins]
    for k in (1, 0, 2):
        for j in range(n):
            ex.put(ic[k][j], At(ins[k], ex.z(j), ALL, 1 - r), from_c[k].at[ex.z(j)], ex.C)
    for c in own:
        c.wait()

    def add(to, *parts):
        def step(rows, cols):
            total = to[rows, cols].astype(jnp.float32)
            for part in parts:
                total += part[rows, cols].astype(jnp.float32)
            to[rows, cols] = total.astype(to.dtype)

        by_tile(to.shape, step)

    def way(k, j):
        return (ex.X, ex.xn, ex.Y, ex.yn) if by_x(k, j) else (ex.Y, ex.yn, ex.X, ex.xn)

    def first(k, js):
        m = mine[k]
        for j in js:
            t = ex.z(j)
            ex.got(ic[k][j], from_c[k].at[t])
            add(m.at[t, ex.dn], from_c[k].at[t, ex.dn])
            ex.put(i1b[k][j], At(m, t, ex.dn), one[k].at[j, 1], way(k, j)[0])
        for j in js:
            t, (peer, near, _, other) = ex.z(j), way(k, j)
            add(m.at[t, near], from_c[k].at[t, near])
            ex.put(i1[k][j], At(m, t, near), one[k].at[j, 0], peer)
        for j in js:
            t, other = ex.z(j), way(k, j)[3]
            add(m.at[t, other], from_c[k].at[t, other])
            add(m.at[t, h], from_c[k].at[t, h])

    def second(k, js):
        m = mine[k]
        for j in js:
            t, (_, _, peer, other) = ex.z(j), way(k, j)
            ex.got(i1b[k][j], one[k].at[j, 1])
            add(m.at[t, other], one[k].at[j, 1])
            ex.put(i2[k][j], At(m, t, other), two[k].at[j], peer)

    def third(k, js):
        m = mine[k]
        for j in js:
            t = ex.z(j)
            ex.got(i1[k][j], one[k].at[j, 0])
            ex.got(i2[k][j], two[k].at[j])
            add(m.at[t, h], one[k].at[j, 0], two[k].at[j])
            if j:
                ex.put(iz[k][j], At(m, t, h), from_z[k].at[j], ex.Z[j])

    def last():
        for k, (m, o) in enumerate(zip(mine, outs)):
            for j in range(1, n):
                ex.got(iz[k][j], from_z[k].at[j])

            def step(rows, cols):
                total = m[s, h, rows, cols].astype(jnp.float32)
                for j in range(1, n):
                    total += from_z[k][j, rows, cols].astype(jnp.float32)
                o[rows, cols] = total

            by_tile(o.shape, step)

        ex.close()

    return ex, dict(first=first, second=second, third=third), last


HD = 64


GATHER_PLAN = {
    (2, 0): [("relay", 0, 0), ("relay", 1, 0)],
    (3, 1): [("forward", 1, 1, 3, 2)],
    (4, 1): [("relay", 1, 1, 3, 2), ("forward", 0, 1)],
    (4, 4): [("forward", 0, 3)],
    (5, 2): [("forward", 0, 2), ("relay", 0, 1), ("across", 1, 0, 1, 3, 2)],
    (6, 0): [("relay", 0, 3)],
    (6, 3): [("relay", 0, 2), ("across", 0, 0, 1), ("forward", 2, 1)],
    (7, 0): [("forward", 2, 3)],
    (7, 2): [("forward", 2, 2), ("across", 0, 3, 2)],
}


def attend_kernel(count, inv, blk, q_ref, kv_ref, *refs):
    ins, outs = refs[:count], refs[count + 3 : 2 * count + 3]
    o_ref, low_ref, lse_ref = refs[count : count + 3]
    qt, ks, vt, os, sc, send, recv, local = refs[2 * count + 3 :]
    npair, U, W = q_ref.shape
    nh = W // HD
    B = kv_ref.shape[1]
    TQ, TK = 2 * U, 2 * B
    steps, last = gather_steps(ins, outs, send, recv, local)

    @pl.loop(0, npair)
    def _(i):
        p = inv[i]
        qt[:, pl.ds(pl.multiple_of(i * U, U), U)] = q_ref[p].T
        kv = kv_ref[p]
        for h in range(nh):
            ks[h, pl.ds(i * B, B), :] = kv[:, h * HD : (h + 1) * HD]
        vct = kv[:, W:].T
        for h in range(nh):
            vt[h, 0:HD, pl.ds(pl.multiple_of(i * B, B), B)] = vct[h * HD : (h + 1) * HD]
            vt[h, HD:, pl.ds(pl.multiple_of(i * B, B), B)] = jnp.ones((vt.shape[1] - HD, B), vt.dtype)

    def scores(m, c, carry, masked):
        out = []
        rows = pl.ds(pl.multiple_of(c * TK, TK), TK)
        for h in range(nh):
            qh = qt[h * HD : (h + 1) * HD, pl.ds(pl.multiple_of(m * TQ, TQ), TQ)]
            s = jnp.dot(ks[h, rows, :], qh, preferred_element_type=jnp.float32)
            if masked:
                row = lax.broadcasted_iota(jnp.int32, s.shape, 0)
                col = lax.broadcasted_iota(jnp.int32, s.shape, 1)
                s = jnp.where((row >= B) & (col < U), NEG, s)
            sc[h, rows, :] = s
            out.append(jnp.maximum(carry[h], jnp.max(s.reshape(TK // 8, 8, TQ), axis=0)))
        return tuple(out)

    def values(c, carry, tops):
        out = []
        rows = pl.ds(pl.multiple_of(c * TK, TK), TK)
        for h in range(nh):
            p = jnp.exp(sc[h, rows, :] - tops[h]).astype(jnp.bfloat16)
            out.append(carry[h] + jnp.dot(vt[h, :, rows], p, preferred_element_type=jnp.float32))
        return tuple(out)

    @pl.loop(0, npair // 2)
    def _(m):
        tops = tuple(jnp.full((8, TQ), NEG, jnp.float32) for _ in range(nh))
        tops = lax.fori_loop(0, m, lambda c, x: scores(m, c, x, False), tops)
        tops = [jnp.max(t, axis=0, keepdims=True) for t in scores(m, m, tops, True)]

        def step(c, x):
            x = values(c, x, tops)
            act(GATHER_PLAN, steps, m, c, False)
            return x

        init = tuple(jnp.zeros((vt.shape[1], TQ), jnp.float32) for _ in range(nh))
        carry = values(m, lax.fori_loop(0, m, step, init), tops)
        carry = list(zip(tops, carry))
        rows = []
        for h in range(nh):
            mx, acc = carry[h]
            tot = acc[HD : HD + 1]
            rows.append(acc[:HD] / tot)
            lse_ref[h : h + 1, pl.ds(pl.multiple_of(m * TQ, TQ), TQ)] = mx + jnp.log(tot)
        os[pl.ds(pl.multiple_of(m * TQ, TQ), TQ), :] = jnp.concatenate(rows, axis=0).T
        act(GATHER_PLAN, steps, m, m, True)

    @pl.loop(0, npair)
    def _(p):
        o = os[pl.ds(blk[p] * U, U), :]
        o_ref[pl.ds(pl.multiple_of(p * U, U), U), :] = o
        low_ref[pl.ds(pl.multiple_of(p * U, U), U), :] = o.astype(jnp.bfloat16)

    last()


SMEM = pl.BlockSpec(memory_space=pltpu.SMEM)


def attend(inv, blk, q, kv, *weights):
    npair, U, W = q.shape
    R, K = npair * U, npair * kv.shape[1]
    nh = W // HD
    S, H, Q = (lax.axis_size(a) for a in AXES)
    n = len(weights)
    f32, bf16 = jnp.float32, jnp.bfloat16
    return remote_call(
        partial(attend_kernel, n),
        1,
        [
            jax.ShapeDtypeStruct((R, W), f32),
            jax.ShapeDtypeStruct((R, W), bf16),
            jax.ShapeDtypeStruct((8, R), f32),
        ]
        + [jax.ShapeDtypeStruct((S, H, Q) + a.shape, a.dtype) for a in weights[:-1]]
        + [jax.ShapeDtypeStruct((S, H) + weights[-1].shape, bf16)],
        [SMEM] * 2 + [VMEM] * 2 + [ANY] * n,
        [VMEM] * 3 + [ANY] * n,
        [
            pltpu.VMEM((W, R), bf16),
            pltpu.VMEM((nh, K, HD), bf16),
            pltpu.VMEM((nh, HD + 16, K), bf16),
            pltpu.VMEM((R, W), f32),
            pltpu.VMEM((nh, K, 2 * U), f32),
        ],
        5 * S * n,
        "attend",
    )(inv, blk, q, kv, *weights)


REDUCE_PLAN = {
    (7, 0): [("first", 1, 1, 2, 3, 0)],
    (7, 5): [("second", 1, 1, 2, 3, 0)],
    (7, 6): [("first", 0, 1, 2, 3, 0)],
    (5, 2): [("third", 1, 1, 2, 3, 0)],
    (5, 3): [("second", 0, 1, 2, 3, 0)],
    (5, 4): [("first", 2, 1, 2, 3, 0)],
    (3, 0): [("third", 0, 1, 2, 3, 0), ("second", 2, 1, 2, 3, 0)],
    (2, 0): [("third", 2, 1, 2, 3, 0)],
}


def attend_back_kernel(count, inv, blk, q_ref, kv_ref, g_ref, o_ref, lse_ref, out_ref, *refs):
    ins, gm_ref, lo_ref, outs = refs[:count], refs[count], refs[count + 1], refs[count + 2 : 2 * count + 2]
    bufs = refs[2 * count + 2 : 7 * count + 2]
    qt, gt, qx, gx, ks, vs, kt, delta, dkv, dqs, over, back, send, recv, local = refs[7 * count + 2 :]
    npair, U, W = q_ref.shape
    nh = W // HD
    B = kv_ref.shape[1]
    TQ, TK = 2 * U, 2 * B
    f32, bf16 = jnp.float32, jnp.bfloat16
    ex, steps, last = reduce_steps(ins, outs, bufs, send, recv, local)
    swap = ex.slots(npair // 2)
    il = ex.slots(ex.planes)
    keep = pltpu.make_async_copy(out_ref.at[ex.s], lo_ref.at[ex.s], local.at[count])
    keep.start()
    for j in range(1, ex.planes):
        ex.put(il[j], out_ref.at[ex.z(j)], lo_ref.at[ex.s], ex.Z[j])

    @pl.loop(0, npair)
    def _(i):
        p = inv[i]
        qc = q_ref[p]
        gc = g_ref[p]
        oc = o_ref[pl.ds(p * U, U), :]
        cols = pl.ds(pl.multiple_of(i * U, U), U)
        qt[:, cols] = qc.T
        gt[:, cols] = gc.T
        prod = (oc * gc.astype(f32)).T
        zero = jnp.zeros((U, HD), bf16)
        for h in range(nh):
            delta[h : h + 1, cols] = jnp.sum(prod[h * HD : (h + 1) * HD], axis=0, keepdims=True)
            qx[h, pl.ds(i * U, U), :] = jnp.concatenate([zero, qc[:, h * HD : (h + 1) * HD]], axis=1)
            gx[h, pl.ds(i * U, U), :] = jnp.concatenate([gc[:, h * HD : (h + 1) * HD], zero], axis=1)
        kv = kv_ref[p]
        kc, vc = kv[:, :W], kv[:, W:]
        kt[:, pl.ds(pl.multiple_of(i * B, B), B)] = kc.T
        for h in range(nh):
            ks[h, pl.ds(i * B, B), :] = kc[:, h * HD : (h + 1) * HD]
            vs[h, pl.ds(i * B, B), :] = vc[:, h * HD : (h + 1) * HD]

    dkv[...] = jnp.zeros_like(dkv)

    def tile(m, c, carry, masked):
        out = []
        qcols = pl.ds(pl.multiple_of(m * TQ, TQ), TQ)
        krows = pl.ds(pl.multiple_of(c * TK, TK), TK)
        for h in range(nh):
            hs = slice(h * HD, (h + 1) * HD)
            s = jnp.dot(ks[h, krows, :], qt[hs, qcols], preferred_element_type=f32)
            p = jnp.exp(s - lse_ref[h : h + 1, qcols])
            if masked:
                row = lax.broadcasted_iota(jnp.int32, s.shape, 0)
                col = lax.broadcasted_iota(jnp.int32, s.shape, 1)
                p = jnp.where((row >= B) & (col < U), 0.0, p)
            dp = jnp.dot(vs[h, krows, :], gt[hs, qcols], preferred_element_type=f32)
            ds = (p * (dp - delta[h : h + 1, qcols])).astype(bf16)
            dkv[h, krows, :] += jnp.dot(
                p.astype(bf16), gx[h, qcols, :], preferred_element_type=f32
            ) + jnp.dot(ds, qx[h, qcols, :], preferred_element_type=f32)
            out.append(carry[h] + jnp.dot(kt[hs, krows], ds, preferred_element_type=f32))
        return tuple(out)

    def halves(b, half):
        rows = pl.ds(pl.multiple_of(b * B + half * U, U), U)
        parts = [dkv[h, rows, :] for h in range(nh)]
        return jnp.concatenate([x[:, HD:] for x in parts] + [x[:, :HD] for x in parts], axis=1)

    @pl.loop(0, npair // 2)
    def _(turn):
        m = npair // 2 - 1 - turn
        init = tuple(jnp.zeros((HD, TQ), f32) for _ in range(nh))

        def step(c, x):
            x = tile(m, c, x, False)
            act(REDUCE_PLAN, steps, m, c, False)
            return x

        carry = lax.fori_loop(0, m, step, init)
        carry = tile(m, m, carry, True)
        dqs[pl.ds(pl.multiple_of(m * TQ, TQ), TQ), :] = (jnp.concatenate(carry, axis=0).T * 0.125).astype(bf16)
        for k in range(2):
            over[2 * m + k] = halves(2 * m + k, 1).astype(bf16)
        ex.copy(swap[0] + m, over.at[pl.ds(2 * m, 2)], back.at[pl.ds(2 * m, 2)], ex.C).start()
        act(REDUCE_PLAN, steps, m, m, True)

    @pl.loop(0, npair // 2)
    def _(m):
        moved = ex.copy(swap[0] + m, over.at[pl.ds(2 * m, 2)], back.at[pl.ds(2 * m, 2)], ex.C)
        moved.wait_recv()
        moved.wait_send()

    @pl.loop(0, npair)
    def _(p):
        b = blk[p]
        rows = pl.ds(b * B, U)
        parts = [dkv[h, rows, :] for h in range(nh)]
        own = jnp.concatenate([x[:, HD:] for x in parts] + [x[:, :HD] for x in parts], axis=1)
        own = (own + back[b].astype(f32)).astype(bf16)
        gm_ref[p] = jnp.concatenate([dqs[pl.ds(b * U, U), :], own], axis=1)

    for j in range(1, ex.planes):
        ex.got(il[ex.planes - j], lo_ref.at[ex.z(j)])
    keep.wait()
    last()


def attend_back(inv, blk, q, kv, g, o, lse, out, *grads):
    npair, U, W = q.shape
    R, K = npair * U, npair * kv.shape[1]
    nh = W // HD
    S, H, Q = (lax.axis_size(a) for a in AXES)
    n = len(grads)
    f32, bf16 = jnp.float32, jnp.bfloat16
    tails = [a.shape[3:] for a in grads]
    buffers = [[pltpu.VMEM(lead + t, bf16) for t in tails] for lead in ((S, H), (S, H), (S, 2), (S,), (S,))]
    return remote_call(
        partial(attend_back_kernel, n),
        2,
        [jax.ShapeDtypeStruct((npair, R // npair, 3 * W), bf16), jax.ShapeDtypeStruct(out.shape, bf16)]
        + [jax.ShapeDtypeStruct(t, f32) for t in tails],
        [SMEM] * 2 + [VMEM] * 5 + [ANY] * (n + 1),
        [VMEM, ANY] + [VMEM] * n,
        sum(buffers, [])
        + [
            pltpu.VMEM((W, R), bf16),
            pltpu.VMEM((W, R), bf16),
            pltpu.VMEM((nh, R, 2 * HD), bf16),
            pltpu.VMEM((nh, R, 2 * HD), bf16),
            pltpu.VMEM((nh, K, HD), bf16),
            pltpu.VMEM((nh, K, HD), bf16),
            pltpu.VMEM((W, K), bf16),
            pltpu.VMEM((8, R), f32),
            pltpu.VMEM((nh, K, 2 * HD), f32),
            pltpu.VMEM((R, W), bf16),
            pltpu.VMEM((npair, R // npair, 2 * W), bf16),
            pltpu.VMEM((npair, R // npair, 2 * W), bf16),
        ],
        5 * S * n + npair // 2 + S,
        "attend_back",
        60 << 20,
    )(inv, blk, q, kv, g, o, lse, out, *grads)


def front_kernel(
    x_ref, w_ref, v_ref, norm_ref, q_ref, kv_ref, wt_ref, vec_ref, xo_ref,
    xa, ws, wa, wf, kv_far, send, recv, local,
):
    f32, bf16 = jnp.float32, jnp.bfloat16
    ex = Exchange(send, recv)
    s, h, r, n = ex.s, ex.h, ex.r, ex.planes
    H, U, D = xa.shape[1:]
    d, N = w_ref.shape
    W = N // 3 // H
    own = pltpu.make_async_copy(x_ref.at[s], xa.at[s, h], local.at[0])
    own.start()
    for k in range(H):
        ws[k] = jnp.concatenate(
            [w_ref[:, c * D + k * W : c * D + (k + 1) * W] for c in range(3)] + [v_ref[...]], axis=1
        )
    ex.greet([ex.X, ex.Y, ex.D, ex.C] + ex.Z[1:])
    iw, ix, iy, ir, iz, iwz, iwc, ik = (ex.slots(n) for _ in range(8))
    for j in range(1, n):
        ex.put(iz[j], x_ref.at[ex.z(j)], xa.at[s, h], ex.Z[j])
    for k, (peer, to) in enumerate(((ex.X, ex.xn), (ex.Y, ex.yn), (ex.D, ex.dn))):
        ex.put(iw[k], ws.at[to], wa.at[s, h, r], peer)
    wa[s, h, r] = ws[h]
    own.wait()

    def forward(j):
        t = ex.z(j)
        if j:
            ex.got(iz[n - j], xa.at[t, h])
        ex.put(ix[j], xa.at[t, h], xa.at[t, h], ex.X)
        ex.put(iy[j], xa.at[t, h], xa.at[t, h], ex.Y)

    def relay(j):
        t = ex.z(j)
        slots, frm, peer = (ix, ex.xn, ex.Y) if by_x(0, j) else (iy, ex.yn, ex.X)
        ex.got(slots[j], xa.at[t, frm])
        ex.put(ir[j], xa.at[t, frm], xa.at[t, frm], peer)

    def weights(j):
        if j:
            ex.got(iwz[n - j], wa.at[ex.z(j), :, r])
        ex.put(iwc[j], wa.at[ex.z(j), :, r], wa.at[ex.z(j), :, r], ex.C)

    forward(0)
    for k, frm in enumerate((ex.xn, ex.yn, ex.dn)):
        ex.got(iw[k], wa.at[s, frm, r])
    for j in range(1, n):
        ex.put(iwz[j], wa.at[s, :, r], wa.at[s, :, r], ex.Z[j])
    weights(0)
    relay(0)
    for a, b in ((1, None), (3, 1), (2, 3)):
        forward(a)
        if b is not None:
            relay(b)
    for j in (1, 3, 2):
        weights(j)
    for j in range(n):
        ex.got(iwc[j], wa.at[ex.z(j), :, 1 - r])
    rows = H * 2 * d
    for t in range(n):
        block = wa[t].astype(f32).reshape(rows, N // H + 128)
        wf[t * rows : (t + 1) * rows] = block
    wt_ref[...] = wf[:, : N // H].T.astype(bf16)
    vec_ref[...] = wf[:, N // H :].T[:16]
    w = wf[:, : N // H].astype(bf16)
    gain, bias = vec_ref[0:1], vec_ref[1:2]

    def mine(row):
        picked = jnp.zeros((1, W), f32)
        for k in range(H):
            picked = jnp.where(h == k, vec_ref[row : row + 1, k * W : (k + 1) * W], picked)
        return picked

    bq, bv = mine(2), mine(3)

    def batch(j):
        t = ex.z(j)
        slots, frm = (iy, ex.yn) if by_x(0, j) else (ix, ex.xn)
        ex.got(slots[j], xa.at[t, frm])
        ex.got(ir[j], xa.at[t, ex.dn])
        x = xa[t].reshape(H * U, D).astype(f32)
        normed = layer_norm(x, gain, bias).astype(bf16)
        norm_ref[t] = normed.reshape(H, U, D)
        mixed = jnp.dot(normed, w, preferred_element_type=f32)
        q = (mixed[:, :W] + bq).astype(bf16) * jnp.asarray(0.125, bf16)
        q_ref[t] = q.reshape(H, U, W)
        kv = jnp.concatenate([mixed[:, W : 2 * W], mixed[:, 2 * W :] + bv], axis=1).astype(bf16)
        kv_ref[t, :, 0] = kv.reshape(H, U, 2 * W)
        ex.put(ik[j], kv_ref.at[t, :, 0], kv_far.at[t], ex.C)

    batch(0)
    relay(2)
    batch(1)
    batch(3)
    batch(2)
    xo_ref[...] = xa[:, h]
    for j in (0, 1, 3, 2):
        t = ex.z(j)
        ex.got(ik[j], kv_far.at[t])
        kv_ref[t, :, 1] = kv_far[t]
    ex.close()


def front(x, w, v):
    S, U, D = x.shape
    d, N = w.shape
    H, Q = (lax.axis_size(a) for a in AXES[1:])
    W = N // 3 // H
    f32, bf16 = jnp.float32, jnp.bfloat16
    return remote_call(
        front_kernel,
        0,
        [
            jax.ShapeDtypeStruct((S, H, U, D), bf16),
            jax.ShapeDtypeStruct((S, H, U, W), bf16),
            jax.ShapeDtypeStruct((S, H, Q, U, 2 * W), bf16),
            jax.ShapeDtypeStruct((N // H, D), bf16),
            jax.ShapeDtypeStruct((16, D), f32),
            jax.ShapeDtypeStruct((S, U, D), bf16),
        ],
        [ANY, VMEM, VMEM],
        [VMEM] * 6,
        [
            pltpu.VMEM((S, H, U, D), bf16),
            pltpu.VMEM((H, d, N // H + 128), bf16),
            pltpu.VMEM((S, H, Q, d, N // H + 128), bf16),
            pltpu.VMEM((D, N // H + 128), f32),
            pltpu.VMEM((S, H, U, 2 * W), bf16),
        ],
        8 * S,
        "front",
    )(x, w, v)


def middle_kernel(
    low_ref, x_ref, g_ref, vec_ref, bf_ref, fc_ref, proj_ref, wo_ref,
    lo_ref, gmid_ref, small_ref, ga_ref, gfc_ref, gproj_ref, gout_ref,
    ra, fc, wp, wo_in, wf, wo, act_ref, dpre, deriv, g, att, mid, z_ref, n2, n2t, y, t2, gb, sb, gfc, gproj, gout,
    send, recv, local,
):
    f32, bf16 = jnp.float32, jnp.bfloat16
    ex = Exchange(send, recv)
    s, h, r, n = ex.s, ex.h, ex.r, ex.planes
    H, U, W = low_ref.shape[1:]
    R, D = att.shape
    d = fc.shape[3]
    loads = [
        pltpu.make_async_copy(a, b, local.at[i])
        for i, (a, b) in enumerate(
            (
                (wo_ref, wo_in),
                (proj_ref.at[:, h], wp.at[:, h, r]),
                (fc_ref, fc),
                (low_ref.at[:, h], ra.at[h]),
                (g_ref.at[s], g.at[s]),
                (proj_ref.at[:, ex.xn], wp.at[:, ex.xn, r]),
                (proj_ref.at[:, ex.yn], wp.at[:, ex.yn, r]),
            )
        )
    ]
    for c in loads:
        c.start()
    ex.greet([ex.X, ex.Y, ex.D, ex.C] + ex.Z[1:])
    there, back = ex.slots(3), ex.slots(3)
    ir, ic, ig = (ex.slots(n) for _ in range(3))
    sides = ((ex.X, ex.xn), (ex.Y, ex.yn), (ex.D, ex.dn))
    for k, (peer, to) in enumerate(sides):
        ex.put(there[k], low_ref.at[:, to], ra.at[h], peer)
    for j in range(n):
        frm, peer = (ex.xn, ex.Y) if by_x(0, j) else (ex.yn, ex.X)
        ex.put(ir[j], proj_ref.at[ex.z(j), frm], wp.at[ex.z(j), frm, r], peer)
    for j in range(1, n):
        ex.put(ig[j], g_ref.at[ex.z(j)], g.at[s], ex.Z[j])

    def across(j):
        ex.got(ir[j], wp.at[ex.z(j), ex.dn, r])
        ex.put(ic[j], wp.at[ex.z(j), :, r], wp.at[ex.z(j), :, r], ex.C)

    dot = partial(jnp.dot, preferred_element_type=f32)
    dot_nt = lambda a, b: lax.dot_general(a, b, (((1,), (1,)), ((), ())), preferred_element_type=f32)
    dot_tn = lambda a, b: lax.dot_general(a, b, (((0,), (0,)), ((), ())), preferred_element_type=f32)
    loads[0].wait()
    wo[...] = wo_in[:, :, :, :d].astype(f32).reshape(D, D).astype(bf16)
    loads[2].wait()

    @pl.loop(0, n)
    def _(b):
        cols = pl.ds(pl.multiple_of(b * D, D), D)
        wf[b] = fc[:, :, :, :, cols].astype(f32).reshape(D, D).astype(bf16)

    y[...] = jnp.zeros_like(y)
    t2[...] = jnp.zeros_like(t2)
    gout[...] = jnp.zeros_like(gout)
    loads[3].wait()
    for k, (peer, frm) in enumerate(sides):
        ex.got(there[k], ra.at[frm])
    att[...] = jnp.concatenate([ra[k].reshape(R, W) for k in range(H)], axis=1)
    m = x_ref[...].astype(f32) + dot(att[...], wo[...]) + vec_ref[4:5]
    mid[...] = m
    center = m - jnp.mean(m, axis=-1, keepdims=True)
    rstd = lax.rsqrt(jnp.mean(center * center, axis=-1, keepdims=True) + 1e-05)
    z = center * rstd
    z_ref[...] = z
    normed = (z * vec_ref[5:6] + vec_ref[6:7]).astype(bf16)
    n2[...] = normed
    n2t[...] = normed.T
    slope = math.sqrt(2.0 / math.pi)

    def up(b):
        cols = slice(b * D, (b + 1) * D)
        pre = dot(n2[...], wf[b]) + bf_ref[0:1, cols]
        square = pre * pre
        tanh = jnp.tanh(slope * pre * (1.0 + 0.044715 * square))
        half = 0.5 * (1.0 + tanh)
        act_ref[b] = (pre * half).astype(bf16)
        deriv[b] = half + 0.5 * pre * (1.0 - tanh * tanh) * (slope * (1.0 + 3 * 0.044715 * square))

    up(0)
    for i in (1, 5, 6):
        loads[i].wait()
    across(0)
    across(1)
    up(1)
    across(2)
    across(3)
    up(2)
    up(3)
    loads[4].wait()
    for j in range(1, n):
        ex.got(ig[n - j], g.at[ex.z(j)])

    def down(j):
        b = ex.z(j)
        ex.got(ic[j], wp.at[b, :, 1 - r])
        pre = dot_nt(g[...].reshape(R, D), wp[b].reshape(D, D)) * deriv[b]
        dpre[b] = pre.astype(bf16)
        small_ref[pl.ds(b + 4, 1)] = jnp.sum(dpre[b].astype(f32), axis=0, keepdims=True)
        t2[...] += dot_nt(dpre[b], wf[b])

    for j in range(n):
        down(j)
    t, z = t2[...], z_ref[...]
    g32 = g[...].reshape(R, D).astype(f32)
    e = t * vec_ref[5:6]
    inner = e - jnp.mean(e, axis=-1, keepdims=True) - z * jnp.mean(e * z, axis=-1, keepdims=True)
    gm = g32 + inner * rstd
    gmid_ref[...] = gm
    gb[...] = gm.astype(bf16)
    ga = dot_nt(gb[...], wo[...]).astype(bf16)
    for k in range(H):
        sb[k] = ga[:, k * W : (k + 1) * W].reshape(sb.shape[1:])
    for k, (peer, to) in enumerate(sides):
        ex.put(back[k], sb.at[to], ga_ref.at[:, h], peer)
    mine = pltpu.make_async_copy(sb.at[h], ga_ref.at[:, h], local.at[3])
    mine.start()
    stores = []

    def store(src, dst):
        stores.append(pltpu.make_async_copy(src, dst, local.at[4 + len(stores)]))
        stores[-1].start()

    for b in range(n):
        grad = g[...].reshape(R, D)
        gproj[b] = dot_tn(act_ref[b], grad).astype(bf16).reshape(gproj.shape[1:])
        gfc[:, :, :, :, b * D : (b + 1) * D] = dot(n2t[...], dpre[b]).reshape(gfc.shape[:4] + (D,)).astype(bf16)
        y[...] += dot(act_ref[b], wp[b].reshape(D, D))
    store(gproj, gproj_ref)
    store(gfc, gfc_ref)
    gout[:, :, :, :d] = dot_tn(att[...], gb[...]).reshape(gout.shape[:3] + (d, D)).astype(bf16)
    store(gout, gout_ref)
    lo_ref[...] = (mid[...] + y[...] + vec_ref[7:8]).astype(bf16)
    small_ref[1:2] = jnp.sum(t2[...] * z_ref[...], axis=0, keepdims=True)
    small_ref[2:3] = jnp.sum(t2[...], axis=0, keepdims=True)
    small_ref[0:1] = jnp.sum(gb[...].astype(f32), axis=0, keepdims=True)
    small_ref[3:4] = jnp.sum(g[...].reshape(R, D).astype(f32), axis=0, keepdims=True)
    for k, (peer, frm) in enumerate(sides):
        ex.got(back[k], ga_ref.at[:, frm])
    for c in stores + [mine]:
        c.wait()
    ex.close()


def middle(low, x, g, vecs, bias, fc, proj, wo):
    S, H, U, W = low.shape
    R, D = x.shape
    whole = fc.shape[:3] + proj.shape[2:]
    f32, bf16 = jnp.float32, jnp.bfloat16
    vm = pltpu.VMEM
    return remote_call(
        middle_kernel,
        4,
        [
            jax.ShapeDtypeStruct((R, D), bf16),
            jax.ShapeDtypeStruct((R, D), f32),
            jax.ShapeDtypeStruct((8, D), f32),
            jax.ShapeDtypeStruct(low.shape, bf16),
            jax.ShapeDtypeStruct(fc.shape, bf16),
            jax.ShapeDtypeStruct(whole, bf16),
            jax.ShapeDtypeStruct(wo.shape, bf16),
        ],
        [ANY, VMEM, ANY, VMEM, VMEM] + [ANY] * 3,
        [VMEM] * 3 + [ANY] * 4,
        [
            vm((H, S, U, W), bf16),
            vm(fc.shape, bf16),
            vm(whole, bf16),
            vm(wo.shape, bf16),
            vm((S, D, D), bf16),
            vm((D, D), bf16),
            vm((S, R, D), bf16),
            vm((S, R, D), bf16),
            vm((S, R, D), f32),
            vm((S, U, D), bf16),
            vm((R, D), bf16),
            vm((R, D), f32),
            vm((R, D), f32),
            vm((R, D), bf16),
            vm((D, R), bf16),
            vm((R, D), f32),
            vm((R, D), f32),
            vm((R, D), bf16),
            vm((H, S, U, W), bf16),
            vm(fc.shape, bf16),
            vm(whole, bf16),
            vm(wo.shape, bf16),
        ],
        6 + 3 * S,
        "middle",
        60 << 20,
    )(low, x, g, vecs, bias, fc, proj, wo)


def norm_back(x, t, gain, grad):
    mean = jnp.mean(x, axis=-1, keepdims=True)
    center = x - mean
    rstd = lax.rsqrt(jnp.mean(center * center, axis=-1, keepdims=True) + 1e-05)
    z = center * rstd
    e = t * gain
    inner = e - jnp.mean(e, axis=-1, keepdims=True) - z * jnp.mean(e * z, axis=-1, keepdims=True)
    return grad + rstd * inner


def finish_kernel(
    gm_ref, wt_ref, norm_ref, x_ref, gmid_ref, gain_ref, small_ref,
    gh_ref, gq_ref, vec_ref,
    t_ref, one, two, hid, gw, gw_c, gw_z, gw_sum, vec, send, recv, local,
):
    f32, bf16 = jnp.float32, jnp.bfloat16
    ex = Exchange(send, recv)
    s, h, r, n = ex.s, ex.h, ex.r, ex.planes
    half = n // 2
    H, N = gm_ref.shape[1], gm_ref.shape[3]
    U, D = t_ref.shape[2], t_ref.shape[3]
    W = N // 3
    d = gw.shape[3]
    ex.greet([ex.X, ex.Y, ex.D, ex.C] + ex.Z[1:])
    i1, i1b, i2, ih, ic, iz, iq = (ex.slots(n) for _ in range(7))
    iv = ex.slots(3 + n)
    acc = [jnp.zeros((1, D), f32), jnp.zeros((1, D), f32)]
    way = lambda j: (ex.X, ex.xn, ex.Y, ex.yn) if by_x(0, j) else (ex.Y, ex.yn, ex.X, ex.xn)

    def product(j, pair):
        t = ex.z(j)
        g = jnp.concatenate([gm_ref[t, to] for to in pair], axis=0)
        prod = jnp.dot(g, wt_ref[...], preferred_element_type=f32)
        for k, to in enumerate(pair):
            part = prod[k * U : (k + 1) * U]
            t_ref[t, to] = part.astype(bf16)
            acc[0] += jnp.sum(part * norm_ref[t, to].astype(f32), axis=0, keepdims=True)
            acc[1] += jnp.sum(part, axis=0, keepdims=True)

    def leave(j):
        peer, near, _, _ = way(j)
        ex.put(i1b[j], t_ref.at[ex.z(j), ex.dn], one.at[j, 1], peer)
        ex.put(i1[j], t_ref.at[ex.z(j), near], one.at[j, 0], peer)

    def relay(j):
        t = ex.z(j)
        _, _, peer, other = way(j)
        ex.got(i1b[j], one.at[j, 1])
        t_ref[t, other] = (t_ref[t, other].astype(f32) + one[j, 1].astype(f32)).astype(bf16)
        ex.put(i2[j], t_ref.at[t, other], two.at[j], peer)

    g_all = gm_ref[...].reshape(n * H * U, N)
    def qkv_rows(t0):
        width = H * 2 * d
        nt = norm_ref[:, :, :, t0 * width : (t0 + half) * width].reshape(n * H * U, half * width)
        part = lax.dot_general(nt, g_all, (((0,), (0,)), ((), ())), preferred_element_type=f32)
        gw[t0 : t0 + half] = part.reshape(half, H, 2, d, N).astype(bf16)
        for t in range(t0, t0 + half):
            ex.put(ic[t], gw.at[t, :, 1 - r], gw_c.at[t], ex.C)

    def done(j):
        t = ex.z(j)
        ex.got(i1[j], one.at[j, 0])
        ex.got(i2[j], two.at[j])
        total = t_ref[t, h].astype(f32) + one[j, 0].astype(f32) + two[j].astype(f32)
        hid[t] = norm_back(x_ref[t].astype(f32), total, gain_ref[0:1], gmid_ref[t]).astype(bf16)
        if j:
            ex.put(ih[j], hid.at[t], gh_ref.at[s], ex.Z[j])

    for j in (1, 2):
        product(j, (ex.dn, way(j)[1]))
        leave(j)
    qkv_rows(0)
    qkv_rows(half)
    for j in (1, 2):
        product(j, (way(j)[3], h))
    for t in range(n):
        ex.got(ic[t], gw_c.at[t])
        gw_c[t] = (gw_c[t].astype(f32) + gw[t, :, r].astype(f32)).astype(bf16)
    for j in range(1, n):
        ex.put(iz[j], gw_c.at[ex.z(j)], gw_z.at[s], ex.Z[j])
    relay(1)
    relay(2)
    for j in (3, 0):
        product(j, (ex.dn, way(j)[1]))
        leave(j)
    for j in (3, 0):
        product(j, (way(j)[3], h))
    cols = jnp.sum(g_all.astype(f32), axis=0, keepdims=True)
    lane = lax.broadcasted_iota(jnp.int32, (1, D), 1) // W

    def placed(c):
        return jnp.where(lane == h, jnp.concatenate([c] * H, axis=1), 0.0)

    vec[0, 0:1] = acc[0]
    vec[0, 1:2] = acc[1]
    vec[0, 2:3] = placed(cols[:, :W])
    vec[0, 3:4] = placed(cols[:, 2 * W :])
    vec[0, 4:8] = jnp.zeros((4, D), f32)
    vec[0, 8:] = small_ref[...]
    ex.put(iv[0], vec.at[0], vec.at[1], ex.C)

    done(1)
    done(2)
    ex.got(iv[0], vec.at[1])
    vec[2] = vec[0] + vec[1]
    ex.put(iv[1], vec.at[2], vec.at[3], ex.X)
    relay(3)
    relay(0)
    ex.got(iv[1], vec.at[3])
    vec[4] = vec[2] + vec[3]
    ex.put(iv[2], vec.at[4], vec.at[5], ex.Y)
    total = gw_c[s].astype(f32)
    for j in range(1, n):
        ex.got(iz[n - j], gw_z.at[ex.z(j)])
        total += gw_z[ex.z(j)].astype(f32)
    gw_sum[...] = total
    for k, (peer, to) in enumerate(((ex.X, ex.xn), (ex.Y, ex.yn), (ex.D, ex.dn))):
        ex.put(iq[k], gw_sum.at[to], gq_ref.at[h], peer)
    mine = pltpu.make_async_copy(gw_sum.at[h], gq_ref.at[h], local.at[2])
    mine.start()
    ex.got(iv[2], vec.at[5])
    vec[6] = vec[4] + vec[5]
    for j in range(1, n):
        ex.put(iv[2 + j], vec.at[6], vec.at[6 + j], ex.Z[j])
    done(3)
    done(0)
    own = pltpu.make_async_copy(hid.at[s], gh_ref.at[s], local.at[1])
    own.start()
    for j in range(1, n):
        ex.got(iv[2 + j], vec.at[6 + j])
    vec_ref[...] = vec[6] + vec[7] + vec[8] + vec[9]
    for k, frm in enumerate((ex.xn, ex.yn, ex.dn)):
        ex.got(iq[k], gq_ref.at[frm])
    for j in range(1, n):
        ex.got(ih[n - j], gh_ref.at[ex.z(j)])
    for c in (own, mine):
        c.wait()
    ex.close()


def finish(gm, wt, norm, x, gmid, gain, small):
    S, H, U, N = gm.shape
    D = wt.shape[1]
    Q = lax.axis_size("r")
    d = D // (S * H * Q)
    f32, bf16 = jnp.float32, jnp.bfloat16
    return remote_call(
        finish_kernel,
        3,
        [
            jax.ShapeDtypeStruct((S, U, D), bf16),
            jax.ShapeDtypeStruct((H, d, N), f32),
            jax.ShapeDtypeStruct((16, D), f32),
        ],
        [VMEM] * 7,
        [ANY, ANY, VMEM],
        [
            pltpu.VMEM((S, H, U, D), bf16),
            pltpu.VMEM((S, 2, U, D), bf16),
            pltpu.VMEM((S, U, D), bf16),
            pltpu.VMEM((S, U, D), bf16),
            pltpu.VMEM((S, H, Q, d, N), bf16),
            pltpu.VMEM((S, H, d, N), bf16),
            pltpu.VMEM((S, H, d, N), bf16),
            pltpu.VMEM((H, d, N), f32),
            pltpu.VMEM((10, 16, D), f32),
        ],
        8 * S + 3,
        "finish",
    )(gm, wt, norm, x, gmid, gain, small)


def planes(
    hidden_in,
    block_pairs,
    ln1_gain,
    ln1_bias,
    qkv_weight,
    query_bias,
    value_bias,
    out_weight,
    out_bias,
    ln2_gain,
    ln2_bias,
    fc_weight,
    fc_bias,
    proj_weight,
    proj_bias,
    out_grad,
):
    f32, bf16 = jnp.float32, jnp.bfloat16
    s, h, r = (lax.axis_index(a) for a in AXES)
    S, H, Q = (lax.axis_size(a) for a in AXES)
    rows, D = hidden_in.shape
    U = rows // SEQS
    W = D // H
    bfn = fc_bias.shape[0]
    d = qkv_weight.shape[0]
    lines = [ln1_gain, ln1_bias, query_bias, value_bias, out_bias, ln2_gain, ln2_bias, proj_bias]
    lines = jnp.concatenate([jnp.stack(lines), fc_bias.reshape(-1, d)]).T
    lines = jnp.pad(lines, ((0, 0), (0, 128 - lines.shape[1])))
    normed, q_all, kv_all, w_t, vecs, x_own = front(hidden_in.reshape(S, U, D), qkv_weight, lines)
    g1, b1, _, _, bo, g2, b2, bp = (vecs[i] for i in range(8))
    bf = vecs[8 : 8 + bfn // d].reshape(-1, S * H * Q, d).swapaxes(0, 1).reshape(-1)
    pad8 = lambda y: jnp.concatenate([y, jnp.zeros((8, y.shape[1]), y.dtype)])

    blk = block_pairs[::2]
    blk = jnp.where(s % 2 == 0, blk, blk.shape[0] - 1 - blk)
    blk = blk.astype(jnp.int32)
    npair = blk.shape[0]
    inv = jnp.sum(
        jnp.where(blk[None, :] == jnp.arange(npair)[:, None], jnp.arange(npair)[None, :], 0), axis=1
    ).astype(jnp.int32)

    q_all = q_all.reshape(npair, U, W)
    kv_all = kv_all.reshape(npair, 2 * U, 2 * W)
    att, att_low, lse, w_fc, w_out, w_proj = attend(
        inv, blk, q_all, kv_all, fc_weight, pad8(out_weight), proj_weight
    )
    layer_out, grad_middle, small, g_att, grad_fc, grad_proj, grad_wout = middle(
        att_low.reshape(S, H, U, W),
        x_own.reshape(rows, D),
        out_grad.reshape(S, U, D),
        vecs,
        jnp.broadcast_to(bf[None], (8, bf.shape[0])),
        w_fc,
        w_proj,
        w_out,
    )
    grad_mixed, layer_out, gfc, gproj, gout = attend_back(
        inv,
        blk,
        q_all,
        kv_all,
        g_att.reshape(npair, U, W),
        att,
        lse,
        layer_out.reshape(S, U, D),
        grad_fc,
        grad_proj,
        grad_wout,
    )
    grad_hidden, gq, vec = finish(
        grad_mixed.reshape(S, H, U, 3 * W),
        w_t,
        normed,
        x_own,
        grad_middle.reshape(S, U, D),
        jnp.broadcast_to(g1[None], (8, D)),
        small,
    )
    gq = gq.reshape(H, d, 3, W).transpose(1, 2, 0, 3).reshape(d, 3 * D)
    index = (s * H + h) * Q + r
    pick = lambda v: lax.dynamic_slice_in_dim(v, index * d, d)
    return (
        layer_out.reshape(rows, D),
        grad_hidden.reshape(rows, D),
        pick((vec[0] - b1 * vec[1]) / g1),
        pick(vec[1]),
        gq,
        pick(vec[2]),
        pick(vec[3]),
        gout[:d],
        pick(vec[8]),
        pick(vec[9]),
        pick(vec[10]),
        gfc,
        lax.dynamic_slice_in_dim(vec[12:].reshape(-1), index * bfn, bfn),
        gproj,
        pick(vec[11]),
    )


def solution(mesh):
    n = mesh.shape["ctx"]
    if n // (PLANES * SEQS) != 2:
        return solution_any(mesh)
    split = Mesh(mesh.devices.reshape(PLANES, SEQS, -1), AXES)
    row, vec = P(AXES, None), P(AXES)
    return jax.shard_map(
        planes,
        mesh=split,
        in_specs=(row, P(), vec, vec, row, vec, vec, row, vec, vec, vec, row, vec, row, vec, row),
        out_specs=(row, row, vec, vec, row, vec, vec, row, vec, vec, vec, row, vec, row, vec),
        check_vma=False,
    )
```

```python
from functools import partial
import math

import jax
import jax.numpy as jnp
from jax import lax
from jax.sharding import PartitionSpec as P
from jax.experimental import pallas as pl
from jax.experimental.pallas import tpu as pltpu
from jax.sharding import Mesh

HEADS = 12
SEQS = 4


NEG = -1e30


def from_partner(value, axis, bit):
    return lax.ppermute(value, axis, [(i, i ^ 1 << bit) for i in range(lax.axis_size(axis))])


def layer_norm(values, gain, bias):
    center = values - jnp.mean(values, axis=-1, keepdims=True)
    spread_sq = jnp.mean(center * center, axis=-1, keepdims=True)
    return center * lax.rsqrt(spread_sq + 1e-05) * gain + bias


def gelu_tanh(values):
    return jax.nn.gelu(values, approximate=True)


def heads_of(tensor, head_count):
    return tensor.reshape(tensor.shape[:-1] + (head_count, tensor.shape[-1] // head_count))


def pick_own(owned, chosen):
    selector = chosen.reshape((1, -1) + (1,) * (owned.ndim - 2))
    return jnp.where(selector, owned[:, 0:1], owned[:, 1:2])


def pick_piece(piece, chosen):
    selector = chosen.reshape((1, -1) + (1,) * (piece.ndim - 3))
    return jnp.where(selector, piece[:, 0], piece[:, 1])


def parity_masks(chosen, usable):
    return jnp.stack([chosen & usable, jnp.logical_not(chosen) & usable])


def spread(values, parity):
    shaped = parity.reshape((1,) + parity.shape + (1,) * (values.ndim - 2))
    return jnp.sum(jnp.where(shaped, values[:, None], 0.0), axis=2)


def group_loop(pieces, unit_rows, table, stepper, carried):
    piece_rows = pieces[0].shape[2]
    group_size = min(unit_rows, piece_rows)
    group_count = piece_rows // group_size
    batch_groups = math.gcd(group_count, max(1, 1024 // group_size))
    turn_count = group_count // batch_groups
    shaped = tuple(
        (
            item.reshape(item.shape[:2] + (group_count, group_size) + item.shape[3:])
            for item in pieces
        )
    )
    device_ids = jnp.arange(group_count, dtype=jnp.int32) * group_size // unit_rows
    table_size = table.shape[0]
    blocks = jnp.sum(
        jnp.where(
            device_ids[:, None] == jnp.arange(table_size, dtype=jnp.int32)[None, :],
            table[None, :],
            0,
        ),
        axis=1,
    )

    def one_turn(position, current):
        pieces_now = tuple(
            (
                lax.dynamic_slice_in_dim(item, position * batch_groups, batch_groups, 2)
                for item in shaped
            )
        )
        chosen = lax.dynamic_slice_in_dim(blocks, position * batch_groups, batch_groups, 0)
        return stepper(current, pieces_now, chosen)

    return lax.fori_loop(0, turn_count, one_turn, carried)


def attend_step(q_heads, my_block, score_scale, head_count, carried, pieces_now, chosen):
    key_piece = heads_of(pieces_now[0], head_count)
    value_piece = heads_of(pieces_now[1], head_count)
    earlier = chosen < my_block
    usable = chosen != my_block
    parity = parity_masks(earlier, usable)
    query_sel = pick_own(q_heads, earlier)
    key_sel = pick_piece(key_piece, earlier)
    value_sel = pick_piece(value_piece, earlier)
    scores = (
        jnp.einsum("jgqhe,jgkhe->jghqk", query_sel, key_sel, preferred_element_type=jnp.float32)
        * score_scale
    )
    usable_mask = usable.reshape(1, -1, 1, 1, 1)
    scores = jnp.where(usable_mask, scores, NEG)
    old_max, old_total, old_sum = carried
    group_max = jnp.max(scores, axis=-1)
    candidate = jnp.max(jnp.where(parity.reshape(1, 2, -1, 1, 1), group_max[:, None], NEG), axis=2)
    new_max = jnp.maximum(old_max, candidate)
    max_sel = pick_own(new_max, earlier)
    weights_exp = jnp.where(usable_mask, jnp.exp(scores - max_sel[..., None]), 0.0)
    moved = jnp.einsum(
        "jghqk,jgkhe->jgqhe",
        weights_exp.astype(jnp.bfloat16),
        value_sel,
        preferred_element_type=jnp.float32,
    )
    factor = jnp.exp(old_max - new_max)
    new_total = old_total * factor + spread(jnp.sum(weights_exp, axis=-1), parity)
    new_sum = old_sum * jnp.swapaxes(factor, 2, 3)[..., None] + spread(moved, parity)
    return (new_max, new_total, new_sum)


def query_grad_step(
    q_heads,
    grad_heads,
    lse_heads,
    delta_heads,
    my_block,
    score_scale,
    head_count,
    carried,
    pieces_now,
    chosen,
):
    key_piece = heads_of(pieces_now[0], head_count)
    value_piece = heads_of(pieces_now[1], head_count)
    earlier = chosen < my_block
    usable = chosen != my_block
    parity = parity_masks(earlier, usable)
    query_sel = pick_own(q_heads, earlier)
    grad_sel = pick_own(grad_heads, earlier)
    lse_sel = pick_own(lse_heads, earlier)
    delta_sel = pick_own(delta_heads, earlier)
    key_sel = pick_piece(key_piece, earlier)
    value_sel = pick_piece(value_piece, earlier)
    scores = (
        jnp.einsum("jgqhe,jgkhe->jghqk", query_sel, key_sel, preferred_element_type=jnp.float32)
        * score_scale
    )
    usable_mask = usable.reshape(1, -1, 1, 1, 1)
    probabilities = jnp.where(usable_mask, jnp.exp(scores - lse_sel[..., None]), 0.0)
    grad_probs = jnp.einsum(
        "jgqhe,jgkhe->jghqk", grad_sel, value_sel, preferred_element_type=jnp.float32
    )
    grad_scores = (probabilities * (grad_probs - delta_sel[..., None])).astype(jnp.bfloat16)
    term = (
        jnp.einsum("jghqk,jgkhe->jgqhe", grad_scores, key_sel, preferred_element_type=jnp.float32)
        * score_scale
    )
    return carried + spread(term, parity)


def key_grad_step(k_heads, v_heads, my_block, score_scale, head_count, carried, pieces_now, chosen):
    query_piece = heads_of(pieces_now[0], head_count)
    grad_piece = heads_of(pieces_now[1], head_count)
    later = my_block < chosen
    usable = chosen != my_block
    parity = parity_masks(later, usable)
    query_sel = pick_piece(query_piece, later)
    grad_sel = pick_piece(grad_piece, later)
    lse_sel = jnp.swapaxes(pick_piece(pieces_now[2], later), 2, 3)
    delta_sel = jnp.swapaxes(pick_piece(pieces_now[3], later), 2, 3)
    key_sel = pick_own(k_heads, later)
    value_sel = pick_own(v_heads, later)
    scores = (
        jnp.einsum("jgqhe,jgkhe->jghqk", query_sel, key_sel, preferred_element_type=jnp.float32)
        * score_scale
    )
    usable_mask = usable.reshape(1, -1, 1, 1, 1)
    probabilities = jnp.where(usable_mask, jnp.exp(scores - lse_sel[..., None]), 0.0)
    grad_probs = jnp.einsum(
        "jgqhe,jgkhe->jghqk", grad_sel, value_sel, preferred_element_type=jnp.float32
    )
    grad_scores = (probabilities * (grad_probs - delta_sel[..., None])).astype(jnp.bfloat16)
    key_term = (
        jnp.einsum("jghqk,jgqhe->jgkhe", grad_scores, query_sel, preferred_element_type=jnp.float32)
        * score_scale
    )
    value_term = jnp.einsum(
        "jghqk,jgqhe->jgkhe",
        probabilities.astype(jnp.bfloat16),
        grad_sel,
        preferred_element_type=jnp.float32,
    )
    return (carried[0] + spread(key_term, parity), carried[1] + spread(value_term, parity))


def shards(
    hidden_in,
    block_pairs,
    ln1_gain,
    ln1_bias,
    qkv_weight,
    query_bias,
    value_bias,
    out_weight,
    out_bias,
    ln2_gain,
    ln2_bias,
    fc_weight,
    fc_bias,
    proj_weight,
    proj_bias,
    out_grad,
):
    params = (
        ln1_gain,
        ln1_bias,
        qkv_weight,
        query_bias,
        value_bias,
        out_weight,
        out_bias,
        ln2_gain,
        ln2_bias,
        fc_weight,
        fc_bias,
        proj_weight,
        proj_bias,
    )
    gathered = (
        lax.all_gather(params[0], "ctx", axis=0, tiled=True),
        lax.all_gather(params[1], "ctx", axis=0, tiled=True),
        lax.all_gather(params[2], "ctx", axis=0, tiled=True),
        lax.all_gather(params[3], "ctx", axis=0, tiled=True),
        lax.all_gather(params[4], "ctx", axis=0, tiled=True),
        lax.all_gather(params[5], "ctx", axis=0, tiled=True),
        lax.all_gather(params[6], "ctx", axis=0, tiled=True),
        lax.all_gather(params[7], "ctx", axis=0, tiled=True),
        lax.all_gather(params[8], "ctx", axis=0, tiled=True),
        lax.all_gather(params[9], "ctx", axis=0, tiled=True),
        lax.all_gather(params[10], "ctx", axis=0, tiled=True),
        lax.all_gather(params[11], "ctx", axis=0, tiled=True),
        lax.all_gather(params[12], "ctx", axis=0, tiled=True),
    )
    (
        gain_one,
        bias_one,
        w_qkv,
        b_query,
        b_value,
        w_out,
        b_out,
        gain_two,
        bias_two,
        w_fc,
        b_fc,
        w_proj,
        b_proj,
    ) = gathered
    device = lax.axis_index("ctx")
    partner = device + 1 - 2 * (device % 2)
    row_count = hidden_in.shape[0]
    model_width = hidden_in.shape[1]
    unit_rows = row_count // SEQS
    halves = SEQS // 2
    head_count = HEADS
    head_size = model_width // head_count
    score_scale = 1.0 / math.sqrt(head_size)
    my_block = block_pairs[device]
    seq_shape = (halves, 2, unit_rows, model_width)
    head_shape = (halves, 2, unit_rows, head_count, head_size)
    inputs = hidden_in.astype(jnp.float32)
    normed = layer_norm(inputs, gain_one.astype(jnp.float32), bias_one.astype(jnp.float32)).astype(
        jnp.bfloat16
    )
    mixed_proj = jnp.dot(normed, w_qkv, preferred_element_type=jnp.float32)
    queries = (mixed_proj[:, :model_width] + b_query.astype(jnp.float32)).astype(jnp.bfloat16)
    key_rows = mixed_proj[:, model_width : 2 * model_width].astype(jnp.bfloat16)
    value_rows = (mixed_proj[:, 2 * model_width :] + b_value.astype(jnp.float32)).astype(
        jnp.bfloat16
    )
    q_seq = queries.reshape(seq_shape)
    k_seq = key_rows.reshape(seq_shape)
    v_seq = value_rows.reshape(seq_shape)
    q_heads = queries.reshape(head_shape)
    k_heads = key_rows.reshape(head_shape)
    v_heads = value_rows.reshape(head_shape)
    far_keys, far_values = from_partner((k_seq, v_seq), "ctx", 0)
    near_keys = jnp.concatenate([k_heads, heads_of(far_keys, head_count)], axis=2)
    near_values = jnp.concatenate([v_heads, heads_of(far_values, head_count)], axis=2)
    scores = (
        jnp.einsum("jpqhe,jpkhe->jphqk", q_heads, near_keys, preferred_element_type=jnp.float32)
        * score_scale
    )
    row_max = jnp.max(scores, axis=-1)
    weights_exp = jnp.exp(scores - row_max[..., None])
    row_total = jnp.sum(weights_exp, axis=-1)
    summed = jnp.einsum(
        "jphqk,jpkhe->jpqhe",
        weights_exp.astype(jnp.bfloat16),
        near_values,
        preferred_element_type=jnp.float32,
    )
    forward_stepper = partial(attend_step, q_heads, my_block, score_scale, head_count)
    row_max, row_total, summed = group_loop(
        (
            lax.all_gather(k_seq, "ctx", axis=2, tiled=True),
            lax.all_gather(v_seq, "ctx", axis=2, tiled=True),
        ),
        unit_rows,
        block_pairs,
        forward_stepper,
        (row_max, row_total, summed),
    )
    attended = summed / jnp.swapaxes(row_total, 2, 3)[..., None]
    log_total = row_max + jnp.log(row_total)
    att_low = attended.reshape(row_count, model_width).astype(jnp.bfloat16)
    branch = jnp.dot(att_low, w_out, preferred_element_type=jnp.float32) + b_out.astype(jnp.float32)
    middle = inputs + branch
    normed_two = layer_norm(
        middle, gain_two.astype(jnp.float32), bias_two.astype(jnp.float32)
    ).astype(jnp.bfloat16)
    pre_act = jnp.dot(normed_two, w_fc, preferred_element_type=jnp.float32) + b_fc.astype(
        jnp.float32
    )
    activation = gelu_tanh(pre_act).astype(jnp.bfloat16)
    result = (
        middle
        + jnp.dot(activation, w_proj, preferred_element_type=jnp.float32)
        + b_proj.astype(jnp.float32)
    )
    layer_out = result.astype(jnp.bfloat16)
    grad_out = out_grad.astype(jnp.float32)
    grad_proj = jnp.dot(activation.T, out_grad, preferred_element_type=jnp.float32)
    grad_bproj = jnp.sum(grad_out, axis=0)
    grad_activ = jnp.dot(out_grad, w_proj.T, preferred_element_type=jnp.float32)
    _, gelu_back = jax.vjp(gelu_tanh, pre_act)
    grad_pre = gelu_back(grad_activ)[0].astype(jnp.bfloat16)
    grad_fc = jnp.dot(normed_two.T, grad_pre, preferred_element_type=jnp.float32)
    grad_bfc = jnp.sum(grad_pre.astype(jnp.float32), axis=0)
    grad_normed_two = jnp.dot(grad_pre, w_fc.T, preferred_element_type=jnp.float32)
    _, norm_back_two = jax.vjp(
        layer_norm, middle, gain_two.astype(jnp.float32), bias_two.astype(jnp.float32)
    )
    grad_middle, grad_gain_two, grad_bias_two = norm_back_two(grad_normed_two)
    grad_middle = grad_middle + grad_out
    grad_branch = grad_middle.astype(jnp.bfloat16)
    grad_wout = jnp.dot(att_low.T, grad_branch, preferred_element_type=jnp.float32)
    grad_bout = jnp.sum(grad_branch.astype(jnp.float32), axis=0)
    grad_att = jnp.dot(grad_branch, w_out.T, preferred_element_type=jnp.float32).astype(
        jnp.bfloat16
    )
    grad_seq = grad_att.reshape(seq_shape)
    grad_heads = grad_att.reshape(head_shape)
    row_delta = jnp.sum(grad_heads.astype(jnp.float32) * attended, axis=-1)
    delta_heads = jnp.swapaxes(row_delta, 2, 3)
    all_lse, all_delta = (
        lax.all_gather(jnp.swapaxes(log_total, 2, 3), "ctx", axis=2, tiled=True),
        lax.all_gather(row_delta, "ctx", axis=2, tiled=True),
    )
    partner_lse = jnp.swapaxes(
        lax.dynamic_slice_in_dim(all_lse, partner * unit_rows, unit_rows, 2), 2, 3
    )
    partner_delta = jnp.swapaxes(
        lax.dynamic_slice_in_dim(all_delta, partner * unit_rows, unit_rows, 2), 2, 3
    )
    far_queries, far_grads = from_partner((q_seq, grad_seq), "ctx", 0)
    near_queries = jnp.concatenate([q_heads, heads_of(far_queries, head_count)], axis=2)
    near_grads = jnp.concatenate([grad_heads, heads_of(far_grads, head_count)], axis=2)
    near_lse = jnp.concatenate([log_total, partner_lse], axis=3)
    near_delta = jnp.concatenate([delta_heads, partner_delta], axis=3)
    local_scores = (
        jnp.einsum(
            "jpqhe,jpkhe->jphqk", near_queries, near_keys, preferred_element_type=jnp.float32
        )
        * score_scale
    )
    probabilities = jnp.exp(local_scores - near_lse[..., None])
    grad_probs = jnp.einsum(
        "jpqhe,jpkhe->jphqk", near_grads, near_values, preferred_element_type=jnp.float32
    )
    grad_scores = (probabilities * (grad_probs - near_delta[..., None])).astype(jnp.bfloat16)
    grad_q_local = (
        jnp.einsum(
            "jphqk,jpkhe->jpqhe",
            grad_scores[:, :, :, :unit_rows, :],
            near_keys,
            preferred_element_type=jnp.float32,
        )
        * score_scale
    )
    grad_k_local = (
        jnp.einsum(
            "jphqk,jpqhe->jpkhe",
            grad_scores[..., :unit_rows],
            near_queries,
            preferred_element_type=jnp.float32,
        )
        * score_scale
    )
    grad_v_local = jnp.einsum(
        "jphqk,jpqhe->jpkhe",
        probabilities.astype(jnp.bfloat16)[..., :unit_rows],
        near_grads,
        preferred_element_type=jnp.float32,
    )
    query_stepper = partial(
        query_grad_step,
        q_heads,
        grad_heads,
        log_total,
        delta_heads,
        my_block,
        score_scale,
        head_count,
    )
    key_stepper = partial(key_grad_step, k_heads, v_heads, my_block, score_scale, head_count)

    def query_piece(carried, pieces, offset):
        return group_loop(pieces, unit_rows, block_pairs, query_stepper, carried)

    def key_piece(carried, pieces, offset):
        return group_loop(
            (pieces[0], pieces[1], all_lse, all_delta), unit_rows, block_pairs, key_stepper, carried
        )

    grad_q_all = query_piece(
        grad_q_local,
        (
            lax.all_gather(k_seq, "ctx", axis=2, tiled=True),
            lax.all_gather(v_seq, "ctx", axis=2, tiled=True),
        ),
        jnp.int32(0),
    )
    grad_k_all, grad_v_all = key_piece(
        (grad_k_local, grad_v_local),
        (
            lax.all_gather(q_seq, "ctx", axis=2, tiled=True),
            lax.all_gather(grad_seq, "ctx", axis=2, tiled=True),
        ),
        jnp.int32(0),
    )
    grad_queries = grad_q_all.reshape(row_count, model_width).astype(jnp.bfloat16)
    grad_keys = grad_k_all.reshape(row_count, model_width).astype(jnp.bfloat16)
    grad_values = grad_v_all.reshape(row_count, model_width).astype(jnp.bfloat16)
    grad_mixed = jnp.concatenate([grad_queries, grad_keys, grad_values], axis=1)
    grad_qkv = jnp.dot(normed.T, grad_mixed, preferred_element_type=jnp.float32)
    grad_bquery = jnp.sum(grad_queries.astype(jnp.float32), axis=0)
    grad_bvalue = jnp.sum(grad_values.astype(jnp.float32), axis=0)
    grad_normed = jnp.dot(grad_mixed, w_qkv.T, preferred_element_type=jnp.float32)
    _, norm_back_one = jax.vjp(
        layer_norm, inputs, gain_one.astype(jnp.float32), bias_one.astype(jnp.float32)
    )
    grad_inputs, grad_gain_one, grad_bias_one = norm_back_one(grad_normed)
    grad_hidden = (grad_inputs + grad_middle).astype(jnp.bfloat16)
    totals = (
        lax.psum_scatter(grad_gain_one, "ctx", scatter_dimension=0, tiled=True),
        lax.psum_scatter(grad_bias_one, "ctx", scatter_dimension=0, tiled=True),
        lax.psum_scatter(grad_qkv, "ctx", scatter_dimension=0, tiled=True),
        lax.psum_scatter(grad_bquery, "ctx", scatter_dimension=0, tiled=True),
        lax.psum_scatter(grad_bvalue, "ctx", scatter_dimension=0, tiled=True),
        lax.psum_scatter(grad_wout, "ctx", scatter_dimension=0, tiled=True),
        lax.psum_scatter(grad_bout, "ctx", scatter_dimension=0, tiled=True),
        lax.psum_scatter(grad_gain_two, "ctx", scatter_dimension=0, tiled=True),
        lax.psum_scatter(grad_bias_two, "ctx", scatter_dimension=0, tiled=True),
        lax.psum_scatter(grad_fc, "ctx", scatter_dimension=0, tiled=True),
        lax.psum_scatter(grad_bfc, "ctx", scatter_dimension=0, tiled=True),
        lax.psum_scatter(grad_proj, "ctx", scatter_dimension=0, tiled=True),
        lax.psum_scatter(grad_bproj, "ctx", scatter_dimension=0, tiled=True),
    )
    return (
        layer_out,
        grad_hidden,
        totals[0],
        totals[1],
        totals[2],
        totals[3],
        totals[4],
        totals[5],
        totals[6],
        totals[7],
        totals[8],
        totals[9],
        totals[10],
        totals[11],
        totals[12],
    )


def solution_any(mesh):
    return jax.shard_map(
        shards,
        mesh=mesh,
        in_specs=(
            P("ctx", None),
            P(),
            P("ctx"),
            P("ctx"),
            P("ctx", None),
            P("ctx"),
            P("ctx"),
            P("ctx", None),
            P("ctx"),
            P("ctx"),
            P("ctx"),
            P("ctx", None),
            P("ctx"),
            P("ctx", None),
            P("ctx"),
            P("ctx", None),
        ),
        out_specs=(
            P("ctx", None),
            P("ctx", None),
            P("ctx"),
            P("ctx"),
            P("ctx", None),
            P("ctx"),
            P("ctx"),
            P("ctx", None),
            P("ctx"),
            P("ctx"),
            P("ctx"),
            P("ctx", None),
            P("ctx"),
            P("ctx", None),
            P("ctx"),
        ),
        check_vma=False,
    )


AXES = ("s", "h", "r")
PLANES = 4


MESH_IDS = pl.DeviceIdType.MESH


class At:
    def __init__(self, ref, *index):
        self.ref, self.index = ref, index

    def now(self):
        return self.ref.at[self.index]

    def still(self):
        return self.ref.at[tuple(i if isinstance(i, slice) else 0 for i in self.index)]


ALL = slice(None)


class Exchange:
    def __init__(self, send, recv):
        self.send, self.recv, self.used, self.open = send, recv, 0, []
        self.s, self.h, self.r = (lax.axis_index(a) for a in AXES)
        self.planes = lax.axis_size("s")
        self.xn = self.h + 1 - 2 * lax.rem(self.h, 2)
        self.yn = lax.rem(self.h + 2, 4)
        self.dn = lax.rem(self.xn + 2, 4)
        self.z = lambda j: lax.rem(self.s + j, self.planes)
        self.X, self.Y, self.D = ({"h": i} for i in (self.xn, self.yn, self.dn))
        self.C = {"r": 1 - self.r}
        self.Z = [None] + [{"s": self.z(j)} for j in range(1, self.planes)]

    def greet(self, peers, meanwhile=None):
        barrier = pltpu.get_barrier_semaphore()
        for peer in peers:
            pl.semaphore_signal(barrier, inc=1, device_id=peer, device_id_type=MESH_IDS)
        if meanwhile:
            meanwhile()
        pl.semaphore_wait(barrier, len(peers))

    def slots(self, count):
        self.used += count
        return range(self.used - count, self.used)

    def copy(self, i, src, dst, peer):
        return pltpu.make_async_remote_copy(
            src_ref=src,
            dst_ref=dst,
            send_sem=self.send.at[i],
            recv_sem=self.recv.at[i],
            device_id=peer,
            device_id_type=MESH_IDS,
        )

    def put(self, i, src, dst, peer):
        self.copy(i, src.now() if isinstance(src, At) else src, dst, peer).start()
        self.open.append((i, src))

    def got(self, i, dst):
        self.copy(i, dst, dst, self.X).wait_recv()

    def close(self):
        for i, src in self.open:
            src = src.still() if isinstance(src, At) else src
            self.copy(i, src, src, self.X).wait_send()


def remote_call(kernel, cid, out_shape, in_specs, out_specs, scratch, sems, name, vmem=56 << 20):
    return pl.pallas_call(
        kernel,
        out_shape=out_shape,
        in_specs=in_specs,
        out_specs=out_specs,
        scratch_shapes=scratch
        + [pltpu.SemaphoreType.DMA((sems,)), pltpu.SemaphoreType.DMA((sems,)), pltpu.SemaphoreType.DMA((8,))],
        compiler_params=pltpu.CompilerParams(
            collective_id=cid, has_side_effects=True, vmem_limit_bytes=vmem
        ),
        name=name,
    )


ANY = pl.BlockSpec(memory_space=pl.ANY)
VMEM = pl.BlockSpec(memory_space=pltpu.VMEM)


def by_x(k, j):
    return (k + j) % 2 == 0


def act(plan, steps, m, c, last_tile):
    for (em, ec), todo in plan.items():
        if (em == ec) == last_tile:

            @pl.when(m == em if last_tile else (m == em) & (c == ec))
            def _():
                for step, k, *js in todo:
                    steps[step](k, js)


def gather_steps(ex, ins, outs, local):
    s, h, r, n = ex.s, ex.h, ex.r, ex.planes
    part = len(ins) - 1
    place = lambda k, t, c: (t, c) if k == part else (t, c, r)
    slab = lambda k, t, c: outs[k].at[place(k, t, c)]
    own = [pltpu.make_async_copy(ins[k], slab(k, s, h), local.at[k + 1]) for k in range(part + 1)]
    for c in own:
        c.start()
    iz, ix, iy, ir, ic = ([ex.slots(n) for _ in outs] for _ in range(5))

    def cross(k, j):
        ex.put(iz[k][j], ins[k], slab(k, s, h), ex.Z[j])

    def forward(k, j):
        t = ex.z(j)
        if j:
            ex.got(iz[k][n - j], slab(k, t, h))
        src = At(outs[k], *place(k, t, h)) if j else ins[k]
        ex.put(ix[k][j], src, slab(k, t, h), ex.X)
        ex.put(iy[k][j], src, slab(k, t, h), ex.Y)

    def relay(k, j):
        t = ex.z(j)
        slots, frm, peer = (ix, ex.xn, ex.Y) if by_x(k, j) else (iy, ex.yn, ex.X)
        ex.got(slots[k][j], slab(k, t, frm))
        ex.put(ir[k][j], At(outs[k], *place(k, t, frm)), slab(k, t, frm), peer)

    def across(k, j):
        t = ex.z(j)
        slots, frm = (iy, ex.yn) if by_x(k, j) else (ix, ex.xn)
        ex.got(slots[k][j], slab(k, t, frm))
        ex.got(ir[k][j], slab(k, t, ex.dn))
        if not j:
            own[k].wait()
        ex.put(ic[k][j], At(outs[k], t, ALL, r), outs[k].at[t, :, r], ex.C)

    def last():
        for j in range(n):
            for k in range(part):
                ex.got(ic[k][j], outs[k].at[ex.z(j), :, 1 - r])
            ex.got(ix[part][j], slab(part, ex.z(j), ex.xn))
            ex.got(iy[part][j], slab(part, ex.z(j), ex.yn))
        own[part].wait()

    each = lambda step: lambda k, js: [step(k, j) for j in js]
    return dict(cross=each(cross), forward=each(forward), relay=each(relay), across=each(across)), last


def by_tile(shape, step):
    height, width = shape
    if height % 16:

        @pl.loop(0, width // 768)
        def _(i):
            step(slice(None), pl.ds(pl.multiple_of(i * 768, 768), 768))
    else:

        @pl.loop(0, height // 32)
        def _(i):
            step(pl.ds(pl.multiple_of(i * 32, 32), 32), slice(None))


def reduce_steps(ins, outs, bufs, send, recv, local):
    count = len(ins)
    mine, from_c, one, two, from_z = (bufs[i * count : (i + 1) * count] for i in range(5))
    ex = Exchange(send, recv)
    s, h, r, n = ex.s, ex.h, ex.r, ex.planes
    own = [
        pltpu.make_async_copy(a.at[:, :, r], m, local.at[k]) for k, (a, m) in enumerate(zip(ins, mine))
    ]
    for c in own:
        c.start()
    ex.greet([ex.X, ex.Y, ex.C] + ex.Z[1:])
    ic, i1, i2, iz = ([ex.slots(n) for _ in ins] for _ in range(4))
    i1b = [ex.slots(n) for _ in ins]
    for k in (1, 0, 2):
        for j in range(n):
            ex.put(ic[k][j], At(ins[k], ex.z(j), ALL, 1 - r), from_c[k].at[ex.z(j)], ex.C)
    for c in own:
        c.wait()

    def add(to, *parts):
        def step(rows, cols):
            total = to[rows, cols].astype(jnp.float32)
            for part in parts:
                total += part[rows, cols].astype(jnp.float32)
            to[rows, cols] = total.astype(to.dtype)

        by_tile(to.shape, step)

    def way(k, j):
        return (ex.X, ex.xn, ex.Y, ex.yn) if by_x(k, j) else (ex.Y, ex.yn, ex.X, ex.xn)

    def first(k, js):
        m = mine[k]
        for j in js:
            t = ex.z(j)
            ex.got(ic[k][j], from_c[k].at[t])
            add(m.at[t, ex.dn], from_c[k].at[t, ex.dn])
            ex.put(i1b[k][j], At(m, t, ex.dn), one[k].at[j, 1], way(k, j)[0])
        for j in js:
            t, (peer, near, _, other) = ex.z(j), way(k, j)
            add(m.at[t, near], from_c[k].at[t, near])
            ex.put(i1[k][j], At(m, t, near), one[k].at[j, 0], peer)
        for j in js:
            t, other = ex.z(j), way(k, j)[3]
            add(m.at[t, other], from_c[k].at[t, other])
            add(m.at[t, h], from_c[k].at[t, h])

    def second(k, js):
        m = mine[k]
        for j in js:
            t, (_, _, peer, other) = ex.z(j), way(k, j)
            ex.got(i1b[k][j], one[k].at[j, 1])
            add(m.at[t, other], one[k].at[j, 1])
            ex.put(i2[k][j], At(m, t, other), two[k].at[j], peer)

    def third(k, js):
        m = mine[k]
        for j in js:
            t = ex.z(j)
            ex.got(i1[k][j], one[k].at[j, 0])
            ex.got(i2[k][j], two[k].at[j])
            add(m.at[t, h], one[k].at[j, 0], two[k].at[j])
            if j:
                ex.put(iz[k][j], At(m, t, h), from_z[k].at[j], ex.Z[j])

    def last():
        for k, (m, o) in enumerate(zip(mine, outs)):
            for j in range(1, n):
                ex.got(iz[k][j], from_z[k].at[j])

            def step(rows, cols):
                total = m[s, h, rows, cols].astype(jnp.float32)
                for j in range(1, n):
                    total += from_z[k][j, rows, cols].astype(jnp.float32)
                o[rows, cols] = total

            by_tile(o.shape, step)

        ex.close()

    return ex, dict(first=first, second=second, third=third), last


HD = 64


GATHER_PLAN = {
    (0, 0): [("forward", 0, 1, 3, 2), ("relay", 1, 1, 3, 2)],
    (4, 2): [("relay", 0, 1, 3, 2), ("across", 1, 0, 1, 3, 2)],
    (5, 1): [("forward", 2, 1, 3, 2)],
    (6, 1): [("across", 0, 0, 1, 3, 2)],
}
GATHER_FIRST = [("forward", 1, 1, 3, 2), ("relay", 1, 0), ("relay", 0, 0), ("cross", 2, 1, 3, 2), ("forward", 2, 0)]
GATHER_START = [("cross", 1, 1, 3, 2), ("cross", 0, 1, 3, 2), ("forward", 1, 0), ("forward", 0, 0)]


SMEM = pl.BlockSpec(memory_space=pltpu.SMEM)


def forward_kernel(vectors, inv, blk, x_ref, w_ref, *refs):
    count = 3
    v_refs, refs = refs[:vectors], refs[vectors:]
    ins, refs = refs[:count], refs[count:]
    norm_ref, q_ref, kv_ref, w_out, vec_ref, xo_ref, o_ref, low_ref, lse_ref = refs[:9]
    outs = refs[9 : 9 + count]
    xa, ws, wa, wf, qt, ks, vt, os, sc, send, recv, local = refs[9 + count :]
    f32, bf16 = jnp.float32, jnp.bfloat16
    ex = Exchange(send, recv)
    s, h, r, n = ex.s, ex.h, ex.r, ex.planes
    H, U, D = xa.shape[1:]
    d, N = w_ref.shape
    W = N // 3 // H
    own = pltpu.make_async_copy(x_ref.at[s], xa.at[s, h], local.at[0])
    own.start()

    def slabs():
        lines = [v[...].astype(f32) for v in v_refs]
        lines = [v[:, i : i + d] for v in lines for i in range(0, v.shape[1], d)]
        lines = jnp.concatenate(lines + [jnp.zeros((64 - len(lines), d), f32)], axis=0).T.astype(bf16)
        for k in range(H):
            ws[k] = jnp.concatenate(
                [w_ref[:, c * D + k * W : c * D + (k + 1) * W] for c in range(3)] + [lines], axis=1
            )

    ex.greet([ex.X, ex.Y, ex.D, ex.C] + ex.Z[1:], slabs)
    iw, ix, iy, ir, iz, iwz, iwc, ik = (ex.slots(n) for _ in range(8))
    steps, last = gather_steps(ex, ins, outs, local)
    cross = lambda j: ex.put(iz[j], x_ref.at[ex.z(j)], xa.at[s, h], ex.Z[j])
    cross(1)
    for k, (peer, to) in enumerate(((ex.X, ex.xn), (ex.Y, ex.yn), (ex.D, ex.dn))):
        ex.put(iw[k], ws.at[to], wa.at[s, h, r], peer)
    wa[s, h, r] = ws[h]
    own.wait()

    def forward(j):
        t = ex.z(j)
        if j:
            ex.got(iz[n - j], xa.at[t, h])
        if j in after:
            cross(after[j])
        ex.put(ix[j], xa.at[t, h], xa.at[t, h], ex.X)
        ex.put(iy[j], xa.at[t, h], xa.at[t, h], ex.Y)

    def relay(j):
        t = ex.z(j)
        slots, frm, peer = (ix, ex.xn, ex.Y) if by_x(0, j) else (iy, ex.yn, ex.X)
        ex.got(slots[j], xa.at[t, frm])
        ex.put(ir[j], xa.at[t, frm], xa.at[t, frm], peer)

    def weights(j):
        if j:
            ex.got(iwz[n - j], wa.at[ex.z(j), :, r])
        ex.put(iwc[j], wa.at[ex.z(j), :, r], wa.at[ex.z(j), :, r], ex.C)

    after = {3: 3, 1: 2}
    forward(0)
    for k, frm in enumerate((ex.xn, ex.yn, ex.dn)):
        ex.got(iw[k], wa.at[s, frm, r])
    forward(3)
    relay(0)
    forward(1)
    for j in range(1, n):
        ex.put(iwz[j], wa.at[s, :, r], wa.at[s, :, r], ex.Z[j])
    weights(0)
    relay(3)
    relay(1)
    forward(2)
    for j in (1, 3, 2):
        weights(j)
    for step, k, *js in GATHER_START:
        steps[step](k, js)
    for j in range(n):
        ex.got(iwc[j], wa.at[ex.z(j), :, 1 - r])
    rows = H * 2 * d
    for t in range(n):
        block = wa[t].astype(f32).reshape(rows, N // H + 64)
        wf[t * rows : (t + 1) * rows] = block
    vec_ref[...] = wf[:, N // H :].T[:16]
    w = wf[:, : N // H].astype(bf16)
    w_out[...] = w
    gain, bias = vec_ref[0:1], vec_ref[1:2]

    def mine(row):
        picked = jnp.zeros((1, W), f32)
        for k in range(H):
            picked = jnp.where(h == k, vec_ref[row : row + 1, k * W : (k + 1) * W], picked)
        return picked

    bq, bv = mine(2), mine(3)

    def batch(j):
        t = ex.z(j)
        slots, frm = (iy, ex.yn) if by_x(0, j) else (ix, ex.xn)
        ex.got(slots[j], xa.at[t, frm])
        ex.got(ir[j], xa.at[t, ex.dn])
        x = xa[t].reshape(H * U, D).astype(f32)
        normed = layer_norm(x, gain, bias).astype(bf16)
        pairs = pl.ds(t * H, H)
        norm_ref[t] = normed.reshape(H, U, D)
        mixed = jnp.dot(normed, w, preferred_element_type=f32)
        q = (mixed[:, :W] + bq).astype(bf16) * jnp.asarray(0.125, bf16)
        q_ref[pairs] = q.reshape(H, U, W)
        kv = jnp.concatenate([mixed[:, W : 2 * W], mixed[:, 2 * W :] + bv], axis=1).astype(bf16)
        kv_ref[pairs, 0] = kv.reshape(H, U, 2 * W)
        ex.put(ik[j], kv_ref.at[pairs, 0], kv_ref.at[pairs, 1], ex.C)

    relay(2)
    batch(0)
    batch(3)
    batch(1)
    batch(2)
    for step, k, *js in GATHER_FIRST:
        steps[step](k, js)
    xo_ref[...] = xa[:, h]
    for j in (0, 1, 3, 2):
        ex.got(ik[j], kv_ref.at[pl.ds(ex.z(j) * H, H), 1])

    npair = inv.shape[0]
    nh = W // HD
    B = 2 * U
    TQ, TK = 2 * U, 2 * B

    @pl.loop(0, npair, unroll=2)
    def _(i):
        p = inv[i]
        qt[:, pl.ds(pl.multiple_of(i * U, U), U)] = q_ref[p].T
        kv = kv_ref[p].reshape(B, 2 * W)
        for h in range(nh):
            ks[h, pl.ds(i * B, B), :] = kv[:, h * HD : (h + 1) * HD]
        vct = kv[:, W:].T
        for h in range(nh):
            vt[h, 0:HD, pl.ds(pl.multiple_of(i * B, B), B)] = vct[h * HD : (h + 1) * HD]
            vt[h, HD:, pl.ds(pl.multiple_of(i * B, B), B)] = jnp.ones((vt.shape[1] - HD, B), vt.dtype)

    def scores(m, c, carry, masked):
        out = []
        rows = pl.ds(pl.multiple_of(c * TK, TK), TK)
        for h in range(nh):
            qh = qt[h * HD : (h + 1) * HD, pl.ds(pl.multiple_of(m * TQ, TQ), TQ)]
            s = jnp.dot(ks[h, rows, :], qh, preferred_element_type=jnp.float32)
            if masked:
                row = lax.broadcasted_iota(jnp.int32, s.shape, 0)
                col = lax.broadcasted_iota(jnp.int32, s.shape, 1)
                s = jnp.where((row >= B) & (col < U), NEG, s)
            sc[h, rows, :] = s
            out.append(jnp.maximum(carry[h], jnp.max(s.reshape(TK // 8, 8, TQ), axis=0)))
        return tuple(out)

    def values(c, carry, tops):
        out = []
        rows = pl.ds(pl.multiple_of(c * TK, TK), TK)
        for h in range(nh):
            p = jnp.exp(sc[h, rows, :] - tops[h]).astype(jnp.bfloat16)
            out.append(carry[h] + jnp.dot(vt[h, :, rows], p, preferred_element_type=jnp.float32))
        return tuple(out)

    @pl.loop(0, npair // 2)
    def _(m):
        tops = tuple(jnp.full((8, TQ), NEG, jnp.float32) for _ in range(nh))
        tops = lax.fori_loop(0, m, lambda c, x: scores(m, c, x, False), tops)
        tops = [jnp.max(t, axis=0, keepdims=True) for t in scores(m, m, tops, True)]

        def step(c, x):
            x = values(c, x, tops)
            act(GATHER_PLAN, steps, m, c, False)
            return x

        init = tuple(jnp.zeros((vt.shape[1], TQ), jnp.float32) for _ in range(nh))
        carry = values(m, lax.fori_loop(0, m, step, init), tops)
        carry = list(zip(tops, carry))
        rows = []
        for h in range(nh):
            mx, acc = carry[h]
            tot = acc[HD : HD + 1]
            rows.append(acc[:HD] / tot)
            lse_ref[h : h + 1, pl.ds(pl.multiple_of(m * TQ, TQ), TQ)] = mx + jnp.log(tot)
        os[pl.ds(pl.multiple_of(m * TQ, TQ), TQ), :] = jnp.concatenate(rows, axis=0).T
        act(GATHER_PLAN, steps, m, m, True)

    @pl.loop(0, npair)
    def _(p):
        o = os[pl.ds(blk[p] * U, U), :]
        o_ref[pl.ds(pl.multiple_of(p * U, U), U), :] = o
        low_ref[pl.ds(pl.multiple_of(p * U, U), U), :] = o.astype(jnp.bfloat16)

    last()
    ex.close()


def forward(inv, blk, x, w, vectors, *weights):
    S, U, D = x.shape
    d, N = w.shape
    H, Q = (lax.axis_size(a) for a in AXES[1:])
    W = N // 3 // H
    npair = S * H
    R, K = npair * U, npair * Q * U
    nh = W // HD
    f32, bf16 = jnp.float32, jnp.bfloat16
    n = len(weights)
    shape = jax.ShapeDtypeStruct
    return remote_call(
        partial(forward_kernel, len(vectors)),
        0,
        [
            shape((S, H, U, D), bf16),
            shape((npair, U, W), bf16),
            shape((npair, Q, U, 2 * W), bf16),
            shape((D, N // H), bf16),
            shape((16, D), f32),
            shape((S, U, D), bf16),
            shape((R, W), f32),
            shape((R, W), bf16),
            shape((8, R), f32),
        ]
        + [shape((S, H, Q) + a.shape, a.dtype) for a in weights[:-1]]
        + [shape((S, H) + weights[-1].shape, bf16)],
        [SMEM] * 2 + [ANY] + [VMEM] * (1 + len(vectors)) + [ANY] * n,
        [VMEM] * 9 + [ANY] * n,
        [
            pltpu.VMEM((S, H, U, D), bf16),
            pltpu.VMEM((H, d, N // H + 64), bf16),
            pltpu.VMEM((S, H, Q, d, N // H + 64), bf16),
            pltpu.VMEM((D, N // H + 64), f32),
            pltpu.VMEM((W, R), bf16),
            pltpu.VMEM((nh, K, HD), bf16),
            pltpu.VMEM((nh, HD + 16, K), bf16),
            pltpu.VMEM((R, W), f32),
            pltpu.VMEM((nh, K, 2 * U), f32),
        ],
        8 * S + 5 * S * n,
        "forward",
    )(inv, blk, x, w, *vectors, *weights)


REDUCE_PLAN = {
    (7, 0): [("first", 1, 1, 2, 3, 0)],
    (7, 5): [("second", 1, 1, 2, 3, 0)],
    (7, 6): [("first", 0, 1, 2, 3, 0)],
    (5, 2): [("third", 1, 1, 2, 3, 0)],
    (5, 3): [("second", 0, 1, 2, 3, 0)],
    (5, 4): [("first", 2, 1, 2, 3, 0)],
    (3, 0): [("third", 0, 1, 2, 3, 0), ("second", 2, 1, 2, 3, 0)],
    (2, 0): [("third", 2, 1, 2, 3, 0)],
}


def attend_back_kernel(count, inv, blk, q_ref, kv_ref, g_ref, o_ref, lse_ref, out_ref, *refs):
    ins, gm_ref, lo_ref, outs = refs[:count], refs[count], refs[count + 1], refs[count + 2 : 2 * count + 2]
    bufs = refs[2 * count + 2 : 7 * count + 2]
    qt, gt, qx, gx, ks, vs, kt, delta, dkv, dqs, over, back, send, recv, local = refs[7 * count + 2 :]
    npair, U, W = q_ref.shape
    nh = W // HD
    B = kv_ref.shape[1]
    TQ, TK = 2 * U, 2 * B
    f32, bf16 = jnp.float32, jnp.bfloat16
    ex, steps, last = reduce_steps(ins, outs, bufs, send, recv, local)
    swap = ex.slots(npair // 2)
    il = ex.slots(ex.planes)
    keep = pltpu.make_async_copy(out_ref.at[ex.s], lo_ref.at[ex.s], local.at[count])
    keep.start()
    for j in range(1, ex.planes):
        ex.put(il[j], out_ref.at[ex.z(j)], lo_ref.at[ex.s], ex.Z[j])

    @pl.loop(0, npair, unroll=2)
    def _(i):
        p = inv[i]
        qc = q_ref[p]
        gc = g_ref[p]
        oc = o_ref[pl.ds(p * U, U), :]
        cols = pl.ds(pl.multiple_of(i * U, U), U)
        qt[:, cols] = qc.T
        gt[:, cols] = gc.T
        prod = (oc * gc.astype(f32)).T
        zero = jnp.zeros((U, HD), bf16)
        for h in range(nh):
            delta[h : h + 1, cols] = jnp.sum(prod[h * HD : (h + 1) * HD], axis=0, keepdims=True)
            qx[h, pl.ds(i * U, U), :] = jnp.concatenate([zero, qc[:, h * HD : (h + 1) * HD]], axis=1)
            gx[h, pl.ds(i * U, U), :] = jnp.concatenate([gc[:, h * HD : (h + 1) * HD], zero], axis=1)
        kv = kv_ref[p]
        kc, vc = kv[:, :W], kv[:, W:]
        kt[:, pl.ds(pl.multiple_of(i * B, B), B)] = kc.T
        for h in range(nh):
            ks[h, pl.ds(i * B, B), :] = kc[:, h * HD : (h + 1) * HD]
            vs[h, pl.ds(i * B, B), :] = vc[:, h * HD : (h + 1) * HD]

    dkv[...] = jnp.zeros_like(dkv)

    def tile(m, c, carry, masked):
        out = []
        qcols = pl.ds(pl.multiple_of(m * TQ, TQ), TQ)
        krows = pl.ds(pl.multiple_of(c * TK, TK), TK)
        for h in range(nh):
            hs = slice(h * HD, (h + 1) * HD)
            s = jnp.dot(ks[h, krows, :], qt[hs, qcols], preferred_element_type=f32)
            p = jnp.exp(s - lse_ref[h : h + 1, qcols])
            if masked:
                row = lax.broadcasted_iota(jnp.int32, s.shape, 0)
                col = lax.broadcasted_iota(jnp.int32, s.shape, 1)
                p = jnp.where((row >= B) & (col < U), 0.0, p)
            dp = jnp.dot(vs[h, krows, :], gt[hs, qcols], preferred_element_type=f32)
            ds = (p * (dp - delta[h : h + 1, qcols])).astype(bf16)
            dkv[h, krows, :] += jnp.dot(
                p.astype(bf16), gx[h, qcols, :], preferred_element_type=f32
            ) + jnp.dot(ds, qx[h, qcols, :], preferred_element_type=f32)
            out.append(carry[h] + jnp.dot(kt[hs, krows], ds, preferred_element_type=f32))
        return tuple(out)

    def halves(b, half):
        rows = pl.ds(pl.multiple_of(b * B + half * U, U), U)
        parts = [dkv[h, rows, :] for h in range(nh)]
        return jnp.concatenate([x[:, HD:] for x in parts] + [x[:, :HD] for x in parts], axis=1)

    @pl.loop(0, npair // 2)
    def _(turn):
        m = npair // 2 - 1 - turn
        init = tuple(jnp.zeros((HD, TQ), f32) for _ in range(nh))

        def step(c, x):
            x = tile(m, c, x, False)
            act(REDUCE_PLAN, steps, m, c, False)
            return x

        carry = lax.fori_loop(0, m, step, init)
        carry = tile(m, m, carry, True)
        dqs[pl.ds(pl.multiple_of(m * TQ, TQ), TQ), :] = (jnp.concatenate(carry, axis=0).T * 0.125).astype(bf16)
        for k in range(2):
            over[2 * m + k] = halves(2 * m + k, 1).astype(bf16)
        ex.copy(swap[0] + m, over.at[pl.ds(2 * m, 2)], back.at[pl.ds(2 * m, 2)], ex.C).start()
        act(REDUCE_PLAN, steps, m, m, True)

    @pl.loop(0, npair // 2)
    def _(m):
        moved = ex.copy(swap[0] + m, over.at[pl.ds(2 * m, 2)], back.at[pl.ds(2 * m, 2)], ex.C)
        moved.wait_recv()
        moved.wait_send()

    @pl.loop(0, npair)
    def _(p):
        b = blk[p]
        rows = pl.ds(b * B, U)
        parts = [dkv[h, rows, :] for h in range(nh)]
        own = jnp.concatenate([x[:, HD:] for x in parts] + [x[:, :HD] for x in parts], axis=1)
        own = (own + back[b].astype(f32)).astype(bf16)
        gm_ref[p] = jnp.concatenate([dqs[pl.ds(b * U, U), :], own], axis=1)

    for j in range(1, ex.planes):
        ex.got(il[ex.planes - j], lo_ref.at[ex.z(j)])
    keep.wait()
    last()


def attend_back(inv, blk, q, kv, g, o, lse, out, *grads):
    npair, U, W = q.shape
    R, K = npair * U, npair * kv.shape[1]
    nh = W // HD
    S, H, Q = (lax.axis_size(a) for a in AXES)
    n = len(grads)
    f32, bf16 = jnp.float32, jnp.bfloat16
    tails = [a.shape[3:] for a in grads]
    buffers = [[pltpu.VMEM(lead + t, bf16) for t in tails] for lead in ((S, H), (S, H), (S, 2), (S,), (S,))]
    return remote_call(
        partial(attend_back_kernel, n),
        2,
        [jax.ShapeDtypeStruct((npair, R // npair, 3 * W), bf16), jax.ShapeDtypeStruct(out.shape, bf16)]
        + [jax.ShapeDtypeStruct(t, f32) for t in tails],
        [SMEM] * 2 + [VMEM] * 5 + [ANY] * (n + 1),
        [VMEM, ANY] + [VMEM] * n,
        sum(buffers, [])
        + [
            pltpu.VMEM((W, R), bf16),
            pltpu.VMEM((W, R), bf16),
            pltpu.VMEM((nh, R, 2 * HD), bf16),
            pltpu.VMEM((nh, R, 2 * HD), bf16),
            pltpu.VMEM((nh, K, HD), bf16),
            pltpu.VMEM((nh, K, HD), bf16),
            pltpu.VMEM((W, K), bf16),
            pltpu.VMEM((8, R), f32),
            pltpu.VMEM((nh, K, 2 * HD), f32),
            pltpu.VMEM((R, W), bf16),
            pltpu.VMEM((npair, R // npair, 2 * W), bf16),
            pltpu.VMEM((npair, R // npair, 2 * W), bf16),
        ],
        5 * S * n + npair // 2 + S,
        "attend_back",
        60 << 20,
    )(inv, blk, q, kv, g, o, lse, out, *grads)


def middle_kernel(
    low_ref, x_ref, g_ref, vec_ref, bf_ref, fc_ref, proj_ref, wo_ref,
    lo_ref, gmid_ref, small_ref, ga_ref, gfc_ref, gproj_ref, gout_ref,
    ra, fc, wp, wo_in, wf, wo, act_ref, dpre, deriv, g, att, mid, z_ref, n2, n2t, y, t2, gb, sb, gfc, gproj, gout,
    send, recv, local,
):
    f32, bf16 = jnp.float32, jnp.bfloat16
    ex = Exchange(send, recv)
    s, h, r, n = ex.s, ex.h, ex.r, ex.planes
    H, U, W = low_ref.shape[1:]
    R, D = att.shape
    d = fc.shape[3]
    loads = [
        pltpu.make_async_copy(a, b, local.at[i])
        for i, (a, b) in enumerate(
            (
                (wo_ref, wo_in),
                (proj_ref.at[:, h], wp.at[:, h, r]),
                (fc_ref, fc),
                (low_ref.at[:, h], ra.at[h]),
                (g_ref.at[s], g.at[s]),
                (proj_ref.at[:, ex.xn], wp.at[:, ex.xn, r]),
                (proj_ref.at[:, ex.yn], wp.at[:, ex.yn, r]),
            )
        )
    ]
    for c in loads:
        c.start()
    ex.greet([ex.X, ex.Y, ex.D, ex.C] + ex.Z[1:])
    there, back = ex.slots(3), ex.slots(3)
    ir, ic, ig = (ex.slots(n) for _ in range(3))
    sides = ((ex.X, ex.xn), (ex.Y, ex.yn), (ex.D, ex.dn))
    for k, (peer, to) in enumerate(sides):
        ex.put(there[k], low_ref.at[:, to], ra.at[h], peer)
    for j in range(n):
        frm, peer = (ex.xn, ex.Y) if by_x(0, j) else (ex.yn, ex.X)
        ex.put(ir[j], proj_ref.at[ex.z(j), frm], wp.at[ex.z(j), frm, r], peer)
    for j in range(1, n):
        ex.put(ig[j], g_ref.at[ex.z(j)], g.at[s], ex.Z[j])

    def across(j):
        ex.got(ir[j], wp.at[ex.z(j), ex.dn, r])
        ex.put(ic[j], wp.at[ex.z(j), :, r], wp.at[ex.z(j), :, r], ex.C)

    dot = partial(jnp.dot, preferred_element_type=f32)
    dot_nt = lambda a, b: lax.dot_general(a, b, (((1,), (1,)), ((), ())), preferred_element_type=f32)
    dot_tn = lambda a, b: lax.dot_general(a, b, (((0,), (0,)), ((), ())), preferred_element_type=f32)
    loads[0].wait()
    wo[...] = wo_in[:, :, :, :d].astype(f32).reshape(D, D).astype(bf16)
    loads[2].wait()

    @pl.loop(0, n)
    def _(b):
        cols = pl.ds(pl.multiple_of(b * D, D), D)
        wf[b] = fc[:, :, :, :, cols].astype(f32).reshape(D, D).astype(bf16)

    y[...] = jnp.zeros_like(y)
    t2[...] = jnp.zeros_like(t2)
    gout[...] = jnp.zeros_like(gout)
    loads[3].wait()
    for k, (peer, frm) in enumerate(sides):
        ex.got(there[k], ra.at[frm])
    att[...] = jnp.concatenate([ra[k].reshape(R, W) for k in range(H)], axis=1)
    m = x_ref[...].astype(f32) + dot(att[...], wo[...]) + vec_ref[4:5]
    mid[...] = m
    center = m - jnp.mean(m, axis=-1, keepdims=True)
    rstd = lax.rsqrt(jnp.mean(center * center, axis=-1, keepdims=True) + 1e-05)
    z = center * rstd
    z_ref[...] = z
    normed = (z * vec_ref[5:6] + vec_ref[6:7]).astype(bf16)
    n2[...] = normed
    n2t[...] = normed.T
    slope = math.sqrt(2.0 / math.pi)

    def up(b):
        cols = slice(b * D, (b + 1) * D)
        pre = dot(n2[...], wf[b]) + bf_ref[0:1, cols]
        square = pre * pre
        tanh = jnp.tanh(slope * pre * (1.0 + 0.044715 * square))
        half = 0.5 * (1.0 + tanh)
        act_ref[b] = (pre * half).astype(bf16)
        deriv[b] = half + 0.5 * pre * (1.0 - tanh * tanh) * (slope * (1.0 + 3 * 0.044715 * square))

    up(0)
    for i in (1, 5, 6):
        loads[i].wait()
    across(0)
    across(1)
    up(1)
    across(2)
    across(3)
    up(2)
    up(3)
    loads[4].wait()
    for j in range(1, n):
        ex.got(ig[n - j], g.at[ex.z(j)])

    def down(j):
        b = ex.z(j)
        ex.got(ic[j], wp.at[b, :, 1 - r])
        pre = dot_nt(g[...].reshape(R, D), wp[b].reshape(D, D)) * deriv[b]
        dpre[b] = pre.astype(bf16)
        small_ref[pl.ds(b + 4, 1)] = jnp.sum(dpre[b].astype(f32), axis=0, keepdims=True)
        t2[...] += dot_nt(dpre[b], wf[b])

    for j in range(n):
        down(j)
    t, z = t2[...], z_ref[...]
    g32 = g[...].reshape(R, D).astype(f32)
    e = t * vec_ref[5:6]
    inner = e - jnp.mean(e, axis=-1, keepdims=True) - z * jnp.mean(e * z, axis=-1, keepdims=True)
    gm = g32 + inner * rstd
    gmid_ref[...] = gm
    gb[...] = gm.astype(bf16)
    ga = dot_nt(gb[...], wo[...]).astype(bf16)
    for k in range(H):
        sb[k] = ga[:, k * W : (k + 1) * W].reshape(sb.shape[1:])
    for k, (peer, to) in enumerate(sides):
        ex.put(back[k], sb.at[to], ga_ref.at[:, h], peer)
    mine = pltpu.make_async_copy(sb.at[h], ga_ref.at[:, h], local.at[3])
    mine.start()
    stores = []

    def store(src, dst):
        stores.append(pltpu.make_async_copy(src, dst, local.at[4 + len(stores)]))
        stores[-1].start()

    for b in range(n):
        grad = g[...].reshape(R, D)
        gproj[b] = dot_tn(act_ref[b], grad).astype(bf16).reshape(gproj.shape[1:])
        gfc[:, :, :, :, b * D : (b + 1) * D] = dot(n2t[...], dpre[b]).reshape(gfc.shape[:4] + (D,)).astype(bf16)
        y[...] += dot(act_ref[b], wp[b].reshape(D, D))
    store(gproj, gproj_ref)
    store(gfc, gfc_ref)
    gout[:, :, :, :d] = dot_tn(att[...], gb[...]).reshape(gout.shape[:3] + (d, D)).astype(bf16)
    store(gout, gout_ref)
    lo_ref[...] = (mid[...] + y[...] + vec_ref[7:8]).astype(bf16)
    small_ref[1:2] = jnp.sum(t2[...] * z_ref[...], axis=0, keepdims=True)
    small_ref[2:3] = jnp.sum(t2[...], axis=0, keepdims=True)
    small_ref[0:1] = jnp.sum(gb[...].astype(f32), axis=0, keepdims=True)
    small_ref[3:4] = jnp.sum(g[...].reshape(R, D).astype(f32), axis=0, keepdims=True)
    for k, (peer, frm) in enumerate(sides):
        ex.got(back[k], ga_ref.at[:, frm])
    for c in stores + [mine]:
        c.wait()
    ex.close()


def middle(low, x, g, vecs, bias, fc, proj, wo):
    S, H, U, W = low.shape
    R, D = x.shape
    whole = fc.shape[:3] + proj.shape[2:]
    f32, bf16 = jnp.float32, jnp.bfloat16
    vm = pltpu.VMEM
    return remote_call(
        middle_kernel,
        4,
        [
            jax.ShapeDtypeStruct((R, D), bf16),
            jax.ShapeDtypeStruct((R, D), f32),
            jax.ShapeDtypeStruct((8, D), f32),
            jax.ShapeDtypeStruct(low.shape, bf16),
            jax.ShapeDtypeStruct(fc.shape, bf16),
            jax.ShapeDtypeStruct(whole, bf16),
            jax.ShapeDtypeStruct(wo.shape, bf16),
        ],
        [ANY, VMEM, ANY, VMEM, VMEM] + [ANY] * 3,
        [VMEM] * 3 + [ANY] * 4,
        [
            vm((H, S, U, W), bf16),
            vm(fc.shape, bf16),
            vm(whole, bf16),
            vm(wo.shape, bf16),
            vm((S, D, D), bf16),
            vm((D, D), bf16),
            vm((S, R, D), bf16),
            vm((S, R, D), bf16),
            vm((S, R, D), f32),
            vm((S, U, D), bf16),
            vm((R, D), bf16),
            vm((R, D), f32),
            vm((R, D), f32),
            vm((R, D), bf16),
            vm((D, R), bf16),
            vm((R, D), f32),
            vm((R, D), f32),
            vm((R, D), bf16),
            vm((H, S, U, W), bf16),
            vm(fc.shape, bf16),
            vm(whole, bf16),
            vm(wo.shape, bf16),
        ],
        6 + 3 * S,
        "middle",
        60 << 20,
    )(low, x, g, vecs, bias, fc, proj, wo)


def norm_back(x, t, gain, grad):
    mean = jnp.mean(x, axis=-1, keepdims=True)
    center = x - mean
    rstd = lax.rsqrt(jnp.mean(center * center, axis=-1, keepdims=True) + 1e-05)
    z = center * rstd
    e = t * gain
    inner = e - jnp.mean(e, axis=-1, keepdims=True) - z * jnp.mean(e * z, axis=-1, keepdims=True)
    return grad + rstd * inner


def finish_kernel(
    gm_ref, w_ref, norm_ref, x_ref, gmid_ref, line_ref, small_ref,
    gh_ref, gqkv_ref, own_ref,
    gq_ref, t_ref, one, two, hid, gw, gw_c, gw_z, gw_sum, vec, send, recv, local,
):
    f32, bf16 = jnp.float32, jnp.bfloat16
    ex = Exchange(send, recv)
    s, h, r, n = ex.s, ex.h, ex.r, ex.planes
    half = n // 2
    H, N = gm_ref.shape[1], gm_ref.shape[3]
    U, D = t_ref.shape[2], t_ref.shape[3]
    W = N // 3
    d = gw.shape[3]
    ex.greet([ex.X, ex.Y, ex.D, ex.C] + ex.Z[1:])
    i1, i1b, i2, ih, ic, iz, iq = (ex.slots(n) for _ in range(7))
    iv = ex.slots(3 + n)
    acc = [jnp.zeros((1, D), f32), jnp.zeros((1, D), f32)]
    way = lambda j: (ex.X, ex.xn, ex.Y, ex.yn) if by_x(0, j) else (ex.Y, ex.yn, ex.X, ex.xn)

    def product(j, pair):
        t = ex.z(j)
        g = jnp.concatenate([gm_ref[t, to] for to in pair], axis=0)
        prod = lax.dot_general(g, w_ref[...], (((1,), (1,)), ((), ())), preferred_element_type=f32)
        for k, to in enumerate(pair):
            part = prod[k * U : (k + 1) * U]
            t_ref[t, to] = part.astype(bf16)
            acc[0] += jnp.sum(part * norm_ref[t, to].astype(f32), axis=0, keepdims=True)
            acc[1] += jnp.sum(part, axis=0, keepdims=True)

    def leave(j):
        peer, near, _, _ = way(j)
        ex.put(i1b[j], t_ref.at[ex.z(j), ex.dn], one.at[j, 1], peer)
        ex.put(i1[j], t_ref.at[ex.z(j), near], one.at[j, 0], peer)

    def relay(j):
        t = ex.z(j)
        _, _, peer, other = way(j)
        ex.got(i1b[j], one.at[j, 1])
        t_ref[t, other] = (t_ref[t, other].astype(f32) + one[j, 1].astype(f32)).astype(bf16)
        ex.put(i2[j], t_ref.at[t, other], two.at[j], peer)

    g_all = gm_ref[...].reshape(n * H * U, N)
    def qkv_rows(t0):
        width = H * 2 * d
        nt = norm_ref[:, :, :, t0 * width : (t0 + half) * width].reshape(n * H * U, half * width)
        part = lax.dot_general(nt, g_all, (((0,), (0,)), ((), ())), preferred_element_type=f32)
        gw[t0 : t0 + half] = part.reshape(half, H, 2, d, N).astype(bf16)
        for t in range(t0, t0 + half):
            ex.put(ic[t], gw.at[t, :, 1 - r], gw_c.at[t], ex.C)

    def done(j):
        t = ex.z(j)
        ex.got(i1[j], one.at[j, 0])
        ex.got(i2[j], two.at[j])
        total = t_ref[t, h].astype(f32) + one[j, 0].astype(f32) + two[j].astype(f32)
        hid[t] = norm_back(x_ref[t].astype(f32), total, line_ref[0:1], gmid_ref[t]).astype(bf16)
        if j:
            ex.put(ih[j], hid.at[t], gh_ref.at[s], ex.Z[j])

    for j in (1, 2):
        product(j, (ex.dn, way(j)[1]))
        leave(j)
    qkv_rows(0)
    qkv_rows(half)
    for j in (1, 2):
        product(j, (way(j)[3], h))
    for t in range(n):
        ex.got(ic[t], gw_c.at[t])
        gw_c[t] = (gw_c[t].astype(f32) + gw[t, :, r].astype(f32)).astype(bf16)
    for j in range(1, n):
        ex.put(iz[j], gw_c.at[ex.z(j)], gw_z.at[s], ex.Z[j])
    relay(1)
    relay(2)
    for j in (3, 0):
        product(j, (ex.dn, way(j)[1]))
        leave(j)
    for j in (3, 0):
        product(j, (way(j)[3], h))
    cols = jnp.sum(g_all.astype(f32), axis=0, keepdims=True)
    lane = lax.broadcasted_iota(jnp.int32, (1, D), 1) // W

    def placed(c):
        return jnp.where(lane == h, jnp.concatenate([c] * H, axis=1), 0.0)

    vec[0, 0:1] = acc[0]
    vec[0, 1:2] = acc[1]
    vec[0, 2:3] = placed(cols[:, :W])
    vec[0, 3:4] = placed(cols[:, 2 * W :])
    vec[0, 4:8] = jnp.zeros((4, D), f32)
    vec[0, 8:] = small_ref[...]
    ex.put(iv[0], vec.at[0], vec.at[1], ex.C)

    done(1)
    done(2)
    ex.got(iv[0], vec.at[1])
    vec[2] = vec[0] + vec[1]
    ex.put(iv[1], vec.at[2], vec.at[3], ex.X)
    relay(3)
    relay(0)
    ex.got(iv[1], vec.at[3])
    vec[4] = vec[2] + vec[3]
    ex.put(iv[2], vec.at[4], vec.at[5], ex.Y)
    total = gw_c[s].astype(f32)
    for j in range(1, n):
        ex.got(iz[n - j], gw_z.at[ex.z(j)])
        total += gw_z[ex.z(j)].astype(f32)
    gw_sum[...] = total
    for k, (peer, to) in enumerate(((ex.X, ex.xn), (ex.Y, ex.yn), (ex.D, ex.dn))):
        ex.put(iq[k], gw_sum.at[to], gq_ref.at[h], peer)
    mine = pltpu.make_async_copy(gw_sum.at[h], gq_ref.at[h], local.at[2])
    mine.start()
    ex.got(iv[2], vec.at[5])
    vec[6] = vec[4] + vec[5]
    for j in range(1, n):
        ex.put(iv[2 + j], vec.at[6], vec.at[6 + j], ex.Z[j])
    done(3)
    done(0)
    own = pltpu.make_async_copy(hid.at[s], gh_ref.at[s], local.at[1])
    own.start()
    for j in range(1, n):
        ex.got(iv[2 + j], vec.at[6 + j])
    sums = vec[6] + vec[7] + vec[8] + vec[9]
    gain = (sums[0:1] - line_ref[1:2] * sums[1:2]) / line_ref[0:1]
    rows = jnp.concatenate([gain, sums[1:12], jnp.zeros((4, D), f32)], axis=0)
    wide = jnp.zeros((1, D), f32)
    for k in range(n):
        wide = jnp.where(s == k, sums[12 + k : 13 + k], wide)
    at = h * 2 + r
    begin = (s * H * 2 + at) * d
    own_ref[...] = pltpu.roll(rows, lax.rem(D - begin, D), 1)[:, :128]
    own_ref[12:13] = pltpu.roll(jnp.broadcast_to(wide, (8, D)), lax.rem(D - at * n * d, D), 1)[0:1, :128]
    for k, frm in enumerate((ex.xn, ex.yn, ex.dn)):
        ex.got(iq[k], gq_ref.at[frm])
    mine.wait()
    for k in range(H):
        for c in range(3):
            gqkv_ref[:, c * D + k * W : c * D + (k + 1) * W] = gq_ref[k, :, c * W : (c + 1) * W]
    for j in range(1, n):
        ex.got(ih[n - j], gh_ref.at[ex.z(j)])
    own.wait()
    ex.close()


def finish(gm, w, norm, x, gmid, lines, small):
    S, H, U, N = gm.shape
    D = w.shape[0]
    Q = lax.axis_size("r")
    d = D // (S * H * Q)
    f32, bf16 = jnp.float32, jnp.bfloat16
    return remote_call(
        finish_kernel,
        3,
        [
            jax.ShapeDtypeStruct((S, U, D), bf16),
            jax.ShapeDtypeStruct((d, H * N), f32),
            jax.ShapeDtypeStruct((16, 128), f32),
        ],
        [VMEM] * 7,
        [ANY, VMEM, VMEM],
        [
            pltpu.VMEM((H, d, N), f32),
            pltpu.VMEM((S, H, U, D), bf16),
            pltpu.VMEM((S, 2, U, D), bf16),
            pltpu.VMEM((S, U, D), bf16),
            pltpu.VMEM((S, U, D), bf16),
            pltpu.VMEM((S, H, Q, d, N), bf16),
            pltpu.VMEM((S, H, d, N), bf16),
            pltpu.VMEM((S, H, d, N), bf16),
            pltpu.VMEM((H, d, N), f32),
            pltpu.VMEM((10, 16, D), f32),
        ],
        8 * S + 3,
        "finish",
    )(gm, w, norm, x, gmid, lines, small)


def planes(
    hidden_in,
    block_pairs,
    ln1_gain,
    ln1_bias,
    qkv_weight,
    query_bias,
    value_bias,
    out_weight,
    out_bias,
    ln2_gain,
    ln2_bias,
    fc_weight,
    fc_bias,
    proj_weight,
    proj_bias,
    out_grad,
):
    f32, bf16 = jnp.float32, jnp.bfloat16
    s, h, r = (lax.axis_index(a) for a in AXES)
    S, H, Q = (lax.axis_size(a) for a in AXES)
    rows, D = hidden_in.shape
    U = rows // SEQS
    W = D // H
    bfn = fc_bias.shape[0]
    d = qkv_weight.shape[0]
    lines = [ln1_gain, ln1_bias, query_bias, value_bias, out_bias, ln2_gain, ln2_bias, proj_bias, fc_bias]
    pad8 = lambda y: jnp.concatenate([y, jnp.zeros((8, y.shape[1]), y.dtype)])
    blk = block_pairs[::2]
    blk = jnp.where(s % 2 == 0, blk, blk.shape[0] - 1 - blk)
    blk = blk.astype(jnp.int32)
    npair = blk.shape[0]
    inv = jnp.sum(
        jnp.where(blk[None, :] == jnp.arange(npair)[:, None], jnp.arange(npair)[None, :], 0), axis=1
    ).astype(jnp.int32)
    normed, q_all, kv_all, w_h, vecs, x_own, att, att_low, lse, w_fc, w_out, w_proj = forward(
        inv,
        blk,
        hidden_in.reshape(S, U, D),
        qkv_weight,
        [v[None] for v in lines],
        fc_weight,
        pad8(out_weight),
        proj_weight,
    )
    bf = vecs[8 : 8 + bfn // d].reshape(-1, S * H * Q, d).swapaxes(0, 1).reshape(-1)
    layer_out, grad_middle, small, g_att, grad_fc, grad_proj, grad_wout = middle(
        att_low.reshape(S, H, U, W),
        x_own.reshape(rows, D),
        out_grad.reshape(S, U, D),
        vecs,
        jnp.broadcast_to(bf[None], (8, bf.shape[0])),
        w_fc,
        w_proj,
        w_out,
    )
    grad_mixed, layer_out, gfc, gproj, gout = attend_back(
        inv,
        blk,
        q_all,
        kv_all.reshape(npair, Q * U, 2 * W),
        g_att.reshape(npair, U, W),
        att,
        lse,
        layer_out.reshape(S, U, D),
        grad_fc,
        grad_proj,
        grad_wout,
    )
    grad_hidden, gq, own = finish(
        grad_mixed.reshape(S, H, U, 3 * W),
        w_h,
        normed,
        x_own,
        grad_middle.reshape(S, U, D),
        vecs,
        small,
    )
    g1s, b1s, bqs, bvs = (own[i, :d] for i in range(4))
    bos, g2s, b2s, bps = (own[i, :d] for i in range(8, 12))
    return (
        layer_out.reshape(rows, D),
        grad_hidden.reshape(rows, D),
        g1s,
        b1s,
        gq,
        bqs,
        bvs,
        gout[:d],
        bos,
        g2s,
        b2s,
        gfc,
        own[12, :bfn],
        gproj,
        bps,
    )


def solution(mesh):
    n = mesh.shape["ctx"]
    if n // (PLANES * SEQS) != 2:
        return solution_any(mesh)
    split = Mesh(mesh.devices.reshape(PLANES, SEQS, -1), AXES)
    row, vec = P(AXES, None), P(AXES)
    return jax.shard_map(
        planes,
        mesh=split,
        in_specs=(row, P(), vec, vec, row, vec, vec, row, vec, vec, vec, row, vec, row, vec, row),
        out_specs=(row, row, vec, vec, row, vec, vec, row, vec, vec, vec, row, vec, row, vec),
        check_vma=False,
    )
```

```python
from functools import partial
import math

import jax
import jax.numpy as jnp
from jax import lax
from jax.sharding import PartitionSpec as P
from jax.experimental import pallas as pl
from jax.experimental.pallas import tpu as pltpu
from jax.sharding import Mesh

HEADS = 12
SEQS = 4


NEG = -1e30


def from_partner(value, axis, bit):
    return lax.ppermute(value, axis, [(i, i ^ 1 << bit) for i in range(lax.axis_size(axis))])


def layer_norm(values, gain, bias):
    center = values - jnp.mean(values, axis=-1, keepdims=True)
    spread_sq = jnp.mean(center * center, axis=-1, keepdims=True)
    return center * lax.rsqrt(spread_sq + 1e-05) * gain + bias


def gelu_tanh(values):
    return jax.nn.gelu(values, approximate=True)


def heads_of(tensor, head_count):
    return tensor.reshape(tensor.shape[:-1] + (head_count, tensor.shape[-1] // head_count))


def pick_own(owned, chosen):
    selector = chosen.reshape((1, -1) + (1,) * (owned.ndim - 2))
    return jnp.where(selector, owned[:, 0:1], owned[:, 1:2])


def pick_piece(piece, chosen):
    selector = chosen.reshape((1, -1) + (1,) * (piece.ndim - 3))
    return jnp.where(selector, piece[:, 0], piece[:, 1])


def parity_masks(chosen, usable):
    return jnp.stack([chosen & usable, jnp.logical_not(chosen) & usable])


def spread(values, parity):
    shaped = parity.reshape((1,) + parity.shape + (1,) * (values.ndim - 2))
    return jnp.sum(jnp.where(shaped, values[:, None], 0.0), axis=2)


def group_loop(pieces, unit_rows, table, stepper, carried):
    piece_rows = pieces[0].shape[2]
    group_size = min(unit_rows, piece_rows)
    group_count = piece_rows // group_size
    batch_groups = math.gcd(group_count, max(1, 1024 // group_size))
    turn_count = group_count // batch_groups
    shaped = tuple(
        (
            item.reshape(item.shape[:2] + (group_count, group_size) + item.shape[3:])
            for item in pieces
        )
    )
    device_ids = jnp.arange(group_count, dtype=jnp.int32) * group_size // unit_rows
    table_size = table.shape[0]
    blocks = jnp.sum(
        jnp.where(
            device_ids[:, None] == jnp.arange(table_size, dtype=jnp.int32)[None, :],
            table[None, :],
            0,
        ),
        axis=1,
    )

    def one_turn(position, current):
        pieces_now = tuple(
            (
                lax.dynamic_slice_in_dim(item, position * batch_groups, batch_groups, 2)
                for item in shaped
            )
        )
        chosen = lax.dynamic_slice_in_dim(blocks, position * batch_groups, batch_groups, 0)
        return stepper(current, pieces_now, chosen)

    return lax.fori_loop(0, turn_count, one_turn, carried)


def attend_step(q_heads, my_block, score_scale, head_count, carried, pieces_now, chosen):
    key_piece = heads_of(pieces_now[0], head_count)
    value_piece = heads_of(pieces_now[1], head_count)
    earlier = chosen < my_block
    usable = chosen != my_block
    parity = parity_masks(earlier, usable)
    query_sel = pick_own(q_heads, earlier)
    key_sel = pick_piece(key_piece, earlier)
    value_sel = pick_piece(value_piece, earlier)
    scores = (
        jnp.einsum("jgqhe,jgkhe->jghqk", query_sel, key_sel, preferred_element_type=jnp.float32)
        * score_scale
    )
    usable_mask = usable.reshape(1, -1, 1, 1, 1)
    scores = jnp.where(usable_mask, scores, NEG)
    old_max, old_total, old_sum = carried
    group_max = jnp.max(scores, axis=-1)
    candidate = jnp.max(jnp.where(parity.reshape(1, 2, -1, 1, 1), group_max[:, None], NEG), axis=2)
    new_max = jnp.maximum(old_max, candidate)
    max_sel = pick_own(new_max, earlier)
    weights_exp = jnp.where(usable_mask, jnp.exp(scores - max_sel[..., None]), 0.0)
    moved = jnp.einsum(
        "jghqk,jgkhe->jgqhe",
        weights_exp.astype(jnp.bfloat16),
        value_sel,
        preferred_element_type=jnp.float32,
    )
    factor = jnp.exp(old_max - new_max)
    new_total = old_total * factor + spread(jnp.sum(weights_exp, axis=-1), parity)
    new_sum = old_sum * jnp.swapaxes(factor, 2, 3)[..., None] + spread(moved, parity)
    return (new_max, new_total, new_sum)


def query_grad_step(
    q_heads,
    grad_heads,
    lse_heads,
    delta_heads,
    my_block,
    score_scale,
    head_count,
    carried,
    pieces_now,
    chosen,
):
    key_piece = heads_of(pieces_now[0], head_count)
    value_piece = heads_of(pieces_now[1], head_count)
    earlier = chosen < my_block
    usable = chosen != my_block
    parity = parity_masks(earlier, usable)
    query_sel = pick_own(q_heads, earlier)
    grad_sel = pick_own(grad_heads, earlier)
    lse_sel = pick_own(lse_heads, earlier)
    delta_sel = pick_own(delta_heads, earlier)
    key_sel = pick_piece(key_piece, earlier)
    value_sel = pick_piece(value_piece, earlier)
    scores = (
        jnp.einsum("jgqhe,jgkhe->jghqk", query_sel, key_sel, preferred_element_type=jnp.float32)
        * score_scale
    )
    usable_mask = usable.reshape(1, -1, 1, 1, 1)
    probabilities = jnp.where(usable_mask, jnp.exp(scores - lse_sel[..., None]), 0.0)
    grad_probs = jnp.einsum(
        "jgqhe,jgkhe->jghqk", grad_sel, value_sel, preferred_element_type=jnp.float32
    )
    grad_scores = (probabilities * (grad_probs - delta_sel[..., None])).astype(jnp.bfloat16)
    term = (
        jnp.einsum("jghqk,jgkhe->jgqhe", grad_scores, key_sel, preferred_element_type=jnp.float32)
        * score_scale
    )
    return carried + spread(term, parity)


def key_grad_step(k_heads, v_heads, my_block, score_scale, head_count, carried, pieces_now, chosen):
    query_piece = heads_of(pieces_now[0], head_count)
    grad_piece = heads_of(pieces_now[1], head_count)
    later = my_block < chosen
    usable = chosen != my_block
    parity = parity_masks(later, usable)
    query_sel = pick_piece(query_piece, later)
    grad_sel = pick_piece(grad_piece, later)
    lse_sel = jnp.swapaxes(pick_piece(pieces_now[2], later), 2, 3)
    delta_sel = jnp.swapaxes(pick_piece(pieces_now[3], later), 2, 3)
    key_sel = pick_own(k_heads, later)
    value_sel = pick_own(v_heads, later)
    scores = (
        jnp.einsum("jgqhe,jgkhe->jghqk", query_sel, key_sel, preferred_element_type=jnp.float32)
        * score_scale
    )
    usable_mask = usable.reshape(1, -1, 1, 1, 1)
    probabilities = jnp.where(usable_mask, jnp.exp(scores - lse_sel[..., None]), 0.0)
    grad_probs = jnp.einsum(
        "jgqhe,jgkhe->jghqk", grad_sel, value_sel, preferred_element_type=jnp.float32
    )
    grad_scores = (probabilities * (grad_probs - delta_sel[..., None])).astype(jnp.bfloat16)
    key_term = (
        jnp.einsum("jghqk,jgqhe->jgkhe", grad_scores, query_sel, preferred_element_type=jnp.float32)
        * score_scale
    )
    value_term = jnp.einsum(
        "jghqk,jgqhe->jgkhe",
        probabilities.astype(jnp.bfloat16),
        grad_sel,
        preferred_element_type=jnp.float32,
    )
    return (carried[0] + spread(key_term, parity), carried[1] + spread(value_term, parity))


def shards(
    hidden_in,
    block_pairs,
    ln1_gain,
    ln1_bias,
    qkv_weight,
    query_bias,
    value_bias,
    out_weight,
    out_bias,
    ln2_gain,
    ln2_bias,
    fc_weight,
    fc_bias,
    proj_weight,
    proj_bias,
    out_grad,
):
    params = (
        ln1_gain,
        ln1_bias,
        qkv_weight,
        query_bias,
        value_bias,
        out_weight,
        out_bias,
        ln2_gain,
        ln2_bias,
        fc_weight,
        fc_bias,
        proj_weight,
        proj_bias,
    )
    gathered = (
        lax.all_gather(params[0], "ctx", axis=0, tiled=True),
        lax.all_gather(params[1], "ctx", axis=0, tiled=True),
        lax.all_gather(params[2], "ctx", axis=0, tiled=True),
        lax.all_gather(params[3], "ctx", axis=0, tiled=True),
        lax.all_gather(params[4], "ctx", axis=0, tiled=True),
        lax.all_gather(params[5], "ctx", axis=0, tiled=True),
        lax.all_gather(params[6], "ctx", axis=0, tiled=True),
        lax.all_gather(params[7], "ctx", axis=0, tiled=True),
        lax.all_gather(params[8], "ctx", axis=0, tiled=True),
        lax.all_gather(params[9], "ctx", axis=0, tiled=True),
        lax.all_gather(params[10], "ctx", axis=0, tiled=True),
        lax.all_gather(params[11], "ctx", axis=0, tiled=True),
        lax.all_gather(params[12], "ctx", axis=0, tiled=True),
    )
    (
        gain_one,
        bias_one,
        w_qkv,
        b_query,
        b_value,
        w_out,
        b_out,
        gain_two,
        bias_two,
        w_fc,
        b_fc,
        w_proj,
        b_proj,
    ) = gathered
    device = lax.axis_index("ctx")
    partner = device + 1 - 2 * (device % 2)
    row_count = hidden_in.shape[0]
    model_width = hidden_in.shape[1]
    unit_rows = row_count // SEQS
    halves = SEQS // 2
    head_count = HEADS
    head_size = model_width // head_count
    score_scale = 1.0 / math.sqrt(head_size)
    my_block = block_pairs[device]
    seq_shape = (halves, 2, unit_rows, model_width)
    head_shape = (halves, 2, unit_rows, head_count, head_size)
    inputs = hidden_in.astype(jnp.float32)
    normed = layer_norm(inputs, gain_one.astype(jnp.float32), bias_one.astype(jnp.float32)).astype(
        jnp.bfloat16
    )
    mixed_proj = jnp.dot(normed, w_qkv, preferred_element_type=jnp.float32)
    queries = (mixed_proj[:, :model_width] + b_query.astype(jnp.float32)).astype(jnp.bfloat16)
    key_rows = mixed_proj[:, model_width : 2 * model_width].astype(jnp.bfloat16)
    value_rows = (mixed_proj[:, 2 * model_width :] + b_value.astype(jnp.float32)).astype(
        jnp.bfloat16
    )
    q_seq = queries.reshape(seq_shape)
    k_seq = key_rows.reshape(seq_shape)
    v_seq = value_rows.reshape(seq_shape)
    q_heads = queries.reshape(head_shape)
    k_heads = key_rows.reshape(head_shape)
    v_heads = value_rows.reshape(head_shape)
    far_keys, far_values = from_partner((k_seq, v_seq), "ctx", 0)
    near_keys = jnp.concatenate([k_heads, heads_of(far_keys, head_count)], axis=2)
    near_values = jnp.concatenate([v_heads, heads_of(far_values, head_count)], axis=2)
    scores = (
        jnp.einsum("jpqhe,jpkhe->jphqk", q_heads, near_keys, preferred_element_type=jnp.float32)
        * score_scale
    )
    row_max = jnp.max(scores, axis=-1)
    weights_exp = jnp.exp(scores - row_max[..., None])
    row_total = jnp.sum(weights_exp, axis=-1)
    summed = jnp.einsum(
        "jphqk,jpkhe->jpqhe",
        weights_exp.astype(jnp.bfloat16),
        near_values,
        preferred_element_type=jnp.float32,
    )
    forward_stepper = partial(attend_step, q_heads, my_block, score_scale, head_count)
    row_max, row_total, summed = group_loop(
        (
            lax.all_gather(k_seq, "ctx", axis=2, tiled=True),
            lax.all_gather(v_seq, "ctx", axis=2, tiled=True),
        ),
        unit_rows,
        block_pairs,
        forward_stepper,
        (row_max, row_total, summed),
    )
    attended = summed / jnp.swapaxes(row_total, 2, 3)[..., None]
    log_total = row_max + jnp.log(row_total)
    att_low = attended.reshape(row_count, model_width).astype(jnp.bfloat16)
    branch = jnp.dot(att_low, w_out, preferred_element_type=jnp.float32) + b_out.astype(jnp.float32)
    middle = inputs + branch
    normed_two = layer_norm(
        middle, gain_two.astype(jnp.float32), bias_two.astype(jnp.float32)
    ).astype(jnp.bfloat16)
    pre_act = jnp.dot(normed_two, w_fc, preferred_element_type=jnp.float32) + b_fc.astype(
        jnp.float32
    )
    activation = gelu_tanh(pre_act).astype(jnp.bfloat16)
    result = (
        middle
        + jnp.dot(activation, w_proj, preferred_element_type=jnp.float32)
        + b_proj.astype(jnp.float32)
    )
    layer_out = result.astype(jnp.bfloat16)
    grad_out = out_grad.astype(jnp.float32)
    grad_proj = jnp.dot(activation.T, out_grad, preferred_element_type=jnp.float32)
    grad_bproj = jnp.sum(grad_out, axis=0)
    grad_activ = jnp.dot(out_grad, w_proj.T, preferred_element_type=jnp.float32)
    _, gelu_back = jax.vjp(gelu_tanh, pre_act)
    grad_pre = gelu_back(grad_activ)[0].astype(jnp.bfloat16)
    grad_fc = jnp.dot(normed_two.T, grad_pre, preferred_element_type=jnp.float32)
    grad_bfc = jnp.sum(grad_pre.astype(jnp.float32), axis=0)
    grad_normed_two = jnp.dot(grad_pre, w_fc.T, preferred_element_type=jnp.float32)
    _, norm_back_two = jax.vjp(
        layer_norm, middle, gain_two.astype(jnp.float32), bias_two.astype(jnp.float32)
    )
    grad_middle, grad_gain_two, grad_bias_two = norm_back_two(grad_normed_two)
    grad_middle = grad_middle + grad_out
    grad_branch = grad_middle.astype(jnp.bfloat16)
    grad_wout = jnp.dot(att_low.T, grad_branch, preferred_element_type=jnp.float32)
    grad_bout = jnp.sum(grad_branch.astype(jnp.float32), axis=0)
    grad_att = jnp.dot(grad_branch, w_out.T, preferred_element_type=jnp.float32).astype(
        jnp.bfloat16
    )
    grad_seq = grad_att.reshape(seq_shape)
    grad_heads = grad_att.reshape(head_shape)
    row_delta = jnp.sum(grad_heads.astype(jnp.float32) * attended, axis=-1)
    delta_heads = jnp.swapaxes(row_delta, 2, 3)
    all_lse, all_delta = (
        lax.all_gather(jnp.swapaxes(log_total, 2, 3), "ctx", axis=2, tiled=True),
        lax.all_gather(row_delta, "ctx", axis=2, tiled=True),
    )
    partner_lse = jnp.swapaxes(
        lax.dynamic_slice_in_dim(all_lse, partner * unit_rows, unit_rows, 2), 2, 3
    )
    partner_delta = jnp.swapaxes(
        lax.dynamic_slice_in_dim(all_delta, partner * unit_rows, unit_rows, 2), 2, 3
    )
    far_queries, far_grads = from_partner((q_seq, grad_seq), "ctx", 0)
    near_queries = jnp.concatenate([q_heads, heads_of(far_queries, head_count)], axis=2)
    near_grads = jnp.concatenate([grad_heads, heads_of(far_grads, head_count)], axis=2)
    near_lse = jnp.concatenate([log_total, partner_lse], axis=3)
    near_delta = jnp.concatenate([delta_heads, partner_delta], axis=3)
    local_scores = (
        jnp.einsum(
            "jpqhe,jpkhe->jphqk", near_queries, near_keys, preferred_element_type=jnp.float32
        )
        * score_scale
    )
    probabilities = jnp.exp(local_scores - near_lse[..., None])
    grad_probs = jnp.einsum(
        "jpqhe,jpkhe->jphqk", near_grads, near_values, preferred_element_type=jnp.float32
    )
    grad_scores = (probabilities * (grad_probs - near_delta[..., None])).astype(jnp.bfloat16)
    grad_q_local = (
        jnp.einsum(
            "jphqk,jpkhe->jpqhe",
            grad_scores[:, :, :, :unit_rows, :],
            near_keys,
            preferred_element_type=jnp.float32,
        )
        * score_scale
    )
    grad_k_local = (
        jnp.einsum(
            "jphqk,jpqhe->jpkhe",
            grad_scores[..., :unit_rows],
            near_queries,
            preferred_element_type=jnp.float32,
        )
        * score_scale
    )
    grad_v_local = jnp.einsum(
        "jphqk,jpqhe->jpkhe",
        probabilities.astype(jnp.bfloat16)[..., :unit_rows],
        near_grads,
        preferred_element_type=jnp.float32,
    )
    query_stepper = partial(
        query_grad_step,
        q_heads,
        grad_heads,
        log_total,
        delta_heads,
        my_block,
        score_scale,
        head_count,
    )
    key_stepper = partial(key_grad_step, k_heads, v_heads, my_block, score_scale, head_count)

    def query_piece(carried, pieces, offset):
        return group_loop(pieces, unit_rows, block_pairs, query_stepper, carried)

    def key_piece(carried, pieces, offset):
        return group_loop(
            (pieces[0], pieces[1], all_lse, all_delta), unit_rows, block_pairs, key_stepper, carried
        )

    grad_q_all = query_piece(
        grad_q_local,
        (
            lax.all_gather(k_seq, "ctx", axis=2, tiled=True),
            lax.all_gather(v_seq, "ctx", axis=2, tiled=True),
        ),
        jnp.int32(0),
    )
    grad_k_all, grad_v_all = key_piece(
        (grad_k_local, grad_v_local),
        (
            lax.all_gather(q_seq, "ctx", axis=2, tiled=True),
            lax.all_gather(grad_seq, "ctx", axis=2, tiled=True),
        ),
        jnp.int32(0),
    )
    grad_queries = grad_q_all.reshape(row_count, model_width).astype(jnp.bfloat16)
    grad_keys = grad_k_all.reshape(row_count, model_width).astype(jnp.bfloat16)
    grad_values = grad_v_all.reshape(row_count, model_width).astype(jnp.bfloat16)
    grad_mixed = jnp.concatenate([grad_queries, grad_keys, grad_values], axis=1)
    grad_qkv = jnp.dot(normed.T, grad_mixed, preferred_element_type=jnp.float32)
    grad_bquery = jnp.sum(grad_queries.astype(jnp.float32), axis=0)
    grad_bvalue = jnp.sum(grad_values.astype(jnp.float32), axis=0)
    grad_normed = jnp.dot(grad_mixed, w_qkv.T, preferred_element_type=jnp.float32)
    _, norm_back_one = jax.vjp(
        layer_norm, inputs, gain_one.astype(jnp.float32), bias_one.astype(jnp.float32)
    )
    grad_inputs, grad_gain_one, grad_bias_one = norm_back_one(grad_normed)
    grad_hidden = (grad_inputs + grad_middle).astype(jnp.bfloat16)
    totals = (
        lax.psum_scatter(grad_gain_one, "ctx", scatter_dimension=0, tiled=True),
        lax.psum_scatter(grad_bias_one, "ctx", scatter_dimension=0, tiled=True),
        lax.psum_scatter(grad_qkv, "ctx", scatter_dimension=0, tiled=True),
        lax.psum_scatter(grad_bquery, "ctx", scatter_dimension=0, tiled=True),
        lax.psum_scatter(grad_bvalue, "ctx", scatter_dimension=0, tiled=True),
        lax.psum_scatter(grad_wout, "ctx", scatter_dimension=0, tiled=True),
        lax.psum_scatter(grad_bout, "ctx", scatter_dimension=0, tiled=True),
        lax.psum_scatter(grad_gain_two, "ctx", scatter_dimension=0, tiled=True),
        lax.psum_scatter(grad_bias_two, "ctx", scatter_dimension=0, tiled=True),
        lax.psum_scatter(grad_fc, "ctx", scatter_dimension=0, tiled=True),
        lax.psum_scatter(grad_bfc, "ctx", scatter_dimension=0, tiled=True),
        lax.psum_scatter(grad_proj, "ctx", scatter_dimension=0, tiled=True),
        lax.psum_scatter(grad_bproj, "ctx", scatter_dimension=0, tiled=True),
    )
    return (
        layer_out,
        grad_hidden,
        totals[0],
        totals[1],
        totals[2],
        totals[3],
        totals[4],
        totals[5],
        totals[6],
        totals[7],
        totals[8],
        totals[9],
        totals[10],
        totals[11],
        totals[12],
    )


def solution_any(mesh):
    return jax.shard_map(
        shards,
        mesh=mesh,
        in_specs=(
            P("ctx", None),
            P(),
            P("ctx"),
            P("ctx"),
            P("ctx", None),
            P("ctx"),
            P("ctx"),
            P("ctx", None),
            P("ctx"),
            P("ctx"),
            P("ctx"),
            P("ctx", None),
            P("ctx"),
            P("ctx", None),
            P("ctx"),
            P("ctx", None),
        ),
        out_specs=(
            P("ctx", None),
            P("ctx", None),
            P("ctx"),
            P("ctx"),
            P("ctx", None),
            P("ctx"),
            P("ctx"),
            P("ctx", None),
            P("ctx"),
            P("ctx"),
            P("ctx"),
            P("ctx", None),
            P("ctx"),
            P("ctx", None),
            P("ctx"),
        ),
        check_vma=False,
    )


AXES = ("s", "h", "r")
PLANES = 4


MESH_IDS = pl.DeviceIdType.MESH


class At:
    def __init__(self, ref, *index):
        self.ref, self.index = ref, index

    def now(self):
        return self.ref.at[self.index]

    def still(self):
        return self.ref.at[tuple(i if isinstance(i, slice) else 0 for i in self.index)]


ALL = slice(None)


class Exchange:
    def __init__(self, send, recv):
        self.send, self.recv, self.used, self.open = send, recv, 0, []
        self.s, self.h, self.r = (lax.axis_index(a) for a in AXES)
        self.planes = lax.axis_size("s")
        self.xn = self.h + 1 - 2 * lax.rem(self.h, 2)
        self.yn = lax.rem(self.h + 2, 4)
        self.dn = lax.rem(self.xn + 2, 4)
        self.z = lambda j: lax.rem(self.s + j, self.planes)
        self.X, self.Y, self.D = ({"h": i} for i in (self.xn, self.yn, self.dn))
        self.C = {"r": 1 - self.r}
        self.Z = [None] + [{"s": self.z(j)} for j in range(1, self.planes)]

    def greet(self, peers, meanwhile=None):
        barrier = pltpu.get_barrier_semaphore()
        for peer in peers:
            pl.semaphore_signal(barrier, inc=1, device_id=peer, device_id_type=MESH_IDS)
        if meanwhile:
            meanwhile()
        pl.semaphore_wait(barrier, len(peers))

    def slots(self, count):
        self.used += count
        return range(self.used - count, self.used)

    def copy(self, i, src, dst, peer):
        return pltpu.make_async_remote_copy(
            src_ref=src,
            dst_ref=dst,
            send_sem=self.send.at[i],
            recv_sem=self.recv.at[i],
            device_id=peer,
            device_id_type=MESH_IDS,
        )

    def put(self, i, src, dst, peer):
        self.copy(i, src.now() if isinstance(src, At) else src, dst, peer).start()
        self.open.append((i, src))

    def got(self, i, dst):
        self.copy(i, dst, dst, self.X).wait_recv()

    def close(self):
        for i, src in self.open:
            src = src.still() if isinstance(src, At) else src
            self.copy(i, src, src, self.X).wait_send()


def remote_call(kernel, cid, out_shape, in_specs, out_specs, scratch, sems, name, vmem=56 << 20):
    return pl.pallas_call(
        kernel,
        out_shape=out_shape,
        in_specs=in_specs,
        out_specs=out_specs,
        scratch_shapes=scratch
        + [pltpu.SemaphoreType.DMA((sems,)), pltpu.SemaphoreType.DMA((sems,)), pltpu.SemaphoreType.DMA((8,))],
        compiler_params=pltpu.CompilerParams(
            collective_id=cid, has_side_effects=True, vmem_limit_bytes=vmem
        ),
        name=name,
    )


ANY = pl.BlockSpec(memory_space=pl.ANY)
VMEM = pl.BlockSpec(memory_space=pltpu.VMEM)


def by_x(k, j):
    return (k + j) % 2 == 0


def act(plan, steps, m, c, last_tile):
    for (em, ec), todo in plan.items():
        if (em == ec) == last_tile:

            @pl.when(m == em if last_tile else (m == em) & (c == ec))
            def _():
                for step, k, *js in todo:
                    steps[step](k, js)


def gather_steps(ex, ins, outs, local):
    s, h, r, n = ex.s, ex.h, ex.r, ex.planes
    part = len(ins) - 1
    place = lambda k, t, c: (t, c) if k == part else (t, c, r)
    slab = lambda k, t, c: outs[k].at[place(k, t, c)]
    own = [pltpu.make_async_copy(ins[k], slab(k, s, h), local.at[k + 1]) for k in range(part + 1)]
    for c in own:
        c.start()
    iz, ix, iy, ir, ic = ([ex.slots(n) for _ in outs] for _ in range(5))

    def cross(k, j):
        ex.put(iz[k][j], ins[k], slab(k, s, h), ex.Z[j])

    def forward(k, j):
        t = ex.z(j)
        if j:
            ex.got(iz[k][n - j], slab(k, t, h))
        src = At(outs[k], *place(k, t, h)) if j else ins[k]
        ex.put(ix[k][j], src, slab(k, t, h), ex.X)
        ex.put(iy[k][j], src, slab(k, t, h), ex.Y)

    def relay(k, j):
        t = ex.z(j)
        slots, frm, peer = (ix, ex.xn, ex.Y) if by_x(k, j) else (iy, ex.yn, ex.X)
        ex.got(slots[k][j], slab(k, t, frm))
        ex.put(ir[k][j], At(outs[k], *place(k, t, frm)), slab(k, t, frm), peer)

    def across(k, j):
        t = ex.z(j)
        slots, frm = (iy, ex.yn) if by_x(k, j) else (ix, ex.xn)
        ex.got(slots[k][j], slab(k, t, frm))
        ex.got(ir[k][j], slab(k, t, ex.dn))
        if not j:
            own[k].wait()
        ex.put(ic[k][j], At(outs[k], t, ALL, r), outs[k].at[t, :, r], ex.C)

    def last():
        for j in range(n):
            for k in range(part):
                ex.got(ic[k][j], outs[k].at[ex.z(j), :, 1 - r])
            ex.got(ix[part][j], slab(part, ex.z(j), ex.xn))
            ex.got(iy[part][j], slab(part, ex.z(j), ex.yn))
        own[part].wait()

    each = lambda step: lambda k, js: [step(k, j) for j in js]
    return dict(cross=each(cross), forward=each(forward), relay=each(relay), across=each(across)), last


def by_tile(shape, step):
    height, width = shape
    if height % 48:

        @pl.loop(0, width // 768)
        def _(i):
            step(slice(None), pl.ds(pl.multiple_of(i * 768, 768), 768))
    else:

        @pl.loop(0, height // 48)
        def _(i):
            step(pl.ds(pl.multiple_of(i * 48, 48), 48), slice(None))


def reduce_steps(ins, outs, bufs, send, recv, local):
    count = len(ins)
    mine, from_c, one, two, from_z = (bufs[i * count : (i + 1) * count] for i in range(5))
    ex = Exchange(send, recv)
    s, h, r, n = ex.s, ex.h, ex.r, ex.planes
    own = [
        pltpu.make_async_copy(a.at[:, :, r], m, local.at[k]) for k, (a, m) in enumerate(zip(ins, mine))
    ]
    for c in own:
        c.start()
    ex.greet([ex.X, ex.Y, ex.C] + ex.Z[1:])
    ic, i1, i2, iz = ([ex.slots(n) for _ in ins] for _ in range(4))
    i1b = [ex.slots(n) for _ in ins]
    for k in (1, 0, 2):
        for j in range(n):
            ex.put(ic[k][j], At(ins[k], ex.z(j), ALL, 1 - r), from_c[k].at[ex.z(j)], ex.C)
    for c in own:
        c.wait()

    def add(to, *parts):
        def step(rows, cols):
            total = to[rows, cols].astype(jnp.float32)
            for part in parts:
                total += part[rows, cols].astype(jnp.float32)
            to[rows, cols] = total.astype(to.dtype)

        by_tile(to.shape, step)

    def way(k, j):
        return (ex.X, ex.xn, ex.Y, ex.yn) if by_x(k, j) else (ex.Y, ex.yn, ex.X, ex.xn)

    def first(k, js):
        m = mine[k]
        for j in js:
            t = ex.z(j)
            ex.got(ic[k][j], from_c[k].at[t])
            add(m.at[t, ex.dn], from_c[k].at[t, ex.dn])
            ex.put(i1b[k][j], At(m, t, ex.dn), one[k].at[j, 1], way(k, j)[0])
        for j in js:
            t, (peer, near, _, _) = ex.z(j), way(k, j)
            add(m.at[t, near], from_c[k].at[t, near])
            ex.put(i1[k][j], At(m, t, near), one[k].at[j, 0], peer)

    def second(k, js):
        m = mine[k]
        for j in js:
            t, (_, _, peer, other) = ex.z(j), way(k, j)
            ex.got(i1b[k][j], one[k].at[j, 1])
            add(m.at[t, other], from_c[k].at[t, other], one[k].at[j, 1])
            ex.put(i2[k][j], At(m, t, other), two[k].at[j], peer)

    def third(k, js):
        m = mine[k]
        for j in js:
            t = ex.z(j)
            ex.got(i1[k][j], one[k].at[j, 0])
            ex.got(i2[k][j], two[k].at[j])
            add(m.at[t, h], from_c[k].at[t, h], one[k].at[j, 0], two[k].at[j])
            if j:
                ex.put(iz[k][j], At(m, t, h), from_z[k].at[j], ex.Z[j])

    def last():
        for k, (m, o) in enumerate(zip(mine, outs)):
            for j in range(1, n):
                ex.got(iz[k][j], from_z[k].at[j])

            def step(rows, cols):
                total = m[s, h, rows, cols].astype(jnp.float32)
                for j in range(1, n):
                    total += from_z[k][j, rows, cols].astype(jnp.float32)
                o[rows, cols] = total

            by_tile(o.shape, step)

        ex.close()

    return ex, dict(first=first, second=second, third=third), last


HD = 64


GATHER_PLAN = {
    (0, 0): [("forward", 0, 1, 3, 2), ("relay", 1, 1, 3, 2)],
    (4, 0): [("relay", 0, 1)],
    (4, 3): [("relay", 0, 3)],
    (5, 1): [("relay", 0, 2), ("forward", 2, 1, 3, 2)],
    (5, 5): [("across", 1, 0, 1, 3, 2)],
    (7, 0): [("across", 0, 0, 1, 3, 2)],
}
GATHER_FIRST = [("forward", 1, 1, 3, 2), ("relay", 1, 0), ("relay", 0, 0), ("cross", 2, 1, 3, 2), ("forward", 2, 0)]
GATHER_START = [("cross", 1, 1, 3, 2), ("cross", 0, 1, 3, 2), ("forward", 1, 0), ("forward", 0, 0)]


SMEM = pl.BlockSpec(memory_space=pltpu.SMEM)


def forward_kernel(vectors, inv, blk, x_ref, w_ref, *refs):
    count = 3
    v_refs, refs = refs[:vectors], refs[vectors:]
    ins, refs = refs[:count], refs[count:]
    norm_ref, q_ref, kv_ref, w_out, vec_ref, xo_ref, o_ref, low_ref, lse_ref = refs[:9]
    outs = refs[9 : 9 + count]
    xa, ws, wa, wf, qt, ks, vt, os, sc, send, recv, local = refs[9 + count :]
    f32, bf16 = jnp.float32, jnp.bfloat16
    ex = Exchange(send, recv)
    s, h, r, n = ex.s, ex.h, ex.r, ex.planes
    H, U, D = xa.shape[1:]
    d, N = w_ref.shape
    W = N // 3 // H
    own = pltpu.make_async_copy(x_ref.at[s], xa.at[s, h], local.at[0])
    own.start()

    def slabs():
        lines = [v[...].astype(f32) for v in v_refs]
        lines = [v[:, i : i + d] for v in lines for i in range(0, v.shape[1], d)]
        lines = jnp.concatenate(lines + [jnp.zeros((64 - len(lines), d), f32)], axis=0).T.astype(bf16)
        for k in range(H):
            ws[k] = jnp.concatenate(
                [w_ref[:, c * D + k * W : c * D + (k + 1) * W] for c in range(3)] + [lines], axis=1
            )

    ex.greet([ex.X, ex.Y, ex.D, ex.C] + ex.Z[1:], slabs)
    iw, ix, iy, ir, iz, iwz, iwc, ik = (ex.slots(n) for _ in range(8))
    steps, last = gather_steps(ex, ins, outs, local)
    cross = lambda j: ex.put(iz[j], x_ref.at[ex.z(j)], xa.at[s, h], ex.Z[j])
    cross(1)
    for k, (peer, to) in enumerate(((ex.X, ex.xn), (ex.Y, ex.yn), (ex.D, ex.dn))):
        ex.put(iw[k], ws.at[to], wa.at[s, h, r], peer)
    wa[s, h, r] = ws[h]
    own.wait()

    def forward(j):
        t = ex.z(j)
        if j:
            ex.got(iz[n - j], xa.at[t, h])
        if j in after:
            cross(after[j])
        ex.put(ix[j], xa.at[t, h], xa.at[t, h], ex.X)
        ex.put(iy[j], xa.at[t, h], xa.at[t, h], ex.Y)

    def relay(j):
        t = ex.z(j)
        slots, frm, peer = (ix, ex.xn, ex.Y) if by_x(0, j) else (iy, ex.yn, ex.X)
        ex.got(slots[j], xa.at[t, frm])
        ex.put(ir[j], xa.at[t, frm], xa.at[t, frm], peer)

    def weights(j):
        if j:
            ex.got(iwz[n - j], wa.at[ex.z(j), :, r])
        ex.put(iwc[j], wa.at[ex.z(j), :, r], wa.at[ex.z(j), :, r], ex.C)

    after = {3: 3, 1: 2}
    forward(0)
    for k, frm in enumerate((ex.xn, ex.yn, ex.dn)):
        ex.got(iw[k], wa.at[s, frm, r])
    forward(3)
    relay(0)
    forward(1)
    for j in range(1, n):
        ex.put(iwz[j], wa.at[s, :, r], wa.at[s, :, r], ex.Z[j])
    weights(0)
    relay(3)
    relay(1)
    forward(2)
    for j in (1, 3, 2):
        weights(j)
    for step, k, *js in GATHER_START:
        steps[step](k, js)
    for j in range(n):
        ex.got(iwc[j], wa.at[ex.z(j), :, 1 - r])
    rows = H * 2 * d
    for t in range(n):
        block = wa[t].astype(f32).reshape(rows, N // H + 64)
        wf[t * rows : (t + 1) * rows] = block
    vec_ref[...] = wf[:, N // H :].T[:16]
    w = wf[:, : N // H].astype(bf16)
    w_out[...] = w
    gain, bias = vec_ref[0:1], vec_ref[1:2]

    def mine(row):
        picked = jnp.zeros((1, W), f32)
        for k in range(H):
            picked = jnp.where(h == k, vec_ref[row : row + 1, k * W : (k + 1) * W], picked)
        return picked

    bq, bv = mine(2), mine(3)

    def batch(j):
        t = ex.z(j)
        slots, frm = (iy, ex.yn) if by_x(0, j) else (ix, ex.xn)
        ex.got(slots[j], xa.at[t, frm])
        ex.got(ir[j], xa.at[t, ex.dn])
        x = xa[t].reshape(H * U, D).astype(f32)
        normed = layer_norm(x, gain, bias).astype(bf16)
        pairs = pl.ds(t * H, H)
        norm_ref[t] = normed.reshape(H, U, D)
        mixed = jnp.dot(normed, w, preferred_element_type=f32)
        q = (mixed[:, :W] + bq).astype(bf16) * jnp.asarray(0.125, bf16)
        q_ref[pairs] = q.reshape(H, U, W)
        kv = jnp.concatenate([mixed[:, W : 2 * W], mixed[:, 2 * W :] + bv], axis=1).astype(bf16)
        kv_ref[pairs, 0] = kv.reshape(H, U, 2 * W)
        ex.put(ik[j], kv_ref.at[pairs, 0], kv_ref.at[pairs, 1], ex.C)

    relay(2)
    batch(0)
    batch(3)
    batch(1)
    batch(2)
    for step, k, *js in GATHER_FIRST:
        steps[step](k, js)
    xo_ref[...] = xa[:, h]
    for j in (0, 1, 3, 2):
        ex.got(ik[j], kv_ref.at[pl.ds(ex.z(j) * H, H), 1])

    npair = inv.shape[0]
    nh = W // HD
    B = 2 * U
    TQ, TK = 2 * U, 2 * B

    @pl.loop(0, npair, unroll=2)
    def _(i):
        p = inv[i]
        qt[:, pl.ds(pl.multiple_of(i * U, U), U)] = q_ref[p].T
        kv = kv_ref[p].reshape(B, 2 * W)
        for h in range(nh):
            ks[h, pl.ds(i * B, B), :] = kv[:, h * HD : (h + 1) * HD]
        vct = kv[:, W:].T
        for h in range(nh):
            vt[h, 0:HD, pl.ds(pl.multiple_of(i * B, B), B)] = vct[h * HD : (h + 1) * HD]
            vt[h, HD:, pl.ds(pl.multiple_of(i * B, B), B)] = jnp.ones((vt.shape[1] - HD, B), vt.dtype)

    def scores(m, c, carry, masked):
        out = []
        rows = pl.ds(pl.multiple_of(c * TK, TK), TK)
        for h in range(nh):
            qh = qt[h * HD : (h + 1) * HD, pl.ds(pl.multiple_of(m * TQ, TQ), TQ)]
            s = jnp.dot(ks[h, rows, :], qh, preferred_element_type=jnp.float32)
            if masked:
                row = lax.broadcasted_iota(jnp.int32, s.shape, 0)
                col = lax.broadcasted_iota(jnp.int32, s.shape, 1)
                s = jnp.where((row >= B) & (col < U), NEG, s)
            sc[h, rows, :] = s
            out.append(jnp.maximum(carry[h], jnp.max(s.reshape(TK // 8, 8, TQ), axis=0)))
        return tuple(out)

    def values(c, carry, tops):
        out = []
        rows = pl.ds(pl.multiple_of(c * TK, TK), TK)
        for h in range(nh):
            p = jnp.exp(sc[h, rows, :] - tops[h]).astype(jnp.bfloat16)
            out.append(carry[h] + jnp.dot(vt[h, :, rows], p, preferred_element_type=jnp.float32))
        return tuple(out)

    @pl.loop(0, npair // 2)
    def _(m):
        tops = tuple(jnp.full((8, TQ), NEG, jnp.float32) for _ in range(nh))
        tops = lax.fori_loop(0, m, lambda c, x: scores(m, c, x, False), tops)
        tops = [jnp.max(t, axis=0, keepdims=True) for t in scores(m, m, tops, True)]

        def step(c, x):
            x = values(c, x, tops)
            act(GATHER_PLAN, steps, m, c, False)
            return x

        init = tuple(jnp.zeros((vt.shape[1], TQ), jnp.float32) for _ in range(nh))
        carry = values(m, lax.fori_loop(0, m, step, init), tops)
        carry = list(zip(tops, carry))
        rows = []
        for h in range(nh):
            mx, acc = carry[h]
            tot = acc[HD : HD + 1]
            rows.append(acc[:HD] / tot)
            lse_ref[h : h + 1, pl.ds(pl.multiple_of(m * TQ, TQ), TQ)] = mx + jnp.log(tot)
        os[pl.ds(pl.multiple_of(m * TQ, TQ), TQ), :] = jnp.concatenate(rows, axis=0).T
        act(GATHER_PLAN, steps, m, m, True)

    @pl.loop(0, npair)
    def _(p):
        o = os[pl.ds(blk[p] * U, U), :]
        o_ref[pl.ds(pl.multiple_of(p * U, U), U), :] = o
        low_ref[pl.ds(pl.multiple_of(p * U, U), U), :] = o.astype(jnp.bfloat16)

    last()
    ex.close()


def forward(inv, blk, x, w, vectors, *weights):
    S, U, D = x.shape
    d, N = w.shape
    H, Q = (lax.axis_size(a) for a in AXES[1:])
    W = N // 3 // H
    npair = S * H
    R, K = npair * U, npair * Q * U
    nh = W // HD
    f32, bf16 = jnp.float32, jnp.bfloat16
    n = len(weights)
    shape = jax.ShapeDtypeStruct
    return remote_call(
        partial(forward_kernel, len(vectors)),
        0,
        [
            shape((S, H, U, D), bf16),
            shape((npair, U, W), bf16),
            shape((npair, Q, U, 2 * W), bf16),
            shape((D, N // H), bf16),
            shape((16, D), f32),
            shape((S, U, D), bf16),
            shape((R, W), f32),
            shape((R, W), bf16),
            shape((8, R), f32),
        ]
        + [shape((S, H, Q) + a.shape, a.dtype) for a in weights[:-1]]
        + [shape((S, H) + weights[-1].shape, bf16)],
        [SMEM] * 2 + [ANY] + [VMEM] * (1 + len(vectors)) + [ANY] * n,
        [VMEM] * 9 + [ANY] * n,
        [
            pltpu.VMEM((S, H, U, D), bf16),
            pltpu.VMEM((H, d, N // H + 64), bf16),
            pltpu.VMEM((S, H, Q, d, N // H + 64), bf16),
            pltpu.VMEM((D, N // H + 64), f32),
            pltpu.VMEM((W, R), bf16),
            pltpu.VMEM((nh, K, HD), bf16),
            pltpu.VMEM((nh, HD + 16, K), bf16),
            pltpu.VMEM((R, W), f32),
            pltpu.VMEM((nh, K, 2 * U), f32),
        ],
        8 * S + 5 * S * n,
        "forward",
    )(inv, blk, x, w, *vectors, *weights)


REDUCE_PLAN = {
    (7, 1): [("first", 1, 1, 2, 3, 0)],
    (7, 6): [("second", 1, 1, 2, 3, 0)],
    (7, 7): [("first", 0, 1, 2, 3, 0)],
    (5, 3): [("third", 1, 1, 2, 3, 0)],
    (5, 4): [("second", 0, 1, 2, 3, 0)],
    (4, 0): [("first", 2, 1, 2, 3, 0)],
    (3, 1): [("third", 0, 1, 2, 3, 0)],
    (3, 2): [("second", 2, 1, 2, 3, 0)],
    (2, 1): [("third", 2, 1, 2, 3, 0)],
}


def attend_back_kernel(count, inv, blk, q_ref, kv_ref, g_ref, o_ref, lse_ref, out_ref, *refs):
    ins, gm_ref, lo_ref, outs = refs[:count], refs[count], refs[count + 1], refs[count + 2 : 2 * count + 2]
    bufs = refs[2 * count + 2 : 7 * count + 2]
    qt, gt, qx, gx, ks, vs, kt, delta, dkv, dqs, over, back, send, recv, local = refs[7 * count + 2 :]
    npair, U, W = q_ref.shape
    nh = W // HD
    B = kv_ref.shape[1]
    TQ, TK = 2 * U, 2 * B
    f32, bf16 = jnp.float32, jnp.bfloat16
    ex, steps, last = reduce_steps(ins, outs, bufs, send, recv, local)
    swap = ex.slots(npair // 2)
    il = ex.slots(ex.planes)
    keep = pltpu.make_async_copy(out_ref.at[ex.s], lo_ref.at[ex.s], local.at[count])
    keep.start()
    for j in range(1, ex.planes):
        ex.put(il[j], out_ref.at[ex.z(j)], lo_ref.at[ex.s], ex.Z[j])

    @pl.loop(0, npair, unroll=2)
    def _(i):
        p = inv[i]
        qc = q_ref[p]
        gc = g_ref[p]
        oc = o_ref[pl.ds(p * U, U), :]
        cols = pl.ds(pl.multiple_of(i * U, U), U)
        qt[:, cols] = qc.T
        gt[:, cols] = gc.T
        prod = (oc * gc.astype(f32)).T
        zero = jnp.zeros((U, HD), bf16)
        for h in range(nh):
            delta[h : h + 1, cols] = jnp.sum(prod[h * HD : (h + 1) * HD], axis=0, keepdims=True)
            qx[h, pl.ds(i * U, U), :] = jnp.concatenate([zero, qc[:, h * HD : (h + 1) * HD]], axis=1)
            gx[h, pl.ds(i * U, U), :] = jnp.concatenate([gc[:, h * HD : (h + 1) * HD], zero], axis=1)
        kv = kv_ref[p]
        kc, vc = kv[:, :W], kv[:, W:]
        kt[:, pl.ds(pl.multiple_of(i * B, B), B)] = kc.T
        for h in range(nh):
            ks[h, pl.ds(i * B, B), :] = kc[:, h * HD : (h + 1) * HD]
            vs[h, pl.ds(i * B, B), :] = vc[:, h * HD : (h + 1) * HD]

    dkv[...] = jnp.zeros_like(dkv)

    def tile(m, c, carry, masked):
        out = []
        qcols = pl.ds(pl.multiple_of(m * TQ, TQ), TQ)
        krows = pl.ds(pl.multiple_of(c * TK, TK), TK)
        for h in range(nh):
            hs = slice(h * HD, (h + 1) * HD)
            s = jnp.dot(ks[h, krows, :], qt[hs, qcols], preferred_element_type=f32)
            p = jnp.exp(s - lse_ref[h : h + 1, qcols])
            if masked:
                row = lax.broadcasted_iota(jnp.int32, s.shape, 0)
                col = lax.broadcasted_iota(jnp.int32, s.shape, 1)
                p = jnp.where((row >= B) & (col < U), 0.0, p)
            dp = jnp.dot(vs[h, krows, :], gt[hs, qcols], preferred_element_type=f32)
            ds = (p * (dp - delta[h : h + 1, qcols])).astype(bf16)
            dkv[h, krows, :] += jnp.dot(
                p.astype(bf16), gx[h, qcols, :], preferred_element_type=f32
            ) + jnp.dot(ds, qx[h, qcols, :], preferred_element_type=f32)
            out.append(carry[h] + jnp.dot(kt[hs, krows], ds, preferred_element_type=f32))
        return tuple(out)

    def halves(b, half):
        rows = pl.ds(pl.multiple_of(b * B + half * U, U), U)
        parts = [dkv[h, rows, :] for h in range(nh)]
        return jnp.concatenate([x[:, HD:] for x in parts] + [x[:, :HD] for x in parts], axis=1)

    @pl.loop(0, npair // 2)
    def _(turn):
        m = npair // 2 - 1 - turn
        init = tuple(jnp.zeros((HD, TQ), f32) for _ in range(nh))

        def step(c, x):
            x = tile(m, c, x, False)
            act(REDUCE_PLAN, steps, m, c, False)
            return x

        carry = lax.fori_loop(0, m, step, init)
        carry = tile(m, m, carry, True)
        dqs[pl.ds(pl.multiple_of(m * TQ, TQ), TQ), :] = (jnp.concatenate(carry, axis=0).T * 0.125).astype(bf16)
        for k in range(2):
            over[2 * m + k] = halves(2 * m + k, 1).astype(bf16)
        ex.copy(swap[0] + m, over.at[pl.ds(2 * m, 2)], back.at[pl.ds(2 * m, 2)], ex.C).start()
        act(REDUCE_PLAN, steps, m, m, True)

    @pl.loop(0, npair // 2)
    def _(m):
        moved = ex.copy(swap[0] + m, over.at[pl.ds(2 * m, 2)], back.at[pl.ds(2 * m, 2)], ex.C)
        moved.wait_recv()
        moved.wait_send()

    @pl.loop(0, npair)
    def _(p):
        b = blk[p]
        rows = pl.ds(b * B, U)
        parts = [dkv[h, rows, :] for h in range(nh)]
        own = jnp.concatenate([x[:, HD:] for x in parts] + [x[:, :HD] for x in parts], axis=1)
        own = (own + back[b].astype(f32)).astype(bf16)
        gm_ref[p] = jnp.concatenate([dqs[pl.ds(b * U, U), :], own], axis=1)

    for j in range(1, ex.planes):
        ex.got(il[ex.planes - j], lo_ref.at[ex.z(j)])
    keep.wait()
    last()


def attend_back(inv, blk, q, kv, g, o, lse, out, *grads):
    npair, U, W = q.shape
    R, K = npair * U, npair * kv.shape[1]
    nh = W // HD
    S, H, Q = (lax.axis_size(a) for a in AXES)
    n = len(grads)
    f32, bf16 = jnp.float32, jnp.bfloat16
    tails = [a.shape[3:] for a in grads]
    buffers = [[pltpu.VMEM(lead + t, bf16) for t in tails] for lead in ((S, H), (S, H), (S, 2), (S,), (S,))]
    return remote_call(
        partial(attend_back_kernel, n),
        2,
        [jax.ShapeDtypeStruct((npair, R // npair, 3 * W), bf16), jax.ShapeDtypeStruct(out.shape, bf16)]
        + [jax.ShapeDtypeStruct(t, f32) for t in tails],
        [SMEM] * 2 + [VMEM] * 5 + [ANY] * (n + 1),
        [VMEM, ANY] + [VMEM] * n,
        sum(buffers, [])
        + [
            pltpu.VMEM((W, R), bf16),
            pltpu.VMEM((W, R), bf16),
            pltpu.VMEM((nh, R, 2 * HD), bf16),
            pltpu.VMEM((nh, R, 2 * HD), bf16),
            pltpu.VMEM((nh, K, HD), bf16),
            pltpu.VMEM((nh, K, HD), bf16),
            pltpu.VMEM((W, K), bf16),
            pltpu.VMEM((8, R), f32),
            pltpu.VMEM((nh, K, 2 * HD), f32),
            pltpu.VMEM((R, W), bf16),
            pltpu.VMEM((npair, R // npair, 2 * W), bf16),
            pltpu.VMEM((npair, R // npair, 2 * W), bf16),
        ],
        5 * S * n + npair // 2 + S,
        "attend_back",
        60 << 20,
    )(inv, blk, q, kv, g, o, lse, out, *grads)


def middle_kernel(
    low_ref, x_ref, g_ref, vec_ref, bf_ref, fc_ref, proj_ref, wo_ref,
    lo_ref, gmid_ref, small_ref, ga_ref, gfc_ref, gproj_ref, gout_ref,
    ra, fc, wp, wo_in, wf, wo, act_ref, dpre, deriv, g, att, mid, z_ref, n2, n2t, y, t2, gb, sb, gfc, gproj, gout,
    send, recv, local,
):
    f32, bf16 = jnp.float32, jnp.bfloat16
    ex = Exchange(send, recv)
    s, h, r, n = ex.s, ex.h, ex.r, ex.planes
    H, U, W = low_ref.shape[1:]
    R, D = att.shape
    d = fc.shape[3]
    loads = [
        pltpu.make_async_copy(a, b, local.at[i])
        for i, (a, b) in enumerate(
            (
                (wo_ref, wo_in),
                (proj_ref.at[:, h], wp.at[:, h, r]),
                (fc_ref, fc),
                (low_ref.at[:, h], ra.at[h]),
                (g_ref.at[s], g.at[s]),
                (proj_ref.at[:, ex.xn], wp.at[:, ex.xn, r]),
                (proj_ref.at[:, ex.yn], wp.at[:, ex.yn, r]),
            )
        )
    ]
    for c in loads:
        c.start()
    ex.greet([ex.X, ex.Y, ex.D, ex.C] + ex.Z[1:])
    there, back = ex.slots(3), ex.slots(3)
    ir, ic, ig = (ex.slots(n) for _ in range(3))
    sides = ((ex.X, ex.xn), (ex.Y, ex.yn), (ex.D, ex.dn))
    for k, (peer, to) in enumerate(sides):
        ex.put(there[k], low_ref.at[:, to], ra.at[h], peer)
    for j in range(n):
        frm, peer = (ex.xn, ex.Y) if by_x(0, j) else (ex.yn, ex.X)
        ex.put(ir[j], proj_ref.at[ex.z(j), frm], wp.at[ex.z(j), frm, r], peer)
    for j in range(1, n):
        ex.put(ig[j], g_ref.at[ex.z(j)], g.at[s], ex.Z[j])

    def across(j):
        ex.got(ir[j], wp.at[ex.z(j), ex.dn, r])
        ex.put(ic[j], wp.at[ex.z(j), :, r], wp.at[ex.z(j), :, r], ex.C)

    dot = partial(jnp.dot, preferred_element_type=f32)
    dot_nt = lambda a, b: lax.dot_general(a, b, (((1,), (1,)), ((), ())), preferred_element_type=f32)
    dot_tn = lambda a, b: lax.dot_general(a, b, (((0,), (0,)), ((), ())), preferred_element_type=f32)
    loads[0].wait()
    wo[...] = wo_in[...].astype(f32).reshape(D, D).astype(bf16)
    loads[2].wait()

    @pl.loop(0, n)
    def _(b):
        cols = pl.ds(pl.multiple_of(b * D, D), D)
        wf[b] = fc[:, :, :, :, cols].astype(f32).reshape(D, D).astype(bf16)

    y[...] = jnp.zeros_like(y)
    t2[...] = jnp.zeros_like(t2)
    loads[3].wait()
    for k, (peer, frm) in enumerate(sides):
        ex.got(there[k], ra.at[frm])
    att[...] = jnp.concatenate([ra[k].reshape(R, W) for k in range(H)], axis=1)
    m = x_ref[...].astype(f32) + dot(att[...], wo[...]) + vec_ref[4:5]
    mid[...] = m
    center = m - jnp.mean(m, axis=-1, keepdims=True)
    rstd = lax.rsqrt(jnp.mean(center * center, axis=-1, keepdims=True) + 1e-05)
    z = center * rstd
    z_ref[...] = z
    normed = (z * vec_ref[5:6] + vec_ref[6:7]).astype(bf16)
    n2[...] = normed
    n2t[...] = normed.T
    slope = math.sqrt(2.0 / math.pi)

    def up(b):
        cols = slice(b * D, (b + 1) * D)
        pre = dot(n2[...], wf[b]) + bf_ref[0:1, cols]
        square = pre * pre
        tanh = jnp.tanh(slope * pre * (1.0 + 0.044715 * square))
        half = 0.5 * (1.0 + tanh)
        act_ref[b] = (pre * half).astype(bf16)
        deriv[b] = half + 0.5 * pre * (1.0 - tanh * tanh) * (slope * (1.0 + 3 * 0.044715 * square))

    up(0)
    for i in (1, 5, 6):
        loads[i].wait()
    across(0)
    across(1)
    up(1)
    across(2)
    across(3)
    up(2)
    up(3)
    loads[4].wait()
    for j in range(1, n):
        ex.got(ig[n - j], g.at[ex.z(j)])

    def down(j):
        b = ex.z(j)
        ex.got(ic[j], wp.at[b, :, 1 - r])
        pre = dot_nt(g[...].reshape(R, D), wp[b].reshape(D, D)) * deriv[b]
        dpre[b] = pre.astype(bf16)
        small_ref[pl.ds(b + 4, 1)] = jnp.sum(dpre[b].astype(f32), axis=0, keepdims=True)
        t2[...] += dot_nt(dpre[b], wf[b])

    for j in range(n):
        down(j)
    t, z = t2[...], z_ref[...]
    g32 = g[...].reshape(R, D).astype(f32)
    e = t * vec_ref[5:6]
    inner = e - jnp.mean(e, axis=-1, keepdims=True) - z * jnp.mean(e * z, axis=-1, keepdims=True)
    gm = g32 + inner * rstd
    gmid_ref[...] = gm
    gb[...] = gm.astype(bf16)
    ga = dot_nt(gb[...], wo[...]).astype(bf16)
    for k in range(H):
        sb[k] = ga[:, k * W : (k + 1) * W].reshape(sb.shape[1:])
    for k, (peer, to) in enumerate(sides):
        ex.put(back[k], sb.at[to], ga_ref.at[:, h], peer)
    mine = pltpu.make_async_copy(sb.at[h], ga_ref.at[:, h], local.at[3])
    mine.start()
    stores = []

    def store(src, dst):
        stores.append(pltpu.make_async_copy(src, dst, local.at[4 + len(stores)]))
        stores[-1].start()

    for b in range(n):
        grad = g[...].reshape(R, D)
        gproj[b] = dot_tn(act_ref[b], grad).astype(bf16).reshape(gproj.shape[1:])
        gfc[:, :, :, :, b * D : (b + 1) * D] = dot(n2t[...], dpre[b]).reshape(gfc.shape[:4] + (D,)).astype(bf16)
        y[...] += dot(act_ref[b], wp[b].reshape(D, D))
    store(gproj, gproj_ref)
    store(gfc, gfc_ref)
    gout[...] = dot_tn(att[...], gb[...]).reshape(gout.shape).astype(bf16)
    store(gout, gout_ref)
    lo_ref[...] = (mid[...] + y[...] + vec_ref[7:8]).astype(bf16)
    small_ref[1:2] = jnp.sum(t2[...] * z_ref[...], axis=0, keepdims=True)
    small_ref[2:3] = jnp.sum(t2[...], axis=0, keepdims=True)
    small_ref[0:1] = jnp.sum(gb[...].astype(f32), axis=0, keepdims=True)
    small_ref[3:4] = jnp.sum(g[...].reshape(R, D).astype(f32), axis=0, keepdims=True)
    for k, (peer, frm) in enumerate(sides):
        ex.got(back[k], ga_ref.at[:, frm])
    for c in stores + [mine]:
        c.wait()
    ex.close()


def middle(low, x, g, vecs, bias, fc, proj, wo):
    S, H, U, W = low.shape
    R, D = x.shape
    whole = fc.shape[:3] + proj.shape[2:]
    f32, bf16 = jnp.float32, jnp.bfloat16
    vm = pltpu.VMEM
    return remote_call(
        middle_kernel,
        4,
        [
            jax.ShapeDtypeStruct((R, D), bf16),
            jax.ShapeDtypeStruct((R, D), f32),
            jax.ShapeDtypeStruct((8, D), f32),
            jax.ShapeDtypeStruct(low.shape, bf16),
            jax.ShapeDtypeStruct(fc.shape, bf16),
            jax.ShapeDtypeStruct(whole, bf16),
            jax.ShapeDtypeStruct(wo.shape, bf16),
        ],
        [ANY, VMEM, ANY, VMEM, VMEM] + [ANY] * 3,
        [VMEM] * 3 + [ANY] * 4,
        [
            vm((H, S, U, W), bf16),
            vm(fc.shape, bf16),
            vm(whole, bf16),
            vm(wo.shape, bf16),
            vm((S, D, D), bf16),
            vm((D, D), bf16),
            vm((S, R, D), bf16),
            vm((S, R, D), bf16),
            vm((S, R, D), f32),
            vm((S, U, D), bf16),
            vm((R, D), bf16),
            vm((R, D), f32),
            vm((R, D), f32),
            vm((R, D), bf16),
            vm((D, R), bf16),
            vm((R, D), f32),
            vm((R, D), f32),
            vm((R, D), bf16),
            vm((H, S, U, W), bf16),
            vm(fc.shape, bf16),
            vm(whole, bf16),
            vm(wo.shape, bf16),
        ],
        6 + 3 * S,
        "middle",
        60 << 20,
    )(low, x, g, vecs, bias, fc, proj, wo)


def norm_back(x, t, gain, grad):
    mean = jnp.mean(x, axis=-1, keepdims=True)
    center = x - mean
    rstd = lax.rsqrt(jnp.mean(center * center, axis=-1, keepdims=True) + 1e-05)
    z = center * rstd
    e = t * gain
    inner = e - jnp.mean(e, axis=-1, keepdims=True) - z * jnp.mean(e * z, axis=-1, keepdims=True)
    return grad + rstd * inner


def finish_kernel(
    gm_ref, w_ref, norm_ref, x_ref, gmid_ref, line_ref, small_ref,
    gh_ref, gqkv_ref, own_ref,
    gq_ref, t_ref, one, two, hid, gw, gw_c, gw_z, gw_sum, vec, send, recv, local,
):
    f32, bf16 = jnp.float32, jnp.bfloat16
    ex = Exchange(send, recv)
    s, h, r, n = ex.s, ex.h, ex.r, ex.planes
    half = n // 2
    H, N = gm_ref.shape[1], gm_ref.shape[3]
    U, D = t_ref.shape[2], t_ref.shape[3]
    W = N // 3
    d = gw.shape[3]
    ex.greet([ex.X, ex.Y, ex.D, ex.C] + ex.Z[1:])
    i1, i1b, i2, ih, ic, iz, iq = (ex.slots(n) for _ in range(7))
    iv = ex.slots(3 + n)
    acc = [jnp.zeros((1, D), f32), jnp.zeros((1, D), f32)]
    way = lambda j: (ex.X, ex.xn, ex.Y, ex.yn) if by_x(0, j) else (ex.Y, ex.yn, ex.X, ex.xn)

    def product(j, pair):
        t = ex.z(j)
        g = jnp.concatenate([gm_ref[t, to] for to in pair], axis=0)
        prod = lax.dot_general(g, w_ref[...], (((1,), (1,)), ((), ())), preferred_element_type=f32)
        for k, to in enumerate(pair):
            part = prod[k * U : (k + 1) * U]
            t_ref[t, to] = part.astype(bf16)
            acc[0] += jnp.sum(part * norm_ref[t, to].astype(f32), axis=0, keepdims=True)
            acc[1] += jnp.sum(part, axis=0, keepdims=True)

    def leave(j):
        peer, near, _, _ = way(j)
        ex.put(i1b[j], t_ref.at[ex.z(j), ex.dn], one.at[j, 1], peer)
        ex.put(i1[j], t_ref.at[ex.z(j), near], one.at[j, 0], peer)

    def relay(j):
        t = ex.z(j)
        _, _, peer, other = way(j)
        ex.got(i1b[j], one.at[j, 1])
        t_ref[t, other] = (t_ref[t, other].astype(f32) + one[j, 1].astype(f32)).astype(bf16)
        ex.put(i2[j], t_ref.at[t, other], two.at[j], peer)

    g_all = gm_ref[...].reshape(n * H * U, N)
    def qkv_rows(t0):
        width = H * 2 * d
        nt = norm_ref[:, :, :, t0 * width : (t0 + half) * width].reshape(n * H * U, half * width)
        part = lax.dot_general(nt, g_all, (((0,), (0,)), ((), ())), preferred_element_type=f32)
        gw[t0 : t0 + half] = part.reshape(half, H, 2, d, N).astype(bf16)
        for t in range(t0, t0 + half):
            ex.put(ic[t], gw.at[t, :, 1 - r], gw_c.at[t], ex.C)

    def done(j):
        t = ex.z(j)
        ex.got(i1[j], one.at[j, 0])
        ex.got(i2[j], two.at[j])
        total = t_ref[t, h].astype(f32) + one[j, 0].astype(f32) + two[j].astype(f32)
        hid[t] = norm_back(x_ref[t].astype(f32), total, line_ref[0:1], gmid_ref[t]).astype(bf16)
        if j:
            ex.put(ih[j], hid.at[t], gh_ref.at[s], ex.Z[j])

    for j in (1, 2):
        product(j, (ex.dn, way(j)[1]))
        leave(j)
    qkv_rows(0)
    qkv_rows(half)
    for j in (1, 2):
        product(j, (way(j)[3], h))
    for t in range(n):
        ex.got(ic[t], gw_c.at[t])
        gw_c[t] = (gw_c[t].astype(f32) + gw[t, :, r].astype(f32)).astype(bf16)
    for j in range(1, n):
        ex.put(iz[j], gw_c.at[ex.z(j)], gw_z.at[s], ex.Z[j])
    relay(1)
    relay(2)
    for j in (3, 0):
        product(j, (ex.dn, way(j)[1]))
        leave(j)
    for j in (3, 0):
        product(j, (way(j)[3], h))
    cols = jnp.sum(g_all.astype(f32), axis=0, keepdims=True)
    lane = lax.broadcasted_iota(jnp.int32, (1, D), 1) // W

    def placed(c):
        return jnp.where(lane == h, jnp.concatenate([c] * H, axis=1), 0.0)

    vec[0, 0:1] = acc[0]
    vec[0, 1:2] = acc[1]
    vec[0, 2:3] = placed(cols[:, :W])
    vec[0, 3:4] = placed(cols[:, 2 * W :])
    vec[0, 4:8] = jnp.zeros((4, D), f32)
    vec[0, 8:] = small_ref[...]
    ex.put(iv[0], vec.at[0], vec.at[1], ex.C)

    done(1)
    done(2)
    ex.got(iv[0], vec.at[1])
    vec[2] = vec[0] + vec[1]
    ex.put(iv[1], vec.at[2], vec.at[3], ex.X)
    relay(3)
    relay(0)
    ex.got(iv[1], vec.at[3])
    vec[4] = vec[2] + vec[3]
    ex.put(iv[2], vec.at[4], vec.at[5], ex.Y)
    total = gw_c[s].astype(f32)
    for j in range(1, n):
        ex.got(iz[n - j], gw_z.at[ex.z(j)])
        total += gw_z[ex.z(j)].astype(f32)
    gw_sum[...] = total
    for k, (peer, to) in enumerate(((ex.X, ex.xn), (ex.Y, ex.yn), (ex.D, ex.dn))):
        ex.put(iq[k], gw_sum.at[to], gq_ref.at[h], peer)
    mine = pltpu.make_async_copy(gw_sum.at[h], gq_ref.at[h], local.at[2])
    mine.start()
    ex.got(iv[2], vec.at[5])
    vec[6] = vec[4] + vec[5]
    for j in range(1, n):
        ex.put(iv[2 + j], vec.at[6], vec.at[6 + j], ex.Z[j])
    done(3)
    done(0)
    own = pltpu.make_async_copy(hid.at[s], gh_ref.at[s], local.at[1])
    own.start()
    for j in range(1, n):
        ex.got(iv[2 + j], vec.at[6 + j])
    sums = vec[6] + vec[7] + vec[8] + vec[9]
    gain = (sums[0:1] - line_ref[1:2] * sums[1:2]) / line_ref[0:1]
    rows = jnp.concatenate([gain, sums[1:12], jnp.zeros((4, D), f32)], axis=0)
    wide = jnp.zeros((1, D), f32)
    for k in range(n):
        wide = jnp.where(s == k, sums[12 + k : 13 + k], wide)
    at = h * 2 + r
    begin = (s * H * 2 + at) * d
    own_ref[...] = pltpu.roll(rows, lax.rem(D - begin, D), 1)[:, :128]
    own_ref[12:13] = pltpu.roll(jnp.broadcast_to(wide, (8, D)), lax.rem(D - at * n * d, D), 1)[0:1, :128]
    for k, frm in enumerate((ex.xn, ex.yn, ex.dn)):
        ex.got(iq[k], gq_ref.at[frm])
    mine.wait()
    for k in range(H):
        for c in range(3):
            gqkv_ref[:, c * D + k * W : c * D + (k + 1) * W] = gq_ref[k, :, c * W : (c + 1) * W]
    for j in range(1, n):
        ex.got(ih[n - j], gh_ref.at[ex.z(j)])
    own.wait()
    ex.close()


def finish(gm, w, norm, x, gmid, lines, small):
    S, H, U, N = gm.shape
    D = w.shape[0]
    Q = lax.axis_size("r")
    d = D // (S * H * Q)
    f32, bf16 = jnp.float32, jnp.bfloat16
    return remote_call(
        finish_kernel,
        3,
        [
            jax.ShapeDtypeStruct((S, U, D), bf16),
            jax.ShapeDtypeStruct((d, H * N), f32),
            jax.ShapeDtypeStruct((16, 128), f32),
        ],
        [VMEM] * 7,
        [ANY, VMEM, VMEM],
        [
            pltpu.VMEM((H, d, N), f32),
            pltpu.VMEM((S, H, U, D), bf16),
            pltpu.VMEM((S, 2, U, D), bf16),
            pltpu.VMEM((S, U, D), bf16),
            pltpu.VMEM((S, U, D), bf16),
            pltpu.VMEM((S, H, Q, d, N), bf16),
            pltpu.VMEM((S, H, d, N), bf16),
            pltpu.VMEM((S, H, d, N), bf16),
            pltpu.VMEM((H, d, N), f32),
            pltpu.VMEM((10, 16, D), f32),
        ],
        8 * S + 3,
        "finish",
    )(gm, w, norm, x, gmid, lines, small)


def planes(
    hidden_in,
    block_pairs,
    ln1_gain,
    ln1_bias,
    qkv_weight,
    query_bias,
    value_bias,
    out_weight,
    out_bias,
    ln2_gain,
    ln2_bias,
    fc_weight,
    fc_bias,
    proj_weight,
    proj_bias,
    out_grad,
):
    f32, bf16 = jnp.float32, jnp.bfloat16
    s, h, r = (lax.axis_index(a) for a in AXES)
    S, H, Q = (lax.axis_size(a) for a in AXES)
    rows, D = hidden_in.shape
    U = rows // SEQS
    W = D // H
    bfn = fc_bias.shape[0]
    d = qkv_weight.shape[0]
    lines = [ln1_gain, ln1_bias, query_bias, value_bias, out_bias, ln2_gain, ln2_bias, proj_bias, fc_bias]
    blk = block_pairs[::2]
    blk = jnp.where(s % 2 == 0, blk, blk.shape[0] - 1 - blk)
    blk = blk.astype(jnp.int32)
    npair = blk.shape[0]
    inv = jnp.sum(
        jnp.where(blk[None, :] == jnp.arange(npair)[:, None], jnp.arange(npair)[None, :], 0), axis=1
    ).astype(jnp.int32)
    normed, q_all, kv_all, w_h, vecs, x_own, att, att_low, lse, w_fc, w_out, w_proj = forward(
        inv,
        blk,
        hidden_in.reshape(S, U, D),
        qkv_weight,
        [v[None] for v in lines],
        fc_weight,
        out_weight,
        proj_weight,
    )
    bf = vecs[8 : 8 + bfn // d].reshape(-1, S * H * Q, d).swapaxes(0, 1).reshape(-1)
    layer_out, grad_middle, small, g_att, grad_fc, grad_proj, grad_wout = middle(
        att_low.reshape(S, H, U, W),
        x_own.reshape(rows, D),
        out_grad.reshape(S, U, D),
        vecs,
        jnp.broadcast_to(bf[None], (8, bf.shape[0])),
        w_fc,
        w_proj,
        w_out,
    )
    grad_mixed, layer_out, gfc, gproj, gout = attend_back(
        inv,
        blk,
        q_all,
        kv_all.reshape(npair, Q * U, 2 * W),
        g_att.reshape(npair, U, W),
        att,
        lse,
        layer_out.reshape(S, U, D),
        grad_fc,
        grad_proj,
        grad_wout,
    )
    grad_hidden, gq, own = finish(
        grad_mixed.reshape(S, H, U, 3 * W),
        w_h,
        normed,
        x_own,
        grad_middle.reshape(S, U, D),
        vecs,
        small,
    )
    g1s, b1s, bqs, bvs = (own[i, :d] for i in range(4))
    bos, g2s, b2s, bps = (own[i, :d] for i in range(8, 12))
    return (
        layer_out.reshape(rows, D),
        grad_hidden.reshape(rows, D),
        g1s,
        b1s,
        gq,
        bqs,
        bvs,
        gout,
        bos,
        g2s,
        b2s,
        gfc,
        own[12, :bfn],
        gproj,
        bps,
    )


def solution(mesh):
    n = mesh.shape["ctx"]
    if n // (PLANES * SEQS) != 2:
        return solution_any(mesh)
    split = Mesh(mesh.devices.reshape(PLANES, SEQS, -1), AXES)
    row, vec = P(AXES, None), P(AXES)
    return jax.shard_map(
        planes,
        mesh=split,
        in_specs=(row, P(), vec, vec, row, vec, vec, row, vec, vec, vec, row, vec, row, vec, row),
        out_specs=(row, row, vec, vec, row, vec, vec, row, vec, vec, vec, row, vec, row, vec),
        check_vma=False,
    )
```

```python
from functools import partial
import math

import jax
import jax.numpy as jnp
from jax import lax
from jax.sharding import PartitionSpec as P
from jax.experimental import pallas as pl
from jax.experimental.pallas import tpu as pltpu
from jax.sharding import Mesh

HEADS = 12
SEQS = 4


NEG = -1e30


def from_partner(value, axis, bit):
    return lax.ppermute(value, axis, [(i, i ^ 1 << bit) for i in range(lax.axis_size(axis))])


def layer_norm(values, gain, bias):
    center = values - jnp.mean(values, axis=-1, keepdims=True)
    spread_sq = jnp.mean(center * center, axis=-1, keepdims=True)
    return center * lax.rsqrt(spread_sq + 1e-05) * gain + bias


def gelu_tanh(values):
    return jax.nn.gelu(values, approximate=True)


def heads_of(tensor, head_count):
    return tensor.reshape(tensor.shape[:-1] + (head_count, tensor.shape[-1] // head_count))


def pick_own(owned, chosen):
    selector = chosen.reshape((1, -1) + (1,) * (owned.ndim - 2))
    return jnp.where(selector, owned[:, 0:1], owned[:, 1:2])


def pick_piece(piece, chosen):
    selector = chosen.reshape((1, -1) + (1,) * (piece.ndim - 3))
    return jnp.where(selector, piece[:, 0], piece[:, 1])


def parity_masks(chosen, usable):
    return jnp.stack([chosen & usable, jnp.logical_not(chosen) & usable])


def spread(values, parity):
    shaped = parity.reshape((1,) + parity.shape + (1,) * (values.ndim - 2))
    return jnp.sum(jnp.where(shaped, values[:, None], 0.0), axis=2)


def group_loop(pieces, unit_rows, table, stepper, carried):
    piece_rows = pieces[0].shape[2]
    group_size = min(unit_rows, piece_rows)
    group_count = piece_rows // group_size
    batch_groups = math.gcd(group_count, max(1, 1024 // group_size))
    turn_count = group_count // batch_groups
    shaped = tuple(
        (
            item.reshape(item.shape[:2] + (group_count, group_size) + item.shape[3:])
            for item in pieces
        )
    )
    device_ids = jnp.arange(group_count, dtype=jnp.int32) * group_size // unit_rows
    table_size = table.shape[0]
    blocks = jnp.sum(
        jnp.where(
            device_ids[:, None] == jnp.arange(table_size, dtype=jnp.int32)[None, :],
            table[None, :],
            0,
        ),
        axis=1,
    )

    def one_turn(position, current):
        pieces_now = tuple(
            (
                lax.dynamic_slice_in_dim(item, position * batch_groups, batch_groups, 2)
                for item in shaped
            )
        )
        chosen = lax.dynamic_slice_in_dim(blocks, position * batch_groups, batch_groups, 0)
        return stepper(current, pieces_now, chosen)

    return lax.fori_loop(0, turn_count, one_turn, carried)


def attend_step(q_heads, my_block, score_scale, head_count, carried, pieces_now, chosen):
    key_piece = heads_of(pieces_now[0], head_count)
    value_piece = heads_of(pieces_now[1], head_count)
    earlier = chosen < my_block
    usable = chosen != my_block
    parity = parity_masks(earlier, usable)
    query_sel = pick_own(q_heads, earlier)
    key_sel = pick_piece(key_piece, earlier)
    value_sel = pick_piece(value_piece, earlier)
    scores = (
        jnp.einsum("jgqhe,jgkhe->jghqk", query_sel, key_sel, preferred_element_type=jnp.float32)
        * score_scale
    )
    usable_mask = usable.reshape(1, -1, 1, 1, 1)
    scores = jnp.where(usable_mask, scores, NEG)
    old_max, old_total, old_sum = carried
    group_max = jnp.max(scores, axis=-1)
    candidate = jnp.max(jnp.where(parity.reshape(1, 2, -1, 1, 1), group_max[:, None], NEG), axis=2)
    new_max = jnp.maximum(old_max, candidate)
    max_sel = pick_own(new_max, earlier)
    weights_exp = jnp.where(usable_mask, jnp.exp(scores - max_sel[..., None]), 0.0)
    moved = jnp.einsum(
        "jghqk,jgkhe->jgqhe",
        weights_exp.astype(jnp.bfloat16),
        value_sel,
        preferred_element_type=jnp.float32,
    )
    factor = jnp.exp(old_max - new_max)
    new_total = old_total * factor + spread(jnp.sum(weights_exp, axis=-1), parity)
    new_sum = old_sum * jnp.swapaxes(factor, 2, 3)[..., None] + spread(moved, parity)
    return (new_max, new_total, new_sum)


def query_grad_step(
    q_heads,
    grad_heads,
    lse_heads,
    delta_heads,
    my_block,
    score_scale,
    head_count,
    carried,
    pieces_now,
    chosen,
):
    key_piece = heads_of(pieces_now[0], head_count)
    value_piece = heads_of(pieces_now[1], head_count)
    earlier = chosen < my_block
    usable = chosen != my_block
    parity = parity_masks(earlier, usable)
    query_sel = pick_own(q_heads, earlier)
    grad_sel = pick_own(grad_heads, earlier)
    lse_sel = pick_own(lse_heads, earlier)
    delta_sel = pick_own(delta_heads, earlier)
    key_sel = pick_piece(key_piece, earlier)
    value_sel = pick_piece(value_piece, earlier)
    scores = (
        jnp.einsum("jgqhe,jgkhe->jghqk", query_sel, key_sel, preferred_element_type=jnp.float32)
        * score_scale
    )
    usable_mask = usable.reshape(1, -1, 1, 1, 1)
    probabilities = jnp.where(usable_mask, jnp.exp(scores - lse_sel[..., None]), 0.0)
    grad_probs = jnp.einsum(
        "jgqhe,jgkhe->jghqk", grad_sel, value_sel, preferred_element_type=jnp.float32
    )
    grad_scores = (probabilities * (grad_probs - delta_sel[..., None])).astype(jnp.bfloat16)
    term = (
        jnp.einsum("jghqk,jgkhe->jgqhe", grad_scores, key_sel, preferred_element_type=jnp.float32)
        * score_scale
    )
    return carried + spread(term, parity)


def key_grad_step(k_heads, v_heads, my_block, score_scale, head_count, carried, pieces_now, chosen):
    query_piece = heads_of(pieces_now[0], head_count)
    grad_piece = heads_of(pieces_now[1], head_count)
    later = my_block < chosen
    usable = chosen != my_block
    parity = parity_masks(later, usable)
    query_sel = pick_piece(query_piece, later)
    grad_sel = pick_piece(grad_piece, later)
    lse_sel = jnp.swapaxes(pick_piece(pieces_now[2], later), 2, 3)
    delta_sel = jnp.swapaxes(pick_piece(pieces_now[3], later), 2, 3)
    key_sel = pick_own(k_heads, later)
    value_sel = pick_own(v_heads, later)
    scores = (
        jnp.einsum("jgqhe,jgkhe->jghqk", query_sel, key_sel, preferred_element_type=jnp.float32)
        * score_scale
    )
    usable_mask = usable.reshape(1, -1, 1, 1, 1)
    probabilities = jnp.where(usable_mask, jnp.exp(scores - lse_sel[..., None]), 0.0)
    grad_probs = jnp.einsum(
        "jgqhe,jgkhe->jghqk", grad_sel, value_sel, preferred_element_type=jnp.float32
    )
    grad_scores = (probabilities * (grad_probs - delta_sel[..., None])).astype(jnp.bfloat16)
    key_term = (
        jnp.einsum("jghqk,jgqhe->jgkhe", grad_scores, query_sel, preferred_element_type=jnp.float32)
        * score_scale
    )
    value_term = jnp.einsum(
        "jghqk,jgqhe->jgkhe",
        probabilities.astype(jnp.bfloat16),
        grad_sel,
        preferred_element_type=jnp.float32,
    )
    return (carried[0] + spread(key_term, parity), carried[1] + spread(value_term, parity))


def shards(
    hidden_in,
    block_pairs,
    ln1_gain,
    ln1_bias,
    qkv_weight,
    query_bias,
    value_bias,
    out_weight,
    out_bias,
    ln2_gain,
    ln2_bias,
    fc_weight,
    fc_bias,
    proj_weight,
    proj_bias,
    out_grad,
):
    params = (
        ln1_gain,
        ln1_bias,
        qkv_weight,
        query_bias,
        value_bias,
        out_weight,
        out_bias,
        ln2_gain,
        ln2_bias,
        fc_weight,
        fc_bias,
        proj_weight,
        proj_bias,
    )
    gathered = (
        lax.all_gather(params[0], "ctx", axis=0, tiled=True),
        lax.all_gather(params[1], "ctx", axis=0, tiled=True),
        lax.all_gather(params[2], "ctx", axis=0, tiled=True),
        lax.all_gather(params[3], "ctx", axis=0, tiled=True),
        lax.all_gather(params[4], "ctx", axis=0, tiled=True),
        lax.all_gather(params[5], "ctx", axis=0, tiled=True),
        lax.all_gather(params[6], "ctx", axis=0, tiled=True),
        lax.all_gather(params[7], "ctx", axis=0, tiled=True),
        lax.all_gather(params[8], "ctx", axis=0, tiled=True),
        lax.all_gather(params[9], "ctx", axis=0, tiled=True),
        lax.all_gather(params[10], "ctx", axis=0, tiled=True),
        lax.all_gather(params[11], "ctx", axis=0, tiled=True),
        lax.all_gather(params[12], "ctx", axis=0, tiled=True),
    )
    (
        gain_one,
        bias_one,
        w_qkv,
        b_query,
        b_value,
        w_out,
        b_out,
        gain_two,
        bias_two,
        w_fc,
        b_fc,
        w_proj,
        b_proj,
    ) = gathered
    device = lax.axis_index("ctx")
    partner = device + 1 - 2 * (device % 2)
    row_count = hidden_in.shape[0]
    model_width = hidden_in.shape[1]
    unit_rows = row_count // SEQS
    halves = SEQS // 2
    head_count = HEADS
    head_size = model_width // head_count
    score_scale = 1.0 / math.sqrt(head_size)
    my_block = block_pairs[device]
    seq_shape = (halves, 2, unit_rows, model_width)
    head_shape = (halves, 2, unit_rows, head_count, head_size)
    inputs = hidden_in.astype(jnp.float32)
    normed = layer_norm(inputs, gain_one.astype(jnp.float32), bias_one.astype(jnp.float32)).astype(
        jnp.bfloat16
    )
    mixed_proj = jnp.dot(normed, w_qkv, preferred_element_type=jnp.float32)
    queries = (mixed_proj[:, :model_width] + b_query.astype(jnp.float32)).astype(jnp.bfloat16)
    key_rows = mixed_proj[:, model_width : 2 * model_width].astype(jnp.bfloat16)
    value_rows = (mixed_proj[:, 2 * model_width :] + b_value.astype(jnp.float32)).astype(
        jnp.bfloat16
    )
    q_seq = queries.reshape(seq_shape)
    k_seq = key_rows.reshape(seq_shape)
    v_seq = value_rows.reshape(seq_shape)
    q_heads = queries.reshape(head_shape)
    k_heads = key_rows.reshape(head_shape)
    v_heads = value_rows.reshape(head_shape)
    far_keys, far_values = from_partner((k_seq, v_seq), "ctx", 0)
    near_keys = jnp.concatenate([k_heads, heads_of(far_keys, head_count)], axis=2)
    near_values = jnp.concatenate([v_heads, heads_of(far_values, head_count)], axis=2)
    scores = (
        jnp.einsum("jpqhe,jpkhe->jphqk", q_heads, near_keys, preferred_element_type=jnp.float32)
        * score_scale
    )
    row_max = jnp.max(scores, axis=-1)
    weights_exp = jnp.exp(scores - row_max[..., None])
    row_total = jnp.sum(weights_exp, axis=-1)
    summed = jnp.einsum(
        "jphqk,jpkhe->jpqhe",
        weights_exp.astype(jnp.bfloat16),
        near_values,
        preferred_element_type=jnp.float32,
    )
    forward_stepper = partial(attend_step, q_heads, my_block, score_scale, head_count)
    row_max, row_total, summed = group_loop(
        (
            lax.all_gather(k_seq, "ctx", axis=2, tiled=True),
            lax.all_gather(v_seq, "ctx", axis=2, tiled=True),
        ),
        unit_rows,
        block_pairs,
        forward_stepper,
        (row_max, row_total, summed),
    )
    attended = summed / jnp.swapaxes(row_total, 2, 3)[..., None]
    log_total = row_max + jnp.log(row_total)
    att_low = attended.reshape(row_count, model_width).astype(jnp.bfloat16)
    branch = jnp.dot(att_low, w_out, preferred_element_type=jnp.float32) + b_out.astype(jnp.float32)
    middle = inputs + branch
    normed_two = layer_norm(
        middle, gain_two.astype(jnp.float32), bias_two.astype(jnp.float32)
    ).astype(jnp.bfloat16)
    pre_act = jnp.dot(normed_two, w_fc, preferred_element_type=jnp.float32) + b_fc.astype(
        jnp.float32
    )
    activation = gelu_tanh(pre_act).astype(jnp.bfloat16)
    result = (
        middle
        + jnp.dot(activation, w_proj, preferred_element_type=jnp.float32)
        + b_proj.astype(jnp.float32)
    )
    layer_out = result.astype(jnp.bfloat16)
    grad_out = out_grad.astype(jnp.float32)
    grad_proj = jnp.dot(activation.T, out_grad, preferred_element_type=jnp.float32)
    grad_bproj = jnp.sum(grad_out, axis=0)
    grad_activ = jnp.dot(out_grad, w_proj.T, preferred_element_type=jnp.float32)
    _, gelu_back = jax.vjp(gelu_tanh, pre_act)
    grad_pre = gelu_back(grad_activ)[0].astype(jnp.bfloat16)
    grad_fc = jnp.dot(normed_two.T, grad_pre, preferred_element_type=jnp.float32)
    grad_bfc = jnp.sum(grad_pre.astype(jnp.float32), axis=0)
    grad_normed_two = jnp.dot(grad_pre, w_fc.T, preferred_element_type=jnp.float32)
    _, norm_back_two = jax.vjp(
        layer_norm, middle, gain_two.astype(jnp.float32), bias_two.astype(jnp.float32)
    )
    grad_middle, grad_gain_two, grad_bias_two = norm_back_two(grad_normed_two)
    grad_middle = grad_middle + grad_out
    grad_branch = grad_middle.astype(jnp.bfloat16)
    grad_wout = jnp.dot(att_low.T, grad_branch, preferred_element_type=jnp.float32)
    grad_bout = jnp.sum(grad_branch.astype(jnp.float32), axis=0)
    grad_att = jnp.dot(grad_branch, w_out.T, preferred_element_type=jnp.float32).astype(
        jnp.bfloat16
    )
    grad_seq = grad_att.reshape(seq_shape)
    grad_heads = grad_att.reshape(head_shape)
    row_delta = jnp.sum(grad_heads.astype(jnp.float32) * attended, axis=-1)
    delta_heads = jnp.swapaxes(row_delta, 2, 3)
    all_lse, all_delta = (
        lax.all_gather(jnp.swapaxes(log_total, 2, 3), "ctx", axis=2, tiled=True),
        lax.all_gather(row_delta, "ctx", axis=2, tiled=True),
    )
    partner_lse = jnp.swapaxes(
        lax.dynamic_slice_in_dim(all_lse, partner * unit_rows, unit_rows, 2), 2, 3
    )
    partner_delta = jnp.swapaxes(
        lax.dynamic_slice_in_dim(all_delta, partner * unit_rows, unit_rows, 2), 2, 3
    )
    far_queries, far_grads = from_partner((q_seq, grad_seq), "ctx", 0)
    near_queries = jnp.concatenate([q_heads, heads_of(far_queries, head_count)], axis=2)
    near_grads = jnp.concatenate([grad_heads, heads_of(far_grads, head_count)], axis=2)
    near_lse = jnp.concatenate([log_total, partner_lse], axis=3)
    near_delta = jnp.concatenate([delta_heads, partner_delta], axis=3)
    local_scores = (
        jnp.einsum(
            "jpqhe,jpkhe->jphqk", near_queries, near_keys, preferred_element_type=jnp.float32
        )
        * score_scale
    )
    probabilities = jnp.exp(local_scores - near_lse[..., None])
    grad_probs = jnp.einsum(
        "jpqhe,jpkhe->jphqk", near_grads, near_values, preferred_element_type=jnp.float32
    )
    grad_scores = (probabilities * (grad_probs - near_delta[..., None])).astype(jnp.bfloat16)
    grad_q_local = (
        jnp.einsum(
            "jphqk,jpkhe->jpqhe",
            grad_scores[:, :, :, :unit_rows, :],
            near_keys,
            preferred_element_type=jnp.float32,
        )
        * score_scale
    )
    grad_k_local = (
        jnp.einsum(
            "jphqk,jpqhe->jpkhe",
            grad_scores[..., :unit_rows],
            near_queries,
            preferred_element_type=jnp.float32,
        )
        * score_scale
    )
    grad_v_local = jnp.einsum(
        "jphqk,jpqhe->jpkhe",
        probabilities.astype(jnp.bfloat16)[..., :unit_rows],
        near_grads,
        preferred_element_type=jnp.float32,
    )
    query_stepper = partial(
        query_grad_step,
        q_heads,
        grad_heads,
        log_total,
        delta_heads,
        my_block,
        score_scale,
        head_count,
    )
    key_stepper = partial(key_grad_step, k_heads, v_heads, my_block, score_scale, head_count)

    def query_piece(carried, pieces, offset):
        return group_loop(pieces, unit_rows, block_pairs, query_stepper, carried)

    def key_piece(carried, pieces, offset):
        return group_loop(
            (pieces[0], pieces[1], all_lse, all_delta), unit_rows, block_pairs, key_stepper, carried
        )

    grad_q_all = query_piece(
        grad_q_local,
        (
            lax.all_gather(k_seq, "ctx", axis=2, tiled=True),
            lax.all_gather(v_seq, "ctx", axis=2, tiled=True),
        ),
        jnp.int32(0),
    )
    grad_k_all, grad_v_all = key_piece(
        (grad_k_local, grad_v_local),
        (
            lax.all_gather(q_seq, "ctx", axis=2, tiled=True),
            lax.all_gather(grad_seq, "ctx", axis=2, tiled=True),
        ),
        jnp.int32(0),
    )
    grad_queries = grad_q_all.reshape(row_count, model_width).astype(jnp.bfloat16)
    grad_keys = grad_k_all.reshape(row_count, model_width).astype(jnp.bfloat16)
    grad_values = grad_v_all.reshape(row_count, model_width).astype(jnp.bfloat16)
    grad_mixed = jnp.concatenate([grad_queries, grad_keys, grad_values], axis=1)
    grad_qkv = jnp.dot(normed.T, grad_mixed, preferred_element_type=jnp.float32)
    grad_bquery = jnp.sum(grad_queries.astype(jnp.float32), axis=0)
    grad_bvalue = jnp.sum(grad_values.astype(jnp.float32), axis=0)
    grad_normed = jnp.dot(grad_mixed, w_qkv.T, preferred_element_type=jnp.float32)
    _, norm_back_one = jax.vjp(
        layer_norm, inputs, gain_one.astype(jnp.float32), bias_one.astype(jnp.float32)
    )
    grad_inputs, grad_gain_one, grad_bias_one = norm_back_one(grad_normed)
    grad_hidden = (grad_inputs + grad_middle).astype(jnp.bfloat16)
    totals = (
        lax.psum_scatter(grad_gain_one, "ctx", scatter_dimension=0, tiled=True),
        lax.psum_scatter(grad_bias_one, "ctx", scatter_dimension=0, tiled=True),
        lax.psum_scatter(grad_qkv, "ctx", scatter_dimension=0, tiled=True),
        lax.psum_scatter(grad_bquery, "ctx", scatter_dimension=0, tiled=True),
        lax.psum_scatter(grad_bvalue, "ctx", scatter_dimension=0, tiled=True),
        lax.psum_scatter(grad_wout, "ctx", scatter_dimension=0, tiled=True),
        lax.psum_scatter(grad_bout, "ctx", scatter_dimension=0, tiled=True),
        lax.psum_scatter(grad_gain_two, "ctx", scatter_dimension=0, tiled=True),
        lax.psum_scatter(grad_bias_two, "ctx", scatter_dimension=0, tiled=True),
        lax.psum_scatter(grad_fc, "ctx", scatter_dimension=0, tiled=True),
        lax.psum_scatter(grad_bfc, "ctx", scatter_dimension=0, tiled=True),
        lax.psum_scatter(grad_proj, "ctx", scatter_dimension=0, tiled=True),
        lax.psum_scatter(grad_bproj, "ctx", scatter_dimension=0, tiled=True),
    )
    return (
        layer_out,
        grad_hidden,
        totals[0],
        totals[1],
        totals[2],
        totals[3],
        totals[4],
        totals[5],
        totals[6],
        totals[7],
        totals[8],
        totals[9],
        totals[10],
        totals[11],
        totals[12],
    )


def solution_any(mesh):
    return jax.shard_map(
        shards,
        mesh=mesh,
        in_specs=(
            P("ctx", None),
            P(),
            P("ctx"),
            P("ctx"),
            P("ctx", None),
            P("ctx"),
            P("ctx"),
            P("ctx", None),
            P("ctx"),
            P("ctx"),
            P("ctx"),
            P("ctx", None),
            P("ctx"),
            P("ctx", None),
            P("ctx"),
            P("ctx", None),
        ),
        out_specs=(
            P("ctx", None),
            P("ctx", None),
            P("ctx"),
            P("ctx"),
            P("ctx", None),
            P("ctx"),
            P("ctx"),
            P("ctx", None),
            P("ctx"),
            P("ctx"),
            P("ctx"),
            P("ctx", None),
            P("ctx"),
            P("ctx", None),
            P("ctx"),
        ),
        check_vma=False,
    )


AXES = ("s", "h", "r")
PLANES = 4


MESH_IDS = pl.DeviceIdType.MESH


class At:
    def __init__(self, ref, *index):
        self.ref, self.index = ref, index

    def now(self):
        return self.ref.at[self.index]

    def still(self):
        return self.ref.at[tuple(i if isinstance(i, slice) else 0 for i in self.index)]


ALL = slice(None)


class Exchange:
    def __init__(self, send, recv):
        self.send, self.recv, self.used, self.open = send, recv, 0, []
        self.s, self.h, self.r = (lax.axis_index(a) for a in AXES)
        self.planes = lax.axis_size("s")
        self.xn = self.h + 1 - 2 * lax.rem(self.h, 2)
        self.yn = lax.rem(self.h + 2, 4)
        self.dn = lax.rem(self.xn + 2, 4)
        self.z = lambda j: lax.rem(self.s + j, self.planes)
        self.X, self.Y, self.D = ({"h": i} for i in (self.xn, self.yn, self.dn))
        self.C = {"r": 1 - self.r}
        self.Z = [None] + [{"s": self.z(j)} for j in range(1, self.planes)]

    def greet(self, peers, meanwhile=None):
        barrier = pltpu.get_barrier_semaphore()
        for peer in peers:
            pl.semaphore_signal(barrier, inc=1, device_id=peer, device_id_type=MESH_IDS)
        if meanwhile:
            meanwhile()
        pl.semaphore_wait(barrier, len(peers))

    def slots(self, count):
        self.used += count
        return range(self.used - count, self.used)

    def copy(self, i, src, dst, peer):
        return pltpu.make_async_remote_copy(
            src_ref=src,
            dst_ref=dst,
            send_sem=self.send.at[i],
            recv_sem=self.recv.at[i],
            device_id=peer,
            device_id_type=MESH_IDS,
        )

    def put(self, i, src, dst, peer):
        self.copy(i, src.now() if isinstance(src, At) else src, dst, peer).start()
        self.open.append((i, src))

    def got(self, i, dst):
        self.copy(i, dst, dst, self.X).wait_recv()

    def close(self):
        for i, src in self.open:
            src = src.still() if isinstance(src, At) else src
            self.copy(i, src, src, self.X).wait_send()


def remote_call(kernel, cid, out_shape, in_specs, out_specs, scratch, sems, name, vmem=56 << 20):
    return pl.pallas_call(
        kernel,
        out_shape=out_shape,
        in_specs=in_specs,
        out_specs=out_specs,
        scratch_shapes=scratch
        + [pltpu.SemaphoreType.DMA((sems,)), pltpu.SemaphoreType.DMA((sems,)), pltpu.SemaphoreType.DMA((16,))],
        compiler_params=pltpu.CompilerParams(
            collective_id=cid, has_side_effects=True, vmem_limit_bytes=vmem
        ),
        name=name,
    )


ANY = pl.BlockSpec(memory_space=pl.ANY)
VMEM = pl.BlockSpec(memory_space=pltpu.VMEM)


def by_x(k, j):
    return (k + j) % 2 == 0


def act(plan, steps, m, c, last_tile):
    for (em, ec), todo in plan.items():
        if (em == ec) == last_tile:

            @pl.when(m == em if last_tile else (m == em) & (c == ec))
            def _():
                for step, k, *js in todo:
                    steps[step](k, js)


def gather_steps(ex, ins, outs, local):
    s, h, r, n = ex.s, ex.h, ex.r, ex.planes
    part = len(ins) - 1
    place = lambda k, t, c: (t, c) if k == part else (t, c, r)
    slab = lambda k, t, c: outs[k].at[place(k, t, c)]
    own = [pltpu.make_async_copy(ins[k], slab(k, s, h), local.at[k + 1]) for k in range(part + 1)]
    for c in own:
        c.start()
    iz, ix, iy, ir, ic = ([ex.slots(n) for _ in outs] for _ in range(5))

    def cross(k, j):
        ex.put(iz[k][j], ins[k], slab(k, s, h), ex.Z[j])

    def forward(k, j):
        t = ex.z(j)
        if j:
            ex.got(iz[k][n - j], slab(k, t, h))
        src = At(outs[k], *place(k, t, h)) if j else ins[k]
        ex.put(ix[k][j], src, slab(k, t, h), ex.X)
        ex.put(iy[k][j], src, slab(k, t, h), ex.Y)

    def relay(k, j):
        t = ex.z(j)
        slots, frm, peer = (ix, ex.xn, ex.Y) if by_x(k, j) else (iy, ex.yn, ex.X)
        ex.got(slots[k][j], slab(k, t, frm))
        ex.put(ir[k][j], At(outs[k], *place(k, t, frm)), slab(k, t, frm), peer)

    def across(k, j):
        t = ex.z(j)
        slots, frm = (iy, ex.yn) if by_x(k, j) else (ix, ex.xn)
        ex.got(slots[k][j], slab(k, t, frm))
        ex.got(ir[k][j], slab(k, t, ex.dn))
        if not j:
            own[k].wait()
        ex.put(ic[k][j], At(outs[k], t, ALL, r), outs[k].at[t, :, r], ex.C)

    def last():
        for j in range(n):
            for k in range(part):
                ex.got(ic[k][j], outs[k].at[ex.z(j), :, 1 - r])
            ex.got(ix[part][j], slab(part, ex.z(j), ex.xn))
            ex.got(iy[part][j], slab(part, ex.z(j), ex.yn))
        own[part].wait()

    each = lambda step: lambda k, js: [step(k, j) for j in js]
    return dict(cross=each(cross), forward=each(forward), relay=each(relay), across=each(across)), last


def by_tile(shape, step):
    height, width = shape
    if height % 48:

        @pl.loop(0, width // 768)
        def _(i):
            step(slice(None), pl.ds(pl.multiple_of(i * 768, 768), 768))
    else:

        @pl.loop(0, height // 48)
        def _(i):
            step(pl.ds(pl.multiple_of(i * 48, 48), 48), slice(None))


def reduce_steps(ins, outs, bufs, send, recv, local):
    count = len(ins)
    mine, from_c, one, two, from_z = (bufs[i * count : (i + 1) * count] for i in range(5))
    ex = Exchange(send, recv)
    s, h, r, n = ex.s, ex.h, ex.r, ex.planes
    own = [
        pltpu.make_async_copy(a.at[:, :, r], m, local.at[k]) for k, (a, m) in enumerate(zip(ins, mine))
    ]
    for c in own:
        c.start()
    ex.greet([ex.X, ex.Y, ex.C] + ex.Z[1:])
    ic, i1, i2, iz = ([ex.slots(n) for _ in ins] for _ in range(4))
    i1b = [ex.slots(n) for _ in ins]
    for k in (1, 0, 2):
        for j in range(n):
            ex.put(ic[k][j], At(ins[k], ex.z(j), ALL, 1 - r), from_c[k].at[ex.z(j)], ex.C)
    for c in own:
        c.wait()

    def add(to, *parts):
        def step(rows, cols):
            total = to[rows, cols].astype(jnp.float32)
            for part in parts:
                total += part[rows, cols].astype(jnp.float32)
            to[rows, cols] = total.astype(to.dtype)

        by_tile(to.shape, step)

    def way(k, j):
        return (ex.X, ex.xn, ex.Y, ex.yn) if by_x(k, j) else (ex.Y, ex.yn, ex.X, ex.xn)

    def first(k, js):
        m = mine[k]
        for j in js:
            t = ex.z(j)
            ex.got(ic[k][j], from_c[k].at[t])
            add(m.at[t, ex.dn], from_c[k].at[t, ex.dn])
            ex.put(i1b[k][j], At(m, t, ex.dn), one[k].at[j, 1], way(k, j)[0])
        for j in js:
            t, (peer, near, _, _) = ex.z(j), way(k, j)
            add(m.at[t, near], from_c[k].at[t, near])
            ex.put(i1[k][j], At(m, t, near), one[k].at[j, 0], peer)

    def second(k, js):
        m = mine[k]
        for j in js:
            t, (_, _, peer, other) = ex.z(j), way(k, j)
            ex.got(i1b[k][j], one[k].at[j, 1])
            add(m.at[t, other], from_c[k].at[t, other], one[k].at[j, 1])
            ex.put(i2[k][j], At(m, t, other), two[k].at[j], peer)

    def third(k, js):
        m = mine[k]
        for j in js:
            t = ex.z(j)
            ex.got(i1[k][j], one[k].at[j, 0])
            ex.got(i2[k][j], two[k].at[j])
            add(m.at[t, h], from_c[k].at[t, h], one[k].at[j, 0], two[k].at[j])
            if j:
                ex.put(iz[k][j], At(m, t, h), from_z[k].at[j], ex.Z[j])

    def last():
        for k, (m, o) in enumerate(zip(mine, outs)):
            for j in range(1, n):
                ex.got(iz[k][j], from_z[k].at[j])

            def step(rows, cols):
                total = m[s, h, rows, cols].astype(jnp.float32)
                for j in range(1, n):
                    total += from_z[k][j, rows, cols].astype(jnp.float32)
                o[rows, cols] = total

            by_tile(o.shape, step)

        ex.close()

    return ex, dict(first=first, second=second, third=third), last


HD = 64


GATHER_PLAN = {
    (0, 0): [("forward", 0, 1, 3, 2), ("relay", 1, 1, 3, 2)],
    (4, 0): [("relay", 0, 1)],
    (4, 3): [("relay", 0, 3)],
    (5, 1): [("relay", 0, 2), ("forward", 2, 1, 3, 2)],
    (5, 5): [("across", 1, 0, 1, 3, 2)],
    (7, 0): [("across", 0, 0, 1, 3, 2)],
}
GATHER_FIRST = [("forward", 1, 1, 3, 2), ("relay", 1, 0), ("relay", 0, 0), ("cross", 2, 1, 3, 2), ("forward", 2, 0)]
GATHER_START = [("cross", 1, 1, 3, 2), ("cross", 0, 1, 3, 2), ("forward", 1, 0), ("forward", 0, 0)]


SMEM = pl.BlockSpec(memory_space=pltpu.SMEM)


def forward_kernel(vectors, inv, blk, x_ref, w_ref, *refs):
    count = 3
    v_refs, refs = refs[:vectors], refs[vectors:]
    ins, refs = refs[:count], refs[count:]
    kept, (vec_ref, o_ref, low_ref, lse_ref) = refs[:5], refs[5:9]
    outs = refs[9 : 9 + count]
    norm_ref, q_ref, kv_ref, w_out, xo_ref, xa, ws, wa, wf, qt, ks, vt, os, sc, send, recv, local = refs[9 + count :]
    f32, bf16 = jnp.float32, jnp.bfloat16
    ex = Exchange(send, recv)
    s, h, r, n = ex.s, ex.h, ex.r, ex.planes
    H, U, D = xa.shape[1:]
    d, N = w_ref.shape
    W = N // 3 // H
    own = pltpu.make_async_copy(x_ref.at[s], xa.at[s, h], local.at[0])
    own.start()

    def slabs():
        lines = [v[...].astype(f32) for v in v_refs]
        lines = [v[:, i : i + d] for v in lines for i in range(0, v.shape[1], d)]
        lines = jnp.concatenate(lines + [jnp.zeros((64 - len(lines), d), f32)], axis=0).T.astype(bf16)
        for k in range(H):
            ws[k] = jnp.concatenate(
                [w_ref[:, c * D + k * W : c * D + (k + 1) * W] for c in range(3)] + [lines], axis=1
            )

    ex.greet([ex.X, ex.Y, ex.D, ex.C] + ex.Z[1:], slabs)
    iw, ix, iy, ir, iz, iwz, iwc, ik = (ex.slots(n) for _ in range(8))
    steps, last = gather_steps(ex, ins, outs, local)
    cross = lambda j: ex.put(iz[j], x_ref.at[ex.z(j)], xa.at[s, h], ex.Z[j])
    cross(1)
    for k, (peer, to) in enumerate(((ex.X, ex.xn), (ex.Y, ex.yn), (ex.D, ex.dn))):
        ex.put(iw[k], ws.at[to], wa.at[s, h, r], peer)
    wa[s, h, r] = ws[h]
    own.wait()

    def forward(j):
        t = ex.z(j)
        if j:
            ex.got(iz[n - j], xa.at[t, h])
        if j in after:
            cross(after[j])
        ex.put(ix[j], xa.at[t, h], xa.at[t, h], ex.X)
        ex.put(iy[j], xa.at[t, h], xa.at[t, h], ex.Y)

    def relay(j):
        t = ex.z(j)
        slots, frm, peer = (ix, ex.xn, ex.Y) if by_x(0, j) else (iy, ex.yn, ex.X)
        ex.got(slots[j], xa.at[t, frm])
        ex.put(ir[j], xa.at[t, frm], xa.at[t, frm], peer)

    def weights(j):
        if j:
            ex.got(iwz[n - j], wa.at[ex.z(j), :, r])
        ex.put(iwc[j], wa.at[ex.z(j), :, r], wa.at[ex.z(j), :, r], ex.C)

    after = {3: 3, 1: 2}
    forward(0)
    for k, frm in enumerate((ex.xn, ex.yn, ex.dn)):
        ex.got(iw[k], wa.at[s, frm, r])
    forward(3)
    relay(0)
    forward(1)
    for j in range(1, n):
        ex.put(iwz[j], wa.at[s, :, r], wa.at[s, :, r], ex.Z[j])
    weights(0)
    relay(3)
    relay(1)
    forward(2)
    for j in (1, 3, 2):
        weights(j)
    for step, k, *js in GATHER_START:
        steps[step](k, js)
    for j in range(n):
        ex.got(iwc[j], wa.at[ex.z(j), :, 1 - r])
    rows = H * 2 * d
    for t in range(n):
        block = wa[t].astype(f32).reshape(rows, N // H + 64)
        wf[t * rows : (t + 1) * rows] = block
    vec_ref[...] = wf[:, N // H :].T[:16]
    w = wf[:, : N // H].astype(bf16)
    w_out[...] = w
    gain, bias = vec_ref[0:1], vec_ref[1:2]

    def mine(row):
        picked = jnp.zeros((1, W), f32)
        for k in range(H):
            picked = jnp.where(h == k, vec_ref[row : row + 1, k * W : (k + 1) * W], picked)
        return picked

    bq, bv = mine(2), mine(3)

    def batch(j):
        t = ex.z(j)
        slots, frm = (iy, ex.yn) if by_x(0, j) else (ix, ex.xn)
        ex.got(slots[j], xa.at[t, frm])
        ex.got(ir[j], xa.at[t, ex.dn])
        x = xa[t].reshape(H * U, D).astype(f32)
        normed = layer_norm(x, gain, bias).astype(bf16)
        pairs = pl.ds(t * H, H)
        norm_ref[t] = normed.reshape(H, U, D)
        mixed = jnp.dot(normed, w, preferred_element_type=f32)
        q = (mixed[:, :W] + bq).astype(bf16) * jnp.asarray(0.125, bf16)
        q_ref[pairs] = q.reshape(H, U, W)
        kv = jnp.concatenate([mixed[:, W : 2 * W], mixed[:, 2 * W :] + bv], axis=1).astype(bf16)
        kv_ref[pairs, 0] = kv.reshape(H, U, 2 * W)
        ex.put(ik[j], kv_ref.at[pairs, 0], kv_ref.at[pairs, 1], ex.C)

    relay(2)
    batch(0)
    batch(3)
    batch(1)
    batch(2)
    for step, k, *js in GATHER_FIRST:
        steps[step](k, js)
    xo_ref[...] = xa[:, h]
    for j in (0, 1, 3, 2):
        ex.got(ik[j], kv_ref.at[pl.ds(ex.z(j) * H, H), 1])

    saves = [
        pltpu.make_async_copy(a, b, local.at[4 + i])
        for i, (a, b) in enumerate(zip((norm_ref, q_ref, kv_ref, w_out, xo_ref), kept))
    ]
    for c in saves:
        c.start()

    npair = inv.shape[0]
    nh = W // HD
    B = 2 * U
    TQ, TK = 2 * U, 2 * B

    @pl.loop(0, npair, unroll=2)
    def _(i):
        p = inv[i]
        qt[:, pl.ds(pl.multiple_of(i * U, U), U)] = q_ref[p].T
        kv = kv_ref[p].reshape(B, 2 * W)
        for h in range(nh):
            ks[h, pl.ds(i * B, B), :] = kv[:, h * HD : (h + 1) * HD]
        vct = kv[:, W:].T
        for h in range(nh):
            vt[h, 0:HD, pl.ds(pl.multiple_of(i * B, B), B)] = vct[h * HD : (h + 1) * HD]
            vt[h, HD:, pl.ds(pl.multiple_of(i * B, B), B)] = jnp.ones((vt.shape[1] - HD, B), vt.dtype)

    def scores(m, c, carry, masked):
        out = []
        rows = pl.ds(pl.multiple_of(c * TK, TK), TK)
        for h in range(nh):
            qh = qt[h * HD : (h + 1) * HD, pl.ds(pl.multiple_of(m * TQ, TQ), TQ)]
            s = jnp.dot(ks[h, rows, :], qh, preferred_element_type=jnp.float32)
            if masked:
                row = lax.broadcasted_iota(jnp.int32, s.shape, 0)
                col = lax.broadcasted_iota(jnp.int32, s.shape, 1)
                s = jnp.where((row >= B) & (col < U), NEG, s)
            sc[h, rows, :] = s
            out.append(jnp.maximum(carry[h], jnp.max(s.reshape(TK // 8, 8, TQ), axis=0)))
        return tuple(out)

    def values(c, carry, tops):
        out = []
        rows = pl.ds(pl.multiple_of(c * TK, TK), TK)
        for h in range(nh):
            p = jnp.exp(sc[h, rows, :] - tops[h]).astype(jnp.bfloat16)
            out.append(carry[h] + jnp.dot(vt[h, :, rows], p, preferred_element_type=jnp.float32))
        return tuple(out)

    @pl.loop(0, npair // 2)
    def _(m):
        tops = tuple(jnp.full((8, TQ), NEG, jnp.float32) for _ in range(nh))
        tops = lax.fori_loop(0, m, lambda c, x: scores(m, c, x, False), tops)
        tops = [jnp.max(t, axis=0, keepdims=True) for t in scores(m, m, tops, True)]

        def step(c, x):
            x = values(c, x, tops)
            act(GATHER_PLAN, steps, m, c, False)
            return x

        init = tuple(jnp.zeros((vt.shape[1], TQ), jnp.float32) for _ in range(nh))
        carry = values(m, lax.fori_loop(0, m, step, init), tops)
        carry = list(zip(tops, carry))
        rows = []
        for h in range(nh):
            mx, acc = carry[h]
            tot = acc[HD : HD + 1]
            rows.append(acc[:HD] / tot)
            lse_ref[h : h + 1, pl.ds(pl.multiple_of(m * TQ, TQ), TQ)] = mx + jnp.log(tot)
        os[pl.ds(pl.multiple_of(m * TQ, TQ), TQ), :] = jnp.concatenate(rows, axis=0).T
        act(GATHER_PLAN, steps, m, m, True)

    @pl.loop(0, npair)
    def _(p):
        o = os[pl.ds(blk[p] * U, U), :]
        o_ref[pl.ds(pl.multiple_of(p * U, U), U), :] = o
        low_ref[pl.ds(pl.multiple_of(p * U, U), U), :] = o.astype(jnp.bfloat16)

    last()
    for c in saves:
        c.wait()
    ex.close()


def forward(inv, blk, x, w, vectors, *weights):
    S, U, D = x.shape
    d, N = w.shape
    H, Q = (lax.axis_size(a) for a in AXES[1:])
    W = N // 3 // H
    npair = S * H
    R, K = npair * U, npair * Q * U
    nh = W // HD
    f32, bf16 = jnp.float32, jnp.bfloat16
    n = len(weights)
    shape = jax.ShapeDtypeStruct
    kept = [
        ((S, H, U, D), bf16),
        ((npair, U, W), bf16),
        ((npair, Q, U, 2 * W), bf16),
        ((D, N // H), bf16),
        ((S, U, D), bf16),
    ]
    return remote_call(
        partial(forward_kernel, len(vectors)),
        0,
        [shape(*kind) for kind in kept]
        + [shape((16, D), f32), shape((R, W), f32), shape((R, W), bf16), shape((8, R), f32)]
        + [shape((S, H, Q) + a.shape, a.dtype) for a in weights[:-1]]
        + [shape((S, H) + weights[-1].shape, bf16)],
        [SMEM] * 2 + [ANY] + [VMEM] * (1 + len(vectors)) + [ANY] * n,
        [ANY] * 5 + [VMEM] * 4 + [ANY] * n,
        [pltpu.VMEM(*kind) for kind in kept]
        + [
            pltpu.VMEM((S, H, U, D), bf16),
            pltpu.VMEM((H, d, N // H + 64), bf16),
            pltpu.VMEM((S, H, Q, d, N // H + 64), bf16),
            pltpu.VMEM((D, N // H + 64), f32),
            pltpu.VMEM((W, R), bf16),
            pltpu.VMEM((nh, K, HD), bf16),
            pltpu.VMEM((nh, HD + 16, K), bf16),
            pltpu.VMEM((R, W), f32),
            pltpu.VMEM((nh, K, 2 * U), f32),
        ],
        8 * S + 5 * S * n,
        "forward",
    )(inv, blk, x, w, *vectors, *weights)


REDUCE_PLAN = {
    (7, 1): [("first", 1, 1, 2, 3, 0)],
    (7, 6): [("second", 1, 1, 2, 3, 0)],
    (7, 7): [("first", 0, 1, 2, 3, 0)],
    (5, 3): [("third", 1, 1, 2, 3, 0)],
    (5, 4): [("second", 0, 1, 2, 3, 0)],
    (4, 0): [("first", 2, 1, 2, 3, 0)],
    (3, 1): [("third", 0, 1, 2, 3, 0)],
    (3, 2): [("second", 2, 1, 2, 3, 0)],
    (2, 1): [("third", 2, 1, 2, 3, 0)],
}


def attend_back_kernel(count, inv, blk, q_in, kv_in, g_in, o_in, lse_ref, out_ref, *refs):
    ins, gm_ref, lo_ref, outs = refs[:count], refs[count], refs[count + 1], refs[count + 2 : 2 * count + 2]
    bufs = refs[2 * count + 2 : 7 * count + 2]
    q_ref, kv_ref, g_ref, o_ref = refs[7 * count + 2 : 7 * count + 6]
    qt, gt, qx, gx, ks, vs, kt, delta, dkv, dqs, over, back, send, recv, local = refs[7 * count + 6 :]
    loads = [
        pltpu.make_async_copy(a, b, local.at[8 + i])
        for i, (a, b) in enumerate(((q_in, q_ref), (kv_in, kv_ref), (g_in, g_ref), (o_in, o_ref)))
    ]
    for c in loads:
        c.start()
    npair, U, W = q_ref.shape
    nh = W // HD
    B = kv_ref.shape[1]
    TQ, TK = 2 * U, 2 * B
    f32, bf16 = jnp.float32, jnp.bfloat16
    ex, steps, last = reduce_steps(ins, outs, bufs, send, recv, local)
    swap = ex.slots(npair // 2)
    il = ex.slots(ex.planes)
    keep = pltpu.make_async_copy(out_ref.at[ex.s], lo_ref.at[ex.s], local.at[count])
    keep.start()
    for j in range(1, ex.planes):
        ex.put(il[j], out_ref.at[ex.z(j)], lo_ref.at[ex.s], ex.Z[j])

    for c in loads:
        c.wait()

    @pl.loop(0, npair, unroll=2)
    def _(i):
        p = inv[i]
        qc = q_ref[p]
        gc = g_ref[p]
        oc = o_ref[pl.ds(p * U, U), :]
        cols = pl.ds(pl.multiple_of(i * U, U), U)
        qt[:, cols] = qc.T
        gt[:, cols] = gc.T
        prod = (oc * gc.astype(f32)).T
        zero = jnp.zeros((U, HD), bf16)
        for h in range(nh):
            delta[h : h + 1, cols] = jnp.sum(prod[h * HD : (h + 1) * HD], axis=0, keepdims=True)
            qx[h, pl.ds(i * U, U), :] = jnp.concatenate([zero, qc[:, h * HD : (h + 1) * HD]], axis=1)
            gx[h, pl.ds(i * U, U), :] = jnp.concatenate([gc[:, h * HD : (h + 1) * HD], zero], axis=1)
        kv = kv_ref[p]
        kc, vc = kv[:, :W], kv[:, W:]
        kt[:, pl.ds(pl.multiple_of(i * B, B), B)] = kc.T
        for h in range(nh):
            ks[h, pl.ds(i * B, B), :] = kc[:, h * HD : (h + 1) * HD]
            vs[h, pl.ds(i * B, B), :] = vc[:, h * HD : (h + 1) * HD]

    dkv[...] = jnp.zeros_like(dkv)

    def tile(m, c, carry, masked):
        out = []
        qcols = pl.ds(pl.multiple_of(m * TQ, TQ), TQ)
        krows = pl.ds(pl.multiple_of(c * TK, TK), TK)
        for h in range(nh):
            hs = slice(h * HD, (h + 1) * HD)
            s = jnp.dot(ks[h, krows, :], qt[hs, qcols], preferred_element_type=f32)
            p = jnp.exp(s - lse_ref[h : h + 1, qcols])
            if masked:
                row = lax.broadcasted_iota(jnp.int32, s.shape, 0)
                col = lax.broadcasted_iota(jnp.int32, s.shape, 1)
                p = jnp.where((row >= B) & (col < U), 0.0, p)
            dp = jnp.dot(vs[h, krows, :], gt[hs, qcols], preferred_element_type=f32)
            ds = (p * (dp - delta[h : h + 1, qcols])).astype(bf16)
            dkv[h, krows, :] += jnp.dot(
                p.astype(bf16), gx[h, qcols, :], preferred_element_type=f32
            ) + jnp.dot(ds, qx[h, qcols, :], preferred_element_type=f32)
            out.append(carry[h] + jnp.dot(kt[hs, krows], ds, preferred_element_type=f32))
        return tuple(out)

    def halves(b, half):
        rows = pl.ds(pl.multiple_of(b * B + half * U, U), U)
        parts = [dkv[h, rows, :] for h in range(nh)]
        return jnp.concatenate([x[:, HD:] for x in parts] + [x[:, :HD] for x in parts], axis=1)

    @pl.loop(0, npair // 2)
    def _(turn):
        m = npair // 2 - 1 - turn
        init = tuple(jnp.zeros((HD, TQ), f32) for _ in range(nh))

        def step(c, x):
            x = tile(m, c, x, False)
            act(REDUCE_PLAN, steps, m, c, False)
            return x

        carry = lax.fori_loop(0, m, step, init)
        carry = tile(m, m, carry, True)
        dqs[pl.ds(pl.multiple_of(m * TQ, TQ), TQ), :] = (jnp.concatenate(carry, axis=0).T * 0.125).astype(bf16)
        for k in range(2):
            over[2 * m + k] = halves(2 * m + k, 1).astype(bf16)
        ex.copy(swap[0] + m, over.at[pl.ds(2 * m, 2)], back.at[pl.ds(2 * m, 2)], ex.C).start()
        act(REDUCE_PLAN, steps, m, m, True)

    @pl.loop(0, npair // 2)
    def _(m):
        moved = ex.copy(swap[0] + m, over.at[pl.ds(2 * m, 2)], back.at[pl.ds(2 * m, 2)], ex.C)
        moved.wait_recv()
        moved.wait_send()

    @pl.loop(0, npair)
    def _(p):
        b = blk[p]
        rows = pl.ds(b * B, U)
        parts = [dkv[h, rows, :] for h in range(nh)]
        own = jnp.concatenate([x[:, HD:] for x in parts] + [x[:, :HD] for x in parts], axis=1)
        own = (own + back[b].astype(f32)).astype(bf16)
        gm_ref[p] = jnp.concatenate([dqs[pl.ds(b * U, U), :], own], axis=1)

    for j in range(1, ex.planes):
        ex.got(il[ex.planes - j], lo_ref.at[ex.z(j)])
    keep.wait()
    last()


def attend_back(inv, blk, q, kv, g, o, lse, out, *grads):
    npair, U, W = q.shape
    R, K = npair * U, npair * kv.shape[1]
    nh = W // HD
    S, H, Q = (lax.axis_size(a) for a in AXES)
    n = len(grads)
    f32, bf16 = jnp.float32, jnp.bfloat16
    tails = [a.shape[3:] for a in grads]
    buffers = [[pltpu.VMEM(lead + t, bf16) for t in tails] for lead in ((S, H), (S, H), (S, 2), (S,), (S,))]
    return remote_call(
        partial(attend_back_kernel, n),
        2,
        [jax.ShapeDtypeStruct((npair, R // npair, 3 * W), bf16), jax.ShapeDtypeStruct(out.shape, bf16)]
        + [jax.ShapeDtypeStruct(t, f32) for t in tails],
        [SMEM] * 2 + [ANY] * 4 + [VMEM] + [ANY] * (n + 1),
        [VMEM, ANY] + [VMEM] * n,
        sum(buffers, [])
        + [pltpu.VMEM(a.shape, a.dtype) for a in (q, kv, g, o)]
        + [
            pltpu.VMEM((W, R), bf16),
            pltpu.VMEM((W, R), bf16),
            pltpu.VMEM((nh, R, 2 * HD), bf16),
            pltpu.VMEM((nh, R, 2 * HD), bf16),
            pltpu.VMEM((nh, K, HD), bf16),
            pltpu.VMEM((nh, K, HD), bf16),
            pltpu.VMEM((W, K), bf16),
            pltpu.VMEM((8, R), f32),
            pltpu.VMEM((nh, K, 2 * HD), f32),
            pltpu.VMEM((R, W), bf16),
            pltpu.VMEM((npair, R // npair, 2 * W), bf16),
            pltpu.VMEM((npair, R // npair, 2 * W), bf16),
        ],
        5 * S * n + npair // 2 + S,
        "attend_back",
        60 << 20,
    )(inv, blk, q, kv, g, o, lse, out, *grads)


def middle_kernel(
    low_ref, x_ref, g_ref, vec_ref, fc_ref, proj_ref, wo_ref,
    lo_ref, gmid_ref, small_ref, ga_ref, gfc_ref, gproj_ref, gout_ref,
    bias, ra, fc, wp, wo_in, wf, wo, act_ref, dpre, deriv, g, att, mid, z_ref, n2, n2t, y, t2, gb, sb, gfc, gproj, gout,
    send, recv, local,
):
    f32, bf16 = jnp.float32, jnp.bfloat16
    ex = Exchange(send, recv)
    s, h, r, n = ex.s, ex.h, ex.r, ex.planes
    H, U, W = low_ref.shape[1:]
    R, D = att.shape
    d = fc.shape[3]
    loads = [
        pltpu.make_async_copy(a, b, local.at[i])
        for i, (a, b) in enumerate(
            (
                (wo_ref, wo_in),
                (proj_ref.at[:, h], wp.at[:, h, r]),
                (fc_ref, fc),
                (low_ref.at[:, h], ra.at[h]),
                (g_ref.at[s], g.at[s]),
                (proj_ref.at[:, ex.xn], wp.at[:, ex.xn, r]),
                (proj_ref.at[:, ex.yn], wp.at[:, ex.yn, r]),
            )
        )
    ]
    for c in loads:
        c.start()
    ex.greet([ex.X, ex.Y, ex.D, ex.C] + ex.Z[1:])
    there, back = ex.slots(3), ex.slots(3)
    ir, ic, ig = (ex.slots(n) for _ in range(3))
    sides = ((ex.X, ex.xn), (ex.Y, ex.yn), (ex.D, ex.dn))
    for k, (peer, to) in enumerate(sides):
        ex.put(there[k], low_ref.at[:, to], ra.at[h], peer)
    for j in range(n):
        frm, peer = (ex.xn, ex.Y) if by_x(0, j) else (ex.yn, ex.X)
        ex.put(ir[j], proj_ref.at[ex.z(j), frm], wp.at[ex.z(j), frm, r], peer)
    for j in range(1, n):
        ex.put(ig[j], g_ref.at[ex.z(j)], g.at[s], ex.Z[j])

    def across(j):
        ex.got(ir[j], wp.at[ex.z(j), ex.dn, r])
        ex.put(ic[j], wp.at[ex.z(j), :, r], wp.at[ex.z(j), :, r], ex.C)

    dot = partial(jnp.dot, preferred_element_type=f32)
    dot_nt = lambda a, b: lax.dot_general(a, b, (((1,), (1,)), ((), ())), preferred_element_type=f32)
    dot_tn = lambda a, b: lax.dot_general(a, b, (((0,), (0,)), ((), ())), preferred_element_type=f32)
    loads[0].wait()
    wo[...] = wo_in[...].astype(f32).reshape(D, D).astype(bf16)
    loads[2].wait()

    @pl.loop(0, n)
    def _(b):
        cols = pl.ds(pl.multiple_of(b * D, D), D)
        wf[b] = fc[:, :, :, :, cols].astype(f32).reshape(D, D).astype(bf16)

    each = D // d
    share = bias.shape[1] // each // d
    for i in range(n):
        parts = [(8 + k, e * d) for e in range(i * each // n, (i + 1) * each // n) for k in range(share)]
        bias[0:1, i * D : (i + 1) * D] = jnp.concatenate([vec_ref[k : k + 1, c : c + d] for k, c in parts], axis=1)
    y[...] = jnp.zeros_like(y)
    t2[...] = jnp.zeros_like(t2)
    loads[3].wait()
    for k, (peer, frm) in enumerate(sides):
        ex.got(there[k], ra.at[frm])
    att[...] = jnp.concatenate([ra[k].reshape(R, W) for k in range(H)], axis=1)
    m = x_ref[...].astype(f32) + dot(att[...], wo[...]) + vec_ref[4:5]
    mid[...] = m
    center = m - jnp.mean(m, axis=-1, keepdims=True)
    rstd = lax.rsqrt(jnp.mean(center * center, axis=-1, keepdims=True) + 1e-05)
    z = center * rstd
    z_ref[...] = z
    normed = (z * vec_ref[5:6] + vec_ref[6:7]).astype(bf16)
    n2[...] = normed
    n2t[...] = normed.T
    slope = math.sqrt(2.0 / math.pi)

    def up(b):
        cols = slice(b * D, (b + 1) * D)
        pre = dot(n2[...], wf[b]) + bias[0:1, cols]
        square = pre * pre
        tanh = jnp.tanh(slope * pre * (1.0 + 0.044715 * square))
        half = 0.5 * (1.0 + tanh)
        act_ref[b] = (pre * half).astype(bf16)
        deriv[b] = half + 0.5 * pre * (1.0 - tanh * tanh) * (slope * (1.0 + 3 * 0.044715 * square))

    up(0)
    for i in (1, 5, 6):
        loads[i].wait()
    across(0)
    across(1)
    up(1)
    across(2)
    across(3)
    up(2)
    up(3)
    loads[4].wait()
    for j in range(1, n):
        ex.got(ig[n - j], g.at[ex.z(j)])

    def down(j):
        b = ex.z(j)
        ex.got(ic[j], wp.at[b, :, 1 - r])
        pre = dot_nt(g[...].reshape(R, D), wp[b].reshape(D, D)) * deriv[b]
        dpre[b] = pre.astype(bf16)
        small_ref[pl.ds(b + 4, 1)] = jnp.sum(dpre[b].astype(f32), axis=0, keepdims=True)
        t2[...] += dot_nt(dpre[b], wf[b])

    for j in range(n):
        down(j)
    t, z = t2[...], z_ref[...]
    g32 = g[...].reshape(R, D).astype(f32)
    e = t * vec_ref[5:6]
    inner = e - jnp.mean(e, axis=-1, keepdims=True) - z * jnp.mean(e * z, axis=-1, keepdims=True)
    gm = g32 + inner * rstd
    gmid_ref[...] = gm
    gb[...] = gm.astype(bf16)
    ga = dot_nt(gb[...], wo[...]).astype(bf16)
    for k in range(H):
        sb[k] = ga[:, k * W : (k + 1) * W].reshape(sb.shape[1:])
    for k, (peer, to) in enumerate(sides):
        ex.put(back[k], sb.at[to], ga_ref.at[:, h], peer)
    mine = pltpu.make_async_copy(sb.at[h], ga_ref.at[:, h], local.at[3])
    mine.start()
    stores = []

    def store(src, dst):
        stores.append(pltpu.make_async_copy(src, dst, local.at[4 + len(stores)]))
        stores[-1].start()

    for b in range(n):
        grad = g[...].reshape(R, D)
        gproj[b] = dot_tn(act_ref[b], grad).astype(bf16).reshape(gproj.shape[1:])
        gfc[:, :, :, :, b * D : (b + 1) * D] = dot(n2t[...], dpre[b]).reshape(gfc.shape[:4] + (D,)).astype(bf16)
        y[...] += dot(act_ref[b], wp[b].reshape(D, D))
    store(gproj, gproj_ref)
    store(gfc, gfc_ref)
    gout[...] = dot_tn(att[...], gb[...]).reshape(gout.shape).astype(bf16)
    store(gout, gout_ref)
    lo_ref[...] = (mid[...] + y[...] + vec_ref[7:8]).astype(bf16)
    small_ref[1:2] = jnp.sum(t2[...] * z_ref[...], axis=0, keepdims=True)
    small_ref[2:3] = jnp.sum(t2[...], axis=0, keepdims=True)
    small_ref[0:1] = jnp.sum(gb[...].astype(f32), axis=0, keepdims=True)
    small_ref[3:4] = jnp.sum(g[...].reshape(R, D).astype(f32), axis=0, keepdims=True)
    for k, (peer, frm) in enumerate(sides):
        ex.got(back[k], ga_ref.at[:, frm])
    for c in stores + [mine]:
        c.wait()
    ex.close()


def middle(low, x, g, vecs, fc, proj, wo):
    S, H, U, W = low.shape
    R, D = x.shape
    whole = fc.shape[:3] + proj.shape[2:]
    f32, bf16 = jnp.float32, jnp.bfloat16
    vm = pltpu.VMEM
    return remote_call(
        middle_kernel,
        4,
        [
            jax.ShapeDtypeStruct((R, D), bf16),
            jax.ShapeDtypeStruct((R, D), f32),
            jax.ShapeDtypeStruct((8, D), f32),
            jax.ShapeDtypeStruct(low.shape, bf16),
            jax.ShapeDtypeStruct(fc.shape, bf16),
            jax.ShapeDtypeStruct(whole, bf16),
            jax.ShapeDtypeStruct(wo.shape, bf16),
        ],
        [ANY, VMEM, ANY, VMEM] + [ANY] * 3,
        [VMEM] * 3 + [ANY] * 4,
        [
            vm((8, fc.shape[-1]), f32),
            vm((H, S, U, W), bf16),
            vm(fc.shape, bf16),
            vm(whole, bf16),
            vm(wo.shape, bf16),
            vm((S, D, D), bf16),
            vm((D, D), bf16),
            vm((S, R, D), bf16),
            vm((S, R, D), bf16),
            vm((S, R, D), f32),
            vm((S, U, D), bf16),
            vm((R, D), bf16),
            vm((R, D), f32),
            vm((R, D), f32),
            vm((R, D), bf16),
            vm((D, R), bf16),
            vm((R, D), f32),
            vm((R, D), f32),
            vm((R, D), bf16),
            vm((H, S, U, W), bf16),
            vm(fc.shape, bf16),
            vm(whole, bf16),
            vm(wo.shape, bf16),
        ],
        6 + 3 * S,
        "middle",
        60 << 20,
    )(low, x, g, vecs, fc, proj, wo)


def norm_back(x, t, gain, grad):
    mean = jnp.mean(x, axis=-1, keepdims=True)
    center = x - mean
    rstd = lax.rsqrt(jnp.mean(center * center, axis=-1, keepdims=True) + 1e-05)
    z = center * rstd
    e = t * gain
    inner = e - jnp.mean(e, axis=-1, keepdims=True) - z * jnp.mean(e * z, axis=-1, keepdims=True)
    return grad + rstd * inner


def finish_kernel(
    gm_ref, w_ref, norm_in, x_in, gmid_in, line_ref, small_ref,
    gh_ref, gqkv_ref, own_ref,
    norm_ref, x_ref, gmid_ref, gq_ref, t_ref, one, two, hid, gw, gw_c, gw_z, gw_sum, vec, send, recv, local,
):
    f32, bf16 = jnp.float32, jnp.bfloat16
    loads = [
        pltpu.make_async_copy(a, b, local.at[8 + i])
        for i, (a, b) in enumerate(((norm_in, norm_ref), (x_in, x_ref), (gmid_in, gmid_ref)))
    ]
    for c in loads:
        c.start()
    ex = Exchange(send, recv)
    s, h, r, n = ex.s, ex.h, ex.r, ex.planes
    half = n // 2
    H, N = gm_ref.shape[1], gm_ref.shape[3]
    U, D = t_ref.shape[2], t_ref.shape[3]
    W = N // 3
    d = gw.shape[3]
    ex.greet([ex.X, ex.Y, ex.D, ex.C] + ex.Z[1:])
    i1, i1b, i2, ih, ic, iz, iq = (ex.slots(n) for _ in range(7))
    iv = ex.slots(3 + n)
    acc = [jnp.zeros((1, D), f32), jnp.zeros((1, D), f32)]
    way = lambda j: (ex.X, ex.xn, ex.Y, ex.yn) if by_x(0, j) else (ex.Y, ex.yn, ex.X, ex.xn)

    def product(j, pair):
        t = ex.z(j)
        g = jnp.concatenate([gm_ref[t, to] for to in pair], axis=0)
        prod = lax.dot_general(g, w_ref[...], (((1,), (1,)), ((), ())), preferred_element_type=f32)
        for k, to in enumerate(pair):
            part = prod[k * U : (k + 1) * U]
            t_ref[t, to] = part.astype(bf16)
            acc[0] += jnp.sum(part * norm_ref[t, to].astype(f32), axis=0, keepdims=True)
            acc[1] += jnp.sum(part, axis=0, keepdims=True)

    def leave(j):
        peer, near, _, _ = way(j)
        ex.put(i1b[j], t_ref.at[ex.z(j), ex.dn], one.at[j, 1], peer)
        ex.put(i1[j], t_ref.at[ex.z(j), near], one.at[j, 0], peer)

    def relay(j):
        t = ex.z(j)
        _, _, peer, other = way(j)
        ex.got(i1b[j], one.at[j, 1])
        t_ref[t, other] = (t_ref[t, other].astype(f32) + one[j, 1].astype(f32)).astype(bf16)
        ex.put(i2[j], t_ref.at[t, other], two.at[j], peer)

    g_all = gm_ref[...].reshape(n * H * U, N)
    def qkv_rows(t0):
        width = H * 2 * d
        nt = norm_ref[:, :, :, t0 * width : (t0 + half) * width].reshape(n * H * U, half * width)
        part = lax.dot_general(nt, g_all, (((0,), (0,)), ((), ())), preferred_element_type=f32)
        gw[t0 : t0 + half] = part.reshape(half, H, 2, d, N).astype(bf16)
        for t in range(t0, t0 + half):
            ex.put(ic[t], gw.at[t, :, 1 - r], gw_c.at[t], ex.C)

    def done(j):
        t = ex.z(j)
        ex.got(i1[j], one.at[j, 0])
        ex.got(i2[j], two.at[j])
        total = t_ref[t, h].astype(f32) + one[j, 0].astype(f32) + two[j].astype(f32)
        hid[t] = norm_back(x_ref[t].astype(f32), total, line_ref[0:1], gmid_ref[t]).astype(bf16)
        if j:
            ex.put(ih[j], hid.at[t], gh_ref.at[s], ex.Z[j])

    loads[0].wait()
    for j in (1, 2):
        product(j, (ex.dn, way(j)[1]))
        leave(j)
    qkv_rows(0)
    qkv_rows(half)
    for j in (1, 2):
        product(j, (way(j)[3], h))
    for t in range(n):
        ex.got(ic[t], gw_c.at[t])
        gw_c[t] = (gw_c[t].astype(f32) + gw[t, :, r].astype(f32)).astype(bf16)
    for j in range(1, n):
        ex.put(iz[j], gw_c.at[ex.z(j)], gw_z.at[s], ex.Z[j])
    relay(1)
    relay(2)
    for j in (3, 0):
        product(j, (ex.dn, way(j)[1]))
        leave(j)
    for j in (3, 0):
        product(j, (way(j)[3], h))
    cols = jnp.sum(g_all.astype(f32), axis=0, keepdims=True)
    lane = lax.broadcasted_iota(jnp.int32, (1, D), 1) // W

    def placed(c):
        return jnp.where(lane == h, jnp.concatenate([c] * H, axis=1), 0.0)

    vec[0, 0:1] = acc[0]
    vec[0, 1:2] = acc[1]
    vec[0, 2:3] = placed(cols[:, :W])
    vec[0, 3:4] = placed(cols[:, 2 * W :])
    vec[0, 4:8] = jnp.zeros((4, D), f32)
    vec[0, 8:] = small_ref[...]
    ex.put(iv[0], vec.at[0], vec.at[1], ex.C)

    loads[1].wait()
    loads[2].wait()
    done(1)
    done(2)
    ex.got(iv[0], vec.at[1])
    vec[2] = vec[0] + vec[1]
    ex.put(iv[1], vec.at[2], vec.at[3], ex.X)
    relay(3)
    relay(0)
    ex.got(iv[1], vec.at[3])
    vec[4] = vec[2] + vec[3]
    ex.put(iv[2], vec.at[4], vec.at[5], ex.Y)
    total = gw_c[s].astype(f32)
    for j in range(1, n):
        ex.got(iz[n - j], gw_z.at[ex.z(j)])
        total += gw_z[ex.z(j)].astype(f32)
    gw_sum[...] = total
    for k, (peer, to) in enumerate(((ex.X, ex.xn), (ex.Y, ex.yn), (ex.D, ex.dn))):
        ex.put(iq[k], gw_sum.at[to], gq_ref.at[h], peer)
    mine = pltpu.make_async_copy(gw_sum.at[h], gq_ref.at[h], local.at[2])
    mine.start()
    ex.got(iv[2], vec.at[5])
    vec[6] = vec[4] + vec[5]
    for j in range(1, n):
        ex.put(iv[2 + j], vec.at[6], vec.at[6 + j], ex.Z[j])
    done(3)
    done(0)
    own = pltpu.make_async_copy(hid.at[s], gh_ref.at[s], local.at[1])
    own.start()
    for j in range(1, n):
        ex.got(iv[2 + j], vec.at[6 + j])
    sums = vec[6] + vec[7] + vec[8] + vec[9]
    gain = (sums[0:1] - line_ref[1:2] * sums[1:2]) / line_ref[0:1]
    rows = jnp.concatenate([gain, sums[1:12], jnp.zeros((4, D), f32)], axis=0)
    wide = jnp.zeros((1, D), f32)
    for k in range(n):
        wide = jnp.where(s == k, sums[12 + k : 13 + k], wide)
    at = h * 2 + r
    begin = (s * H * 2 + at) * d
    own_ref[...] = pltpu.roll(rows, lax.rem(D - begin, D), 1)[:, :128]
    own_ref[12:13] = pltpu.roll(jnp.broadcast_to(wide, (8, D)), lax.rem(D - at * n * d, D), 1)[0:1, :128]
    for k, frm in enumerate((ex.xn, ex.yn, ex.dn)):
        ex.got(iq[k], gq_ref.at[frm])
    mine.wait()
    for k in range(H):
        for c in range(3):
            gqkv_ref[:, c * D + k * W : c * D + (k + 1) * W] = gq_ref[k, :, c * W : (c + 1) * W]
    for j in range(1, n):
        ex.got(ih[n - j], gh_ref.at[ex.z(j)])
    own.wait()
    ex.close()


def finish(gm, w, norm, x, gmid, lines, small):
    S, H, U, N = gm.shape
    D = w.shape[0]
    Q = lax.axis_size("r")
    d = D // (S * H * Q)
    f32, bf16 = jnp.float32, jnp.bfloat16
    return remote_call(
        finish_kernel,
        3,
        [
            jax.ShapeDtypeStruct((S, U, D), bf16),
            jax.ShapeDtypeStruct((d, H * N), f32),
            jax.ShapeDtypeStruct((16, 128), f32),
        ],
        [VMEM] * 2 + [ANY] * 3 + [VMEM] * 2,
        [ANY, VMEM, VMEM],
        [
            pltpu.VMEM(norm.shape, bf16),
            pltpu.VMEM(x.shape, bf16),
            pltpu.VMEM(gmid.shape, f32),
            pltpu.VMEM((H, d, N), f32),
            pltpu.VMEM((S, H, U, D), bf16),
            pltpu.VMEM((S, 2, U, D), bf16),
            pltpu.VMEM((S, U, D), bf16),
            pltpu.VMEM((S, U, D), bf16),
            pltpu.VMEM((S, H, Q, d, N), bf16),
            pltpu.VMEM((S, H, d, N), bf16),
            pltpu.VMEM((S, H, d, N), bf16),
            pltpu.VMEM((H, d, N), f32),
            pltpu.VMEM((10, 16, D), f32),
        ],
        8 * S + 3,
        "finish",
    )(gm, w, norm, x, gmid, lines, small)


def planes(
    hidden_in,
    block_pairs,
    ln1_gain,
    ln1_bias,
    qkv_weight,
    query_bias,
    value_bias,
    out_weight,
    out_bias,
    ln2_gain,
    ln2_bias,
    fc_weight,
    fc_bias,
    proj_weight,
    proj_bias,
    out_grad,
):
    f32, bf16 = jnp.float32, jnp.bfloat16
    s, h, r = (lax.axis_index(a) for a in AXES)
    S, H, Q = (lax.axis_size(a) for a in AXES)
    rows, D = hidden_in.shape
    U = rows // SEQS
    W = D // H
    bfn = fc_bias.shape[0]
    d = qkv_weight.shape[0]
    lines = [ln1_gain, ln1_bias, query_bias, value_bias, out_bias, ln2_gain, ln2_bias, proj_bias, fc_bias]
    blk = block_pairs[::2]
    blk = jnp.where(s % 2 == 0, blk, blk.shape[0] - 1 - blk)
    blk = blk.astype(jnp.int32)
    npair = blk.shape[0]
    inv = jnp.sum(
        jnp.where(blk[None, :] == jnp.arange(npair)[:, None], jnp.arange(npair)[None, :], 0), axis=1
    ).astype(jnp.int32)
    normed, q_all, kv_all, w_h, x_own, vecs, att, att_low, lse, w_fc, w_out, w_proj = forward(
        inv,
        blk,
        hidden_in.reshape(S, U, D),
        qkv_weight,
        [v[None] for v in lines],
        fc_weight,
        out_weight,
        proj_weight,
    )
    layer_out, grad_middle, small, g_att, grad_fc, grad_proj, grad_wout = middle(
        att_low.reshape(S, H, U, W),
        x_own.reshape(rows, D),
        out_grad.reshape(S, U, D),
        vecs,
        w_fc,
        w_proj,
        w_out,
    )
    grad_mixed, layer_out, gfc, gproj, gout = attend_back(
        inv,
        blk,
        q_all,
        kv_all.reshape(npair, Q * U, 2 * W),
        g_att.reshape(npair, U, W),
        att,
        lse,
        layer_out.reshape(S, U, D),
        grad_fc,
        grad_proj,
        grad_wout,
    )
    grad_hidden, gq, own = finish(
        grad_mixed.reshape(S, H, U, 3 * W),
        w_h,
        normed,
        x_own,
        grad_middle.reshape(S, U, D),
        vecs,
        small,
    )
    g1s, b1s, bqs, bvs = (own[i, :d] for i in range(4))
    bos, g2s, b2s, bps = (own[i, :d] for i in range(8, 12))
    return (
        layer_out.reshape(rows, D),
        grad_hidden.reshape(rows, D),
        g1s,
        b1s,
        gq,
        bqs,
        bvs,
        gout,
        bos,
        g2s,
        b2s,
        gfc,
        own[12, :bfn],
        gproj,
        bps,
    )


def solution(mesh):
    n = mesh.shape["ctx"]
    if n // (PLANES * SEQS) != 2:
        return solution_any(mesh)
    split = Mesh(mesh.devices.reshape(PLANES, SEQS, -1), AXES)
    row, vec = P(AXES, None), P(AXES)
    return jax.shard_map(
        planes,
        mesh=split,
        in_specs=(row, P(), vec, vec, row, vec, vec, row, vec, vec, vec, row, vec, row, vec, row),
        out_specs=(row, row, vec, vec, row, vec, vec, row, vec, vec, vec, row, vec, row, vec),
        check_vma=False,
    )
```

```python
from functools import partial
import math

import jax
import jax.numpy as jnp
from jax import lax
from jax.sharding import PartitionSpec as P
from jax.experimental import pallas as pl
from jax.experimental.pallas import tpu as pltpu
from jax.sharding import Mesh

HEADS = 12
SEQS = 4


NEG = -1e30


def from_partner(value, axis, bit):
    return lax.ppermute(value, axis, [(i, i ^ 1 << bit) for i in range(lax.axis_size(axis))])


def layer_norm(values, gain, bias):
    center = values - jnp.mean(values, axis=-1, keepdims=True)
    spread_sq = jnp.mean(center * center, axis=-1, keepdims=True)
    return center * lax.rsqrt(spread_sq + 1e-05) * gain + bias


def gelu_tanh(values):
    return jax.nn.gelu(values, approximate=True)


def heads_of(tensor, head_count):
    return tensor.reshape(tensor.shape[:-1] + (head_count, tensor.shape[-1] // head_count))


def pick_own(owned, chosen):
    selector = chosen.reshape((1, -1) + (1,) * (owned.ndim - 2))
    return jnp.where(selector, owned[:, 0:1], owned[:, 1:2])


def pick_piece(piece, chosen):
    selector = chosen.reshape((1, -1) + (1,) * (piece.ndim - 3))
    return jnp.where(selector, piece[:, 0], piece[:, 1])


def parity_masks(chosen, usable):
    return jnp.stack([chosen & usable, jnp.logical_not(chosen) & usable])


def spread(values, parity):
    shaped = parity.reshape((1,) + parity.shape + (1,) * (values.ndim - 2))
    return jnp.sum(jnp.where(shaped, values[:, None], 0.0), axis=2)


def group_loop(pieces, unit_rows, table, stepper, carried):
    piece_rows = pieces[0].shape[2]
    group_size = min(unit_rows, piece_rows)
    group_count = piece_rows // group_size
    batch_groups = math.gcd(group_count, max(1, 1024 // group_size))
    turn_count = group_count // batch_groups
    shaped = tuple(
        (
            item.reshape(item.shape[:2] + (group_count, group_size) + item.shape[3:])
            for item in pieces
        )
    )
    device_ids = jnp.arange(group_count, dtype=jnp.int32) * group_size // unit_rows
    table_size = table.shape[0]
    blocks = jnp.sum(
        jnp.where(
            device_ids[:, None] == jnp.arange(table_size, dtype=jnp.int32)[None, :],
            table[None, :],
            0,
        ),
        axis=1,
    )

    def one_turn(position, current):
        pieces_now = tuple(
            (
                lax.dynamic_slice_in_dim(item, position * batch_groups, batch_groups, 2)
                for item in shaped
            )
        )
        chosen = lax.dynamic_slice_in_dim(blocks, position * batch_groups, batch_groups, 0)
        return stepper(current, pieces_now, chosen)

    return lax.fori_loop(0, turn_count, one_turn, carried)


def attend_step(q_heads, my_block, score_scale, head_count, carried, pieces_now, chosen):
    key_piece = heads_of(pieces_now[0], head_count)
    value_piece = heads_of(pieces_now[1], head_count)
    earlier = chosen < my_block
    usable = chosen != my_block
    parity = parity_masks(earlier, usable)
    query_sel = pick_own(q_heads, earlier)
    key_sel = pick_piece(key_piece, earlier)
    value_sel = pick_piece(value_piece, earlier)
    scores = (
        jnp.einsum("jgqhe,jgkhe->jghqk", query_sel, key_sel, preferred_element_type=jnp.float32)
        * score_scale
    )
    usable_mask = usable.reshape(1, -1, 1, 1, 1)
    scores = jnp.where(usable_mask, scores, NEG)
    old_max, old_total, old_sum = carried
    group_max = jnp.max(scores, axis=-1)
    candidate = jnp.max(jnp.where(parity.reshape(1, 2, -1, 1, 1), group_max[:, None], NEG), axis=2)
    new_max = jnp.maximum(old_max, candidate)
    max_sel = pick_own(new_max, earlier)
    weights_exp = jnp.where(usable_mask, jnp.exp(scores - max_sel[..., None]), 0.0)
    moved = jnp.einsum(
        "jghqk,jgkhe->jgqhe",
        weights_exp.astype(jnp.bfloat16),
        value_sel,
        preferred_element_type=jnp.float32,
    )
    factor = jnp.exp(old_max - new_max)
    new_total = old_total * factor + spread(jnp.sum(weights_exp, axis=-1), parity)
    new_sum = old_sum * jnp.swapaxes(factor, 2, 3)[..., None] + spread(moved, parity)
    return (new_max, new_total, new_sum)


def query_grad_step(
    q_heads,
    grad_heads,
    lse_heads,
    delta_heads,
    my_block,
    score_scale,
    head_count,
    carried,
    pieces_now,
    chosen,
):
    key_piece = heads_of(pieces_now[0], head_count)
    value_piece = heads_of(pieces_now[1], head_count)
    earlier = chosen < my_block
    usable = chosen != my_block
    parity = parity_masks(earlier, usable)
    query_sel = pick_own(q_heads, earlier)
    grad_sel = pick_own(grad_heads, earlier)
    lse_sel = pick_own(lse_heads, earlier)
    delta_sel = pick_own(delta_heads, earlier)
    key_sel = pick_piece(key_piece, earlier)
    value_sel = pick_piece(value_piece, earlier)
    scores = (
        jnp.einsum("jgqhe,jgkhe->jghqk", query_sel, key_sel, preferred_element_type=jnp.float32)
        * score_scale
    )
    usable_mask = usable.reshape(1, -1, 1, 1, 1)
    probabilities = jnp.where(usable_mask, jnp.exp(scores - lse_sel[..., None]), 0.0)
    grad_probs = jnp.einsum(
        "jgqhe,jgkhe->jghqk", grad_sel, value_sel, preferred_element_type=jnp.float32
    )
    grad_scores = (probabilities * (grad_probs - delta_sel[..., None])).astype(jnp.bfloat16)
    term = (
        jnp.einsum("jghqk,jgkhe->jgqhe", grad_scores, key_sel, preferred_element_type=jnp.float32)
        * score_scale
    )
    return carried + spread(term, parity)


def key_grad_step(k_heads, v_heads, my_block, score_scale, head_count, carried, pieces_now, chosen):
    query_piece = heads_of(pieces_now[0], head_count)
    grad_piece = heads_of(pieces_now[1], head_count)
    later = my_block < chosen
    usable = chosen != my_block
    parity = parity_masks(later, usable)
    query_sel = pick_piece(query_piece, later)
    grad_sel = pick_piece(grad_piece, later)
    lse_sel = jnp.swapaxes(pick_piece(pieces_now[2], later), 2, 3)
    delta_sel = jnp.swapaxes(pick_piece(pieces_now[3], later), 2, 3)
    key_sel = pick_own(k_heads, later)
    value_sel = pick_own(v_heads, later)
    scores = (
        jnp.einsum("jgqhe,jgkhe->jghqk", query_sel, key_sel, preferred_element_type=jnp.float32)
        * score_scale
    )
    usable_mask = usable.reshape(1, -1, 1, 1, 1)
    probabilities = jnp.where(usable_mask, jnp.exp(scores - lse_sel[..., None]), 0.0)
    grad_probs = jnp.einsum(
        "jgqhe,jgkhe->jghqk", grad_sel, value_sel, preferred_element_type=jnp.float32
    )
    grad_scores = (probabilities * (grad_probs - delta_sel[..., None])).astype(jnp.bfloat16)
    key_term = (
        jnp.einsum("jghqk,jgqhe->jgkhe", grad_scores, query_sel, preferred_element_type=jnp.float32)
        * score_scale
    )
    value_term = jnp.einsum(
        "jghqk,jgqhe->jgkhe",
        probabilities.astype(jnp.bfloat16),
        grad_sel,
        preferred_element_type=jnp.float32,
    )
    return (carried[0] + spread(key_term, parity), carried[1] + spread(value_term, parity))


def shards(
    hidden_in,
    block_pairs,
    ln1_gain,
    ln1_bias,
    qkv_weight,
    query_bias,
    value_bias,
    out_weight,
    out_bias,
    ln2_gain,
    ln2_bias,
    fc_weight,
    fc_bias,
    proj_weight,
    proj_bias,
    out_grad,
):
    params = (
        ln1_gain,
        ln1_bias,
        qkv_weight,
        query_bias,
        value_bias,
        out_weight,
        out_bias,
        ln2_gain,
        ln2_bias,
        fc_weight,
        fc_bias,
        proj_weight,
        proj_bias,
    )
    gathered = (
        lax.all_gather(params[0], "ctx", axis=0, tiled=True),
        lax.all_gather(params[1], "ctx", axis=0, tiled=True),
        lax.all_gather(params[2], "ctx", axis=0, tiled=True),
        lax.all_gather(params[3], "ctx", axis=0, tiled=True),
        lax.all_gather(params[4], "ctx", axis=0, tiled=True),
        lax.all_gather(params[5], "ctx", axis=0, tiled=True),
        lax.all_gather(params[6], "ctx", axis=0, tiled=True),
        lax.all_gather(params[7], "ctx", axis=0, tiled=True),
        lax.all_gather(params[8], "ctx", axis=0, tiled=True),
        lax.all_gather(params[9], "ctx", axis=0, tiled=True),
        lax.all_gather(params[10], "ctx", axis=0, tiled=True),
        lax.all_gather(params[11], "ctx", axis=0, tiled=True),
        lax.all_gather(params[12], "ctx", axis=0, tiled=True),
    )
    (
        gain_one,
        bias_one,
        w_qkv,
        b_query,
        b_value,
        w_out,
        b_out,
        gain_two,
        bias_two,
        w_fc,
        b_fc,
        w_proj,
        b_proj,
    ) = gathered
    device = lax.axis_index("ctx")
    partner = device + 1 - 2 * (device % 2)
    row_count = hidden_in.shape[0]
    model_width = hidden_in.shape[1]
    unit_rows = row_count // SEQS
    halves = SEQS // 2
    head_count = HEADS
    head_size = model_width // head_count
    score_scale = 1.0 / math.sqrt(head_size)
    my_block = block_pairs[device]
    seq_shape = (halves, 2, unit_rows, model_width)
    head_shape = (halves, 2, unit_rows, head_count, head_size)
    inputs = hidden_in.astype(jnp.float32)
    normed = layer_norm(inputs, gain_one.astype(jnp.float32), bias_one.astype(jnp.float32)).astype(
        jnp.bfloat16
    )
    mixed_proj = jnp.dot(normed, w_qkv, preferred_element_type=jnp.float32)
    queries = (mixed_proj[:, :model_width] + b_query.astype(jnp.float32)).astype(jnp.bfloat16)
    key_rows = mixed_proj[:, model_width : 2 * model_width].astype(jnp.bfloat16)
    value_rows = (mixed_proj[:, 2 * model_width :] + b_value.astype(jnp.float32)).astype(
        jnp.bfloat16
    )
    q_seq = queries.reshape(seq_shape)
    k_seq = key_rows.reshape(seq_shape)
    v_seq = value_rows.reshape(seq_shape)
    q_heads = queries.reshape(head_shape)
    k_heads = key_rows.reshape(head_shape)
    v_heads = value_rows.reshape(head_shape)
    far_keys, far_values = from_partner((k_seq, v_seq), "ctx", 0)
    near_keys = jnp.concatenate([k_heads, heads_of(far_keys, head_count)], axis=2)
    near_values = jnp.concatenate([v_heads, heads_of(far_values, head_count)], axis=2)
    scores = (
        jnp.einsum("jpqhe,jpkhe->jphqk", q_heads, near_keys, preferred_element_type=jnp.float32)
        * score_scale
    )
    row_max = jnp.max(scores, axis=-1)
    weights_exp = jnp.exp(scores - row_max[..., None])
    row_total = jnp.sum(weights_exp, axis=-1)
    summed = jnp.einsum(
        "jphqk,jpkhe->jpqhe",
        weights_exp.astype(jnp.bfloat16),
        near_values,
        preferred_element_type=jnp.float32,
    )
    forward_stepper = partial(attend_step, q_heads, my_block, score_scale, head_count)
    row_max, row_total, summed = group_loop(
        (
            lax.all_gather(k_seq, "ctx", axis=2, tiled=True),
            lax.all_gather(v_seq, "ctx", axis=2, tiled=True),
        ),
        unit_rows,
        block_pairs,
        forward_stepper,
        (row_max, row_total, summed),
    )
    attended = summed / jnp.swapaxes(row_total, 2, 3)[..., None]
    log_total = row_max + jnp.log(row_total)
    att_low = attended.reshape(row_count, model_width).astype(jnp.bfloat16)
    branch = jnp.dot(att_low, w_out, preferred_element_type=jnp.float32) + b_out.astype(jnp.float32)
    middle = inputs + branch
    normed_two = layer_norm(
        middle, gain_two.astype(jnp.float32), bias_two.astype(jnp.float32)
    ).astype(jnp.bfloat16)
    pre_act = jnp.dot(normed_two, w_fc, preferred_element_type=jnp.float32) + b_fc.astype(
        jnp.float32
    )
    activation = gelu_tanh(pre_act).astype(jnp.bfloat16)
    result = (
        middle
        + jnp.dot(activation, w_proj, preferred_element_type=jnp.float32)
        + b_proj.astype(jnp.float32)
    )
    layer_out = result.astype(jnp.bfloat16)
    grad_out = out_grad.astype(jnp.float32)
    grad_proj = jnp.dot(activation.T, out_grad, preferred_element_type=jnp.float32)
    grad_bproj = jnp.sum(grad_out, axis=0)
    grad_activ = jnp.dot(out_grad, w_proj.T, preferred_element_type=jnp.float32)
    _, gelu_back = jax.vjp(gelu_tanh, pre_act)
    grad_pre = gelu_back(grad_activ)[0].astype(jnp.bfloat16)
    grad_fc = jnp.dot(normed_two.T, grad_pre, preferred_element_type=jnp.float32)
    grad_bfc = jnp.sum(grad_pre.astype(jnp.float32), axis=0)
    grad_normed_two = jnp.dot(grad_pre, w_fc.T, preferred_element_type=jnp.float32)
    _, norm_back_two = jax.vjp(
        layer_norm, middle, gain_two.astype(jnp.float32), bias_two.astype(jnp.float32)
    )
    grad_middle, grad_gain_two, grad_bias_two = norm_back_two(grad_normed_two)
    grad_middle = grad_middle + grad_out
    grad_branch = grad_middle.astype(jnp.bfloat16)
    grad_wout = jnp.dot(att_low.T, grad_branch, preferred_element_type=jnp.float32)
    grad_bout = jnp.sum(grad_branch.astype(jnp.float32), axis=0)
    grad_att = jnp.dot(grad_branch, w_out.T, preferred_element_type=jnp.float32).astype(
        jnp.bfloat16
    )
    grad_seq = grad_att.reshape(seq_shape)
    grad_heads = grad_att.reshape(head_shape)
    row_delta = jnp.sum(grad_heads.astype(jnp.float32) * attended, axis=-1)
    delta_heads = jnp.swapaxes(row_delta, 2, 3)
    all_lse, all_delta = (
        lax.all_gather(jnp.swapaxes(log_total, 2, 3), "ctx", axis=2, tiled=True),
        lax.all_gather(row_delta, "ctx", axis=2, tiled=True),
    )
    partner_lse = jnp.swapaxes(
        lax.dynamic_slice_in_dim(all_lse, partner * unit_rows, unit_rows, 2), 2, 3
    )
    partner_delta = jnp.swapaxes(
        lax.dynamic_slice_in_dim(all_delta, partner * unit_rows, unit_rows, 2), 2, 3
    )
    far_queries, far_grads = from_partner((q_seq, grad_seq), "ctx", 0)
    near_queries = jnp.concatenate([q_heads, heads_of(far_queries, head_count)], axis=2)
    near_grads = jnp.concatenate([grad_heads, heads_of(far_grads, head_count)], axis=2)
    near_lse = jnp.concatenate([log_total, partner_lse], axis=3)
    near_delta = jnp.concatenate([delta_heads, partner_delta], axis=3)
    local_scores = (
        jnp.einsum(
            "jpqhe,jpkhe->jphqk", near_queries, near_keys, preferred_element_type=jnp.float32
        )
        * score_scale
    )
    probabilities = jnp.exp(local_scores - near_lse[..., None])
    grad_probs = jnp.einsum(
        "jpqhe,jpkhe->jphqk", near_grads, near_values, preferred_element_type=jnp.float32
    )
    grad_scores = (probabilities * (grad_probs - near_delta[..., None])).astype(jnp.bfloat16)
    grad_q_local = (
        jnp.einsum(
            "jphqk,jpkhe->jpqhe",
            grad_scores[:, :, :, :unit_rows, :],
            near_keys,
            preferred_element_type=jnp.float32,
        )
        * score_scale
    )
    grad_k_local = (
        jnp.einsum(
            "jphqk,jpqhe->jpkhe",
            grad_scores[..., :unit_rows],
            near_queries,
            preferred_element_type=jnp.float32,
        )
        * score_scale
    )
    grad_v_local = jnp.einsum(
        "jphqk,jpqhe->jpkhe",
        probabilities.astype(jnp.bfloat16)[..., :unit_rows],
        near_grads,
        preferred_element_type=jnp.float32,
    )
    query_stepper = partial(
        query_grad_step,
        q_heads,
        grad_heads,
        log_total,
        delta_heads,
        my_block,
        score_scale,
        head_count,
    )
    key_stepper = partial(key_grad_step, k_heads, v_heads, my_block, score_scale, head_count)

    def query_piece(carried, pieces, offset):
        return group_loop(pieces, unit_rows, block_pairs, query_stepper, carried)

    def key_piece(carried, pieces, offset):
        return group_loop(
            (pieces[0], pieces[1], all_lse, all_delta), unit_rows, block_pairs, key_stepper, carried
        )

    grad_q_all = query_piece(
        grad_q_local,
        (
            lax.all_gather(k_seq, "ctx", axis=2, tiled=True),
            lax.all_gather(v_seq, "ctx", axis=2, tiled=True),
        ),
        jnp.int32(0),
    )
    grad_k_all, grad_v_all = key_piece(
        (grad_k_local, grad_v_local),
        (
            lax.all_gather(q_seq, "ctx", axis=2, tiled=True),
            lax.all_gather(grad_seq, "ctx", axis=2, tiled=True),
        ),
        jnp.int32(0),
    )
    grad_queries = grad_q_all.reshape(row_count, model_width).astype(jnp.bfloat16)
    grad_keys = grad_k_all.reshape(row_count, model_width).astype(jnp.bfloat16)
    grad_values = grad_v_all.reshape(row_count, model_width).astype(jnp.bfloat16)
    grad_mixed = jnp.concatenate([grad_queries, grad_keys, grad_values], axis=1)
    grad_qkv = jnp.dot(normed.T, grad_mixed, preferred_element_type=jnp.float32)
    grad_bquery = jnp.sum(grad_queries.astype(jnp.float32), axis=0)
    grad_bvalue = jnp.sum(grad_values.astype(jnp.float32), axis=0)
    grad_normed = jnp.dot(grad_mixed, w_qkv.T, preferred_element_type=jnp.float32)
    _, norm_back_one = jax.vjp(
        layer_norm, inputs, gain_one.astype(jnp.float32), bias_one.astype(jnp.float32)
    )
    grad_inputs, grad_gain_one, grad_bias_one = norm_back_one(grad_normed)
    grad_hidden = (grad_inputs + grad_middle).astype(jnp.bfloat16)
    totals = (
        lax.psum_scatter(grad_gain_one, "ctx", scatter_dimension=0, tiled=True),
        lax.psum_scatter(grad_bias_one, "ctx", scatter_dimension=0, tiled=True),
        lax.psum_scatter(grad_qkv, "ctx", scatter_dimension=0, tiled=True),
        lax.psum_scatter(grad_bquery, "ctx", scatter_dimension=0, tiled=True),
        lax.psum_scatter(grad_bvalue, "ctx", scatter_dimension=0, tiled=True),
        lax.psum_scatter(grad_wout, "ctx", scatter_dimension=0, tiled=True),
        lax.psum_scatter(grad_bout, "ctx", scatter_dimension=0, tiled=True),
        lax.psum_scatter(grad_gain_two, "ctx", scatter_dimension=0, tiled=True),
        lax.psum_scatter(grad_bias_two, "ctx", scatter_dimension=0, tiled=True),
        lax.psum_scatter(grad_fc, "ctx", scatter_dimension=0, tiled=True),
        lax.psum_scatter(grad_bfc, "ctx", scatter_dimension=0, tiled=True),
        lax.psum_scatter(grad_proj, "ctx", scatter_dimension=0, tiled=True),
        lax.psum_scatter(grad_bproj, "ctx", scatter_dimension=0, tiled=True),
    )
    return (
        layer_out,
        grad_hidden,
        totals[0],
        totals[1],
        totals[2],
        totals[3],
        totals[4],
        totals[5],
        totals[6],
        totals[7],
        totals[8],
        totals[9],
        totals[10],
        totals[11],
        totals[12],
    )


def solution_any(mesh):
    return jax.shard_map(
        shards,
        mesh=mesh,
        in_specs=(
            P("ctx", None),
            P(),
            P("ctx"),
            P("ctx"),
            P("ctx", None),
            P("ctx"),
            P("ctx"),
            P("ctx", None),
            P("ctx"),
            P("ctx"),
            P("ctx"),
            P("ctx", None),
            P("ctx"),
            P("ctx", None),
            P("ctx"),
            P("ctx", None),
        ),
        out_specs=(
            P("ctx", None),
            P("ctx", None),
            P("ctx"),
            P("ctx"),
            P("ctx", None),
            P("ctx"),
            P("ctx"),
            P("ctx", None),
            P("ctx"),
            P("ctx"),
            P("ctx"),
            P("ctx", None),
            P("ctx"),
            P("ctx", None),
            P("ctx"),
        ),
        check_vma=False,
    )


AXES = ("s", "h", "r")
PLANES = 4


MESH_IDS = pl.DeviceIdType.MESH


class At:
    def __init__(self, ref, *index):
        self.ref, self.index = ref, index

    def now(self):
        return self.ref.at[self.index]

    def still(self):
        return self.ref.at[tuple(i if isinstance(i, slice) else 0 for i in self.index)]


ALL = slice(None)


class Exchange:
    def __init__(self, send, recv):
        self.send, self.recv, self.used, self.open = send, recv, 0, []
        self.s, self.h, self.r = (lax.axis_index(a) for a in AXES)
        self.planes = lax.axis_size("s")
        self.xn = self.h + 1 - 2 * lax.rem(self.h, 2)
        self.yn = lax.rem(self.h + 2, 4)
        self.dn = lax.rem(self.xn + 2, 4)
        self.z = lambda j: lax.rem(self.s + j, self.planes)
        self.X, self.Y, self.D = ({"h": i} for i in (self.xn, self.yn, self.dn))
        self.C = {"r": 1 - self.r}
        self.Z = [None] + [{"s": self.z(j)} for j in range(1, self.planes)]

    def greet(self, peers, meanwhile=None):
        barrier = pltpu.get_barrier_semaphore()
        for peer in peers:
            pl.semaphore_signal(barrier, inc=1, device_id=peer, device_id_type=MESH_IDS)
        if meanwhile:
            meanwhile()
        pl.semaphore_wait(barrier, len(peers))

    def slots(self, count):
        self.used += count
        return range(self.used - count, self.used)

    def copy(self, i, src, dst, peer):
        return pltpu.make_async_remote_copy(
            src_ref=src,
            dst_ref=dst,
            send_sem=self.send.at[i],
            recv_sem=self.recv.at[i],
            device_id=peer,
            device_id_type=MESH_IDS,
        )

    def put(self, i, src, dst, peer):
        self.copy(i, src.now() if isinstance(src, At) else src, dst, peer).start()
        self.open.append((i, src))

    def got(self, i, dst):
        self.copy(i, dst, dst, self.X).wait_recv()

    def close(self):
        for i, src in self.open:
            src = src.still() if isinstance(src, At) else src
            self.copy(i, src, src, self.X).wait_send()


def remote_call(kernel, cid, out_shape, in_specs, out_specs, scratch, sems, name, vmem=56 << 20):
    return pl.pallas_call(
        kernel,
        out_shape=out_shape,
        in_specs=in_specs,
        out_specs=out_specs,
        scratch_shapes=scratch
        + [pltpu.SemaphoreType.DMA((sems,)), pltpu.SemaphoreType.DMA((sems,)), pltpu.SemaphoreType.DMA((16,))],
        compiler_params=pltpu.CompilerParams(
            collective_id=cid, has_side_effects=True, vmem_limit_bytes=vmem
        ),
        name=name,
    )


ANY = pl.BlockSpec(memory_space=pl.ANY)
VMEM = pl.BlockSpec(memory_space=pltpu.VMEM)


def by_x(k, j):
    return (k + j) % 2 == 0


def act(plan, steps, m, c, last_tile):
    for (em, ec), todo in plan.items():
        if (em == ec) == last_tile:

            @pl.when(m == em if last_tile else (m == em) & (c == ec))
            def _():
                for step, k, *js in todo:
                    steps[step](k, js)


def gather_steps(ex, ins, outs, local):
    s, h, r, n = ex.s, ex.h, ex.r, ex.planes
    part = len(ins) - 1
    place = lambda k, t, c: (t, c) if k == part else (t, c, r)
    slab = lambda k, t, c: outs[k].at[place(k, t, c)]
    own = [pltpu.make_async_copy(ins[k], slab(k, s, h), local.at[k + 1]) for k in range(part + 1)]
    for c in own:
        c.start()
    iz, ix, iy, ir, ic = ([ex.slots(n) for _ in outs] for _ in range(5))

    def cross(k, j):
        ex.put(iz[k][j], ins[k], slab(k, s, h), ex.Z[j])

    def forward(k, j):
        t = ex.z(j)
        if j:
            ex.got(iz[k][n - j], slab(k, t, h))
        src = At(outs[k], *place(k, t, h)) if j else ins[k]
        ex.put(ix[k][j], src, slab(k, t, h), ex.X)
        ex.put(iy[k][j], src, slab(k, t, h), ex.Y)

    def relay(k, j):
        t = ex.z(j)
        slots, frm, peer = (ix, ex.xn, ex.Y) if by_x(k, j) else (iy, ex.yn, ex.X)
        ex.got(slots[k][j], slab(k, t, frm))
        ex.put(ir[k][j], At(outs[k], *place(k, t, frm)), slab(k, t, frm), peer)

    def across(k, j):
        t = ex.z(j)
        slots, frm = (iy, ex.yn) if by_x(k, j) else (ix, ex.xn)
        ex.got(slots[k][j], slab(k, t, frm))
        ex.got(ir[k][j], slab(k, t, ex.dn))
        if not j:
            own[k].wait()
        ex.put(ic[k][j], At(outs[k], t, ALL, r), outs[k].at[t, :, r], ex.C)

    def last():
        for j in range(n):
            for k in range(part):
                ex.got(ic[k][j], outs[k].at[ex.z(j), :, 1 - r])
            ex.got(ix[part][j], slab(part, ex.z(j), ex.xn))
            ex.got(iy[part][j], slab(part, ex.z(j), ex.yn))
        own[part].wait()

    each = lambda step: lambda k, js: [step(k, j) for j in js]
    return dict(cross=each(cross), forward=each(forward), relay=each(relay), across=each(across)), last


def by_tile(shape, step):
    height, width = shape
    if height % 48:

        @pl.loop(0, width // 768)
        def _(i):
            step(slice(None), pl.ds(pl.multiple_of(i * 768, 768), 768))
    else:

        @pl.loop(0, height // 48)
        def _(i):
            step(pl.ds(pl.multiple_of(i * 48, 48), 48), slice(None))


def reduce_steps(ins, outs, bufs, send, recv, local):
    count = len(ins)
    mine, from_c, one, two, from_z = (bufs[i * count : (i + 1) * count] for i in range(5))
    ex = Exchange(send, recv)
    s, h, r, n = ex.s, ex.h, ex.r, ex.planes
    own = [
        pltpu.make_async_copy(a.at[:, :, r], m, local.at[k]) for k, (a, m) in enumerate(zip(ins, mine))
    ]
    for c in own:
        c.start()
    ex.greet([ex.X, ex.Y, ex.C] + ex.Z[1:])
    ic, i1, i2, iz = ([ex.slots(n) for _ in ins] for _ in range(4))
    i1b = [ex.slots(n) for _ in ins]
    for k in (1, 0, 2):
        for j in range(n):
            ex.put(ic[k][j], At(ins[k], ex.z(j), ALL, 1 - r), from_c[k].at[ex.z(j)], ex.C)
    for c in own:
        c.wait()

    def add(to, *parts):
        def step(rows, cols):
            total = to[rows, cols].astype(jnp.float32)
            for part in parts:
                total += part[rows, cols].astype(jnp.float32)
            to[rows, cols] = total.astype(to.dtype)

        by_tile(to.shape, step)

    def way(k, j):
        return (ex.X, ex.xn, ex.Y, ex.yn) if by_x(k, j) else (ex.Y, ex.yn, ex.X, ex.xn)

    def first(k, js):
        m = mine[k]
        for j in js:
            t = ex.z(j)
            ex.got(ic[k][j], from_c[k].at[t])
            add(m.at[t, ex.dn], from_c[k].at[t, ex.dn])
            ex.put(i1b[k][j], At(m, t, ex.dn), one[k].at[j, 1], way(k, j)[0])
        for j in js:
            t, (peer, near, _, _) = ex.z(j), way(k, j)
            add(m.at[t, near], from_c[k].at[t, near])
            ex.put(i1[k][j], At(m, t, near), one[k].at[j, 0], peer)

    def second(k, js):
        m = mine[k]
        for j in js:
            t, (_, _, peer, other) = ex.z(j), way(k, j)
            ex.got(i1b[k][j], one[k].at[j, 1])
            add(m.at[t, other], from_c[k].at[t, other], one[k].at[j, 1])
            ex.put(i2[k][j], At(m, t, other), two[k].at[j], peer)

    def third(k, js):
        m = mine[k]
        for j in js:
            t = ex.z(j)
            ex.got(i1[k][j], one[k].at[j, 0])
            ex.got(i2[k][j], two[k].at[j])
            add(m.at[t, h], from_c[k].at[t, h], one[k].at[j, 0], two[k].at[j])
            if j:
                ex.put(iz[k][j], At(m, t, h), from_z[k].at[j], ex.Z[j])

    def last():
        for k, (m, o) in enumerate(zip(mine, outs)):
            for j in range(1, n):
                ex.got(iz[k][j], from_z[k].at[j])

            def step(rows, cols):
                total = m[s, h, rows, cols].astype(jnp.float32)
                for j in range(1, n):
                    total += from_z[k][j, rows, cols].astype(jnp.float32)
                o[rows, cols] = total

            by_tile(o.shape, step)

        ex.close()

    return ex, dict(first=first, second=second, third=third), last


HD = 64


GATHER_PLAN = {
    (0, 0): [("forward", 0, 1, 3, 2), ("relay", 1, 1, 3, 2)],
    (4, 0): [("relay", 0, 1)],
    (4, 3): [("relay", 0, 3)],
    (5, 1): [("relay", 0, 2), ("forward", 2, 1, 3, 2)],
    (5, 5): [("across", 1, 0, 1, 3, 2)],
    (7, 0): [("across", 0, 0, 1, 3, 2)],
}
GATHER_FIRST = [("forward", 1, 1, 3, 2), ("relay", 1, 0), ("relay", 0, 0), ("cross", 2, 1, 3, 2), ("forward", 2, 0)]
GATHER_START = [("cross", 1, 1, 3, 2), ("cross", 0, 1, 3, 2), ("forward", 1, 0), ("forward", 0, 0)]


SMEM = pl.BlockSpec(memory_space=pltpu.SMEM)


def forward_kernel(vectors, inv, blk, x_ref, w_ref, *refs):
    count = 3
    v_refs, refs = refs[:vectors], refs[vectors:]
    ins, refs = refs[:count], refs[count:]
    kept, (vec_ref, low_ref, lse_ref) = refs[:5], refs[5:8]
    outs = refs[8 : 8 + count]
    norm_ref, q_ref, kv_ref, w_out, xo_ref, xa, ws, wa, wf, qt, ks, vt, os, sc, send, recv, local = refs[8 + count :]
    f32, bf16 = jnp.float32, jnp.bfloat16
    ex = Exchange(send, recv)
    s, h, r, n = ex.s, ex.h, ex.r, ex.planes
    H, U, D = xa.shape[1:]
    d, N = w_ref.shape
    W = N // 3 // H
    own = pltpu.make_async_copy(x_ref.at[s], xa.at[s, h], local.at[0])
    own.start()

    def slabs():
        lines = [v[...].astype(f32) for v in v_refs]
        lines = [v[:, i : i + d] for v in lines for i in range(0, v.shape[1], d)]
        lines = jnp.concatenate(lines + [jnp.zeros((64 - len(lines), d), f32)], axis=0).T.astype(bf16)
        for k in range(H):
            ws[k] = jnp.concatenate(
                [w_ref[:, c * D + k * W : c * D + (k + 1) * W] for c in range(3)] + [lines], axis=1
            )

    ex.greet([ex.X, ex.Y, ex.D, ex.C] + ex.Z[1:], slabs)
    iw, ix, iy, ir, iz, iwz, iwc, ik = (ex.slots(n) for _ in range(8))
    steps, last = gather_steps(ex, ins, outs, local)
    cross = lambda j: ex.put(iz[j], x_ref.at[ex.z(j)], xa.at[s, h], ex.Z[j])
    cross(1)
    for k, (peer, to) in enumerate(((ex.X, ex.xn), (ex.Y, ex.yn), (ex.D, ex.dn))):
        ex.put(iw[k], ws.at[to], wa.at[s, h, r], peer)
    wa[s, h, r] = ws[h]
    own.wait()

    def forward(j):
        t = ex.z(j)
        if j:
            ex.got(iz[n - j], xa.at[t, h])
        if j in after:
            cross(after[j])
        ex.put(ix[j], xa.at[t, h], xa.at[t, h], ex.X)
        ex.put(iy[j], xa.at[t, h], xa.at[t, h], ex.Y)

    def relay(j):
        t = ex.z(j)
        slots, frm, peer = (ix, ex.xn, ex.Y) if by_x(0, j) else (iy, ex.yn, ex.X)
        ex.got(slots[j], xa.at[t, frm])
        ex.put(ir[j], xa.at[t, frm], xa.at[t, frm], peer)

    def weights(j):
        if j:
            ex.got(iwz[n - j], wa.at[ex.z(j), :, r])
        ex.put(iwc[j], wa.at[ex.z(j), :, r], wa.at[ex.z(j), :, r], ex.C)

    after = {3: 3, 1: 2}
    forward(0)
    for k, frm in enumerate((ex.xn, ex.yn, ex.dn)):
        ex.got(iw[k], wa.at[s, frm, r])
    forward(3)
    relay(0)
    forward(1)
    for j in range(1, n):
        ex.put(iwz[j], wa.at[s, :, r], wa.at[s, :, r], ex.Z[j])
    weights(0)
    relay(3)
    relay(1)
    forward(2)
    for j in (1, 3, 2):
        weights(j)
    for step, k, *js in GATHER_START:
        steps[step](k, js)
    for j in range(n):
        ex.got(iwc[j], wa.at[ex.z(j), :, 1 - r])
    rows = H * 2 * d
    for t in range(n):
        block = wa[t].astype(f32).reshape(rows, N // H + 64)
        wf[t * rows : (t + 1) * rows] = block
    vec_ref[...] = wf[:, N // H :].T[:16]
    w = wf[:, : N // H].astype(bf16)
    w_out[...] = w
    gain, bias = vec_ref[0:1], vec_ref[1:2]

    def mine(row):
        picked = jnp.zeros((1, W), f32)
        for k in range(H):
            picked = jnp.where(h == k, vec_ref[row : row + 1, k * W : (k + 1) * W], picked)
        return picked

    bq, bv = mine(2), mine(3)

    def batch(j):
        t = ex.z(j)
        slots, frm = (iy, ex.yn) if by_x(0, j) else (ix, ex.xn)
        ex.got(slots[j], xa.at[t, frm])
        ex.got(ir[j], xa.at[t, ex.dn])
        x = xa[t].reshape(H * U, D).astype(f32)
        normed = layer_norm(x, gain, bias).astype(bf16)
        pairs = pl.ds(t * H, H)
        norm_ref[t] = normed.reshape(H, U, D)
        mixed = jnp.dot(normed, w, preferred_element_type=f32)
        q = (mixed[:, :W] + bq).astype(bf16) * jnp.asarray(0.125, bf16)
        q_ref[pairs] = q.reshape(H, U, W)
        kv = jnp.concatenate([mixed[:, W : 2 * W], mixed[:, 2 * W :] + bv], axis=1).astype(bf16)
        kv_ref[pairs, 0] = kv.reshape(H, U, 2 * W)
        ex.put(ik[j], kv_ref.at[pairs, 0], kv_ref.at[pairs, 1], ex.C)

    relay(2)
    batch(0)
    batch(3)
    batch(1)
    batch(2)
    for step, k, *js in GATHER_FIRST:
        steps[step](k, js)
    xo_ref[...] = xa[:, h]
    for j in (0, 1, 3, 2):
        ex.got(ik[j], kv_ref.at[pl.ds(ex.z(j) * H, H), 1])

    saves = [
        pltpu.make_async_copy(a, b, local.at[4 + i])
        for i, (a, b) in enumerate(zip((norm_ref, q_ref, kv_ref, w_out, xo_ref), kept))
    ]
    for c in saves:
        c.start()

    npair = inv.shape[0]
    nh = W // HD
    B = 2 * U
    TQ, TK = 2 * U, 2 * B

    @pl.loop(0, npair, unroll=2)
    def _(i):
        p = inv[i]
        qt[:, pl.ds(pl.multiple_of(i * U, U), U)] = q_ref[p].T
        kv = kv_ref[p].reshape(B, 2 * W)
        for h in range(nh):
            ks[h, pl.ds(i * B, B), :] = kv[:, h * HD : (h + 1) * HD]
        vct = kv[:, W:].T
        for h in range(nh):
            vt[h, 0:HD, pl.ds(pl.multiple_of(i * B, B), B)] = vct[h * HD : (h + 1) * HD]
            vt[h, HD:, pl.ds(pl.multiple_of(i * B, B), B)] = jnp.ones((vt.shape[1] - HD, B), vt.dtype)

    def scores(m, c, carry, masked):
        out = []
        rows = pl.ds(pl.multiple_of(c * TK, TK), TK)
        for h in range(nh):
            qh = qt[h * HD : (h + 1) * HD, pl.ds(pl.multiple_of(m * TQ, TQ), TQ)]
            s = jnp.dot(ks[h, rows, :], qh, preferred_element_type=jnp.float32)
            if masked:
                row = lax.broadcasted_iota(jnp.int32, s.shape, 0)
                col = lax.broadcasted_iota(jnp.int32, s.shape, 1)
                s = jnp.where((row >= B) & (col < U), NEG, s)
            sc[h, rows, :] = s
            out.append(jnp.maximum(carry[h], jnp.max(s.reshape(TK // 8, 8, TQ), axis=0)))
        return tuple(out)

    def values(c, carry, tops):
        out = []
        rows = pl.ds(pl.multiple_of(c * TK, TK), TK)
        for h in range(nh):
            p = jnp.exp(sc[h, rows, :] - tops[h]).astype(jnp.bfloat16)
            out.append(carry[h] + jnp.dot(vt[h, :, rows], p, preferred_element_type=jnp.float32))
        return tuple(out)

    @pl.loop(0, npair // 2)
    def _(m):
        tops = tuple(jnp.full((8, TQ), NEG, jnp.float32) for _ in range(nh))
        tops = lax.fori_loop(0, m, lambda c, x: scores(m, c, x, False), tops)
        tops = [jnp.max(t, axis=0, keepdims=True) for t in scores(m, m, tops, True)]

        def step(c, x):
            x = values(c, x, tops)
            act(GATHER_PLAN, steps, m, c, False)
            return x

        init = tuple(jnp.zeros((vt.shape[1], TQ), jnp.float32) for _ in range(nh))
        carry = values(m, lax.fori_loop(0, m, step, init), tops)
        carry = list(zip(tops, carry))
        rows = []
        for h in range(nh):
            mx, acc = carry[h]
            tot = acc[HD : HD + 1]
            rows.append(acc[:HD] / tot)
            lse_ref[h : h + 1, pl.ds(pl.multiple_of(m * TQ, TQ), TQ)] = mx + jnp.log(tot)
        os[pl.ds(pl.multiple_of(m * TQ, TQ), TQ), :] = jnp.concatenate(rows, axis=0).T.astype(bf16)
        act(GATHER_PLAN, steps, m, m, True)

    @pl.loop(0, npair)
    def _(p):
        low_ref[pl.ds(pl.multiple_of(p * U, U), U), :] = os[pl.ds(blk[p] * U, U), :]

    last()
    for c in saves:
        c.wait()
    ex.close()


def forward(inv, blk, x, w, vectors, *weights):
    S, U, D = x.shape
    d, N = w.shape
    H, Q = (lax.axis_size(a) for a in AXES[1:])
    W = N // 3 // H
    npair = S * H
    R, K = npair * U, npair * Q * U
    nh = W // HD
    f32, bf16 = jnp.float32, jnp.bfloat16
    n = len(weights)
    shape = jax.ShapeDtypeStruct
    kept = [
        ((S, H, U, D), bf16),
        ((npair, U, W), bf16),
        ((npair, Q, U, 2 * W), bf16),
        ((D, N // H), bf16),
        ((S, U, D), bf16),
    ]
    return remote_call(
        partial(forward_kernel, len(vectors)),
        0,
        [shape(*kind) for kind in kept]
        + [shape((16, D), f32), shape((R, W), bf16), shape((8, R), f32)]
        + [shape((S, H, Q) + a.shape, a.dtype) for a in weights[:-1]]
        + [shape((S, H) + weights[-1].shape, bf16)],
        [SMEM] * 2 + [ANY] + [VMEM] * (1 + len(vectors)) + [ANY] * n,
        [ANY] * 5 + [VMEM] * 3 + [ANY] * n,
        [pltpu.VMEM(*kind) for kind in kept]
        + [
            pltpu.VMEM((S, H, U, D), bf16),
            pltpu.VMEM((H, d, N // H + 64), bf16),
            pltpu.VMEM((S, H, Q, d, N // H + 64), bf16),
            pltpu.VMEM((D, N // H + 64), f32),
            pltpu.VMEM((W, R), bf16),
            pltpu.VMEM((nh, K, HD), bf16),
            pltpu.VMEM((nh, HD + 16, K), bf16),
            pltpu.VMEM((R, W), bf16),
            pltpu.VMEM((nh, K, 2 * U), f32),
        ],
        8 * S + 5 * S * n,
        "forward",
    )(inv, blk, x, w, *vectors, *weights)


REDUCE_PLAN = {
    (7, 1): [("first", 1, 1, 2, 3, 0)],
    (7, 6): [("second", 1, 1, 2, 3, 0)],
    (7, 7): [("first", 0, 1, 2, 3, 0)],
    (5, 3): [("third", 1, 1, 2, 3, 0)],
    (5, 4): [("second", 0, 1, 2, 3, 0)],
    (4, 0): [("first", 2, 1, 2, 3, 0)],
    (3, 1): [("third", 0, 1, 2, 3, 0)],
    (3, 2): [("second", 2, 1, 2, 3, 0)],
    (2, 1): [("third", 2, 1, 2, 3, 0)],
}


def attend_back_kernel(count, inv, blk, q_in, kv_in, g_in, o_in, lse_ref, out_ref, *refs):
    ins, gm_ref, lo_ref, outs = refs[:count], refs[count], refs[count + 1], refs[count + 2 : 2 * count + 2]
    bufs = refs[2 * count + 2 : 7 * count + 2]
    q_ref, kv_ref, g_ref, o_ref = refs[7 * count + 2 : 7 * count + 6]
    qt, gt, qx, gx, ks, vs, kt, delta, dkv, dqs, over, back, send, recv, local = refs[7 * count + 6 :]
    loads = [
        pltpu.make_async_copy(a, b, local.at[8 + i])
        for i, (a, b) in enumerate(((q_in, q_ref), (kv_in, kv_ref), (g_in, g_ref), (o_in, o_ref)))
    ]
    for c in loads:
        c.start()
    npair, U, W = q_ref.shape
    nh = W // HD
    B = kv_ref.shape[1]
    TQ, TK = 2 * U, 2 * B
    f32, bf16 = jnp.float32, jnp.bfloat16
    ex, steps, last = reduce_steps(ins, outs, bufs, send, recv, local)
    swap = ex.slots(npair // 2)
    il = ex.slots(ex.planes)
    keep = pltpu.make_async_copy(out_ref.at[ex.s], lo_ref.at[ex.s], local.at[count])
    keep.start()
    for j in range(1, ex.planes):
        ex.put(il[j], out_ref.at[ex.z(j)], lo_ref.at[ex.s], ex.Z[j])

    for c in loads:
        c.wait()

    @pl.loop(0, npair, unroll=2)
    def _(i):
        p = inv[i]
        qc = q_ref[p]
        gc = g_ref[p]
        oc = o_ref[pl.ds(p * U, U), :]
        cols = pl.ds(pl.multiple_of(i * U, U), U)
        qt[:, cols] = qc.T
        gt[:, cols] = gc.T
        prod = (oc.astype(f32) * gc.astype(f32)).T
        zero = jnp.zeros((U, HD), bf16)
        for h in range(nh):
            delta[h : h + 1, cols] = jnp.sum(prod[h * HD : (h + 1) * HD], axis=0, keepdims=True)
            qx[h, pl.ds(i * U, U), :] = jnp.concatenate([zero, qc[:, h * HD : (h + 1) * HD]], axis=1)
            gx[h, pl.ds(i * U, U), :] = jnp.concatenate([gc[:, h * HD : (h + 1) * HD], zero], axis=1)
        kv = kv_ref[p]
        kc, vc = kv[:, :W], kv[:, W:]
        kt[:, pl.ds(pl.multiple_of(i * B, B), B)] = kc.T
        for h in range(nh):
            ks[h, pl.ds(i * B, B), :] = kc[:, h * HD : (h + 1) * HD]
            vs[h, pl.ds(i * B, B), :] = vc[:, h * HD : (h + 1) * HD]

    dkv[...] = jnp.zeros_like(dkv)

    def tile(m, c, carry, masked):
        out = []
        qcols = pl.ds(pl.multiple_of(m * TQ, TQ), TQ)
        krows = pl.ds(pl.multiple_of(c * TK, TK), TK)
        for h in range(nh):
            hs = slice(h * HD, (h + 1) * HD)
            s = jnp.dot(ks[h, krows, :], qt[hs, qcols], preferred_element_type=f32)
            p = jnp.exp(s - lse_ref[h : h + 1, qcols])
            if masked:
                row = lax.broadcasted_iota(jnp.int32, s.shape, 0)
                col = lax.broadcasted_iota(jnp.int32, s.shape, 1)
                p = jnp.where((row >= B) & (col < U), 0.0, p)
            dp = jnp.dot(vs[h, krows, :], gt[hs, qcols], preferred_element_type=f32)
            ds = (p * (dp - delta[h : h + 1, qcols])).astype(bf16)
            dkv[h, krows, :] += jnp.dot(
                p.astype(bf16), gx[h, qcols, :], preferred_element_type=f32
            ) + jnp.dot(ds, qx[h, qcols, :], preferred_element_type=f32)
            out.append(carry[h] + jnp.dot(kt[hs, krows], ds, preferred_element_type=f32))
        return tuple(out)

    def halves(b, half):
        rows = pl.ds(pl.multiple_of(b * B + half * U, U), U)
        parts = [dkv[h, rows, :] for h in range(nh)]
        return jnp.concatenate([x[:, HD:] for x in parts] + [x[:, :HD] for x in parts], axis=1)

    @pl.loop(0, npair // 2)
    def _(turn):
        m = npair // 2 - 1 - turn
        init = tuple(jnp.zeros((HD, TQ), f32) for _ in range(nh))

        def step(c, x):
            x = tile(m, c, x, False)
            act(REDUCE_PLAN, steps, m, c, False)
            return x

        carry = lax.fori_loop(0, m, step, init)
        carry = tile(m, m, carry, True)
        dqs[pl.ds(pl.multiple_of(m * TQ, TQ), TQ), :] = (jnp.concatenate(carry, axis=0).T * 0.125).astype(bf16)
        for k in range(2):
            over[2 * m + k] = halves(2 * m + k, 1).astype(bf16)
        ex.copy(swap[0] + m, over.at[pl.ds(2 * m, 2)], back.at[pl.ds(2 * m, 2)], ex.C).start()
        act(REDUCE_PLAN, steps, m, m, True)

    @pl.loop(0, npair // 2)
    def _(m):
        moved = ex.copy(swap[0] + m, over.at[pl.ds(2 * m, 2)], back.at[pl.ds(2 * m, 2)], ex.C)
        moved.wait_recv()
        moved.wait_send()

    @pl.loop(0, npair)
    def _(p):
        b = blk[p]
        rows = pl.ds(b * B, U)
        parts = [dkv[h, rows, :] for h in range(nh)]
        own = jnp.concatenate([x[:, HD:] for x in parts] + [x[:, :HD] for x in parts], axis=1)
        own = (own + back[b].astype(f32)).astype(bf16)
        gm_ref[p] = jnp.concatenate([dqs[pl.ds(b * U, U), :], own], axis=1)

    for j in range(1, ex.planes):
        ex.got(il[ex.planes - j], lo_ref.at[ex.z(j)])
    keep.wait()
    last()


def attend_back(inv, blk, q, kv, g, o, lse, out, *grads):
    npair, U, W = q.shape
    R, K = npair * U, npair * kv.shape[1]
    nh = W // HD
    S, H, Q = (lax.axis_size(a) for a in AXES)
    n = len(grads)
    f32, bf16 = jnp.float32, jnp.bfloat16
    tails = [a.shape[3:] for a in grads]
    buffers = [[pltpu.VMEM(lead + t, bf16) for t in tails] for lead in ((S, H), (S, H), (S, 2), (S,), (S,))]
    return remote_call(
        partial(attend_back_kernel, n),
        2,
        [jax.ShapeDtypeStruct((npair, R // npair, 3 * W), bf16), jax.ShapeDtypeStruct(out.shape, bf16)]
        + [jax.ShapeDtypeStruct(t, f32) for t in tails],
        [SMEM] * 2 + [ANY] * 4 + [VMEM] + [ANY] * (n + 1),
        [VMEM, ANY] + [VMEM] * n,
        sum(buffers, [])
        + [pltpu.VMEM(a.shape, a.dtype) for a in (q, kv, g, o)]
        + [
            pltpu.VMEM((W, R), bf16),
            pltpu.VMEM((W, R), bf16),
            pltpu.VMEM((nh, R, 2 * HD), bf16),
            pltpu.VMEM((nh, R, 2 * HD), bf16),
            pltpu.VMEM((nh, K, HD), bf16),
            pltpu.VMEM((nh, K, HD), bf16),
            pltpu.VMEM((W, K), bf16),
            pltpu.VMEM((8, R), f32),
            pltpu.VMEM((nh, K, 2 * HD), f32),
            pltpu.VMEM((R, W), bf16),
            pltpu.VMEM((npair, R // npair, 2 * W), bf16),
            pltpu.VMEM((npair, R // npair, 2 * W), bf16),
        ],
        5 * S * n + npair // 2 + S,
        "attend_back",
        60 << 20,
    )(inv, blk, q, kv, g, o, lse, out, *grads)


def middle_kernel(
    low_ref, x_ref, g_ref, vec_ref, fc_ref, proj_ref, wo_ref,
    lo_ref, gmid_ref, small_ref, ga_ref, gfc_ref, gproj_ref, gout_ref,
    bias, ra, fc, wp, wo_in, wf, wo, act_ref, dpre, deriv, g, att, mid, z_ref, n2, n2t, y, t2, gb, sb, gfc, gproj, gout,
    send, recv, local,
):
    f32, bf16 = jnp.float32, jnp.bfloat16
    ex = Exchange(send, recv)
    s, h, r, n = ex.s, ex.h, ex.r, ex.planes
    H, U, W = low_ref.shape[1:]
    R, D = att.shape
    d = fc.shape[3]
    loads = [
        pltpu.make_async_copy(a, b, local.at[i])
        for i, (a, b) in enumerate(
            (
                (wo_ref, wo_in),
                (proj_ref.at[:, h], wp.at[:, h, r]),
                (fc_ref, fc),
                (low_ref.at[:, h], ra.at[h]),
                (g_ref.at[s], g.at[s]),
                (proj_ref.at[:, ex.xn], wp.at[:, ex.xn, r]),
                (proj_ref.at[:, ex.yn], wp.at[:, ex.yn, r]),
            )
        )
    ]
    for c in loads:
        c.start()
    ex.greet([ex.X, ex.Y, ex.D, ex.C] + ex.Z[1:])
    there, back = ex.slots(3), ex.slots(3)
    ir, ic, ig = (ex.slots(n) for _ in range(3))
    sides = ((ex.X, ex.xn), (ex.Y, ex.yn), (ex.D, ex.dn))
    for k, (peer, to) in enumerate(sides):
        ex.put(there[k], low_ref.at[:, to], ra.at[h], peer)
    for j in range(n):
        frm, peer = (ex.xn, ex.Y) if by_x(0, j) else (ex.yn, ex.X)
        ex.put(ir[j], proj_ref.at[ex.z(j), frm], wp.at[ex.z(j), frm, r], peer)
    for j in range(1, n):
        ex.put(ig[j], g_ref.at[ex.z(j)], g.at[s], ex.Z[j])

    def across(j):
        ex.got(ir[j], wp.at[ex.z(j), ex.dn, r])
        ex.put(ic[j], wp.at[ex.z(j), :, r], wp.at[ex.z(j), :, r], ex.C)

    dot = partial(jnp.dot, preferred_element_type=f32)
    dot_nt = lambda a, b: lax.dot_general(a, b, (((1,), (1,)), ((), ())), preferred_element_type=f32)
    dot_tn = lambda a, b: lax.dot_general(a, b, (((0,), (0,)), ((), ())), preferred_element_type=f32)
    loads[0].wait()
    wo[...] = wo_in[...].astype(f32).reshape(D, D).astype(bf16)
    loads[2].wait()

    @pl.loop(0, n)
    def _(b):
        cols = pl.ds(pl.multiple_of(b * D, D), D)
        wf[b] = fc[:, :, :, :, cols].astype(f32).reshape(D, D).astype(bf16)

    each = D // d
    share = bias.shape[1] // each // d
    for i in range(n):
        parts = [(8 + k, e * d) for e in range(i * each // n, (i + 1) * each // n) for k in range(share)]
        bias[0:1, i * D : (i + 1) * D] = jnp.concatenate([vec_ref[k : k + 1, c : c + d] for k, c in parts], axis=1)
    y[...] = jnp.zeros_like(y)
    t2[...] = jnp.zeros_like(t2)
    loads[3].wait()
    for k, (peer, frm) in enumerate(sides):
        ex.got(there[k], ra.at[frm])
    att[...] = jnp.concatenate([ra[k].reshape(R, W) for k in range(H)], axis=1)
    m = x_ref[...].astype(f32) + dot(att[...], wo[...]) + vec_ref[4:5]
    mid[...] = m
    center = m - jnp.mean(m, axis=-1, keepdims=True)
    rstd = lax.rsqrt(jnp.mean(center * center, axis=-1, keepdims=True) + 1e-05)
    z = center * rstd
    z_ref[...] = z
    normed = (z * vec_ref[5:6] + vec_ref[6:7]).astype(bf16)
    n2[...] = normed
    n2t[...] = normed.T
    slope = math.sqrt(2.0 / math.pi)

    def up(b):
        cols = slice(b * D, (b + 1) * D)
        pre = dot(n2[...], wf[b]) + bias[0:1, cols]
        square = pre * pre
        tanh = jnp.tanh(slope * pre * (1.0 + 0.044715 * square))
        half = 0.5 * (1.0 + tanh)
        act_ref[b] = (pre * half).astype(bf16)
        deriv[b] = half + 0.5 * pre * (1.0 - tanh * tanh) * (slope * (1.0 + 3 * 0.044715 * square))

    up(0)
    for i in (1, 5, 6):
        loads[i].wait()
    across(0)
    across(1)
    up(1)
    across(2)
    across(3)
    up(2)
    up(3)
    loads[4].wait()
    for j in range(1, n):
        ex.got(ig[n - j], g.at[ex.z(j)])

    def down(j):
        b = ex.z(j)
        ex.got(ic[j], wp.at[b, :, 1 - r])
        pre = dot_nt(g[...].reshape(R, D), wp[b].reshape(D, D)) * deriv[b]
        dpre[b] = pre.astype(bf16)
        small_ref[pl.ds(b + 4, 1)] = jnp.sum(dpre[b].astype(f32), axis=0, keepdims=True)
        t2[...] += dot_nt(dpre[b], wf[b])

    for j in range(n):
        down(j)
    t, z = t2[...], z_ref[...]
    g32 = g[...].reshape(R, D).astype(f32)
    e = t * vec_ref[5:6]
    inner = e - jnp.mean(e, axis=-1, keepdims=True) - z * jnp.mean(e * z, axis=-1, keepdims=True)
    gm = g32 + inner * rstd
    gmid_ref[...] = gm
    gb[...] = gm.astype(bf16)
    ga = dot_nt(gb[...], wo[...]).astype(bf16)
    for k in range(H):
        sb[k] = ga[:, k * W : (k + 1) * W].reshape(sb.shape[1:])
    for k, (peer, to) in enumerate(sides):
        ex.put(back[k], sb.at[to], ga_ref.at[:, h], peer)
    mine = pltpu.make_async_copy(sb.at[h], ga_ref.at[:, h], local.at[3])
    mine.start()
    stores = []

    def store(src, dst):
        stores.append(pltpu.make_async_copy(src, dst, local.at[4 + len(stores)]))
        stores[-1].start()

    for b in range(n):
        grad = g[...].reshape(R, D)
        gproj[b] = dot_tn(act_ref[b], grad).astype(bf16).reshape(gproj.shape[1:])
        gfc[:, :, :, :, b * D : (b + 1) * D] = dot(n2t[...], dpre[b]).reshape(gfc.shape[:4] + (D,)).astype(bf16)
        y[...] += dot(act_ref[b], wp[b].reshape(D, D))
    store(gproj, gproj_ref)
    store(gfc, gfc_ref)
    gout[...] = dot_tn(att[...], gb[...]).reshape(gout.shape).astype(bf16)
    store(gout, gout_ref)
    lo_ref[...] = (mid[...] + y[...] + vec_ref[7:8]).astype(bf16)
    small_ref[1:2] = jnp.sum(t2[...] * z_ref[...], axis=0, keepdims=True)
    small_ref[2:3] = jnp.sum(t2[...], axis=0, keepdims=True)
    small_ref[0:1] = jnp.sum(gb[...].astype(f32), axis=0, keepdims=True)
    small_ref[3:4] = jnp.sum(g[...].reshape(R, D).astype(f32), axis=0, keepdims=True)
    for k, (peer, frm) in enumerate(sides):
        ex.got(back[k], ga_ref.at[:, frm])
    for c in stores + [mine]:
        c.wait()
    ex.close()


def middle(low, x, g, vecs, fc, proj, wo):
    S, H, U, W = low.shape
    R, D = x.shape
    whole = fc.shape[:3] + proj.shape[2:]
    f32, bf16 = jnp.float32, jnp.bfloat16
    vm = pltpu.VMEM
    return remote_call(
        middle_kernel,
        4,
        [
            jax.ShapeDtypeStruct((R, D), bf16),
            jax.ShapeDtypeStruct((R, D), f32),
            jax.ShapeDtypeStruct((8, D), f32),
            jax.ShapeDtypeStruct(low.shape, bf16),
            jax.ShapeDtypeStruct(fc.shape, bf16),
            jax.ShapeDtypeStruct(whole, bf16),
            jax.ShapeDtypeStruct(wo.shape, bf16),
        ],
        [ANY, VMEM, ANY, VMEM] + [ANY] * 3,
        [VMEM] * 3 + [ANY] * 4,
        [
            vm((8, fc.shape[-1]), f32),
            vm((H, S, U, W), bf16),
            vm(fc.shape, bf16),
            vm(whole, bf16),
            vm(wo.shape, bf16),
            vm((S, D, D), bf16),
            vm((D, D), bf16),
            vm((S, R, D), bf16),
            vm((S, R, D), bf16),
            vm((S, R, D), f32),
            vm((S, U, D), bf16),
            vm((R, D), bf16),
            vm((R, D), f32),
            vm((R, D), f32),
            vm((R, D), bf16),
            vm((D, R), bf16),
            vm((R, D), f32),
            vm((R, D), f32),
            vm((R, D), bf16),
            vm((H, S, U, W), bf16),
            vm(fc.shape, bf16),
            vm(whole, bf16),
            vm(wo.shape, bf16),
        ],
        6 + 3 * S,
        "middle",
        60 << 20,
    )(low, x, g, vecs, fc, proj, wo)


def norm_back(x, t, gain, grad):
    mean = jnp.mean(x, axis=-1, keepdims=True)
    center = x - mean
    rstd = lax.rsqrt(jnp.mean(center * center, axis=-1, keepdims=True) + 1e-05)
    z = center * rstd
    e = t * gain
    inner = e - jnp.mean(e, axis=-1, keepdims=True) - z * jnp.mean(e * z, axis=-1, keepdims=True)
    return grad + rstd * inner


def finish_kernel(
    gm_ref, w_ref, norm_in, x_in, gmid_in, line_ref, small_ref,
    gh_ref, gqkv_ref, own_ref,
    norm_ref, x_ref, gmid_ref, gq_ref, t_ref, one, two, hid, gw, gw_c, gw_z, gw_sum, vec, send, recv, local,
):
    f32, bf16 = jnp.float32, jnp.bfloat16
    loads = [
        pltpu.make_async_copy(a, b, local.at[8 + i])
        for i, (a, b) in enumerate(((norm_in, norm_ref), (x_in, x_ref), (gmid_in, gmid_ref)))
    ]
    for c in loads:
        c.start()
    ex = Exchange(send, recv)
    s, h, r, n = ex.s, ex.h, ex.r, ex.planes
    half = n // 2
    H, N = gm_ref.shape[1], gm_ref.shape[3]
    U, D = t_ref.shape[2], t_ref.shape[3]
    W = N // 3
    d = gw.shape[3]
    ex.greet([ex.X, ex.Y, ex.D, ex.C] + ex.Z[1:])
    i1, i1b, i2, ih, ic, iz, iq = (ex.slots(n) for _ in range(7))
    iv = ex.slots(3 + n)
    acc = [jnp.zeros((1, D), f32), jnp.zeros((1, D), f32)]
    way = lambda j: (ex.X, ex.xn, ex.Y, ex.yn) if by_x(0, j) else (ex.Y, ex.yn, ex.X, ex.xn)

    def product(j, pair):
        t = ex.z(j)
        g = jnp.concatenate([gm_ref[t, to] for to in pair], axis=0)
        prod = lax.dot_general(g, w_ref[...], (((1,), (1,)), ((), ())), preferred_element_type=f32)
        for k, to in enumerate(pair):
            part = prod[k * U : (k + 1) * U]
            t_ref[t, to] = part.astype(bf16)
            acc[0] += jnp.sum(part * norm_ref[t, to].astype(f32), axis=0, keepdims=True)
            acc[1] += jnp.sum(part, axis=0, keepdims=True)

    def leave(j):
        peer, near, _, _ = way(j)
        ex.put(i1b[j], t_ref.at[ex.z(j), ex.dn], one.at[j, 1], peer)
        ex.put(i1[j], t_ref.at[ex.z(j), near], one.at[j, 0], peer)

    def relay(j):
        t = ex.z(j)
        _, _, peer, other = way(j)
        ex.got(i1b[j], one.at[j, 1])
        t_ref[t, other] = (t_ref[t, other].astype(f32) + one[j, 1].astype(f32)).astype(bf16)
        ex.put(i2[j], t_ref.at[t, other], two.at[j], peer)

    g_all = gm_ref[...].reshape(n * H * U, N)
    def qkv_rows(t0):
        width = H * 2 * d
        nt = norm_ref[:, :, :, t0 * width : (t0 + half) * width].reshape(n * H * U, half * width)
        part = lax.dot_general(nt, g_all, (((0,), (0,)), ((), ())), preferred_element_type=f32)
        gw[t0 : t0 + half] = part.reshape(half, H, 2, d, N).astype(bf16)
        for t in range(t0, t0 + half):
            ex.put(ic[t], gw.at[t, :, 1 - r], gw_c.at[t], ex.C)

    def done(j):
        t = ex.z(j)
        ex.got(i1[j], one.at[j, 0])
        ex.got(i2[j], two.at[j])
        total = t_ref[t, h].astype(f32) + one[j, 0].astype(f32) + two[j].astype(f32)
        hid[t] = norm_back(x_ref[t].astype(f32), total, line_ref[0:1], gmid_ref[t]).astype(bf16)
        if j:
            ex.put(ih[j], hid.at[t], gh_ref.at[s], ex.Z[j])

    loads[0].wait()
    for j in (1, 2):
        product(j, (ex.dn, way(j)[1]))
        leave(j)
    qkv_rows(0)
    qkv_rows(half)
    for j in (1, 2):
        product(j, (way(j)[3], h))
    for t in range(n):
        ex.got(ic[t], gw_c.at[t])
        gw_c[t] = (gw_c[t].astype(f32) + gw[t, :, r].astype(f32)).astype(bf16)
    for j in range(1, n):
        ex.put(iz[j], gw_c.at[ex.z(j)], gw_z.at[s], ex.Z[j])
    relay(1)
    relay(2)
    for j in (3, 0):
        product(j, (ex.dn, way(j)[1]))
        leave(j)
    for j in (3, 0):
        product(j, (way(j)[3], h))
    cols = jnp.sum(g_all.astype(f32), axis=0, keepdims=True)
    lane = lax.broadcasted_iota(jnp.int32, (1, D), 1) // W

    def placed(c):
        return jnp.where(lane == h, jnp.concatenate([c] * H, axis=1), 0.0)

    vec[0, 0:1] = acc[0]
    vec[0, 1:2] = acc[1]
    vec[0, 2:3] = placed(cols[:, :W])
    vec[0, 3:4] = placed(cols[:, 2 * W :])
    vec[0, 4:8] = jnp.zeros((4, D), f32)
    vec[0, 8:] = small_ref[...]
    ex.put(iv[0], vec.at[0], vec.at[1], ex.C)

    loads[1].wait()
    loads[2].wait()
    done(1)
    done(2)
    ex.got(iv[0], vec.at[1])
    vec[2] = vec[0] + vec[1]
    ex.put(iv[1], vec.at[2], vec.at[3], ex.X)
    relay(3)
    relay(0)
    ex.got(iv[1], vec.at[3])
    vec[4] = vec[2] + vec[3]
    ex.put(iv[2], vec.at[4], vec.at[5], ex.Y)
    total = gw_c[s].astype(f32)
    for j in range(1, n):
        ex.got(iz[n - j], gw_z.at[ex.z(j)])
        total += gw_z[ex.z(j)].astype(f32)
    gw_sum[...] = total
    for k, (peer, to) in enumerate(((ex.X, ex.xn), (ex.Y, ex.yn), (ex.D, ex.dn))):
        ex.put(iq[k], gw_sum.at[to], gq_ref.at[h], peer)
    mine = pltpu.make_async_copy(gw_sum.at[h], gq_ref.at[h], local.at[2])
    mine.start()
    ex.got(iv[2], vec.at[5])
    vec[6] = vec[4] + vec[5]
    for j in range(1, n):
        ex.put(iv[2 + j], vec.at[6], vec.at[6 + j], ex.Z[j])
    done(3)
    done(0)
    gh_ref[s] = hid[s]
    for j in range(1, n):
        ex.got(iv[2 + j], vec.at[6 + j])
    sums = vec[6] + vec[7] + vec[8] + vec[9]
    gain = (sums[0:1] - line_ref[1:2] * sums[1:2]) / line_ref[0:1]
    rows = jnp.concatenate([gain, sums[1:12], jnp.zeros((4, D), f32)], axis=0)
    wide = jnp.zeros((1, D), f32)
    for k in range(n):
        wide = jnp.where(s == k, sums[12 + k : 13 + k], wide)
    at = h * 2 + r
    begin = (s * H * 2 + at) * d
    own_ref[...] = pltpu.roll(rows, lax.rem(D - begin, D), 1)[:, :128]
    own_ref[12:13] = pltpu.roll(jnp.broadcast_to(wide, (8, D)), lax.rem(D - at * n * d, D), 1)[0:1, :128]
    for k, frm in enumerate((ex.xn, ex.yn, ex.dn)):
        ex.got(iq[k], gq_ref.at[frm])
    mine.wait()
    for k in range(H):
        for c in range(3):
            gqkv_ref[:, c * D + k * W : c * D + (k + 1) * W] = gq_ref[k, :, c * W : (c + 1) * W]
    for j in range(1, n):
        ex.got(ih[n - j], gh_ref.at[ex.z(j)])
    ex.close()


def finish(gm, w, norm, x, gmid, lines, small):
    S, H, U, N = gm.shape
    D = w.shape[0]
    Q = lax.axis_size("r")
    d = D // (S * H * Q)
    f32, bf16 = jnp.float32, jnp.bfloat16
    return remote_call(
        finish_kernel,
        3,
        [
            jax.ShapeDtypeStruct((S, U, D), bf16),
            jax.ShapeDtypeStruct((d, H * N), f32),
            jax.ShapeDtypeStruct((16, 128), f32),
        ],
        [VMEM] * 2 + [ANY] * 3 + [VMEM] * 2,
        [VMEM, VMEM, VMEM],
        [
            pltpu.VMEM(norm.shape, bf16),
            pltpu.VMEM(x.shape, bf16),
            pltpu.VMEM(gmid.shape, f32),
            pltpu.VMEM((H, d, N), f32),
            pltpu.VMEM((S, H, U, D), bf16),
            pltpu.VMEM((S, 2, U, D), bf16),
            pltpu.VMEM((S, U, D), bf16),
            pltpu.VMEM((S, U, D), bf16),
            pltpu.VMEM((S, H, Q, d, N), bf16),
            pltpu.VMEM((S, H, d, N), bf16),
            pltpu.VMEM((S, H, d, N), bf16),
            pltpu.VMEM((H, d, N), f32),
            pltpu.VMEM((10, 16, D), f32),
        ],
        8 * S + 3,
        "finish",
    )(gm, w, norm, x, gmid, lines, small)


def planes(
    hidden_in,
    block_pairs,
    ln1_gain,
    ln1_bias,
    qkv_weight,
    query_bias,
    value_bias,
    out_weight,
    out_bias,
    ln2_gain,
    ln2_bias,
    fc_weight,
    fc_bias,
    proj_weight,
    proj_bias,
    out_grad,
):
    f32, bf16 = jnp.float32, jnp.bfloat16
    s, h, r = (lax.axis_index(a) for a in AXES)
    S, H, Q = (lax.axis_size(a) for a in AXES)
    rows, D = hidden_in.shape
    U = rows // SEQS
    W = D // H
    bfn = fc_bias.shape[0]
    d = qkv_weight.shape[0]
    lines = [ln1_gain, ln1_bias, query_bias, value_bias, out_bias, ln2_gain, ln2_bias, proj_bias, fc_bias]
    blk = block_pairs[::2]
    blk = jnp.where(s % 2 == 0, blk, blk.shape[0] - 1 - blk)
    blk = blk.astype(jnp.int32)
    npair = blk.shape[0]
    inv = jnp.sum(
        jnp.where(blk[None, :] == jnp.arange(npair)[:, None], jnp.arange(npair)[None, :], 0), axis=1
    ).astype(jnp.int32)
    normed, q_all, kv_all, w_h, x_own, vecs, att_low, lse, w_fc, w_out, w_proj = forward(
        inv,
        blk,
        hidden_in.reshape(S, U, D),
        qkv_weight,
        [v[None] for v in lines],
        fc_weight,
        out_weight,
        proj_weight,
    )
    layer_out, grad_middle, small, g_att, grad_fc, grad_proj, grad_wout = middle(
        att_low.reshape(S, H, U, W),
        x_own.reshape(rows, D),
        out_grad.reshape(S, U, D),
        vecs,
        w_fc,
        w_proj,
        w_out,
    )
    grad_mixed, layer_out, gfc, gproj, gout = attend_back(
        inv,
        blk,
        q_all,
        kv_all.reshape(npair, Q * U, 2 * W),
        g_att.reshape(npair, U, W),
        att_low,
        lse,
        layer_out.reshape(S, U, D),
        grad_fc,
        grad_proj,
        grad_wout,
    )
    grad_hidden, gq, own = finish(
        grad_mixed.reshape(S, H, U, 3 * W),
        w_h,
        normed,
        x_own,
        grad_middle.reshape(S, U, D),
        vecs,
        small,
    )
    g1s, b1s, bqs, bvs = (own[i, :d] for i in range(4))
    bos, g2s, b2s, bps = (own[i, :d] for i in range(8, 12))
    return (
        layer_out.reshape(rows, D),
        grad_hidden.reshape(rows, D),
        g1s,
        b1s,
        gq,
        bqs,
        bvs,
        gout,
        bos,
        g2s,
        b2s,
        gfc,
        own[12, :bfn],
        gproj,
        bps,
    )


def solution(mesh):
    n = mesh.shape["ctx"]
    if n // (PLANES * SEQS) != 2:
        return solution_any(mesh)
    split = Mesh(mesh.devices.reshape(PLANES, SEQS, -1), AXES)
    row, vec = P(AXES, None), P(AXES)
    return jax.shard_map(
        planes,
        mesh=split,
        in_specs=(row, P(), vec, vec, row, vec, vec, row, vec, vec, vec, row, vec, row, vec, row),
        out_specs=(row, row, vec, vec, row, vec, vec, row, vec, vec, vec, row, vec, row, vec),
        check_vma=False,
    )
```
